32 devices in a mesh: mode: 4 (over y, x), mer: 8 (over z, core).
Axes of the slice: x: 2, y: 2, z: 4, core: 2. Of those that a mesh axis runs over, the one named last changes fastest.
Arguments:
- mode_fields: bfloat16 [12, 128, 2, 16384], P(None, 'mode', None, 'mer'), may hold values from -0.5 to 0.5
- radius: float32 [16384], P('mer'), may hold values from 1 to 4
- radial_blocks: bfloat16 [5, 64, 16384], P(None, None, 'mer'), may hold values from -6 to 6
- axial_blocks: bfloat16 [5, 64, 16384], P(None, None, 'mer'), may hold values from -6 to 6
- block_columns: int32 [256, 5], P('mer'), may hold values from 0 to 39, as said below
- interface_nodes: int32 [16, 256], P('mer'), may hold values from 0 to 2047, as said below
Outputs:
- induction: float32 [3, 128, 2, 16384], P(None, 'mode', None, 'mer')
- momentum: float32 [3, 128, 2, 16384], P(None, 'mode', None, 'mer')
The draws below stay inside these ranges and needn't reach their ends.
Inputs may be any that keep to these rules, and one draw needn't show every extreme that they name: `block_columns`: indices into the extended list of a subdomain's block row: its 2048 nodes, then the 256 nodes received from the previous subdomain, then the 256 from the next, counted in blocks of 64. `interface_nodes`: row 2 d lists the local nodes subdomain d sends to subdomain d - 1, row 2 d + 1 those it sends to d + 1; each row holds 256 distinct local node indices.
All inputs are finite; a program needn't handle non-finite values.
Results may differ from the reference program's by a relative error of at most 0.0057.
Values may be sent and summed in bfloat16 or wider, within the bound.
No kernel may reach another device: no remote copies, remote signals or barrier semaphores. Data moves between devices by JAX's collectives and lax.ppermute only.
A program may use at most 64 MiB of HBM per device.

```python
import math
import jax
import jax.numpy as jnp
from jax import lax

M = 128
THETA = 256
NODE_DEV = 2048
BLK = 64
NNZB = 5
HALO = 256
NODES = 16384
N_MER = 8


def draw_block_columns(key, part):
    key = jax.random.fold_in(key, 11)
    row_total = NODES // BLK
    block_rows = NODE_DEV // BLK
    halo_blocks = HALO // BLK
    extent = block_rows + 2 * halo_blocks
    within = jnp.arange(row_total, dtype=jnp.int32) % block_rows
    before = jnp.where(within > 0, within - 1, block_rows + halo_blocks - 1)
    after = jnp.where(within < block_rows - 1, within + 1, block_rows + halo_blocks)
    distant = jax.random.randint(key, (row_total, 2), 0, extent, dtype=jnp.int32)
    second = jnp.where(within == 0, extent - 1, distant[:, 1])
    return jnp.stack([within, before, after, distant[:, 0], second], axis=1).astype(jnp.int32)


def draw_interface_nodes(key, part):
    key = jax.random.fold_in(key, 23)
    keys = jax.random.split(key, 2 * N_MER)

    def one_row(row_key):
        shuffled = jax.random.permutation(row_key, NODE_DEV - 2).astype(jnp.int32) + 1
        first = jnp.zeros((1,), jnp.int32)
        final = jnp.full((1,), NODE_DEV - 1, jnp.int32)
        return jnp.concatenate([first, shuffled[:HALO - 2], final])
    return jax.vmap(one_row)(keys).astype(jnp.int32)


def shard_levels(key, shape, cuts, smallest, top_value):
    def one(axis_at, shards_of):
        steps = jax.random.uniform(jax.random.fold_in(jax.random.fold_in(key, 6), axis_at), (shards_of,), jnp.float32, smallest / len(cuts), top_value / len(cuts))
        return jnp.repeat(jnp.exp(steps), shape[axis_at] // shards_of).reshape((-1,) + (1,) * (len(shape) - axis_at - 1))

    factor_of = one(*cuts[0])
    for cut in cuts[1:]:
        factor_of = factor_of * one(*cut)
    return factor_of


def scatter_about(own_key, shape, width, reach, cuts=(), kind=jnp.bfloat16):
    factor_of = shard_levels(own_key, shape, cuts, -0.22, 0.18) if cuts else 1.0
    values = jax.random.normal(own_key, shape, jnp.float32) * width * factor_of
    return jnp.minimum(jnp.maximum(values, -reach), reach).astype(kind)


def setup_inputs(seed: int = 0) -> dict:
    seeds = jax.random.split(jax.random.key(seed), 7)
    mode_fields = scatter_about(seeds[0], (12, M, 2, NODES), 0.0625, 0.5, ((1, 4), (3, 8)))
    radius = jnp.clip(jnp.exp(math.log(4.0) - 1.3862944 * jax.random.uniform(seeds[1], (NODES,), jnp.float32) ** shard_levels(seeds[1], (NODES,), ((0, 8),), -0.2, 0.2)), 1.0, 4.0)
    radial_blocks = scatter_about(seeds[2], (NNZB, BLK, NODES), 1.0, 6.0, ((2, 8),))
    axial_blocks = scatter_about(seeds[3], (NNZB, BLK, NODES), 1.0, 6.0, ((2, 8),))
    block_columns = draw_block_columns(jax.random.fold_in(seeds[6], 71), 0)
    interface_nodes = draw_interface_nodes(jax.random.fold_in(seeds[6], 71), 0)
    return {"mode_fields": mode_fields, "radius": radius, "radial_blocks": radial_blocks, "axial_blocks": axial_blocks, "block_columns": block_columns, "interface_nodes": interface_nodes}


def tables(mode_total, angle_total):
    mode_ids = jnp.arange(mode_total, dtype=jnp.int32)
    angle_ids = jnp.arange(angle_total, dtype=jnp.int32)
    phase = (angle_ids[:, None] * mode_ids[None, :]) % angle_total
    angle = phase.astype(jnp.float32) * (2.0 * math.pi / angle_total)
    weight = jnp.where(mode_ids == 0, 1.0, 2.0).astype(jnp.float32)
    cosines = jnp.cos(angle)
    sines = jnp.sin(angle)
    inverse = jnp.stack([weight * cosines, -weight * sines], axis=-1).astype(jnp.bfloat16)
    forward = (jnp.stack([cosines.T, -sines.T], axis=1) / angle_total).astype(jnp.bfloat16)
    return inverse, forward


def cross_product(first, second):
    return jnp.stack([first[1] * second[2] - first[2] * second[1],
                      first[2] * second[0] - first[0] * second[2],
                      first[0] * second[1] - first[1] * second[0]])


def nonlinear(received, inverse, forward):
    physical = jnp.einsum('tmp,cmpn->ctn', inverse.astype(jnp.float32), received.astype(jnp.float32))
    velocity = physical[0:3]
    magnetic = physical[3:6]
    current = physical[6:9]
    vorticity = physical[9:12]
    energy = 0.5 * jnp.sum(velocity * velocity, axis=0, keepdims=True)
    lorentz = cross_product(current, magnetic) + cross_product(velocity, vorticity)
    products = jnp.concatenate([cross_product(velocity, magnetic), energy, lorentz], axis=0).astype(jnp.bfloat16)
    return jnp.einsum('mpt,ctn->cmpn', forward.astype(jnp.float32), products.astype(jnp.float32)).astype(jnp.bfloat16)


def rotated(values, mode_values):
    return jnp.stack([-mode_values[:, None] * values[:, 1], mode_values[:, None] * values[:, 0]], axis=1)


def derive(extended, local, radial_part, axial_part, columns, radius, mode_values):
    mode_count = local.shape[1]
    node_count = local.shape[3]
    block_count = node_count // BLK
    vectors = extended.reshape(4 * mode_count * 2, extended.shape[3] // BLK, BLK)
    picked = vectors[:, columns].astype(jnp.float32)
    radial_four = radial_part.reshape(NNZB, BLK, block_count, BLK).astype(jnp.float32)
    axial_four = axial_part.reshape(NNZB, BLK, block_count, BLK).astype(jnp.float32)
    along_r = jnp.einsum('vbkc,kcbr->vbr', picked, radial_four).reshape(4, mode_count, 2, node_count)
    along_z = jnp.einsum('vbkc,kcbr->vbr', picked, axial_four).reshape(4, mode_count, 2, node_count)
    values = local.astype(jnp.float32)
    inv_radius = 1.0 / radius
    induction = jnp.stack([
        rotated(values[2], mode_values) * inv_radius - along_z[1],
        along_z[0] - along_r[2],
        along_r[1] + values[1] * inv_radius - rotated(values[0], mode_values) * inv_radius])
    momentum = jnp.stack([
        values[4] - along_r[3],
        values[5] - rotated(values[3], mode_values) * inv_radius,
        values[6] - along_z[3]])
    return induction, momentum


def reference(mode_fields, radius, radial_blocks, axial_blocks, block_columns, interface_nodes):
    inverse, forward = tables(M, THETA)
    groups = jnp.moveaxis(mode_fields.reshape(12, M, 2, N_MER, NODE_DEV), 3, 0)
    terms = lax.map(lambda group: nonlinear(group, inverse, forward), groups)
    mode_values = jnp.arange(M, dtype=jnp.int32).astype(jnp.float32)
    block_rows = NODE_DEV // BLK

    def one_domain(device):
        local = terms[device]
        prev_dev = jnp.maximum(device - 1, 0)
        next_dev = jnp.minimum(device + 1, N_MER - 1)
        from_prev = terms[prev_dev, 0:4][..., interface_nodes[2 * prev_dev + 1]] * (device > 0).astype(jnp.bfloat16)
        from_next = terms[next_dev, 0:4][..., interface_nodes[2 * next_dev]] * (device < N_MER - 1).astype(jnp.bfloat16)
        extended = jnp.concatenate([local[0:4], from_prev, from_next], axis=3)
        columns = lax.dynamic_slice_in_dim(block_columns, device * block_rows, block_rows, 0)
        radial_part = lax.dynamic_slice_in_dim(radial_blocks, device * NODE_DEV, NODE_DEV, 2)
        axial_part = lax.dynamic_slice_in_dim(axial_blocks, device * NODE_DEV, NODE_DEV, 2)
        local_radius = lax.dynamic_slice_in_dim(radius, device * NODE_DEV, NODE_DEV, 0)
        return derive(extended, local, radial_part, axial_part, columns, local_radius, mode_values)

    induction, momentum = lax.map(one_domain, jnp.arange(N_MER, dtype=jnp.int32))
    induction = jnp.moveaxis(induction, 0, 3).reshape(3, M, 2, NODES)
    momentum = jnp.moveaxis(momentum, 0, 3).reshape(3, M, 2, NODES)
    return induction, momentum
```

```python
import functools
import math

import jax
import jax.numpy as jnp
import ml_dtypes
import numpy as np
from jax import lax
from jax.experimental import pallas as pl
from jax.experimental.pallas import tpu as pltpu
from jax.sharding import PartitionSpec as P

M = 128
THETA = 256
BLK = 64
NNZB = 5
LANES = 128
VMEM_LIMIT = 40 * 1024 * 1024


def params():
    return pltpu.CompilerParams(vmem_limit_bytes=VMEM_LIMIT)


def vmem():
    return pl.BlockSpec(memory_space=pltpu.VMEM)


def cost(flops, read_written):
    return pl.CostEstimate(flops=int(flops), bytes_accessed=int(read_written), transcendentals=0)


def dest_of(me, step, count):
    if count & (count - 1) == 0:
        return jnp.bitwise_xor(me, step)
    return lax.rem(me + step, count)


def source_of(me, step, count):
    if count & (count - 1) == 0:
        return jnp.bitwise_xor(me, step)
    return lax.rem(me + count - step, count)


def exchange(pieces):
    count = len(pieces)
    power = count & (count - 1) == 0
    received = [pieces[0]]
    for step in range(1, count):
        pairs = [(i, i ^ step if power else (i + step) % count) for i in range(count)]
        received.append(lax.ppermute(pieces[step], "mode", pairs))
    return received


def from_behind(value, axis, steps):
    count = lax.axis_size(axis)
    initial, last = (max(0, -steps), min(count, count - steps))
    return lax.ppermute(value, axis, [(source, source + steps) for source in range(initial, last)])


def tables(mode_total, angle_total, share_count):
    mode_ids = np.arange(mode_total)
    angle_ids = np.arange(angle_total)
    phase = angle_ids[:, None] * mode_ids[None, :] % angle_total
    angle = phase.astype(np.float32) * np.float32(2.0 * math.pi / angle_total)
    weight = np.where(mode_ids == 0, 1.0, 2.0).astype(np.float32)
    cosines = np.cos(angle)
    sines = np.sin(angle)
    inverse = np.stack([weight * cosines, -weight * sines], axis=-1).astype(ml_dtypes.bfloat16)
    forward = np.stack([cosines.T, -sines.T], axis=1) / np.float32(angle_total)
    forward = forward.reshape(share_count, mode_total // share_count, 2, angle_total)
    forward = forward.transpose(0, 2, 1, 3).reshape(2 * mode_total, angle_total).astype(ml_dtypes.bfloat16)
    return (inverse.reshape(angle_total, 2 * mode_total), forward)


def pack_kernel(count, tiles, x_ref, *out_refs):
    me = lax.axis_index("mode")
    for step in range(count):
        share = dest_of(me, step, count)
        for t in range(tiles):
            start = pl.multiple_of((share * tiles + t) * LANES, LANES)
            out_refs[step][0, t] = x_ref[0, :, :, pl.ds(start, LANES)]


def pack(fields, first, components, count):
    _, mode_count, _, width = fields.shape
    tiles = width // count // LANES
    shape = (components, tiles, mode_count, 2, LANES)
    size = components * mode_count * 2 * width * 2
    return pl.pallas_call(
        functools.partial(pack_kernel, count, tiles),
        grid=(components,),
        in_specs=[pl.BlockSpec((1, mode_count, 2, width), lambda c: (c + first, 0, 0, 0))],
        out_specs=[pl.BlockSpec((1,) + shape[1:], lambda c: (c, 0, 0, 0, 0))] * count,
        out_shape=[jax.ShapeDtypeStruct(shape, jnp.bfloat16)] * count,
        compiler_params=params(),
        cost_estimate=cost(0, 2 * size),
    )(fields)


def cross(a, b):
    return [a[1] * b[2] - a[2] * b[1], a[2] * b[0] - a[0] * b[2], a[0] * b[1] - a[1] * b[0]]


def to_physical(count, in_refs, inverse, x_ref, store):
    me = lax.axis_index("mode")
    components, tiles, rows, _ = in_refs[0].shape
    for step in range(count):
        at = pl.multiple_of(source_of(me, step, count) * rows, rows)
        for c in range(components):
            for t in range(tiles):
                x_ref[c, pl.ds(at, rows), t * LANES : (t + 1) * LANES] = in_refs[step][c, t]
    for c in range(components):
        store(c, jnp.dot(inverse, x_ref[c], preferred_element_type=jnp.float32))


def to_modes(count, forward_ref, table_ref, product_ref, out_refs):
    me = lax.axis_index("mode")
    components, tiles, rows, _ = out_refs[0].shape
    for step in range(count):
        at = pl.multiple_of(dest_of(me, step, count) * rows, rows)
        table_ref[step * rows : (step + 1) * rows] = forward_ref[pl.ds(at, rows)]
    for c in range(components):
        terms = jnp.dot(table_ref[...], product_ref[c], preferred_element_type=jnp.float32)
        terms = terms.astype(jnp.bfloat16)
        for step in range(count):
            for t in range(tiles):
                out_refs[step][c, t] = terms[step * rows : (step + 1) * rows, t * LANES : (t + 1) * LANES]


CHUNK = 32


def first_kernel(count, *refs):
    in_refs, (inverse_ref, forward_ref) = refs[:count], refs[count : count + 2]
    out_refs, (physical_ref, x_ref, product_ref, table_ref) = refs[count + 2 : 2 * count + 2], refs[2 * count + 2 :]

    def store(c, value):
        physical_ref[c] = value

    to_physical(count, in_refs, inverse_ref[...], x_ref, store)
    for i in range(THETA // CHUNK):
        at = slice(i * CHUNK, (i + 1) * CHUNK)
        velocity = [physical_ref[c, at] for c in range(3)]
        magnetic = [physical_ref[c, at] for c in range(3, 6)]
        energy = 0.5 * (velocity[0] * velocity[0] + velocity[1] * velocity[1] + velocity[2] * velocity[2])
        for c, value in enumerate(cross(velocity, magnetic) + [energy]):
            product_ref[c, at] = value.astype(jnp.bfloat16)
    to_modes(count, forward_ref, table_ref, product_ref, out_refs)


def second_kernel(count, *refs):
    in_refs, (first_ref, inverse_ref, forward_ref) = refs[:count], refs[count : count + 3]
    out_refs, (physical_ref, x_ref, product_ref, table_ref) = refs[count + 3 : 2 * count + 3], refs[2 * count + 3 :]

    def store(c, value):
        physical_ref[c] = value

    to_physical(count, in_refs, inverse_ref[...], x_ref, store)
    for i in range(THETA // CHUNK):
        at = slice(i * CHUNK, (i + 1) * CHUNK)
        velocity = [first_ref[c, at] for c in range(3)]
        magnetic = [first_ref[c, at] for c in range(3, 6)]
        current = [physical_ref[c, at] for c in range(3)]
        vorticity = [physical_ref[c, at] for c in range(3, 6)]
        lorentz = [a + b for a, b in zip(cross(current, magnetic), cross(velocity, vorticity))]
        for c, value in enumerate(lorentz):
            product_ref[c, at] = value.astype(jnp.bfloat16)
    to_modes(count, forward_ref, table_ref, product_ref, out_refs)


def physics(kernel, received, extra, inverse, forward, outputs, keep):
    count = len(received)
    components, tiles, rows, _ = received[0].shape
    group = 2 if tiles % 2 == 0 else 1
    steps = tiles // group
    width = group * LANES
    share = tiles * LANES
    in_block = pl.BlockSpec((components, group, rows, LANES), lambda i: (0, i, 0, 0))
    out_block = pl.BlockSpec((outputs, group, rows, LANES), lambda i: (0, i, 0, 0))
    whole = pl.BlockSpec((THETA, 2 * M), lambda i: (0, 0))
    turned = pl.BlockSpec((2 * M, THETA), lambda i: (0, 0))
    kept = pl.BlockSpec((6, THETA, width), lambda i: (0, 0, i))
    kept_shape = jax.ShapeDtypeStruct((6, THETA, share), jnp.float32)
    scratch = [
        pltpu.VMEM((components, 2 * M, width), jnp.bfloat16),
        pltpu.VMEM((outputs, THETA, width), jnp.bfloat16),
        pltpu.VMEM((2 * M, THETA), jnp.bfloat16),
    ]
    if not keep:
        scratch = [pltpu.VMEM((components, THETA, width), jnp.float32)] + scratch
    out_shape = [jax.ShapeDtypeStruct((outputs, tiles, rows, LANES), jnp.bfloat16)] * count
    flops = 2 * THETA * 2 * M * share * (components + outputs)
    moved = (components + outputs) * share * 2 * M * 2 + 6 * THETA * share * 4
    return pl.pallas_call(
        functools.partial(kernel, count),
        grid=(steps,),
        in_specs=[in_block] * count + [kept] * len(extra) + [whole, turned],
        out_specs=[out_block] * count + ([kept] if keep else []),
        out_shape=out_shape + ([kept_shape] if keep else []),
        scratch_shapes=scratch,
        compiler_params=params(),
        cost_estimate=cost(flops, moved),
    )(*received, *extra, inverse, forward)


def interface_kernel(count, *refs):
    in_refs, (nodes_ref,), (prev_ref, next_ref) = refs[:count], refs[count : count + 1], refs[count + 1 :]
    me = lax.axis_index("mode")
    components, tiles, rows, _ = in_refs[0].shape
    halo = nodes_ref.shape[1]
    totals = [jnp.zeros((components * rows, halo), jnp.float32) for _ in range(2)]
    inner = lax.broadcasted_iota(jnp.int32, (LANES, halo), 0)
    for step in range(count):
        share = source_of(me, step, count)
        for t in range(tiles):
            ids = inner + (share * tiles + t) * LANES
            values = in_refs[step][:, t].reshape(components * rows, LANES)
            for way in range(2):
                chosen = jnp.where(ids == nodes_ref[way : way + 1, :], 1.0, 0.0).astype(jnp.bfloat16)
                totals[way] += jnp.dot(values, chosen, preferred_element_type=jnp.float32)
    for out_ref, total in zip((prev_ref, next_ref), totals):
        picked = total.astype(jnp.bfloat16)
        for c in range(components):
            for t in range(halo // LANES):
                out_ref[c, t] = picked[c * rows : (c + 1) * rows, t * LANES : (t + 1) * LANES]


def interface(received, interface_nodes):
    count = len(received)
    components, tiles, rows, _ = received[0].shape
    halo = interface_nodes.shape[1]
    shape = jax.ShapeDtypeStruct((components, halo // LANES, rows, LANES), jnp.bfloat16)
    width = count * tiles * LANES
    return pl.pallas_call(
        functools.partial(interface_kernel, count),
        in_specs=[vmem()] * (count + 1),
        out_specs=[vmem()] * 2,
        out_shape=[shape] * 2,
        compiler_params=params(),
        cost_estimate=cost(2 * components * rows * width * 2 * halo, components * rows * width * 4),
    )(*received, interface_nodes)


def derive_kernel(count, *refs):
    in_refs = refs[:count]
    prev_ref, next_ref, radial_ref, axial_ref, radius_ref, columns_ref = refs[count : count + 6]
    induction_ref, momentum_ref, extended_ref = refs[count + 6 :]
    me = lax.axis_index("mode")
    components, tiles, rows, _ = in_refs[0].shape
    mode_count = rows // 2
    node_tiles = count * tiles
    halo_tiles = prev_ref.shape[1]
    for step in range(count):
        share = source_of(me, step, count)
        for t in range(tiles):
            extended_ref[share * tiles + t] = in_refs[step][:, t].reshape(components * rows, LANES)
    for t in range(halo_tiles):
        extended_ref[node_tiles + t] = prev_ref[:, t].reshape(components * rows, LANES)
        extended_ref[node_tiles + halo_tiles + t] = next_ref[:, t].reshape(components * rows, LANES)
    modes = (lax.broadcasted_iota(jnp.int32, (mode_count, LANES), 0) + me * mode_count).astype(jnp.float32)
    lane = lax.broadcasted_iota(jnp.int32, (1, 2 * LANES), 1)
    in_first = jnp.where(lax.rem(lane, LANES) < BLK, 1.0, 0.0)
    in_half = [in_first, 1.0 - in_first]

    def rotated(values):
        return jnp.concatenate([-modes * values[mode_count:], modes * values[:mode_count]], axis=0)

    def pair(b, carry):
        here = pl.ds(pl.multiple_of(b * LANES, LANES), LANES)
        total = jnp.zeros((components * rows, 2 * LANES), jnp.float32)
        for k in range(NNZB):
            weights = jnp.concatenate([radial_ref[k, :, here], axial_ref[k, :, here]], axis=1)
            left, right = [], []
            for half in range(2):
                column = columns_ref[2 * b + half, k]
                odd = lax.rem(column, 2).astype(jnp.float32)
                left.append(extended_ref[lax.div(column, 2)])
                right.append(weights * (in_half[half] * (1.0 - odd)).astype(jnp.bfloat16))
                right.append(weights * (in_half[half] * odd).astype(jnp.bfloat16))
            total += jnp.dot(
                jnp.concatenate(left, axis=1),
                jnp.concatenate(right, axis=0),
                preferred_element_type=jnp.float32,
            )
        along_r = [total[c * rows : (c + 1) * rows, :LANES] for c in range(components)]
        along_z = [total[c * rows : (c + 1) * rows, LANES:] for c in range(components)]
        values = [extended_ref[b, c * rows : (c + 1) * rows].astype(jnp.float32) for c in range(components)]
        inv_radius = 1.0 / radius_ref[:, here]
        induction = [
            rotated(values[2]) * inv_radius - along_z[1],
            along_z[0] - along_r[2],
            along_r[1] + values[1] * inv_radius - rotated(values[0]) * inv_radius,
        ]
        stride = 2 * node_tiles
        for i, value in enumerate(induction):
            for p in range(2):
                induction_ref[pl.ds(i * mode_count * stride + 2 * b + p, mode_count, stride=stride), :] = value[
                    p * mode_count : (p + 1) * mode_count
                ]
        momentum_ref[0, b] = along_r[3]
        momentum_ref[1, b] = rotated(values[3]) * inv_radius
        momentum_ref[2, b] = along_z[3]
        return carry

    lax.fori_loop(0, node_tiles, pair, 0)


def derive(received, from_prev, from_next, radial_blocks, axial_blocks, radius, columns):
    count = len(received)
    components, tiles, rows, _ = received[0].shape
    node_tiles = count * tiles
    halo_tiles = from_prev.shape[1]
    out_rows = 3 * rows * node_tiles
    return pl.pallas_call(
        functools.partial(derive_kernel, count),
        in_specs=[vmem()] * (count + 5) + [pl.BlockSpec(memory_space=pltpu.SMEM)],
        out_specs=[vmem()] * 2,
        out_shape=[
            jax.ShapeDtypeStruct((out_rows, LANES), jnp.float32),
            jax.ShapeDtypeStruct((3, node_tiles, rows, LANES), jnp.float32),
        ],
        scratch_shapes=[pltpu.VMEM((node_tiles + 2 * halo_tiles, components * rows, LANES), jnp.bfloat16)],
        compiler_params=params(),
        cost_estimate=cost(
            2 * components * rows * node_tiles * 2 * LANES * 2 * LANES * NNZB,
            8 * out_rows * LANES + 4 * NNZB * BLK * node_tiles * LANES,
        ),
    )(*received, from_prev, from_next, radial_blocks, axial_blocks, radius, columns)


def momentum_kernel(count, *refs):
    in_refs, (gradient_ref, out_ref) = refs[:count], refs[count:]
    me = lax.axis_index("mode")
    _, tiles, rows, _ = in_refs[0].shape
    mode_count = rows // 2
    stride = 2 * count * tiles
    for step in range(count):
        share = source_of(me, step, count)
        for t in range(tiles):
            at = share * tiles + t
            value = in_refs[step][0, t].astype(jnp.float32) - gradient_ref[0, at]
            for p in range(2):
                out_ref[pl.ds(2 * at + p, mode_count, stride=stride), :] = value[
                    p * mode_count : (p + 1) * mode_count
                ]


def momentum_of(received, gradient):
    count = len(received)
    components, tiles, rows, _ = received[0].shape
    node_tiles = count * tiles
    out_rows = rows * node_tiles
    return pl.pallas_call(
        functools.partial(momentum_kernel, count),
        grid=(components,),
        in_specs=[pl.BlockSpec((1, tiles, rows, LANES), lambda c: (c, 0, 0, 0))] * count
        + [pl.BlockSpec((1, node_tiles, rows, LANES), lambda c: (c, 0, 0, 0))],
        out_specs=pl.BlockSpec((out_rows, LANES), lambda c: (c, 0)),
        out_shape=jax.ShapeDtypeStruct((components * out_rows, LANES), jnp.float32),
        compiler_params=params(),
        cost_estimate=cost(components * out_rows * LANES, components * out_rows * LANES * 10),
    )(*received, gradient)


def whole_output(value, mode_count, width):
    value = value.reshape(3, mode_count, width // LANES, 2, LANES)
    return value.transpose(0, 1, 3, 2, 4).reshape(3, mode_count, 2, width)


def body(mode_fields, radius, radial_blocks, axial_blocks, block_columns, interface_nodes):
    _, mode_count, _, width = mode_fields.shape
    count = lax.axis_size("mode")
    rows = 2 * mode_count
    inverse, forward = tables(M, THETA, count)
    inverse, forward = jnp.asarray(inverse), jnp.asarray(forward)

    def sent(first):
        pieces = exchange(pack(mode_fields, first, 6, count))
        return [piece.reshape(piece.shape[:2] + (rows, LANES)) for piece in pieces]

    flow = sent(0)
    sources = sent(6)
    *terms, physical = physics(first_kernel, flow, [], inverse, forward, 4, True)
    local = exchange(terms)
    toward_prev, toward_next = interface(local, interface_nodes)
    from_prev = from_behind(toward_next, "mer", 1)
    from_next = from_behind(toward_prev, "mer", -1)
    induction, gradient = derive(
        local, from_prev, from_next, radial_blocks, axial_blocks, radius.reshape(1, width), block_columns
    )
    lorentz = exchange(physics(second_kernel, sources, [physical], inverse, forward, 3, False))
    momentum = momentum_of(lorentz, gradient)
    return (whole_output(induction, mode_count, width), whole_output(momentum, mode_count, width))


def solution(mesh):
    placed = (
        P(None, "mode", None, "mer"),
        P("mer"),
        P(None, None, "mer"),
        P(None, None, "mer"),
        P("mer", None),
        P("mer", None),
    )
    return jax.shard_map(
        body,
        mesh=mesh,
        in_specs=placed,
        out_specs=(P(None, "mode", None, "mer"), P(None, "mode", None, "mer")),
        check_vma=False,
    )
```

```python
import functools
import math

import jax
import jax.numpy as jnp
import ml_dtypes
import numpy as np
from jax import lax
from jax.experimental import pallas as pl
from jax.experimental.pallas import tpu as pltpu
from jax.sharding import PartitionSpec as P

M = 128
THETA = 256
BLK = 64
NNZB = 5
LANES = 128
VMEM_LIMIT = 40 * 1024 * 1024
FIRST_LIMIT = 62 * 1024 * 1024


def params(limit=VMEM_LIMIT):
    return pltpu.CompilerParams(vmem_limit_bytes=limit)


def vmem():
    return pl.BlockSpec(memory_space=pltpu.VMEM)


def cost():
    return pl.CostEstimate(flops=1024, bytes_accessed=1024, transcendentals=0)


def dest_of(me, step, count):
    if count & (count - 1) == 0:
        return jnp.bitwise_xor(me, step)
    return lax.rem(me + step, count)


def source_of(me, step, count):
    if count & (count - 1) == 0:
        return jnp.bitwise_xor(me, step)
    return lax.rem(me + count - step, count)


def exchange(pieces):
    count = len(pieces)
    power = count & (count - 1) == 0
    received = [pieces[0]]
    for step in range(1, count):
        pairs = [(i, i ^ step if power else (i + step) % count) for i in range(count)]
        received.append(lax.ppermute(pieces[step], "mode", pairs))
    return received


def from_behind(value, axis, steps):
    count = lax.axis_size(axis)
    initial, last = (max(0, -steps), min(count, count - steps))
    return lax.ppermute(value, axis, [(source, source + steps) for source in range(initial, last)])


def tables(mode_total, angle_total, share_count):
    mode_ids = np.arange(mode_total)
    angle_ids = np.arange(angle_total)
    phase = angle_ids[:, None] * mode_ids[None, :] % angle_total
    angle = phase.astype(np.float32) * np.float32(2.0 * math.pi / angle_total)
    weight = np.where(mode_ids == 0, 1.0, 2.0).astype(np.float32)
    cosines = np.cos(angle)
    sines = np.sin(angle)
    inverse = np.stack([weight * cosines, -weight * sines], axis=-1).astype(ml_dtypes.bfloat16)
    forward = np.stack([cosines.T, -sines.T], axis=1) / np.float32(angle_total)
    forward = forward.reshape(share_count, mode_total // share_count, 2, angle_total)
    forward = forward.transpose(0, 2, 1, 3).reshape(2 * mode_total, angle_total).astype(ml_dtypes.bfloat16)
    return (inverse.reshape(angle_total, 2 * mode_total), forward)


def pack_kernel(count, first, fields_ref, *refs):
    me = lax.axis_index("mode")
    out_refs, sems = refs[:count], refs[-1]
    extra = refs[count:-1]
    components, tiles = out_refs[0].shape[:2]
    copies = []
    for step in range(count):
        share = dest_of(me, step, count)
        for t in range(tiles):
            start = pl.multiple_of((share * tiles + t) * LANES, LANES)
            source = fields_ref.at[pl.ds(first, components), :, :, pl.ds(start, LANES)]
            copies.append(pltpu.make_async_copy(source, out_refs[step].at[:, t], sems.at[step, t]))
    for copy in copies:
        copy.start()
    for source, target in zip(extra[: len(extra) // 2], extra[len(extra) // 2 :]):
        target[...] = source[...]
    for copy in copies:
        copy.wait()


def pack(fields, first, components, count, carried, limit):
    _, mode_count, _, width = fields.shape
    tiles = width // count // LANES
    shape = (components, tiles, mode_count, 2, LANES)

    def kernel(fields_ref, *refs):
        inputs, rest = refs[: len(carried)], refs[len(carried) :]
        pack_kernel(count, first, fields_ref, *rest[:count], *inputs, *rest[count:])

    return pl.pallas_call(
        kernel,
        in_specs=[pl.BlockSpec(memory_space=pltpu.HBM)] + [vmem()] * len(carried),
        out_specs=[pl.BlockSpec(memory_space=pl.ANY)] * count + [vmem()] * len(carried),
        out_shape=[jax.ShapeDtypeStruct(shape, jnp.bfloat16)] * count
        + [jax.ShapeDtypeStruct(value.shape, value.dtype) for value in carried],
        scratch_shapes=[pltpu.SemaphoreType.DMA((count, tiles))],
        compiler_params=params(limit),
        cost_estimate=cost(),
    )(fields, *carried)


def cross(a, b):
    return [a[1] * b[2] - a[2] * b[1], a[2] * b[0] - a[0] * b[2], a[0] * b[1] - a[1] * b[0]]


def to_physical(count, in_refs, inverse, x_ref, store):
    me = lax.axis_index("mode")
    components, tiles, rows, _ = in_refs[0].shape
    for step in range(count):
        at = pl.multiple_of(source_of(me, step, count) * rows, rows)
        for c in range(components):
            for t in range(tiles):
                x_ref[c, pl.ds(at, rows), t * LANES : (t + 1) * LANES] = in_refs[step][c, t]
    for c in range(components):
        store(c, jnp.dot(inverse, x_ref[c], preferred_element_type=jnp.float32))


def to_modes(count, forward_ref, table_ref, product_ref, out_refs):
    me = lax.axis_index("mode")
    components, tiles, rows, _ = out_refs[0].shape
    for step in range(count):
        at = pl.multiple_of(dest_of(me, step, count) * rows, rows)
        table_ref[step * rows : (step + 1) * rows] = forward_ref[pl.ds(at, rows)]
    for c in range(components):
        terms = jnp.dot(table_ref[...], product_ref[c], preferred_element_type=jnp.float32)
        terms = terms.astype(jnp.bfloat16)
        for step in range(count):
            for t in range(tiles):
                out_refs[step][c, t] = terms[step * rows : (step + 1) * rows, t * LANES : (t + 1) * LANES]


CHUNK = 32


def first_kernel(count, *refs):
    in_refs, (inverse_ref, forward_ref) = refs[:count], refs[count : count + 2]
    out_refs, (physical_ref, x_ref, product_ref, table_ref) = refs[count + 2 : 2 * count + 2], refs[2 * count + 2 :]

    def store(c, value):
        physical_ref[c] = value

    to_physical(count, in_refs, inverse_ref[...], x_ref, store)
    for i in range(THETA // CHUNK):
        at = slice(i * CHUNK, (i + 1) * CHUNK)
        velocity = [physical_ref[c, at] for c in range(3)]
        magnetic = [physical_ref[c, at] for c in range(3, 6)]
        energy = 0.5 * (velocity[0] * velocity[0] + velocity[1] * velocity[1] + velocity[2] * velocity[2])
        for c, value in enumerate(cross(velocity, magnetic) + [energy]):
            product_ref[c, at] = value.astype(jnp.bfloat16)
    to_modes(count, forward_ref, table_ref, product_ref, out_refs)


def second_kernel(count, *refs):
    in_refs, (first_ref, inverse_ref, forward_ref) = refs[:count], refs[count : count + 3]
    out_refs, (physical_ref, x_ref, product_ref, table_ref) = refs[count + 3 : 2 * count + 3], refs[2 * count + 3 :]

    def store(c, value):
        physical_ref[c] = value

    to_physical(count, in_refs, inverse_ref[...], x_ref, store)
    for i in range(THETA // CHUNK):
        at = slice(i * CHUNK, (i + 1) * CHUNK)
        velocity = [first_ref[c, at] for c in range(3)]
        magnetic = [first_ref[c, at] for c in range(3, 6)]
        current = [physical_ref[c, at] for c in range(3)]
        vorticity = [physical_ref[c, at] for c in range(3, 6)]
        lorentz = [a + b for a, b in zip(cross(current, magnetic), cross(velocity, vorticity))]
        for c, value in enumerate(lorentz):
            product_ref[c, at] = value.astype(jnp.bfloat16)
    to_modes(count, forward_ref, table_ref, product_ref, out_refs)


def physics(kernel, received, extra, inverse, forward, outputs, keep):
    count = len(received)
    components, tiles, rows, _ = received[0].shape
    group = 2 if tiles % 2 == 0 else 1
    steps = tiles // group
    width = group * LANES
    share = tiles * LANES
    in_block = pl.BlockSpec((components, group, rows, LANES), lambda i: (0, i, 0, 0))
    out_block = pl.BlockSpec((outputs, group, rows, LANES), lambda i: (0, i, 0, 0))
    whole = pl.BlockSpec((THETA, 2 * M), lambda i: (0, 0))
    turned = pl.BlockSpec((2 * M, THETA), lambda i: (0, 0))
    kept = pl.BlockSpec((6, THETA, width), lambda i: (0, 0, i))
    kept_shape = jax.ShapeDtypeStruct((6, THETA, share), jnp.float32)
    scratch = [
        pltpu.VMEM((components, 2 * M, width), jnp.bfloat16),
        pltpu.VMEM((outputs, THETA, width), jnp.bfloat16),
        pltpu.VMEM((2 * M, THETA), jnp.bfloat16),
    ]
    if not keep:
        scratch = [pltpu.VMEM((components, THETA, width), jnp.float32)] + scratch
    out_shape = [jax.ShapeDtypeStruct((outputs, tiles, rows, LANES), jnp.bfloat16)] * count
    return pl.pallas_call(
        functools.partial(kernel, count),
        grid=(steps,),
        in_specs=[in_block] * count + [kept] * len(extra) + [whole, turned],
        out_specs=[out_block] * count + ([kept] if keep else []),
        out_shape=out_shape + ([kept_shape] if keep else []),
        scratch_shapes=scratch,
        compiler_params=params(),
        cost_estimate=cost(),
    )(*received, *extra, inverse, forward)


def interface_kernel(count, *refs):
    in_refs, (nodes_ref,), (prev_ref, next_ref) = refs[:count], refs[count : count + 1], refs[count + 1 :]
    me = lax.axis_index("mode")
    components, tiles, rows, _ = in_refs[0].shape
    halo = nodes_ref.shape[1]
    totals = [jnp.zeros((components * rows, halo), jnp.float32) for _ in range(2)]
    inner = lax.broadcasted_iota(jnp.int32, (LANES, halo), 0)
    for step in range(count):
        share = source_of(me, step, count)
        for t in range(tiles):
            ids = inner + (share * tiles + t) * LANES
            values = in_refs[step][:, t].reshape(components * rows, LANES)
            for way in range(2):
                chosen = jnp.where(ids == nodes_ref[way : way + 1, :], 1.0, 0.0).astype(jnp.bfloat16)
                totals[way] += jnp.dot(values, chosen, preferred_element_type=jnp.float32)
    for out_ref, total in zip((prev_ref, next_ref), totals):
        picked = total.astype(jnp.bfloat16)
        for c in range(components):
            for t in range(halo // LANES):
                out_ref[c, t] = picked[c * rows : (c + 1) * rows, t * LANES : (t + 1) * LANES]


def interface(received, interface_nodes):
    count = len(received)
    components, tiles, rows, _ = received[0].shape
    halo = interface_nodes.shape[1]
    shape = jax.ShapeDtypeStruct((components, halo // LANES, rows, LANES), jnp.bfloat16)
    width = count * tiles * LANES
    return pl.pallas_call(
        functools.partial(interface_kernel, count),
        in_specs=[vmem()] * (count + 1),
        out_specs=[vmem()] * 2,
        out_shape=[shape] * 2,
        compiler_params=params(),
        cost_estimate=cost(),
    )(*received, interface_nodes)


def derive_kernel(count, *refs):
    in_refs = refs[:count]
    prev_ref, next_ref, radial_ref, axial_ref, radius_ref, columns_ref = refs[count : count + 6]
    induction_ref, momentum_ref, extended_ref = refs[count + 6 :]
    me = lax.axis_index("mode")
    components, tiles, rows, _ = in_refs[0].shape
    mode_count = rows // 2
    node_tiles = count * tiles
    halo_tiles = prev_ref.shape[1]
    for step in range(count):
        share = source_of(me, step, count)
        for t in range(tiles):
            extended_ref[share * tiles + t] = in_refs[step][:, t].reshape(components * rows, LANES)
    for t in range(halo_tiles):
        extended_ref[node_tiles + t] = prev_ref[:, t].reshape(components * rows, LANES)
        extended_ref[node_tiles + halo_tiles + t] = next_ref[:, t].reshape(components * rows, LANES)
    modes = (lax.broadcasted_iota(jnp.int32, (mode_count, LANES), 0) + me * mode_count).astype(jnp.float32)
    lane = lax.broadcasted_iota(jnp.int32, (1, 2 * LANES), 1)
    in_first = jnp.where(lax.rem(lane, LANES) < BLK, 1.0, 0.0)
    in_half = [in_first, 1.0 - in_first]

    def rotated(values):
        return jnp.concatenate([-modes * values[mode_count:], modes * values[:mode_count]], axis=0)

    def pair(b, carry):
        here = pl.ds(pl.multiple_of(b * LANES, LANES), LANES)
        total = jnp.zeros((components * rows, 2 * LANES), jnp.float32)
        for k in range(NNZB):
            weights = jnp.concatenate([radial_ref[k, :, here], axial_ref[k, :, here]], axis=1)
            left, right = [], []
            for half in range(2):
                column = columns_ref[2 * b + half, k]
                odd = lax.rem(column, 2).astype(jnp.float32)
                left.append(extended_ref[lax.div(column, 2)])
                right.append(weights * (in_half[half] * (1.0 - odd)).astype(jnp.bfloat16))
                right.append(weights * (in_half[half] * odd).astype(jnp.bfloat16))
            total += jnp.dot(
                jnp.concatenate(left, axis=1),
                jnp.concatenate(right, axis=0),
                preferred_element_type=jnp.float32,
            )
        along_r = [total[c * rows : (c + 1) * rows, :LANES] for c in range(components)]
        along_z = [total[c * rows : (c + 1) * rows, LANES:] for c in range(components)]
        values = [extended_ref[b, c * rows : (c + 1) * rows].astype(jnp.float32) for c in range(components)]
        inv_radius = 1.0 / radius_ref[:, here]
        induction = [
            rotated(values[2]) * inv_radius - along_z[1],
            along_z[0] - along_r[2],
            along_r[1] + values[1] * inv_radius - rotated(values[0]) * inv_radius,
        ]
        stride = 2 * node_tiles
        for i, value in enumerate(induction):
            for p in range(2):
                induction_ref[pl.ds(i * mode_count * stride + 2 * b + p, mode_count, stride=stride), :] = value[
                    p * mode_count : (p + 1) * mode_count
                ]
        momentum_ref[0, b] = along_r[3]
        momentum_ref[1, b] = rotated(values[3]) * inv_radius
        momentum_ref[2, b] = along_z[3]
        return carry

    lax.fori_loop(0, node_tiles, pair, 0)


def derive(received, from_prev, from_next, radial_blocks, axial_blocks, radius, columns):
    count = len(received)
    components, tiles, rows, _ = received[0].shape
    node_tiles = count * tiles
    halo_tiles = from_prev.shape[1]
    out_rows = 3 * rows * node_tiles
    return pl.pallas_call(
        functools.partial(derive_kernel, count),
        in_specs=[vmem()] * (count + 5) + [pl.BlockSpec(memory_space=pltpu.SMEM)],
        out_specs=[vmem()] * 2,
        out_shape=[
            jax.ShapeDtypeStruct((out_rows, LANES), jnp.float32),
            jax.ShapeDtypeStruct((3, node_tiles, rows, LANES), jnp.float32),
        ],
        scratch_shapes=[pltpu.VMEM((node_tiles + 2 * halo_tiles, components * rows, LANES), jnp.bfloat16)],
        compiler_params=params(),
        cost_estimate=cost(),
    )(*received, from_prev, from_next, radial_blocks, axial_blocks, radius, columns)


def momentum_kernel(count, *refs):
    in_refs, (gradient_ref, out_ref) = refs[:count], refs[count:]
    me = lax.axis_index("mode")
    _, tiles, rows, _ = in_refs[0].shape
    mode_count = rows // 2
    stride = 2 * count * tiles
    for step in range(count):
        share = source_of(me, step, count)
        for t in range(tiles):
            at = share * tiles + t
            value = in_refs[step][0, t].astype(jnp.float32) - gradient_ref[0, at]
            for p in range(2):
                out_ref[pl.ds(2 * at + p, mode_count, stride=stride), :] = value[
                    p * mode_count : (p + 1) * mode_count
                ]


def momentum_of(received, gradient):
    count = len(received)
    components, tiles, rows, _ = received[0].shape
    node_tiles = count * tiles
    out_rows = rows * node_tiles
    return pl.pallas_call(
        functools.partial(momentum_kernel, count),
        grid=(components,),
        in_specs=[pl.BlockSpec((1, tiles, rows, LANES), lambda c: (c, 0, 0, 0))] * count
        + [pl.BlockSpec((1, node_tiles, rows, LANES), lambda c: (c, 0, 0, 0))],
        out_specs=pl.BlockSpec((out_rows, LANES), lambda c: (c, 0)),
        out_shape=jax.ShapeDtypeStruct((components * out_rows, LANES), jnp.float32),
        compiler_params=params(),
        cost_estimate=cost(),
    )(*received, gradient)


def whole_output(value, mode_count, width):
    value = value.reshape(3, mode_count, width // LANES, 2, LANES)
    return value.transpose(0, 1, 3, 2, 4).reshape(3, mode_count, 2, width)


def body(mode_fields, radius, radial_blocks, axial_blocks, block_columns, interface_nodes):
    _, mode_count, _, width = mode_fields.shape
    count = lax.axis_size("mode")
    rows = 2 * mode_count
    inverse, forward = tables(M, THETA, count)
    inverse, forward = jnp.asarray(inverse), jnp.asarray(forward)

    def sent(pieces):
        return [piece.reshape(piece.shape[:2] + (rows, LANES)) for piece in exchange(pieces)]

    flow = sent(pack(mode_fields, 0, 6, count, [], FIRST_LIMIT))
    *pieces, inverse, forward = pack(mode_fields, 6, 6, count, [inverse, forward], VMEM_LIMIT)
    sources = sent(pieces)
    *terms, physical = physics(first_kernel, flow, [], inverse, forward, 4, True)
    local = exchange(terms)
    toward_prev, toward_next = interface(local, interface_nodes)
    from_prev = from_behind(toward_next, "mer", 1)
    from_next = from_behind(toward_prev, "mer", -1)
    induction, gradient = derive(
        local, from_prev, from_next, radial_blocks, axial_blocks, radius.reshape(1, width), block_columns
    )
    lorentz = exchange(physics(second_kernel, sources, [physical], inverse, forward, 3, False))
    momentum = momentum_of(lorentz, gradient)
    return (whole_output(induction, mode_count, width), whole_output(momentum, mode_count, width))


def solution(mesh):
    placed = (
        P(None, "mode", None, "mer"),
        P("mer"),
        P(None, None, "mer"),
        P(None, None, "mer"),
        P("mer", None),
        P("mer", None),
    )
    return jax.shard_map(
        body,
        mesh=mesh,
        in_specs=placed,
        out_specs=(P(None, "mode", None, "mer"), P(None, "mode", None, "mer")),
        check_vma=False,
    )
```

```python
import functools
import math

import jax
import jax.numpy as jnp
import ml_dtypes
import numpy as np
from jax import lax
from jax.experimental import pallas as pl
from jax.experimental.pallas import tpu as pltpu
from jax.sharding import PartitionSpec as P

M = 128
THETA = 256
BLK = 64
NNZB = 5
LANES = 128
VMEM_LIMIT = 24 * 1024 * 1024
FIRST_LIMIT = 61 * 1024 * 1024


def params(limit=VMEM_LIMIT):
    return pltpu.CompilerParams(vmem_limit_bytes=limit)


def vmem():
    return pl.BlockSpec(memory_space=pltpu.VMEM)


def cost():
    return pl.CostEstimate(flops=1024, bytes_accessed=1024, transcendentals=0)


def dest_of(me, step, count):
    if count & (count - 1) == 0:
        return jnp.bitwise_xor(me, step)
    return lax.rem(me + step, count)


def source_of(me, step, count):
    if count & (count - 1) == 0:
        return jnp.bitwise_xor(me, step)
    return lax.rem(me + count - step, count)


def exchange(pieces):
    count = len(pieces)
    power = count & (count - 1) == 0
    received = [pieces[0]]
    for step in range(1, count):
        pairs = [(i, i ^ step if power else (i + step) % count) for i in range(count)]
        received.append(lax.ppermute(pieces[step], "mode", pairs))
    return received


def from_behind(value, axis, steps):
    count = lax.axis_size(axis)
    initial, last = (max(0, -steps), min(count, count - steps))
    return lax.ppermute(value, axis, [(source, source + steps) for source in range(initial, last)])


def tables(mode_total, angle_total, share_count):
    mode_ids = np.arange(mode_total)
    angle_ids = np.arange(angle_total)
    phase = angle_ids[:, None] * mode_ids[None, :] % angle_total
    angle = phase.astype(np.float32) * np.float32(2.0 * math.pi / angle_total)
    weight = np.where(mode_ids == 0, 1.0, 2.0).astype(np.float32)
    cosines = np.cos(angle)
    sines = np.sin(angle)
    inverse = np.stack([weight * cosines, -weight * sines], axis=-1).astype(ml_dtypes.bfloat16)
    forward = np.stack([cosines.T, -sines.T], axis=1) / np.float32(angle_total)
    forward = forward.reshape(share_count, mode_total // share_count, 2, angle_total)
    forward = forward.transpose(0, 2, 1, 3).reshape(2 * mode_total, angle_total).astype(ml_dtypes.bfloat16)
    return (inverse.reshape(angle_total, 2 * mode_total), forward)


def pack_kernel(count, carried, first, fields_ref, *refs):
    me = lax.axis_index("mode")
    inputs, refs = refs[:carried], refs[carried:]
    out_refs, outputs, (fields_vmem, load, sems) = refs[:count], refs[count : count + carried], refs[count + carried :]
    components, tiles = out_refs[0].shape[:2]
    loads = []
    for c in range(components):
        loads.append(pltpu.make_async_copy(fields_ref.at[first + c], fields_vmem.at[c], load.at[c]))
        loads[c].start()
    copies = []
    for c in range(components):
        loads[c].wait()
        for step in range(count):
            share = dest_of(me, step, count)
            for t in range(tiles):
                start = pl.multiple_of((share * tiles + t) * LANES, LANES)
                source = fields_vmem.at[c, :, :, pl.ds(start, LANES)]
                copies.append(pltpu.make_async_copy(source, out_refs[step].at[c, t], sems.at[c, step, t]))
                copies[-1].start()
    for source, target in zip(inputs, outputs):
        target[...] = source[...]
    for copy in copies:
        copy.wait()


def pack(fields, first, components, count, carried, limit):
    _, mode_count, _, width = fields.shape
    tiles = width // count // LANES
    shape = (components, tiles, mode_count, 2, LANES)
    return pl.pallas_call(
        functools.partial(pack_kernel, count, len(carried), first),
        in_specs=[pl.BlockSpec(memory_space=pl.ANY)] + [vmem()] * len(carried),
        out_specs=[vmem()] * (count + len(carried)),
        out_shape=[jax.ShapeDtypeStruct(shape, jnp.bfloat16)] * count
        + [jax.ShapeDtypeStruct(value.shape, value.dtype) for value in carried],
        scratch_shapes=[
            pltpu.VMEM((components, mode_count, 2, width), jnp.bfloat16),
            pltpu.SemaphoreType.DMA((components,)),
            pltpu.SemaphoreType.DMA((components, count, tiles)),
        ],
        compiler_params=params(limit),
        cost_estimate=cost(),
    )(fields, *carried)


def cross(a, b):
    return [a[1] * b[2] - a[2] * b[1], a[2] * b[0] - a[0] * b[2], a[0] * b[1] - a[1] * b[0]]


def to_physical(count, in_refs, inverse, x_ref, store):
    me = lax.axis_index("mode")
    components, tiles, rows, _ = in_refs[0].shape
    for step in range(count):
        at = pl.multiple_of(source_of(me, step, count) * rows, rows)
        for c in range(components):
            for t in range(tiles):
                x_ref[c, pl.ds(at, rows), t * LANES : (t + 1) * LANES] = in_refs[step][c, t]
    for c in range(components):
        store(c, jnp.dot(inverse, x_ref[c], preferred_element_type=jnp.float32))


def to_modes(count, forward_ref, table_ref, product_ref, out_refs):
    me = lax.axis_index("mode")
    components, tiles, rows, _ = out_refs[0].shape
    for step in range(count):
        at = pl.multiple_of(dest_of(me, step, count) * rows, rows)
        table_ref[step * rows : (step + 1) * rows] = forward_ref[pl.ds(at, rows)]
    for c in range(components):
        terms = jnp.dot(table_ref[...], product_ref[c], preferred_element_type=jnp.float32)
        terms = terms.astype(jnp.bfloat16)
        for step in range(count):
            for t in range(tiles):
                out_refs[step][c, t] = terms[step * rows : (step + 1) * rows, t * LANES : (t + 1) * LANES]


CHUNK = 32


def first_kernel(count, *refs):
    in_refs, (inverse_ref, forward_ref) = refs[:count], refs[count : count + 2]
    out_refs, (physical_ref, x_ref, product_ref, table_ref) = refs[count + 2 : 2 * count + 2], refs[2 * count + 2 :]

    def store(c, value):
        physical_ref[c] = value

    to_physical(count, in_refs, inverse_ref[...], x_ref, store)
    for i in range(THETA // CHUNK):
        at = slice(i * CHUNK, (i + 1) * CHUNK)
        velocity = [physical_ref[c, at] for c in range(3)]
        magnetic = [physical_ref[c, at] for c in range(3, 6)]
        energy = 0.5 * (velocity[0] * velocity[0] + velocity[1] * velocity[1] + velocity[2] * velocity[2])
        for c, value in enumerate(cross(velocity, magnetic) + [energy]):
            product_ref[c, at] = value.astype(jnp.bfloat16)
    to_modes(count, forward_ref, table_ref, product_ref, out_refs)


def second_kernel(count, *refs):
    in_refs, (first_ref, inverse_ref, forward_ref) = refs[:count], refs[count : count + 3]
    out_refs, (physical_ref, x_ref, product_ref, table_ref) = refs[count + 3 : 2 * count + 3], refs[2 * count + 3 :]

    def store(c, value):
        physical_ref[c] = value

    to_physical(count, in_refs, inverse_ref[...], x_ref, store)
    for i in range(THETA // CHUNK):
        at = slice(i * CHUNK, (i + 1) * CHUNK)
        velocity = [first_ref[c, at] for c in range(3)]
        magnetic = [first_ref[c, at] for c in range(3, 6)]
        current = [physical_ref[c, at] for c in range(3)]
        vorticity = [physical_ref[c, at] for c in range(3, 6)]
        lorentz = [a + b for a, b in zip(cross(current, magnetic), cross(velocity, vorticity))]
        for c, value in enumerate(lorentz):
            product_ref[c, at] = value.astype(jnp.bfloat16)
    to_modes(count, forward_ref, table_ref, product_ref, out_refs)


def physics(kernel, received, extra, inverse, forward, outputs, keep):
    count = len(received)
    components, tiles, rows, _ = received[0].shape
    group = 2 if tiles % 2 == 0 else 1
    steps = tiles // group
    width = group * LANES
    share = tiles * LANES
    in_block = pl.BlockSpec((components, group, rows, LANES), lambda i: (0, i, 0, 0))
    out_block = pl.BlockSpec((outputs, group, rows, LANES), lambda i: (0, i, 0, 0))
    whole = pl.BlockSpec((THETA, 2 * M), lambda i: (0, 0))
    turned = pl.BlockSpec((2 * M, THETA), lambda i: (0, 0))
    kept = pl.BlockSpec((6, THETA, width), lambda i: (0, 0, i))
    kept_shape = jax.ShapeDtypeStruct((6, THETA, share), jnp.float32)
    scratch = [
        pltpu.VMEM((components, 2 * M, width), jnp.bfloat16),
        pltpu.VMEM((outputs, THETA, width), jnp.bfloat16),
        pltpu.VMEM((2 * M, THETA), jnp.bfloat16),
    ]
    if not keep:
        scratch = [pltpu.VMEM((components, THETA, width), jnp.float32)] + scratch
    out_shape = [jax.ShapeDtypeStruct((outputs, tiles, rows, LANES), jnp.bfloat16)] * count
    return pl.pallas_call(
        functools.partial(kernel, count),
        grid=(steps,),
        in_specs=[in_block] * count + [kept] * len(extra) + [whole, turned],
        out_specs=[out_block] * count + ([kept] if keep else []),
        out_shape=out_shape + ([kept_shape] if keep else []),
        scratch_shapes=scratch,
        compiler_params=params(),
        cost_estimate=cost(),
    )(*received, *extra, inverse, forward)


def interface_kernel(count, *refs):
    in_refs, (nodes_ref,), (prev_ref, next_ref) = refs[:count], refs[count : count + 1], refs[count + 1 :]
    me = lax.axis_index("mode")
    components, tiles, rows, _ = in_refs[0].shape
    halo = nodes_ref.shape[1]
    totals = [jnp.zeros((components * rows, halo), jnp.float32) for _ in range(2)]
    inner = lax.broadcasted_iota(jnp.int32, (LANES, halo), 0)
    for step in range(count):
        share = source_of(me, step, count)
        for t in range(tiles):
            ids = inner + (share * tiles + t) * LANES
            values = in_refs[step][:, t].reshape(components * rows, LANES)
            for way in range(2):
                chosen = jnp.where(ids == nodes_ref[way : way + 1, :], 1.0, 0.0).astype(jnp.bfloat16)
                totals[way] += jnp.dot(values, chosen, preferred_element_type=jnp.float32)
    for out_ref, total in zip((prev_ref, next_ref), totals):
        picked = total.astype(jnp.bfloat16)
        for c in range(components):
            for t in range(halo // LANES):
                out_ref[c, t] = picked[c * rows : (c + 1) * rows, t * LANES : (t + 1) * LANES]


def interface(received, interface_nodes):
    count = len(received)
    components, tiles, rows, _ = received[0].shape
    halo = interface_nodes.shape[1]
    shape = jax.ShapeDtypeStruct((components, halo // LANES, rows, LANES), jnp.bfloat16)
    width = count * tiles * LANES
    return pl.pallas_call(
        functools.partial(interface_kernel, count),
        in_specs=[vmem()] * (count + 1),
        out_specs=[vmem()] * 2,
        out_shape=[shape] * 2,
        compiler_params=params(),
        cost_estimate=cost(),
    )(*received, interface_nodes)


def derive_kernel(count, *refs):
    in_refs = refs[:count]
    prev_ref, next_ref, radial_ref, axial_ref, radius_ref, columns_ref = refs[count : count + 6]
    induction_ref, momentum_ref, extended_ref = refs[count + 6 :]
    me = lax.axis_index("mode")
    components, tiles, rows, _ = in_refs[0].shape
    mode_count = rows // 2
    node_tiles = count * tiles
    halo_tiles = prev_ref.shape[1]

    def extend(at, tile):
        extended_ref[0, at] = tile
        extended_ref[1, at] = jnp.concatenate([tile[:, BLK:], tile[:, :BLK]], axis=1)

    for step in range(count):
        share = source_of(me, step, count)
        for t in range(tiles):
            extend(share * tiles + t, in_refs[step][:, t].reshape(components * rows, LANES))
    for t in range(halo_tiles):
        extend(node_tiles + t, prev_ref[:, t].reshape(components * rows, LANES))
        extend(node_tiles + halo_tiles + t, next_ref[:, t].reshape(components * rows, LANES))
    modes = (lax.broadcasted_iota(jnp.int32, (mode_count, LANES), 0) + me * mode_count).astype(jnp.float32)
    low = lax.broadcasted_iota(jnp.int32, (components * rows, LANES), 1) < BLK
    lane = lax.broadcasted_iota(jnp.int32, (1, 2 * LANES), 1)
    in_first = jnp.where(lax.rem(lane, LANES) < BLK, 1.0, 0.0)
    in_half = [in_first.astype(jnp.bfloat16), (1.0 - in_first).astype(jnp.bfloat16)]

    def rotated(values):
        return jnp.concatenate([-modes * values[mode_count:], modes * values[:mode_count]], axis=0)

    def pair(b, carry):
        here = pl.ds(pl.multiple_of(b * LANES, LANES), LANES)
        left, right = [], []
        for k in range(NNZB):
            weights = jnp.concatenate([radial_ref[k, :, here], axial_ref[k, :, here]], axis=1)
            first, second = columns_ref[k, 2 * b], columns_ref[k, 2 * b + 1]
            first_tile = extended_ref[lax.rem(first, 2), lax.div(first, 2)]
            second_tile = extended_ref[1 - lax.rem(second, 2), lax.div(second, 2)]
            left.append(jnp.where(low, first_tile, second_tile))
            right += [weights * in_half[0], weights * in_half[1]]
        total = jnp.dot(
            jnp.concatenate(left, axis=1),
            jnp.concatenate(right, axis=0),
            preferred_element_type=jnp.float32,
        )
        along_r = [total[c * rows : (c + 1) * rows, :LANES] for c in range(components)]
        along_z = [total[c * rows : (c + 1) * rows, LANES:] for c in range(components)]
        values = [extended_ref[0, b, c * rows : (c + 1) * rows].astype(jnp.float32) for c in range(components)]
        inv_radius = 1.0 / radius_ref[:, here]
        induction = [
            rotated(values[2]) * inv_radius - along_z[1],
            along_z[0] - along_r[2],
            along_r[1] + values[1] * inv_radius - rotated(values[0]) * inv_radius,
        ]
        stride = 2 * node_tiles
        for i, value in enumerate(induction):
            for p in range(2):
                induction_ref[pl.ds(i * mode_count * stride + 2 * b + p, mode_count, stride=stride), :] = value[
                    p * mode_count : (p + 1) * mode_count
                ]
        momentum_ref[0, b] = along_r[3]
        momentum_ref[1, b] = rotated(values[3]) * inv_radius
        momentum_ref[2, b] = along_z[3]
        return carry

    lax.fori_loop(0, node_tiles, pair, 0)


def derive(received, from_prev, from_next, radial_blocks, axial_blocks, radius, columns):
    count = len(received)
    components, tiles, rows, _ = received[0].shape
    node_tiles = count * tiles
    halo_tiles = from_prev.shape[1]
    out_rows = 3 * rows * node_tiles
    return pl.pallas_call(
        functools.partial(derive_kernel, count),
        in_specs=[vmem()] * (count + 5) + [pl.BlockSpec(memory_space=pltpu.SMEM)],
        out_specs=[vmem()] * 2,
        out_shape=[
            jax.ShapeDtypeStruct((out_rows, LANES), jnp.float32),
            jax.ShapeDtypeStruct((3, node_tiles, rows, LANES), jnp.float32),
        ],
        scratch_shapes=[pltpu.VMEM((2, node_tiles + 2 * halo_tiles, components * rows, LANES), jnp.bfloat16)],
        compiler_params=params(),
        cost_estimate=cost(),
    )(*received, from_prev, from_next, radial_blocks, axial_blocks, radius, columns)


def momentum_kernel(count, *refs):
    in_refs, (gradient_ref, out_ref, total_ref, sems) = refs[:count], refs[count:]
    me = lax.axis_index("mode")
    components, tiles, rows, _ = in_refs[0].shape
    mode_count = rows // 2
    stride = 2 * count * tiles
    out_rows = mode_count * stride
    copies = []
    for c in range(components):
        for step in range(count):
            share = source_of(me, step, count)
            for t in range(tiles):
                at = share * tiles + t
                value = in_refs[step][c, t].astype(jnp.float32) - gradient_ref[c, at]
                for p in range(2):
                    total_ref[pl.ds(c * out_rows + 2 * at + p, mode_count, stride=stride), :] = value[
                        p * mode_count : (p + 1) * mode_count
                    ]
        done = pl.ds(c * out_rows, out_rows)
        copies.append(pltpu.make_async_copy(total_ref.at[done], out_ref.at[done], sems.at[c]))
        copies[c].start()
    for copy in copies:
        copy.wait()


def momentum_of(received, gradient):
    count = len(received)
    components, tiles, rows, _ = received[0].shape
    shape = (components * rows * count * tiles, LANES)
    return pl.pallas_call(
        functools.partial(momentum_kernel, count),
        in_specs=[vmem()] * (count + 1),
        out_specs=pl.BlockSpec(memory_space=pl.ANY),
        out_shape=jax.ShapeDtypeStruct(shape, jnp.float32),
        scratch_shapes=[pltpu.VMEM(shape, jnp.float32), pltpu.SemaphoreType.DMA((components,))],
        compiler_params=params(),
        cost_estimate=cost(),
    )(*received, gradient)


def whole_output(value, mode_count, width):
    value = value.reshape(3, mode_count, width // LANES, 2, LANES)
    return value.transpose(0, 1, 3, 2, 4).reshape(3, mode_count, 2, width)


def body(mode_fields, radius, radial_blocks, axial_blocks, block_columns, interface_nodes):
    _, mode_count, _, width = mode_fields.shape
    count = lax.axis_size("mode")
    rows = 2 * mode_count
    inverse, forward = tables(M, THETA, count)
    inverse, forward = jnp.asarray(inverse), jnp.asarray(forward)

    def joined(pieces):
        return [piece.reshape(piece.shape[:2] + (rows, LANES)) for piece in pieces]

    flow = exchange(pack(mode_fields, 0, 6, count, [], FIRST_LIMIT))
    *pieces, inverse, forward = pack(mode_fields, 6, 6, count, [inverse, forward], VMEM_LIMIT)
    flow, pieces = lax.optimization_barrier((flow, pieces))
    flow, sources = joined(flow), joined(exchange(pieces))
    *terms, physical = physics(first_kernel, flow, [], inverse, forward, 4, True)
    local = exchange(terms)
    toward_prev, toward_next = interface(local, interface_nodes)
    from_prev = from_behind(toward_next, "mer", 1)
    from_next = from_behind(toward_prev, "mer", -1)
    induction, gradient = derive(
        local, from_prev, from_next, radial_blocks, axial_blocks, radius.reshape(1, width), block_columns.T
    )
    lorentz = exchange(physics(second_kernel, sources, [physical], inverse, forward, 3, False))
    momentum = momentum_of(lorentz, gradient)
    return (whole_output(induction, mode_count, width), whole_output(momentum, mode_count, width))


def solution(mesh):
    placed = (
        P(None, "mode", None, "mer"),
        P("mer"),
        P(None, None, "mer"),
        P(None, None, "mer"),
        P("mer", None),
        P("mer", None),
    )
    return jax.shard_map(
        body,
        mesh=mesh,
        in_specs=placed,
        out_specs=(P(None, "mode", None, "mer"), P(None, "mode", None, "mer")),
        check_vma=False,
    )
```

```python
import functools
import math

import jax
import jax.numpy as jnp
import ml_dtypes
import numpy as np
from jax import lax
from jax.experimental import pallas as pl
from jax.experimental.pallas import tpu as pltpu
from jax.sharding import PartitionSpec as P

M = 128
THETA = 256
BLK = 64
NNZB = 5
LANES = 128
VMEM_LIMIT = 24 * 1024 * 1024


def params(limit=VMEM_LIMIT):
    return pltpu.CompilerParams(vmem_limit_bytes=limit)


def vmem():
    return pl.BlockSpec(memory_space=pltpu.VMEM)


def cost():
    return pl.CostEstimate(flops=1024, bytes_accessed=1024, transcendentals=0)


def dest_of(me, step, count):
    if count & (count - 1) == 0:
        return jnp.bitwise_xor(me, step)
    return lax.rem(me + step, count)


def source_of(me, step, count):
    if count & (count - 1) == 0:
        return jnp.bitwise_xor(me, step)
    return lax.rem(me + count - step, count)


def exchange(pieces):
    count = len(pieces) + 1
    power = count & (count - 1) == 0
    received = []
    for step in range(1, count):
        pairs = [(i, i ^ step if power else (i + step) % count) for i in range(count)]
        received.append(lax.ppermute(pieces[step - 1], "mode", pairs))
    return received


def from_behind(value, axis, steps):
    count = lax.axis_size(axis)
    initial, last = (max(0, -steps), min(count, count - steps))
    return lax.ppermute(value, axis, [(source, source + steps) for source in range(initial, last)])


def tables(mode_total, angle_total, share_count):
    mode_ids = np.arange(mode_total)
    angle_ids = np.arange(angle_total)
    phase = angle_ids[:, None] * mode_ids[None, :] % angle_total
    angle = phase.astype(np.float32) * np.float32(2.0 * math.pi / angle_total)
    weight = np.where(mode_ids == 0, 1.0, 2.0).astype(np.float32)
    cosines = np.cos(angle)
    sines = np.sin(angle)
    inverse = np.stack([weight * cosines, -weight * sines], axis=-1).astype(ml_dtypes.bfloat16)
    forward = np.stack([cosines.T, -sines.T], axis=1) / np.float32(angle_total)
    forward = forward.reshape(share_count, mode_total // share_count, 2, angle_total)
    forward = forward.transpose(0, 2, 1, 3).reshape(2 * mode_total, angle_total).astype(ml_dtypes.bfloat16)
    return (inverse.reshape(angle_total, 2 * mode_total), forward)


def pieces_of(fields_ref, share, out_ref, first=0):
    components, tiles = out_ref.shape[:2]
    pairs = []
    for t in range(tiles):
        start = pl.multiple_of((share * tiles + t) * LANES, LANES)
        for c in range(components):
            pairs.append((fields_ref.at[first + c, :, :, pl.ds(start, LANES)], out_ref.at[c, t]))
    return pairs


def run_copies(pairs, sems, beside=()):
    copies = [pltpu.make_async_copy(source, target, sems.at[i]) for i, (source, target) in enumerate(pairs)]
    for copy in copies:
        copy.start()
    for source, target in beside:
        target[...] = source[...]
    for copy in copies:
        copy.wait()


def share_shape(fields, count):
    components, mode_count, _, width = fields.shape
    return (components, width // count // LANES, mode_count, 2, LANES)


def pack_step(fields, step, count):
    shape = share_shape(fields, count)

    def kernel(fields_ref, out_ref, sems):
        run_copies(pieces_of(fields_ref, dest_of(lax.axis_index("mode"), step, count), out_ref), sems)

    return pl.pallas_call(
        kernel,
        in_specs=[vmem()],
        out_specs=vmem(),
        out_shape=jax.ShapeDtypeStruct(shape, jnp.bfloat16),
        scratch_shapes=[pltpu.SemaphoreType.DMA((shape[0] * shape[1],))],
        compiler_params=params(),
        cost_estimate=cost(),
    )(fields)


def pack_rest(fields, others, count, carried):
    shape = share_shape(fields, count)

    def kernel(fields_ref, others_ref, *refs):
        inputs, (own_ref, all_ref), outputs = refs[: len(carried)], refs[len(carried) : len(carried) + 2], refs[len(carried) + 2 : -1]
        pairs = pieces_of(fields_ref, lax.axis_index("mode"), own_ref)
        for share in range(count):
            pairs += pieces_of(others_ref, share, all_ref.at[share], shape[0])
        run_copies(pairs, refs[-1], zip(inputs, outputs))

    return pl.pallas_call(
        kernel,
        in_specs=[vmem(), pl.BlockSpec(memory_space=pl.ANY)] + [vmem()] * len(carried),
        out_specs=[vmem()] * (2 + len(carried)),
        out_shape=[jax.ShapeDtypeStruct(shape, jnp.bfloat16), jax.ShapeDtypeStruct((count,) + shape, jnp.bfloat16)]
        + [jax.ShapeDtypeStruct(value.shape, value.dtype) for value in carried],
        scratch_shapes=[pltpu.SemaphoreType.DMA(((count + 1) * shape[0] * shape[1],))],
        compiler_params=params(),
        cost_estimate=cost(),
    )(fields, others, *carried)


def cross(a, b):
    return [a[1] * b[2] - a[2] * b[1], a[2] * b[0] - a[0] * b[2], a[0] * b[1] - a[1] * b[0]]


def to_physical(sources, in_refs, inverse, x_ref, store):
    components, tiles, rows, _ = in_refs[0].shape
    for step, source in enumerate(sources):
        at = pl.multiple_of(source * rows, rows)
        for c in range(components):
            for t in range(tiles):
                x_ref[c, pl.ds(at, rows), t * LANES : (t + 1) * LANES] = in_refs[step][c, t]
    for c in range(components):
        store(c, jnp.dot(inverse, x_ref[c], preferred_element_type=jnp.float32))


def to_modes(count, forward_ref, table_ref, product_ref, out_refs):
    me = lax.axis_index("mode")
    components, tiles, rows, _ = out_refs[0].shape
    for step in range(count):
        at = pl.multiple_of(dest_of(me, step, count) * rows, rows)
        table_ref[step * rows : (step + 1) * rows] = forward_ref[pl.ds(at, rows)]
    for c in range(components):
        terms = jnp.dot(table_ref[...], product_ref[c], preferred_element_type=jnp.float32)
        terms = terms.astype(jnp.bfloat16)
        for step in range(count):
            for t in range(tiles):
                out_refs[step][c, t] = terms[step * rows : (step + 1) * rows, t * LANES : (t + 1) * LANES]


CHUNK = 32


def first_kernel(count, *refs):
    in_refs, (inverse_ref, forward_ref) = refs[:count], refs[count : count + 2]
    out_refs, (physical_ref, x_ref, product_ref, table_ref) = refs[count + 2 : 2 * count + 2], refs[2 * count + 2 :]

    def store(c, value):
        physical_ref[c] = value

    me = lax.axis_index("mode")
    sources = [source_of(me, step, count) for step in range(count)]
    to_physical(sources, in_refs, inverse_ref[...], x_ref, store)
    for i in range(THETA // CHUNK):
        at = slice(i * CHUNK, (i + 1) * CHUNK)
        velocity = [physical_ref[c, at] for c in range(3)]
        magnetic = [physical_ref[c, at] for c in range(3, 6)]
        energy = 0.5 * (velocity[0] * velocity[0] + velocity[1] * velocity[1] + velocity[2] * velocity[2])
        for c, value in enumerate(cross(velocity, magnetic) + [energy]):
            product_ref[c, at] = value.astype(jnp.bfloat16)
    to_modes(count, forward_ref, table_ref, product_ref, out_refs)


def second_kernel(count, *refs):
    in_ref, first_ref, inverse_ref, forward_ref = refs[:4]
    out_refs, (physical_ref, x_ref, product_ref, table_ref) = refs[4 : count + 4], refs[count + 4 :]

    def store(c, value):
        physical_ref[c] = value

    to_physical(range(count), [in_ref.at[source] for source in range(count)], inverse_ref[...], x_ref, store)
    for i in range(THETA // CHUNK):
        at = slice(i * CHUNK, (i + 1) * CHUNK)
        velocity = [first_ref[c, at] for c in range(3)]
        magnetic = [first_ref[c, at] for c in range(3, 6)]
        current = [physical_ref[c, at] for c in range(3)]
        vorticity = [physical_ref[c, at] for c in range(3, 6)]
        lorentz = [a + b for a, b in zip(cross(current, magnetic), cross(velocity, vorticity))]
        for c, value in enumerate(lorentz):
            product_ref[c, at] = value.astype(jnp.bfloat16)
    to_modes(count, forward_ref, table_ref, product_ref, out_refs)


def physics(kernel, received, extra, inverse, forward, outputs, keep):
    components, tiles, rows, _ = received[0].shape[-4:]
    count = 2 * M // rows
    group = 2 if tiles % 2 == 0 else 1
    steps = tiles // group
    width = group * LANES
    share = tiles * LANES
    if keep:
        in_block = pl.BlockSpec((components, group, rows, LANES), lambda i: (0, i, 0, 0))
    else:
        in_block = pl.BlockSpec((count, components, group, rows, LANES), lambda i: (0, 0, i, 0, 0))
    out_block = pl.BlockSpec((outputs, group, rows, LANES), lambda i: (0, i, 0, 0))
    whole = pl.BlockSpec((THETA, 2 * M), lambda i: (0, 0))
    turned = pl.BlockSpec((2 * M, THETA), lambda i: (0, 0))
    kept = pl.BlockSpec((6, THETA, width), lambda i: (0, 0, i))
    kept_shape = jax.ShapeDtypeStruct((6, THETA, share), jnp.float32)
    scratch = [
        pltpu.VMEM((components, 2 * M, width), jnp.bfloat16),
        pltpu.VMEM((outputs, THETA, width), jnp.bfloat16),
        pltpu.VMEM((2 * M, THETA), jnp.bfloat16),
    ]
    if not keep:
        scratch = [pltpu.VMEM((components, THETA, width), jnp.float32)] + scratch
    out_shape = [jax.ShapeDtypeStruct((outputs, tiles, rows, LANES), jnp.bfloat16)] * count
    return pl.pallas_call(
        functools.partial(kernel, count),
        grid=(steps,),
        in_specs=[in_block] * len(received) + [kept] * len(extra) + [whole, turned],
        out_specs=[out_block] * count + ([kept] if keep else []),
        out_shape=out_shape + ([kept_shape] if keep else []),
        scratch_shapes=scratch,
        compiler_params=params(),
        cost_estimate=cost(),
    )(*received, *extra, inverse, forward)


def interface_kernel(count, *refs):
    in_refs, (nodes_ref,), (prev_ref, next_ref) = refs[:count], refs[count : count + 1], refs[count + 1 :]
    me = lax.axis_index("mode")
    components, tiles, rows, _ = in_refs[0].shape
    halo = nodes_ref.shape[1]
    totals = [jnp.zeros((components * rows, halo), jnp.float32) for _ in range(2)]
    inner = lax.broadcasted_iota(jnp.int32, (LANES, halo), 0)
    for step in range(count):
        share = source_of(me, step, count)
        for t in range(tiles):
            ids = inner + (share * tiles + t) * LANES
            values = in_refs[step][:, t].reshape(components * rows, LANES)
            for way in range(2):
                chosen = jnp.where(ids == nodes_ref[way : way + 1, :], 1.0, 0.0).astype(jnp.bfloat16)
                totals[way] += jnp.dot(values, chosen, preferred_element_type=jnp.float32)
    for out_ref, total in zip((prev_ref, next_ref), totals):
        picked = total.astype(jnp.bfloat16)
        for c in range(components):
            for t in range(halo // LANES):
                out_ref[c, t] = picked[c * rows : (c + 1) * rows, t * LANES : (t + 1) * LANES]


def interface(received, interface_nodes):
    count = len(received)
    components, tiles, rows, _ = received[0].shape
    halo = interface_nodes.shape[1]
    shape = jax.ShapeDtypeStruct((components, halo // LANES, rows, LANES), jnp.bfloat16)
    width = count * tiles * LANES
    return pl.pallas_call(
        functools.partial(interface_kernel, count),
        in_specs=[vmem()] * (count + 1),
        out_specs=[vmem()] * 2,
        out_shape=[shape] * 2,
        compiler_params=params(),
        cost_estimate=cost(),
    )(*received, interface_nodes)


def derive_kernel(count, *refs):
    in_refs = refs[:count]
    prev_ref, next_ref, radial_ref, axial_ref, radius_ref, columns_ref = refs[count : count + 6]
    induction_ref, momentum_ref, extended_ref = refs[count + 6 :]
    me = lax.axis_index("mode")
    components, tiles, rows, _ = in_refs[0].shape
    mode_count = rows // 2
    node_tiles = count * tiles
    halo_tiles = prev_ref.shape[1]

    def extend(at, tile):
        extended_ref[0, at] = tile
        extended_ref[1, at] = jnp.concatenate([tile[:, BLK:], tile[:, :BLK]], axis=1)

    for step in range(count):
        share = source_of(me, step, count)
        for t in range(tiles):
            extend(share * tiles + t, in_refs[step][:, t].reshape(components * rows, LANES))
    for t in range(halo_tiles):
        extend(node_tiles + t, prev_ref[:, t].reshape(components * rows, LANES))
        extend(node_tiles + halo_tiles + t, next_ref[:, t].reshape(components * rows, LANES))
    modes = (lax.broadcasted_iota(jnp.int32, (mode_count, LANES), 0) + me * mode_count).astype(jnp.float32)
    low = lax.broadcasted_iota(jnp.int32, (components * rows, LANES), 1) < BLK
    lane = lax.broadcasted_iota(jnp.int32, (1, 2 * LANES), 1)
    in_first = jnp.where(lax.rem(lane, LANES) < BLK, 1.0, 0.0)
    in_half = [in_first.astype(jnp.bfloat16), (1.0 - in_first).astype(jnp.bfloat16)]

    def rotated(values):
        return jnp.concatenate([-modes * values[mode_count:], modes * values[:mode_count]], axis=0)

    def pair(b, carry):
        here = pl.ds(pl.multiple_of(b * LANES, LANES), LANES)
        left, right = [], []
        for k in range(NNZB):
            weights = jnp.concatenate([radial_ref[k, :, here], axial_ref[k, :, here]], axis=1)
            first, second = columns_ref[k, 2 * b], columns_ref[k, 2 * b + 1]
            first_tile = extended_ref[lax.rem(first, 2), lax.div(first, 2)]
            second_tile = extended_ref[1 - lax.rem(second, 2), lax.div(second, 2)]
            left.append(jnp.where(low, first_tile, second_tile))
            right += [weights * in_half[0], weights * in_half[1]]
        total = jnp.dot(
            jnp.concatenate(left, axis=1),
            jnp.concatenate(right, axis=0),
            preferred_element_type=jnp.float32,
        )
        along_r = [total[c * rows : (c + 1) * rows, :LANES] for c in range(components)]
        along_z = [total[c * rows : (c + 1) * rows, LANES:] for c in range(components)]
        values = [extended_ref[0, b, c * rows : (c + 1) * rows].astype(jnp.float32) for c in range(components)]
        inv_radius = 1.0 / radius_ref[:, here]
        induction = [
            rotated(values[2]) * inv_radius - along_z[1],
            along_z[0] - along_r[2],
            along_r[1] + values[1] * inv_radius - rotated(values[0]) * inv_radius,
        ]
        stride = 2 * node_tiles
        for i, value in enumerate(induction):
            for p in range(2):
                induction_ref[pl.ds(i * mode_count * stride + 2 * b + p, mode_count, stride=stride), :] = value[
                    p * mode_count : (p + 1) * mode_count
                ]
        momentum_ref[0, b] = along_r[3]
        momentum_ref[1, b] = rotated(values[3]) * inv_radius
        momentum_ref[2, b] = along_z[3]
        return carry

    lax.fori_loop(0, node_tiles, pair, 0, unroll=2)


def derive(received, from_prev, from_next, radial_blocks, axial_blocks, radius, columns):
    count = len(received)
    components, tiles, rows, _ = received[0].shape
    node_tiles = count * tiles
    halo_tiles = from_prev.shape[1]
    out_rows = 3 * rows * node_tiles
    return pl.pallas_call(
        functools.partial(derive_kernel, count),
        in_specs=[vmem()] * (count + 5) + [pl.BlockSpec(memory_space=pltpu.SMEM)],
        out_specs=[vmem()] * 2,
        out_shape=[
            jax.ShapeDtypeStruct((out_rows, LANES), jnp.float32),
            jax.ShapeDtypeStruct((3, node_tiles, rows, LANES), jnp.float32),
        ],
        scratch_shapes=[pltpu.VMEM((2, node_tiles + 2 * halo_tiles, components * rows, LANES), jnp.bfloat16)],
        compiler_params=params(),
        cost_estimate=cost(),
    )(*received, from_prev, from_next, radial_blocks, axial_blocks, radius, columns)


def momentum_kernel(count, *refs):
    in_refs, (gradient_ref, out_ref, total_ref, sems) = refs[:count], refs[count:]
    me = lax.axis_index("mode")
    components, tiles, rows, _ = in_refs[0].shape
    mode_count = rows // 2
    stride = 2 * count * tiles
    out_rows = mode_count * stride
    copies = []
    for c in range(components):
        for step in range(count):
            share = source_of(me, step, count)
            for t in range(tiles):
                at = share * tiles + t
                value = in_refs[step][c, t].astype(jnp.float32) - gradient_ref[c, at]
                for p in range(2):
                    total_ref[pl.ds(c * out_rows + 2 * at + p, mode_count, stride=stride), :] = value[
                        p * mode_count : (p + 1) * mode_count
                    ]
        done = pl.ds(c * out_rows, out_rows)
        copies.append(pltpu.make_async_copy(total_ref.at[done], out_ref.at[done], sems.at[c]))
        copies[c].start()
    for copy in copies:
        copy.wait()


def momentum_of(received, gradient):
    count = len(received)
    components, tiles, rows, _ = received[0].shape
    shape = (components * rows * count * tiles, LANES)
    return pl.pallas_call(
        functools.partial(momentum_kernel, count),
        in_specs=[vmem()] * (count + 1),
        out_specs=pl.BlockSpec(memory_space=pl.ANY),
        out_shape=jax.ShapeDtypeStruct(shape, jnp.float32),
        scratch_shapes=[pltpu.VMEM(shape, jnp.float32), pltpu.SemaphoreType.DMA((components,))],
        compiler_params=params(),
        cost_estimate=cost(),
    )(*received, gradient)


def whole_output(value, mode_count, width):
    value = value.reshape(3, mode_count, width // LANES, 2, LANES)
    return value.transpose(0, 1, 3, 2, 4).reshape(3, mode_count, 2, width)


def body(mode_fields, radius, radial_blocks, axial_blocks, block_columns, interface_nodes):
    _, mode_count, _, width = mode_fields.shape
    count = lax.axis_size("mode")
    rows = 2 * mode_count
    inverse, forward = tables(M, THETA, count)
    inverse, forward = jnp.asarray(inverse), jnp.asarray(forward)

    def joined(pieces):
        return [piece.reshape(piece.shape[:-3] + (rows, LANES)) for piece in pieces]

    fields = mode_fields[:6]
    arrived = exchange([pack_step(fields, step, count) for step in range(1, count)])
    own, shares, inverse, forward = pack_rest(fields, mode_fields, count, [inverse, forward])
    arrived, shares = lax.optimization_barrier((arrived, shares))
    flow = joined([own] + arrived)
    sources = joined([lax.all_to_all(shares, "mode", 0, 0, tiled=True)])
    *terms, physical = physics(first_kernel, flow, [], inverse, forward, 4, True)
    local = terms[:1] + exchange(terms[1:])
    toward_prev, toward_next = interface(local, interface_nodes)
    from_prev = from_behind(toward_next, "mer", 1)
    from_next = from_behind(toward_prev, "mer", -1)
    induction, gradient = derive(
        local, from_prev, from_next, radial_blocks, axial_blocks, radius.reshape(1, width), block_columns.T
    )
    lorentz = list(physics(second_kernel, sources, [physical], inverse, forward, 3, False))
    lorentz = lorentz[:1] + exchange(lorentz[1:])
    momentum = momentum_of(lorentz, gradient)
    return (whole_output(induction, mode_count, width), whole_output(momentum, mode_count, width))


def solution(mesh):
    placed = (
        P(None, "mode", None, "mer"),
        P("mer"),
        P(None, None, "mer"),
        P(None, None, "mer"),
        P("mer", None),
        P("mer", None),
    )
    return jax.shard_map(
        body,
        mesh=mesh,
        in_specs=placed,
        out_specs=(P(None, "mode", None, "mer"), P(None, "mode", None, "mer")),
        check_vma=False,
    )
```

```python
import functools
import math

import jax
import jax.numpy as jnp
import ml_dtypes
import numpy as np
from jax import lax
from jax.experimental import pallas as pl
from jax.experimental.pallas import tpu as pltpu
from jax.sharding import PartitionSpec as P

M = 128
THETA = 256
BLK = 64
NNZB = 5
LANES = 128
VMEM_LIMIT = 24 * 1024 * 1024


def params(limit=VMEM_LIMIT):
    return pltpu.CompilerParams(vmem_limit_bytes=limit)


def vmem():
    return pl.BlockSpec(memory_space=pltpu.VMEM)


def cost():
    return pl.CostEstimate(flops=1024, bytes_accessed=1024, transcendentals=0)


def dest_of(me, step, count):
    if count & (count - 1) == 0:
        return jnp.bitwise_xor(me, step)
    return lax.rem(me + step, count)


def source_of(me, step, count):
    if count & (count - 1) == 0:
        return jnp.bitwise_xor(me, step)
    return lax.rem(me + count - step, count)


def exchange(pieces):
    count = len(pieces) + 1
    power = count & (count - 1) == 0
    received = []
    for step in range(1, count):
        pairs = [(i, i ^ step if power else (i + step) % count) for i in range(count)]
        received.append(lax.ppermute(pieces[step - 1], "mode", pairs))
    return received


def from_behind(value, axis, steps):
    count = lax.axis_size(axis)
    initial, last = (max(0, -steps), min(count, count - steps))
    return lax.ppermute(value, axis, [(source, source + steps) for source in range(initial, last)])


def tables(mode_total, angle_total, share_count):
    mode_ids = np.arange(mode_total)
    angle_ids = np.arange(angle_total)
    phase = angle_ids[:, None] * mode_ids[None, :] % angle_total
    angle = phase.astype(np.float32) * np.float32(2.0 * math.pi / angle_total)
    weight = np.where(mode_ids == 0, 1.0, 2.0).astype(np.float32)
    cosines = np.cos(angle)
    sines = np.sin(angle)
    inverse = np.stack([weight * cosines, -weight * sines], axis=-1).astype(ml_dtypes.bfloat16)
    forward = np.stack([cosines.T, -sines.T], axis=1) / np.float32(angle_total)
    forward = forward.reshape(share_count, mode_total // share_count, 2, angle_total)
    forward = forward.transpose(0, 2, 1, 3).reshape(2 * mode_total, angle_total).astype(ml_dtypes.bfloat16)
    return (inverse.reshape(angle_total, 2 * mode_total), forward)


def groups_of(tiles):
    return 2 if tiles % 2 == 0 else 1


def pieces_of(fields_ref, first, share, group, out_ref):
    count = lax.axis_size("mode")
    tiles = fields_ref.shape[3] // count // LANES
    components, held = out_ref.shape[:2]
    pairs = []
    for t in range(held):
        start = pl.multiple_of((share * tiles + group * held + t) * LANES, LANES)
        for c in range(components):
            pairs.append((fields_ref.at[first + c, :, :, pl.ds(start, LANES)], out_ref.at[c, t]))
    return pairs


def run_copies(pairs, sems, beside=()):
    copies = [pltpu.make_async_copy(source, target, sems.at[i]) for i, (source, target) in enumerate(pairs)]
    for copy in copies:
        copy.start()
    for source, target in beside:
        target[...] = source[...]
    for copy in copies:
        copy.wait()


def packed_shape(fields, first, last, groups):
    _, mode_count, _, width = fields.shape
    return (last - first, width // lax.axis_size("mode") // LANES // groups, mode_count, 2, LANES)


def pack(fields, first, last, step, group, groups):
    count = lax.axis_size("mode")
    shape = packed_shape(fields, first, last, groups)

    def kernel(fields_ref, out_ref, sems):
        share = dest_of(lax.axis_index("mode"), step, count)
        run_copies(pieces_of(fields_ref, first, share, group, out_ref), sems)

    return pl.pallas_call(
        kernel,
        in_specs=[pl.BlockSpec(memory_space=pl.ANY)],
        out_specs=vmem(),
        out_shape=jax.ShapeDtypeStruct(shape, jnp.bfloat16),
        scratch_shapes=[pltpu.SemaphoreType.DMA((shape[0] * shape[1],))],
        compiler_params=params(),
        cost_estimate=cost(),
    )(fields)


def pack_rest(fields, middle, groups, carried):
    count = lax.axis_size("mode")
    shape = packed_shape(fields, 0, middle, groups)
    full = packed_shape(fields, middle, fields.shape[0], 1)

    def kernel(fields_ref, *refs):
        inputs, refs = refs[: len(carried)], refs[len(carried) :]
        own_refs, all_ref, outputs = refs[:groups], refs[groups], refs[groups + 1 : -1]
        me = lax.axis_index("mode")
        pairs = []
        for group in range(groups):
            pairs += pieces_of(fields_ref, 0, me, group, own_refs[group])
        for share in range(count):
            pairs += pieces_of(fields_ref, middle, share, 0, all_ref.at[share])
        run_copies(pairs, refs[-1], zip(inputs, outputs))

    return pl.pallas_call(
        kernel,
        in_specs=[pl.BlockSpec(memory_space=pl.ANY)] + [vmem()] * len(carried),
        out_specs=[vmem()] * (groups + 1 + len(carried)),
        out_shape=[jax.ShapeDtypeStruct(shape, jnp.bfloat16)] * groups
        + [jax.ShapeDtypeStruct((count,) + full, jnp.bfloat16)]
        + [jax.ShapeDtypeStruct(value.shape, value.dtype) for value in carried],
        scratch_shapes=[pltpu.SemaphoreType.DMA((groups * shape[0] * shape[1] + count * full[0] * full[1],))],
        compiler_params=params(),
        cost_estimate=cost(),
    )(fields, *carried)


def cross(a, b):
    return [a[1] * b[2] - a[2] * b[1], a[2] * b[0] - a[0] * b[2], a[0] * b[1] - a[1] * b[0]]


def to_physical(sources, in_refs, inverse, x_ref, store):
    components, tiles, rows, _ = in_refs[0].shape
    for step, source in enumerate(sources):
        at = pl.multiple_of(source * rows, rows)
        for c in range(components):
            for t in range(tiles):
                x_ref[c, pl.ds(at, rows), t * LANES : (t + 1) * LANES] = in_refs[step][c, t]
    for c in range(components):
        store(c, jnp.dot(inverse, x_ref[c], preferred_element_type=jnp.float32))


def to_modes(count, forward_ref, table_ref, product_ref, out_refs):
    me = lax.axis_index("mode")
    components, tiles, rows, _ = out_refs[0].shape
    for step in range(count):
        at = pl.multiple_of(dest_of(me, step, count) * rows, rows)
        table_ref[step * rows : (step + 1) * rows] = forward_ref[pl.ds(at, rows)]
    for c in range(components):
        terms = jnp.dot(table_ref[...], product_ref[c], preferred_element_type=jnp.float32)
        terms = terms.astype(jnp.bfloat16)
        for step in range(count):
            for t in range(tiles):
                out_refs[step][c, t] = terms[step * rows : (step + 1) * rows, t * LANES : (t + 1) * LANES]


CHUNK = 32


def first_kernel(count, *refs):
    in_refs, (inverse_ref, forward_ref) = refs[:count], refs[count : count + 2]
    out_refs, (physical_ref, x_ref, product_ref, table_ref) = refs[count + 2 : 2 * count + 2], refs[2 * count + 2 :]

    def store(c, value):
        physical_ref[c] = value

    me = lax.axis_index("mode")
    sources = [source_of(me, step, count) for step in range(count)]
    to_physical(sources, in_refs, inverse_ref[...], x_ref, store)
    for i in range(THETA // CHUNK):
        at = slice(i * CHUNK, (i + 1) * CHUNK)
        velocity = [physical_ref[c, at] for c in range(3)]
        magnetic = [physical_ref[c, at] for c in range(3, 6)]
        energy = 0.5 * (velocity[0] * velocity[0] + velocity[1] * velocity[1] + velocity[2] * velocity[2])
        for c, value in enumerate(cross(velocity, magnetic) + [energy]):
            product_ref[c, at] = value.astype(jnp.bfloat16)
    to_modes(count, forward_ref, table_ref, product_ref, out_refs)


def first_physics(received, inverse, forward):
    count = len(received)
    components, tiles, rows, _ = received[0].shape
    width = tiles * LANES
    return pl.pallas_call(
        functools.partial(first_kernel, count),
        in_specs=[vmem()] * (count + 2),
        out_specs=[vmem()] * (count + 1),
        out_shape=[jax.ShapeDtypeStruct((4, tiles, rows, LANES), jnp.bfloat16)] * count
        + [jax.ShapeDtypeStruct((components, THETA, width), jnp.float32)],
        scratch_shapes=[
            pltpu.VMEM((components, 2 * M, width), jnp.bfloat16),
            pltpu.VMEM((4, THETA, width), jnp.bfloat16),
            pltpu.VMEM((2 * M, THETA), jnp.bfloat16),
        ],
        compiler_params=params(),
        cost_estimate=cost(),
    )(*received, inverse, forward)


def second_kernel(count, groups, *refs):
    in_ref, first_refs, (inverse_ref, forward_ref) = refs[0], refs[1 : groups + 1], refs[groups + 1 : groups + 3]
    out_refs, (physical_ref, x_ref, product_ref, table_ref) = refs[groups + 3 : groups + 3 + count], refs[groups + 3 + count :]
    width = first_refs[0].shape[2]

    def store(c, value):
        physical_ref[c] = value

    to_physical(range(count), [in_ref.at[source] for source in range(count)], inverse_ref[...], x_ref, store)
    for group in range(groups):
        lanes = slice(group * width, (group + 1) * width)
        for i in range(THETA // CHUNK):
            at = slice(i * CHUNK, (i + 1) * CHUNK)
            velocity = [first_refs[group][c, at] for c in range(3)]
            magnetic = [first_refs[group][c, at] for c in range(3, 6)]
            current = [physical_ref[c, at, lanes] for c in range(3)]
            vorticity = [physical_ref[c, at, lanes] for c in range(3, 6)]
            lorentz = [a + b for a, b in zip(cross(current, magnetic), cross(velocity, vorticity))]
            for c, value in enumerate(lorentz):
                product_ref[c, at, lanes] = value.astype(jnp.bfloat16)
    to_modes(count, forward_ref, table_ref, product_ref, out_refs)


def second_physics(shares, physical, inverse, forward):
    count, components, tiles, rows, _ = shares.shape
    groups = len(physical)
    width = tiles * LANES
    return pl.pallas_call(
        functools.partial(second_kernel, count, groups),
        in_specs=[vmem()] * (groups + 3),
        out_specs=[vmem()] * count,
        out_shape=[jax.ShapeDtypeStruct((3, tiles, rows, LANES), jnp.bfloat16)] * count,
        scratch_shapes=[
            pltpu.VMEM((components, THETA, width), jnp.float32),
            pltpu.VMEM((components, 2 * M, width), jnp.bfloat16),
            pltpu.VMEM((3, THETA, width), jnp.bfloat16),
            pltpu.VMEM((2 * M, THETA), jnp.bfloat16),
        ],
        compiler_params=params(),
        cost_estimate=cost(),
    )(shares, *physical, inverse, forward)


def tiles_of(in_refs, count):
    me = lax.axis_index("mode")
    components, held, rows, _ = in_refs[0].shape
    groups = len(in_refs) // count
    for group in range(groups):
        for step in range(count):
            share = source_of(me, step, count)
            for t in range(held):
                at = share * (groups * held) + group * held + t
                yield at, in_refs[group * count + step][:, t].reshape(components * rows, LANES)


def interface_kernel(count, arrived, *refs):
    in_refs, (nodes_ref, prev_ref, next_ref) = refs[:arrived], refs[arrived:]
    components, _, rows, _ = in_refs[0].shape
    halo = nodes_ref.shape[1]
    totals = [jnp.zeros((components * rows, halo), jnp.float32) for _ in range(2)]
    inner = lax.broadcasted_iota(jnp.int32, (LANES, halo), 0)
    for at, values in tiles_of(in_refs, count):
        ids = inner + at * LANES
        for way in range(2):
            chosen = jnp.where(ids == nodes_ref[way : way + 1, :], 1.0, 0.0).astype(jnp.bfloat16)
            totals[way] += jnp.dot(values, chosen, preferred_element_type=jnp.float32)
    for out_ref, total in zip((prev_ref, next_ref), totals):
        picked = total.astype(jnp.bfloat16)
        for c in range(components):
            for t in range(halo // LANES):
                out_ref[c, t] = picked[c * rows : (c + 1) * rows, t * LANES : (t + 1) * LANES]


def interface(received, interface_nodes, count):
    components, _, rows, _ = received[0].shape
    halo = interface_nodes.shape[1]
    shape = jax.ShapeDtypeStruct((components, halo // LANES, rows, LANES), jnp.bfloat16)
    return pl.pallas_call(
        functools.partial(interface_kernel, count, len(received)),
        in_specs=[vmem()] * (len(received) + 1),
        out_specs=[vmem()] * 2,
        out_shape=[shape] * 2,
        compiler_params=params(),
        cost_estimate=cost(),
    )(*received, interface_nodes)


def derive_kernel(count, arrived, *refs):
    in_refs = refs[:arrived]
    prev_ref, next_ref, radial_ref, axial_ref, radius_ref, columns_ref = refs[arrived : arrived + 6]
    induction_ref, momentum_ref, extended_ref = refs[arrived + 6 :]
    me = lax.axis_index("mode")
    components, held, rows, _ = in_refs[0].shape
    mode_count = rows // 2
    node_tiles = arrived * held
    halo_tiles = prev_ref.shape[1]

    def extend(at, tile):
        extended_ref[0, at] = tile
        extended_ref[1, at] = jnp.concatenate([tile[:, BLK:], tile[:, :BLK]], axis=1)

    for at, tile in tiles_of(in_refs, count):
        extend(at, tile)
    for t in range(halo_tiles):
        extend(node_tiles + t, prev_ref[:, t].reshape(components * rows, LANES))
        extend(node_tiles + halo_tiles + t, next_ref[:, t].reshape(components * rows, LANES))
    modes = (lax.broadcasted_iota(jnp.int32, (mode_count, LANES), 0) + me * mode_count).astype(jnp.float32)
    low = lax.broadcasted_iota(jnp.int32, (components * rows, LANES), 1) < BLK
    lane = lax.broadcasted_iota(jnp.int32, (1, 2 * LANES), 1)
    in_first = jnp.where(lax.rem(lane, LANES) < BLK, 1.0, 0.0)
    in_half = [in_first.astype(jnp.bfloat16), (1.0 - in_first).astype(jnp.bfloat16)]

    def rotated(values):
        return jnp.concatenate([-modes * values[mode_count:], modes * values[:mode_count]], axis=0)

    def pair(b, carry):
        here = pl.ds(pl.multiple_of(b * LANES, LANES), LANES)
        left, right = [], []
        for k in range(NNZB):
            weights = jnp.concatenate([radial_ref[k, :, here], axial_ref[k, :, here]], axis=1)
            first, second = columns_ref[k, 2 * b], columns_ref[k, 2 * b + 1]
            first_tile = extended_ref[lax.rem(first, 2), lax.div(first, 2)]
            second_tile = extended_ref[1 - lax.rem(second, 2), lax.div(second, 2)]
            left.append(jnp.where(low, first_tile, second_tile))
            right += [weights * in_half[0], weights * in_half[1]]
        total = jnp.dot(
            jnp.concatenate(left, axis=1),
            jnp.concatenate(right, axis=0),
            preferred_element_type=jnp.float32,
        )
        along_r = [total[c * rows : (c + 1) * rows, :LANES] for c in range(components)]
        along_z = [total[c * rows : (c + 1) * rows, LANES:] for c in range(components)]
        values = [extended_ref[0, b, c * rows : (c + 1) * rows].astype(jnp.float32) for c in range(components)]
        inv_radius = 1.0 / radius_ref[:, here]
        induction = [
            rotated(values[2]) * inv_radius - along_z[1],
            along_z[0] - along_r[2],
            along_r[1] + values[1] * inv_radius - rotated(values[0]) * inv_radius,
        ]
        stride = 2 * node_tiles
        for i, value in enumerate(induction):
            for p in range(2):
                induction_ref[pl.ds(i * mode_count * stride + 2 * b + p, mode_count, stride=stride), :] = value[
                    p * mode_count : (p + 1) * mode_count
                ]
        momentum_ref[0, b] = along_r[3]
        momentum_ref[1, b] = rotated(values[3]) * inv_radius
        momentum_ref[2, b] = along_z[3]
        return carry

    lax.fori_loop(0, node_tiles, pair, 0, unroll=2)


def derive(received, from_prev, from_next, radial_blocks, axial_blocks, radius, columns, count):
    components, held, rows, _ = received[0].shape
    node_tiles = len(received) * held
    halo_tiles = from_prev.shape[1]
    out_rows = 3 * rows * node_tiles
    return pl.pallas_call(
        functools.partial(derive_kernel, count, len(received)),
        in_specs=[vmem()] * (len(received) + 5) + [pl.BlockSpec(memory_space=pltpu.SMEM)],
        out_specs=[vmem()] * 2,
        out_shape=[
            jax.ShapeDtypeStruct((out_rows, LANES), jnp.float32),
            jax.ShapeDtypeStruct((3, node_tiles, rows, LANES), jnp.float32),
        ],
        scratch_shapes=[pltpu.VMEM((2, node_tiles + 2 * halo_tiles, components * rows, LANES), jnp.bfloat16)],
        compiler_params=params(),
        cost_estimate=cost(),
    )(*received, from_prev, from_next, radial_blocks, axial_blocks, radius, columns)


def momentum_kernel(count, *refs):
    in_refs, (gradient_ref, out_ref, total_ref, sems) = refs[:count], refs[count:]
    me = lax.axis_index("mode")
    components, tiles, rows, _ = in_refs[0].shape
    mode_count = rows // 2
    stride = 2 * count * tiles
    out_rows = mode_count * stride
    copies = []
    for c in range(components):
        for step in range(count):
            share = source_of(me, step, count)
            for t in range(tiles):
                at = share * tiles + t
                value = in_refs[step][c, t].astype(jnp.float32) - gradient_ref[c, at]
                for p in range(2):
                    total_ref[pl.ds(c * out_rows + 2 * at + p, mode_count, stride=stride), :] = value[
                        p * mode_count : (p + 1) * mode_count
                    ]
        done = pl.ds(c * out_rows, out_rows)
        copies.append(pltpu.make_async_copy(total_ref.at[done], out_ref.at[done], sems.at[c]))
        copies[c].start()
    for copy in copies:
        copy.wait()


def momentum_of(received, gradient):
    count = len(received)
    components, tiles, rows, _ = received[0].shape
    shape = (components * rows * count * tiles, LANES)
    return pl.pallas_call(
        functools.partial(momentum_kernel, count),
        in_specs=[vmem()] * (count + 1),
        out_specs=pl.BlockSpec(memory_space=pl.ANY),
        out_shape=jax.ShapeDtypeStruct(shape, jnp.float32),
        scratch_shapes=[pltpu.VMEM(shape, jnp.float32), pltpu.SemaphoreType.DMA((components,))],
        compiler_params=params(),
        cost_estimate=cost(),
    )(*received, gradient)


def whole_output(value, mode_count, width):
    value = value.reshape(3, mode_count, width // LANES, 2, LANES)
    return value.transpose(0, 1, 3, 2, 4).reshape(3, mode_count, 2, width)


def body(mode_fields, radius, radial_blocks, axial_blocks, block_columns, interface_nodes):
    _, mode_count, _, width = mode_fields.shape
    count = lax.axis_size("mode")
    rows = 2 * mode_count
    inverse, forward = tables(M, THETA, count)
    inverse, forward = jnp.asarray(inverse), jnp.asarray(forward)

    def joined(pieces):
        return [piece.reshape(piece.shape[:-3] + (rows, LANES)) for piece in pieces]

    groups = groups_of(width // count // LANES)
    arrived = []
    for group in range(groups):
        arrived.append(exchange([pack(mode_fields, 0, 6, step, group, groups) for step in range(1, count)]))
    *own, shares, inverse, forward = pack_rest(mode_fields, 6, groups, [inverse, forward])
    local, physical = [], []
    for group in range(groups):
        *terms, velocity_magnetic = first_physics(joined([own[group]] + arrived[group]), inverse, forward)
        back = exchange(terms[1:])
        if group == 0:
            back, shares = lax.optimization_barrier((back, shares))
            shares = lax.all_to_all(shares, "mode", 0, 0, tiled=True)
        local += terms[:1] + back
        physical.append(velocity_magnetic)
    toward_prev, toward_next = interface(local, interface_nodes, count)
    from_prev = from_behind(toward_next, "mer", 1)
    from_next = from_behind(toward_prev, "mer", -1)
    induction, gradient = derive(
        local, from_prev, from_next, radial_blocks, axial_blocks, radius.reshape(1, width), block_columns.T, count
    )
    shares, gradient = lax.optimization_barrier((shares, gradient))
    lorentz = list(second_physics(joined([shares])[0], physical, inverse, forward))
    lorentz = lorentz[:1] + exchange(lorentz[1:])
    momentum = momentum_of(lorentz, gradient)
    return (whole_output(induction, mode_count, width), whole_output(momentum, mode_count, width))


def solution(mesh):
    placed = (
        P(None, "mode", None, "mer"),
        P("mer"),
        P(None, None, "mer"),
        P(None, None, "mer"),
        P("mer", None),
        P("mer", None),
    )
    return jax.shard_map(
        body,
        mesh=mesh,
        in_specs=placed,
        out_specs=(P(None, "mode", None, "mer"), P(None, "mode", None, "mer")),
        check_vma=False,
    )
```

```python
import functools
import math

import jax
import jax.numpy as jnp
import ml_dtypes
import numpy as np
from jax import lax
from jax.experimental import pallas as pl
from jax.experimental.pallas import tpu as pltpu
from jax.sharding import PartitionSpec as P

M = 128
THETA = 256
BLK = 64
NNZB = 5
LANES = 128
VMEM_LIMIT = 24 * 1024 * 1024


def params(limit=VMEM_LIMIT):
    return pltpu.CompilerParams(vmem_limit_bytes=limit)


def vmem():
    return pl.BlockSpec(memory_space=pltpu.VMEM)


def cost():
    return pl.CostEstimate(flops=1024, bytes_accessed=1024, transcendentals=0)


def dest_of(me, step, count):
    if count & (count - 1) == 0:
        return jnp.bitwise_xor(me, step)
    return lax.rem(me + step, count)


def source_of(me, step, count):
    if count & (count - 1) == 0:
        return jnp.bitwise_xor(me, step)
    return lax.rem(me + count - step, count)


def exchange(pieces):
    count = len(pieces) + 1
    power = count & (count - 1) == 0
    received = []
    for step in range(1, count):
        pairs = [(i, i ^ step if power else (i + step) % count) for i in range(count)]
        received.append(lax.ppermute(pieces[step - 1], "mode", pairs))
    return received


def from_behind(value, axis, steps):
    count = lax.axis_size(axis)
    initial, last = (max(0, -steps), min(count, count - steps))
    return lax.ppermute(value, axis, [(source, source + steps) for source in range(initial, last)])


def tables(mode_total, angle_total, share_count):
    mode_ids = np.arange(mode_total)
    angle_ids = np.arange(angle_total)
    phase = angle_ids[:, None] * mode_ids[None, :] % angle_total
    angle = phase.astype(np.float32) * np.float32(2.0 * math.pi / angle_total)
    weight = np.where(mode_ids == 0, 1.0, 2.0).astype(np.float32)
    cosines = np.cos(angle)
    sines = np.sin(angle)
    inverse = np.stack([weight * cosines, -weight * sines], axis=-1).astype(ml_dtypes.bfloat16)
    forward = np.stack([cosines.T, -sines.T], axis=1) / np.float32(angle_total)
    forward = forward.reshape(share_count, mode_total // share_count, 2, angle_total)
    forward = forward.transpose(0, 2, 1, 3).reshape(2 * mode_total, angle_total).astype(ml_dtypes.bfloat16)
    return (inverse.reshape(angle_total, 2 * mode_total), forward)


def groups_of(tiles):
    return 1


def pieces_of(fields_ref, first, share, group, out_ref):
    count = lax.axis_size("mode")
    tiles = fields_ref.shape[3] // count // LANES
    components, held = out_ref.shape[:2]
    pairs = []
    for t in range(held):
        start = pl.multiple_of((share * tiles + group * held + t) * LANES, LANES)
        for c in range(components):
            pairs.append((fields_ref.at[first + c, :, :, pl.ds(start, LANES)], out_ref.at[c, t]))
    return pairs


def run_copies(pairs, sems, beside=()):
    copies = [pltpu.make_async_copy(source, target, sems.at[i]) for i, (source, target) in enumerate(pairs)]
    for copy in copies:
        copy.start()
    for source, target in beside:
        target[...] = source[...]
    for copy in copies:
        copy.wait()


def packed_shape(fields, first, last, groups):
    _, mode_count, _, width = fields.shape
    return (last - first, width // lax.axis_size("mode") // LANES // groups, mode_count, 2, LANES)


def pack(fields, first, last, step, group, groups):
    count = lax.axis_size("mode")
    shape = packed_shape(fields, first, last, groups)

    def kernel(fields_ref, out_ref, sems):
        share = dest_of(lax.axis_index("mode"), step, count)
        run_copies(pieces_of(fields_ref, first, share, group, out_ref), sems)

    return pl.pallas_call(
        kernel,
        in_specs=[pl.BlockSpec(memory_space=pl.ANY)],
        out_specs=vmem(),
        out_shape=jax.ShapeDtypeStruct(shape, jnp.bfloat16),
        scratch_shapes=[pltpu.SemaphoreType.DMA((shape[0] * shape[1],))],
        compiler_params=params(),
        cost_estimate=cost(),
    )(fields)


def pack_rest(fields, middle, groups, carried):
    count = lax.axis_size("mode")
    shape = packed_shape(fields, 0, middle, groups)
    full = packed_shape(fields, middle, fields.shape[0], 1)

    def kernel(fields_ref, *refs):
        inputs, refs = refs[: len(carried)], refs[len(carried) :]
        own_refs, share_refs, outputs = refs[:groups], refs[groups : groups + count], refs[groups + count : -1]
        me = lax.axis_index("mode")
        pairs = []
        for group in range(groups):
            pairs += pieces_of(fields_ref, 0, me, group, own_refs[group])
        for step in range(count):
            pairs += pieces_of(fields_ref, middle, dest_of(me, step, count), 0, share_refs[step])
        run_copies(pairs, refs[-1], zip(inputs, outputs))

    return pl.pallas_call(
        kernel,
        in_specs=[pl.BlockSpec(memory_space=pl.ANY)] + [vmem()] * len(carried),
        out_specs=[vmem()] * (groups + count + len(carried)),
        out_shape=[jax.ShapeDtypeStruct(shape, jnp.bfloat16)] * groups
        + [jax.ShapeDtypeStruct(full, jnp.bfloat16)] * count
        + [jax.ShapeDtypeStruct(value.shape, value.dtype) for value in carried],
        scratch_shapes=[pltpu.SemaphoreType.DMA((groups * shape[0] * shape[1] + count * full[0] * full[1],))],
        compiler_params=params(),
        cost_estimate=cost(),
    )(fields, *carried)


def cross(a, b):
    return [a[1] * b[2] - a[2] * b[1], a[2] * b[0] - a[0] * b[2], a[0] * b[1] - a[1] * b[0]]


def to_physical(sources, in_refs, inverse, x_ref, store):
    components, tiles, rows, _ = in_refs[0].shape
    for step, source in enumerate(sources):
        at = pl.multiple_of(source * rows, rows)
        for c in range(components):
            for t in range(tiles):
                x_ref[c, pl.ds(at, rows), t * LANES : (t + 1) * LANES] = in_refs[step][c, t]
    for c in range(components):
        store(c, jnp.dot(inverse, x_ref[c], preferred_element_type=jnp.float32))


def to_modes(count, forward_ref, table_ref, product_ref, out_refs):
    me = lax.axis_index("mode")
    components, tiles, rows, _ = out_refs[0].shape
    for step in range(count):
        at = pl.multiple_of(dest_of(me, step, count) * rows, rows)
        table_ref[step * rows : (step + 1) * rows] = forward_ref[pl.ds(at, rows)]
    for c in range(components):
        terms = jnp.dot(table_ref[...], product_ref[c], preferred_element_type=jnp.float32)
        terms = terms.astype(jnp.bfloat16)
        for step in range(count):
            for t in range(tiles):
                out_refs[step][c, t] = terms[step * rows : (step + 1) * rows, t * LANES : (t + 1) * LANES]


CHUNK = 32


def first_kernel(count, *refs):
    in_refs, (inverse_ref, forward_ref) = refs[:count], refs[count : count + 2]
    out_refs, (physical_ref, x_ref, product_ref, table_ref) = refs[count + 2 : 2 * count + 2], refs[2 * count + 2 :]

    def store(c, value):
        physical_ref[c] = value

    me = lax.axis_index("mode")
    sources = [source_of(me, step, count) for step in range(count)]
    to_physical(sources, in_refs, inverse_ref[...], x_ref, store)
    for i in range(THETA // CHUNK):
        at = slice(i * CHUNK, (i + 1) * CHUNK)
        velocity = [physical_ref[c, at] for c in range(3)]
        magnetic = [physical_ref[c, at] for c in range(3, 6)]
        energy = 0.5 * (velocity[0] * velocity[0] + velocity[1] * velocity[1] + velocity[2] * velocity[2])
        for c, value in enumerate(cross(velocity, magnetic) + [energy]):
            product_ref[c, at] = value.astype(jnp.bfloat16)
    to_modes(count, forward_ref, table_ref, product_ref, out_refs)


def first_physics(received, inverse, forward):
    count = len(received)
    components, tiles, rows, _ = received[0].shape
    width = tiles * LANES
    return pl.pallas_call(
        functools.partial(first_kernel, count),
        in_specs=[vmem()] * (count + 2),
        out_specs=[vmem()] * (count + 1),
        out_shape=[jax.ShapeDtypeStruct((4, tiles, rows, LANES), jnp.bfloat16)] * count
        + [jax.ShapeDtypeStruct((components, THETA, width), jnp.float32)],
        scratch_shapes=[
            pltpu.VMEM((components, 2 * M, width), jnp.bfloat16),
            pltpu.VMEM((4, THETA, width), jnp.bfloat16),
            pltpu.VMEM((2 * M, THETA), jnp.bfloat16),
        ],
        compiler_params=params(),
        cost_estimate=cost(),
    )(*received, inverse, forward)


def second_kernel(count, groups, *refs):
    in_refs, refs = refs[:count], refs[count:]
    first_refs, (inverse_ref, forward_ref) = refs[:groups], refs[groups : groups + 2]
    out_refs, (physical_ref, x_ref, product_ref, table_ref) = refs[groups + 2 : groups + 2 + count], refs[groups + 2 + count :]
    width = first_refs[0].shape[2]

    def store(c, value):
        physical_ref[c] = value

    me = lax.axis_index("mode")
    sources = [source_of(me, step, count) for step in range(count)]
    to_physical(sources, in_refs, inverse_ref[...], x_ref, store)
    for group in range(groups):
        lanes = slice(group * width, (group + 1) * width)
        for i in range(THETA // CHUNK):
            at = slice(i * CHUNK, (i + 1) * CHUNK)
            velocity = [first_refs[group][c, at] for c in range(3)]
            magnetic = [first_refs[group][c, at] for c in range(3, 6)]
            current = [physical_ref[c, at, lanes] for c in range(3)]
            vorticity = [physical_ref[c, at, lanes] for c in range(3, 6)]
            lorentz = [a + b for a, b in zip(cross(current, magnetic), cross(velocity, vorticity))]
            for c, value in enumerate(lorentz):
                product_ref[c, at, lanes] = value.astype(jnp.bfloat16)
    to_modes(count, forward_ref, table_ref, product_ref, out_refs)


def second_physics(received, physical, inverse, forward):
    count = len(received)
    components, tiles, rows, _ = received[0].shape
    groups = len(physical)
    width = tiles * LANES
    return pl.pallas_call(
        functools.partial(second_kernel, count, groups),
        in_specs=[vmem()] * (count + groups + 2),
        out_specs=[vmem()] * count,
        out_shape=[jax.ShapeDtypeStruct((3, tiles, rows, LANES), jnp.bfloat16)] * count,
        scratch_shapes=[
            pltpu.VMEM((components, THETA, width), jnp.float32),
            pltpu.VMEM((components, 2 * M, width), jnp.bfloat16),
            pltpu.VMEM((3, THETA, width), jnp.bfloat16),
            pltpu.VMEM((2 * M, THETA), jnp.bfloat16),
        ],
        compiler_params=params(),
        cost_estimate=cost(),
    )(*received, *physical, inverse, forward)


def tiles_of(in_refs, count):
    me = lax.axis_index("mode")
    components, held, rows, _ = in_refs[0].shape
    groups = len(in_refs) // count
    for group in range(groups):
        for step in range(count):
            share = source_of(me, step, count)
            for t in range(held):
                at = share * (groups * held) + group * held + t
                yield at, in_refs[group * count + step][:, t].reshape(components * rows, LANES)


def interface_kernel(count, arrived, *refs):
    in_refs, (nodes_ref, prev_ref, next_ref) = refs[:arrived], refs[arrived:]
    components, _, rows, _ = in_refs[0].shape
    halo = nodes_ref.shape[1]
    totals = [jnp.zeros((components * rows, halo), jnp.float32) for _ in range(2)]
    inner = lax.broadcasted_iota(jnp.int32, (LANES, halo), 0)
    for at, values in tiles_of(in_refs, count):
        ids = inner + at * LANES
        for way in range(2):
            chosen = jnp.where(ids == nodes_ref[way : way + 1, :], 1.0, 0.0).astype(jnp.bfloat16)
            totals[way] += jnp.dot(values, chosen, preferred_element_type=jnp.float32)
    for out_ref, total in zip((prev_ref, next_ref), totals):
        picked = total.astype(jnp.bfloat16)
        for c in range(components):
            for t in range(halo // LANES):
                out_ref[c, t] = picked[c * rows : (c + 1) * rows, t * LANES : (t + 1) * LANES]


def interface(received, interface_nodes, count):
    components, _, rows, _ = received[0].shape
    halo = interface_nodes.shape[1]
    shape = jax.ShapeDtypeStruct((components, halo // LANES, rows, LANES), jnp.bfloat16)
    return pl.pallas_call(
        functools.partial(interface_kernel, count, len(received)),
        in_specs=[vmem()] * (len(received) + 1),
        out_specs=[vmem()] * 2,
        out_shape=[shape] * 2,
        compiler_params=params(),
        cost_estimate=cost(),
    )(*received, interface_nodes)


def derive_kernel(count, arrived, *refs):
    in_refs = refs[:arrived]
    prev_ref, next_ref, radial_ref, axial_ref, radius_ref, columns_ref = refs[arrived : arrived + 6]
    induction_ref, momentum_ref, extended_ref = refs[arrived + 6 :]
    me = lax.axis_index("mode")
    components, held, rows, _ = in_refs[0].shape
    mode_count = rows // 2
    node_tiles = arrived * held
    halo_tiles = prev_ref.shape[1]

    def extend(at, tile):
        extended_ref[0, at] = tile
        extended_ref[1, at] = jnp.concatenate([tile[:, BLK:], tile[:, :BLK]], axis=1)

    for at, tile in tiles_of(in_refs, count):
        extend(at, tile)
    for t in range(halo_tiles):
        extend(node_tiles + t, prev_ref[:, t].reshape(components * rows, LANES))
        extend(node_tiles + halo_tiles + t, next_ref[:, t].reshape(components * rows, LANES))
    modes = (lax.broadcasted_iota(jnp.int32, (mode_count, LANES), 0) + me * mode_count).astype(jnp.float32)
    low = lax.broadcasted_iota(jnp.int32, (components * rows, LANES), 1) < BLK
    lane = lax.broadcasted_iota(jnp.int32, (1, 2 * LANES), 1)
    in_first = jnp.where(lax.rem(lane, LANES) < BLK, 1.0, 0.0)
    in_half = [in_first.astype(jnp.bfloat16), (1.0 - in_first).astype(jnp.bfloat16)]

    def rotated(values):
        return jnp.concatenate([-modes * values[mode_count:], modes * values[:mode_count]], axis=0)

    def pair(b, carry):
        here = pl.ds(pl.multiple_of(b * LANES, LANES), LANES)
        left, right = [], []
        for k in range(NNZB):
            weights = jnp.concatenate([radial_ref[k, :, here], axial_ref[k, :, here]], axis=1)
            first, second = columns_ref[k, 2 * b], columns_ref[k, 2 * b + 1]
            first_tile = extended_ref[lax.rem(first, 2), lax.div(first, 2)]
            second_tile = extended_ref[1 - lax.rem(second, 2), lax.div(second, 2)]
            left.append(jnp.where(low, first_tile, second_tile))
            right += [weights * in_half[0], weights * in_half[1]]
        total = jnp.dot(
            jnp.concatenate(left, axis=1),
            jnp.concatenate(right, axis=0),
            preferred_element_type=jnp.float32,
        )
        along_r = [total[c * rows : (c + 1) * rows, :LANES] for c in range(components)]
        along_z = [total[c * rows : (c + 1) * rows, LANES:] for c in range(components)]
        values = [extended_ref[0, b, c * rows : (c + 1) * rows].astype(jnp.float32) for c in range(components)]
        inv_radius = 1.0 / radius_ref[:, here]
        induction = [
            rotated(values[2]) * inv_radius - along_z[1],
            along_z[0] - along_r[2],
            along_r[1] + values[1] * inv_radius - rotated(values[0]) * inv_radius,
        ]
        stride = 2 * node_tiles
        for i, value in enumerate(induction):
            for p in range(2):
                induction_ref[pl.ds(i * mode_count * stride + 2 * b + p, mode_count, stride=stride), :] = value[
                    p * mode_count : (p + 1) * mode_count
                ]
        momentum_ref[0, b] = along_r[3]
        momentum_ref[1, b] = rotated(values[3]) * inv_radius
        momentum_ref[2, b] = along_z[3]
        return carry

    lax.fori_loop(0, node_tiles, pair, 0, unroll=2)


def derive(received, from_prev, from_next, radial_blocks, axial_blocks, radius, columns, count):
    components, held, rows, _ = received[0].shape
    node_tiles = len(received) * held
    halo_tiles = from_prev.shape[1]
    out_rows = 3 * rows * node_tiles
    return pl.pallas_call(
        functools.partial(derive_kernel, count, len(received)),
        in_specs=[vmem()] * (len(received) + 5) + [pl.BlockSpec(memory_space=pltpu.SMEM)],
        out_specs=[vmem()] * 2,
        out_shape=[
            jax.ShapeDtypeStruct((out_rows, LANES), jnp.float32),
            jax.ShapeDtypeStruct((3, node_tiles, rows, LANES), jnp.float32),
        ],
        scratch_shapes=[pltpu.VMEM((2, node_tiles + 2 * halo_tiles, components * rows, LANES), jnp.bfloat16)],
        compiler_params=params(),
        cost_estimate=cost(),
    )(*received, from_prev, from_next, radial_blocks, axial_blocks, radius, columns)


def momentum_kernel(count, *refs):
    in_refs, (gradient_ref, out_ref, total_ref, sems) = refs[:count], refs[count:]
    me = lax.axis_index("mode")
    components, tiles, rows, _ = in_refs[0].shape
    mode_count = rows // 2
    stride = 2 * count * tiles
    out_rows = mode_count * stride
    copies = []
    for c in range(components):
        for step in range(count):
            share = source_of(me, step, count)
            for t in range(tiles):
                at = share * tiles + t
                value = in_refs[step][c, t].astype(jnp.float32) - gradient_ref[c, at]
                for p in range(2):
                    total_ref[pl.ds(c * out_rows + 2 * at + p, mode_count, stride=stride), :] = value[
                        p * mode_count : (p + 1) * mode_count
                    ]
        done = pl.ds(c * out_rows, out_rows)
        copies.append(pltpu.make_async_copy(total_ref.at[done], out_ref.at[done], sems.at[c]))
        copies[c].start()
    for copy in copies:
        copy.wait()


def momentum_of(received, gradient):
    count = len(received)
    components, tiles, rows, _ = received[0].shape
    shape = (components * rows * count * tiles, LANES)
    return pl.pallas_call(
        functools.partial(momentum_kernel, count),
        in_specs=[vmem()] * (count + 1),
        out_specs=pl.BlockSpec(memory_space=pl.ANY),
        out_shape=jax.ShapeDtypeStruct(shape, jnp.float32),
        scratch_shapes=[pltpu.VMEM(shape, jnp.float32), pltpu.SemaphoreType.DMA((components,))],
        compiler_params=params(),
        cost_estimate=cost(),
    )(*received, gradient)


def whole_output(value, mode_count, width):
    value = value.reshape(3, mode_count, width // LANES, 2, LANES)
    return value.transpose(0, 1, 3, 2, 4).reshape(3, mode_count, 2, width)


def body(mode_fields, radius, radial_blocks, axial_blocks, block_columns, interface_nodes):
    _, mode_count, _, width = mode_fields.shape
    count = lax.axis_size("mode")
    rows = 2 * mode_count
    inverse, forward = tables(M, THETA, count)
    inverse, forward = jnp.asarray(inverse), jnp.asarray(forward)

    def joined(pieces):
        return [piece.reshape(piece.shape[:-3] + (rows, LANES)) for piece in pieces]

    groups = groups_of(width // count // LANES)
    arrived = []
    for group in range(groups):
        arrived.append(exchange([pack(mode_fields, 0, 6, step, group, groups) for step in range(1, count)]))
    *packed, inverse, forward = pack_rest(mode_fields, 6, groups, [inverse, forward])
    own, shares = packed[:groups], packed[groups:]
    local, physical = [], []
    for group in range(groups):
        *terms, velocity_magnetic = first_physics(joined([own[group]] + arrived[group]), inverse, forward)
        back = exchange(terms[1:])
        if group == 0:
            back[0], shares = lax.optimization_barrier((back[0], shares))
            shares = shares[:1] + exchange(shares[1:])
        local += terms[:1] + back
        physical.append(velocity_magnetic)
    toward_prev, toward_next = interface(local, interface_nodes, count)
    from_prev = from_behind(toward_next, "mer", 1)
    from_next = from_behind(toward_prev, "mer", -1)
    induction, gradient = derive(
        local, from_prev, from_next, radial_blocks, axial_blocks, radius.reshape(1, width), block_columns.T, count
    )
    shares, gradient = lax.optimization_barrier((shares, gradient))
    lorentz = list(second_physics(joined(shares), physical, inverse, forward))
    lorentz = lorentz[:1] + exchange(lorentz[1:])
    momentum = momentum_of(lorentz, gradient)
    return (whole_output(induction, mode_count, width), whole_output(momentum, mode_count, width))


def solution(mesh):
    placed = (
        P(None, "mode", None, "mer"),
        P("mer"),
        P(None, None, "mer"),
        P(None, None, "mer"),
        P("mer", None),
        P("mer", None),
    )
    return jax.shard_map(
        body,
        mesh=mesh,
        in_specs=placed,
        out_specs=(P(None, "mode", None, "mer"), P(None, "mode", None, "mer")),
        check_vma=False,
    )
```

```python
import functools
import math

import jax
import jax.numpy as jnp
import ml_dtypes
import numpy as np
from jax import lax
from jax.experimental import pallas as pl
from jax.experimental.pallas import tpu as pltpu
from jax.sharding import PartitionSpec as P

M = 128
THETA = 256
BLK = 64
NNZB = 5
LANES = 128
VMEM_LIMIT = 24 * 1024 * 1024


def params(limit=VMEM_LIMIT):
    return pltpu.CompilerParams(vmem_limit_bytes=limit)


def vmem():
    return pl.BlockSpec(memory_space=pltpu.VMEM)


def cost():
    return pl.CostEstimate(flops=1024, bytes_accessed=1024, transcendentals=0)


def dest_of(me, step, count):
    if count & (count - 1) == 0:
        return jnp.bitwise_xor(me, step)
    return lax.rem(me + step, count)


def source_of(me, step, count):
    if count & (count - 1) == 0:
        return jnp.bitwise_xor(me, step)
    return lax.rem(me + count - step, count)


def send(piece, step):
    count = lax.axis_size("mode")
    power = count & (count - 1) == 0
    pairs = [(i, i ^ step if power else (i + step) % count) for i in range(count)]
    return lax.ppermute(piece, "mode", pairs)


def exchange(pieces):
    return [send(piece, step) for step, piece in enumerate(pieces, 1)]


def from_behind(value, axis, steps):
    count = lax.axis_size(axis)
    initial, last = (max(0, -steps), min(count, count - steps))
    return lax.ppermute(value, axis, [(source, source + steps) for source in range(initial, last)])


def tables(mode_total, angle_total, share_count):
    mode_ids = np.arange(mode_total)
    angle_ids = np.arange(angle_total)
    phase = angle_ids[:, None] * mode_ids[None, :] % angle_total
    angle = phase.astype(np.float32) * np.float32(2.0 * math.pi / angle_total)
    weight = np.where(mode_ids == 0, 1.0, 2.0).astype(np.float32)
    cosines = np.cos(angle)
    sines = np.sin(angle)
    inverse = np.stack([weight * cosines, -weight * sines], axis=-1).astype(ml_dtypes.bfloat16)
    forward = np.stack([cosines.T, -sines.T], axis=1) / np.float32(angle_total)
    forward = forward.reshape(share_count, mode_total // share_count, 2, angle_total)
    forward = forward.transpose(0, 2, 1, 3).reshape(2 * mode_total, angle_total).astype(ml_dtypes.bfloat16)
    return (inverse.reshape(angle_total, 2 * mode_total), forward)


def groups_of(tiles):
    return 2 if tiles % 2 == 0 else 1


def pieces_of(fields_ref, first, share, group, out_ref):
    count = lax.axis_size("mode")
    tiles = fields_ref.shape[3] // count // LANES
    components, held = out_ref.shape[:2]
    pairs = []
    for t in range(held):
        start = pl.multiple_of((share * tiles + group * held + t) * LANES, LANES)
        for c in range(components):
            pairs.append((fields_ref.at[first + c, :, :, pl.ds(start, LANES)], out_ref.at[c, t]))
    return pairs


def run_copies(pairs, sems, beside=()):
    copies = [pltpu.make_async_copy(source, target, sems.at[i]) for i, (source, target) in enumerate(pairs)]
    for copy in copies:
        copy.start()
    for source, target in beside:
        target[...] = source[...]
    for copy in copies:
        copy.wait()


def packed_shape(fields, first, last, groups):
    _, mode_count, _, width = fields.shape
    return (last - first, width // lax.axis_size("mode") // LANES // groups, mode_count, 2, LANES)


def pack(fields, first, last, step, group, groups):
    count = lax.axis_size("mode")
    shape = packed_shape(fields, first, last, groups)

    def kernel(fields_ref, out_ref, sems):
        share = dest_of(lax.axis_index("mode"), step, count)
        run_copies(pieces_of(fields_ref, first, share, group, out_ref), sems)

    return pl.pallas_call(
        kernel,
        in_specs=[pl.BlockSpec(memory_space=pl.ANY)],
        out_specs=vmem(),
        out_shape=jax.ShapeDtypeStruct(shape, jnp.bfloat16),
        scratch_shapes=[pltpu.SemaphoreType.DMA((shape[0] * shape[1],))],
        compiler_params=params(),
        cost_estimate=cost(),
    )(fields)


def pack_rest(fields, parcels, carried):
    count = lax.axis_size("mode")
    shapes = [packed_shape(fields, first, last, groups) for first, last, _, _, groups in parcels]

    def kernel(fields_ref, *refs):
        inputs, refs = refs[: len(carried)], refs[len(carried) :]
        parcel_refs, outputs = refs[: len(parcels)], refs[len(parcels) : -1]
        me = lax.axis_index("mode")
        pairs = []
        for (first, _, step, group, _), parcel_ref in zip(parcels, parcel_refs):
            pairs += pieces_of(fields_ref, first, dest_of(me, step, count), group, parcel_ref)
        run_copies(pairs, refs[-1], zip(inputs, outputs))

    return pl.pallas_call(
        kernel,
        in_specs=[pl.BlockSpec(memory_space=pl.ANY)] + [vmem()] * len(carried),
        out_specs=[vmem()] * (len(parcels) + len(carried)),
        out_shape=[jax.ShapeDtypeStruct(shape, jnp.bfloat16) for shape in shapes]
        + [jax.ShapeDtypeStruct(value.shape, value.dtype) for value in carried],
        scratch_shapes=[pltpu.SemaphoreType.DMA((sum(shape[0] * shape[1] for shape in shapes),))],
        compiler_params=params(),
        cost_estimate=cost(),
    )(fields, *carried)


def cross(a, b):
    return [a[1] * b[2] - a[2] * b[1], a[2] * b[0] - a[0] * b[2], a[0] * b[1] - a[1] * b[0]]


def to_physical(count, in_refs, inverse, x_ref, store):
    me = lax.axis_index("mode")
    components, tiles, rows, _ = in_refs[0].shape
    for step in range(count):
        at = pl.multiple_of(source_of(me, step, count) * rows, rows)
        for c in range(components):
            for t in range(tiles):
                x_ref[c, pl.ds(at, rows), t * LANES : (t + 1) * LANES] = in_refs[step][c, t]
    for c in range(components):
        store(c, jnp.dot(inverse, x_ref[c], preferred_element_type=jnp.float32))


def to_modes(count, forward_ref, table_ref, product_ref, out_refs):
    me = lax.axis_index("mode")
    components, tiles, rows, _ = out_refs[0].shape
    for step in range(count):
        at = pl.multiple_of(dest_of(me, step, count) * rows, rows)
        table_ref[step * rows : (step + 1) * rows] = forward_ref[pl.ds(at, rows)]
    for c in range(components):
        terms = jnp.dot(table_ref[...], product_ref[c], preferred_element_type=jnp.float32)
        terms = terms.astype(jnp.bfloat16)
        for step in range(count):
            for t in range(tiles):
                out_refs[step][c, t] = terms[step * rows : (step + 1) * rows, t * LANES : (t + 1) * LANES]


CHUNK = 32


def first_kernel(count, *refs):
    in_refs, (inverse_ref, forward_ref) = refs[:count], refs[count : count + 2]
    out_refs, (physical_ref, x_ref, product_ref, table_ref) = refs[count + 2 : 2 * count + 2], refs[2 * count + 2 :]

    def store(c, value):
        physical_ref[c] = value

    to_physical(count, in_refs, inverse_ref[...], x_ref, store)
    for i in range(THETA // CHUNK):
        at = slice(i * CHUNK, (i + 1) * CHUNK)
        velocity = [physical_ref[c, at] for c in range(3)]
        magnetic = [physical_ref[c, at] for c in range(3, 6)]
        energy = 0.5 * (velocity[0] * velocity[0] + velocity[1] * velocity[1] + velocity[2] * velocity[2])
        for c, value in enumerate(cross(velocity, magnetic) + [energy]):
            product_ref[c, at] = value.astype(jnp.bfloat16)
    to_modes(count, forward_ref, table_ref, product_ref, out_refs)


def first_physics(received, inverse, forward):
    count = len(received)
    components, tiles, rows, _ = received[0].shape
    width = tiles * LANES
    return pl.pallas_call(
        functools.partial(first_kernel, count),
        in_specs=[vmem()] * (count + 2),
        out_specs=[vmem()] * (count + 1),
        out_shape=[jax.ShapeDtypeStruct((4, tiles, rows, LANES), jnp.bfloat16)] * count
        + [jax.ShapeDtypeStruct((components, THETA, width), jnp.float32)],
        scratch_shapes=[
            pltpu.VMEM((components, 2 * M, width), jnp.bfloat16),
            pltpu.VMEM((4, THETA, width), jnp.bfloat16),
            pltpu.VMEM((2 * M, THETA), jnp.bfloat16),
        ],
        compiler_params=params(),
        cost_estimate=cost(),
    )(*received, inverse, forward)


def second_kernel(count, groups, *refs):
    in_refs, refs = refs[:count], refs[count:]
    first_refs, (inverse_ref, forward_ref) = refs[:groups], refs[groups : groups + 2]
    out_refs, (physical_ref, x_ref, product_ref, table_ref) = refs[groups + 2 : groups + 2 + count], refs[groups + 2 + count :]
    width = first_refs[0].shape[2]

    def store(c, value):
        physical_ref[c] = value

    to_physical(count, in_refs, inverse_ref[...], x_ref, store)
    for group in range(groups):
        lanes = slice(group * width, (group + 1) * width)
        for i in range(THETA // CHUNK):
            at = slice(i * CHUNK, (i + 1) * CHUNK)
            velocity = [first_refs[group][c, at] for c in range(3)]
            magnetic = [first_refs[group][c, at] for c in range(3, 6)]
            current = [physical_ref[c, at, lanes] for c in range(3)]
            vorticity = [physical_ref[c, at, lanes] for c in range(3, 6)]
            lorentz = [a + b for a, b in zip(cross(current, magnetic), cross(velocity, vorticity))]
            for c, value in enumerate(lorentz):
                product_ref[c, at, lanes] = value.astype(jnp.bfloat16)
    to_modes(count, forward_ref, table_ref, product_ref, out_refs)


def second_physics(received, physical, inverse, forward):
    count, groups = len(received), len(physical)
    components, tiles, rows, _ = received[0].shape
    width = tiles * LANES
    return pl.pallas_call(
        functools.partial(second_kernel, count, groups),
        in_specs=[vmem()] * (count + groups + 2),
        out_specs=[vmem()] * count,
        out_shape=[jax.ShapeDtypeStruct((3, tiles, rows, LANES), jnp.bfloat16)] * count,
        scratch_shapes=[
            pltpu.VMEM((components, THETA, width), jnp.float32),
            pltpu.VMEM((components, 2 * M, width), jnp.bfloat16),
            pltpu.VMEM((3, THETA, width), jnp.bfloat16),
            pltpu.VMEM((2 * M, THETA), jnp.bfloat16),
        ],
        compiler_params=params(),
        cost_estimate=cost(),
    )(*received, *physical, inverse, forward)


def tiles_of(in_refs, count):
    me = lax.axis_index("mode")
    components, held, rows, _ = in_refs[0].shape
    groups = len(in_refs) // count
    for group in range(groups):
        for step in range(count):
            share = source_of(me, step, count)
            for t in range(held):
                at = share * (groups * held) + group * held + t
                yield at, in_refs[group * count + step][:, t].reshape(components * rows, LANES)


def interface_kernel(count, arrived, *refs):
    in_refs, (nodes_ref, prev_ref, next_ref) = refs[:arrived], refs[arrived:]
    components, _, rows, _ = in_refs[0].shape
    halo = nodes_ref.shape[1]
    totals = [jnp.zeros((components * rows, halo), jnp.float32) for _ in range(2)]
    inner = lax.broadcasted_iota(jnp.int32, (LANES, halo), 0)
    for at, values in tiles_of(in_refs, count):
        ids = inner + at * LANES
        for way in range(2):
            chosen = jnp.where(ids == nodes_ref[way : way + 1, :], 1.0, 0.0).astype(jnp.bfloat16)
            totals[way] += jnp.dot(values, chosen, preferred_element_type=jnp.float32)
    for out_ref, total in zip((prev_ref, next_ref), totals):
        picked = total.astype(jnp.bfloat16)
        for c in range(components):
            for t in range(halo // LANES):
                out_ref[c, t] = picked[c * rows : (c + 1) * rows, t * LANES : (t + 1) * LANES]


def interface(received, interface_nodes, count):
    components, _, rows, _ = received[0].shape
    halo = interface_nodes.shape[1]
    shape = jax.ShapeDtypeStruct((components, halo // LANES, rows, LANES), jnp.bfloat16)
    return pl.pallas_call(
        functools.partial(interface_kernel, count, len(received)),
        in_specs=[vmem()] * (len(received) + 1),
        out_specs=[vmem()] * 2,
        out_shape=[shape] * 2,
        compiler_params=params(),
        cost_estimate=cost(),
    )(*received, interface_nodes)


def derive_kernel(count, arrived, *refs):
    in_refs = refs[:arrived]
    prev_ref, next_ref, radial_ref, axial_ref, radius_ref, columns_ref = refs[arrived : arrived + 6]
    induction_ref, momentum_ref, extended_ref = refs[arrived + 6 :]
    me = lax.axis_index("mode")
    components, held, rows, _ = in_refs[0].shape
    mode_count = rows // 2
    node_tiles = arrived * held
    halo_tiles = prev_ref.shape[1]

    def extend(at, tile):
        extended_ref[0, at] = tile
        extended_ref[1, at] = jnp.concatenate([tile[:, BLK:], tile[:, :BLK]], axis=1)

    for at, tile in tiles_of(in_refs, count):
        extend(at, tile)
    for t in range(halo_tiles):
        extend(node_tiles + t, prev_ref[:, t].reshape(components * rows, LANES))
        extend(node_tiles + halo_tiles + t, next_ref[:, t].reshape(components * rows, LANES))
    modes = (lax.broadcasted_iota(jnp.int32, (mode_count, LANES), 0) + me * mode_count).astype(jnp.float32)
    low = lax.broadcasted_iota(jnp.int32, (components * rows, LANES), 1) < BLK
    lane = lax.broadcasted_iota(jnp.int32, (1, 2 * LANES), 1)
    in_first = jnp.where(lax.rem(lane, LANES) < BLK, 1.0, 0.0)
    in_half = [in_first.astype(jnp.bfloat16), (1.0 - in_first).astype(jnp.bfloat16)]

    def rotated(values):
        return jnp.concatenate([-modes * values[mode_count:], modes * values[:mode_count]], axis=0)

    def pair(b, carry):
        here = pl.ds(pl.multiple_of(b * LANES, LANES), LANES)
        left, right = [], []
        for k in range(NNZB):
            weights = jnp.concatenate([radial_ref[k, :, here], axial_ref[k, :, here]], axis=1)
            first, second = columns_ref[k, 2 * b], columns_ref[k, 2 * b + 1]
            first_tile = extended_ref[lax.rem(first, 2), lax.div(first, 2)]
            second_tile = extended_ref[1 - lax.rem(second, 2), lax.div(second, 2)]
            left.append(jnp.where(low, first_tile, second_tile))
            right += [weights * in_half[0], weights * in_half[1]]
        total = jnp.dot(
            jnp.concatenate(left, axis=1),
            jnp.concatenate(right, axis=0),
            preferred_element_type=jnp.float32,
        )
        along_r = [total[c * rows : (c + 1) * rows, :LANES] for c in range(components)]
        along_z = [total[c * rows : (c + 1) * rows, LANES:] for c in range(components)]
        values = [extended_ref[0, b, c * rows : (c + 1) * rows].astype(jnp.float32) for c in range(components)]
        inv_radius = 1.0 / radius_ref[:, here]
        induction = [
            rotated(values[2]) * inv_radius - along_z[1],
            along_z[0] - along_r[2],
            along_r[1] + values[1] * inv_radius - rotated(values[0]) * inv_radius,
        ]
        stride = 2 * node_tiles
        for i, value in enumerate(induction):
            for p in range(2):
                induction_ref[pl.ds(i * mode_count * stride + 2 * b + p, mode_count, stride=stride), :] = value[
                    p * mode_count : (p + 1) * mode_count
                ]
        momentum_ref[0, b] = along_r[3]
        momentum_ref[1, b] = rotated(values[3]) * inv_radius
        momentum_ref[2, b] = along_z[3]
        return carry

    lax.fori_loop(0, node_tiles, pair, 0, unroll=2)


def derive(received, from_prev, from_next, radial_blocks, axial_blocks, radius, columns, count):
    components, held, rows, _ = received[0].shape
    node_tiles = len(received) * held
    halo_tiles = from_prev.shape[1]
    out_rows = 3 * rows * node_tiles
    return pl.pallas_call(
        functools.partial(derive_kernel, count, len(received)),
        in_specs=[vmem()] * (len(received) + 5) + [pl.BlockSpec(memory_space=pltpu.SMEM)],
        out_specs=[vmem()] * 2,
        out_shape=[
            jax.ShapeDtypeStruct((out_rows, LANES), jnp.float32),
            jax.ShapeDtypeStruct((3, node_tiles, rows, LANES), jnp.float32),
        ],
        scratch_shapes=[pltpu.VMEM((2, node_tiles + 2 * halo_tiles, components * rows, LANES), jnp.bfloat16)],
        compiler_params=params(),
        cost_estimate=cost(),
    )(*received, from_prev, from_next, radial_blocks, axial_blocks, radius, columns)


SUBLANES = 8


def interleaved(parts):
    parts = list(parts)
    row = lax.broadcasted_iota(jnp.int32, parts[0].shape, 1)
    for distance in (1, 2, 4):
        upper = jnp.bitwise_and(row, distance) != 0
        for k in range(SUBLANES):
            if k & distance == 0:
                first, second = parts[k], parts[k + distance]
                parts[k] = jnp.where(upper, pltpu.roll(second, distance, 1), first)
                parts[k + distance] = jnp.where(upper, second, pltpu.roll(first, SUBLANES - distance, 1))
    return parts


def momentum_kernel(count, arrived, *refs):
    in_refs, (gradient_ref, out_ref, total_ref, sems) = refs[:arrived], refs[arrived:]
    me = lax.axis_index("mode")
    components, held, rows, _ = in_refs[0].shape
    mode_count = rows // 2
    tiles = arrived // count * held
    stride = 2 * count * tiles
    out_rows = mode_count * stride
    copies = []
    for c in range(components):
        for step in range(count):
            share = source_of(me, step, count)
            for start in range(0, tiles, SUBLANES // 2):
                parts = []
                for t in range(start, min(tiles, start + SUBLANES // 2)):
                    at = share * tiles + t
                    piece_ref = in_refs[t // held * count + step]
                    value = piece_ref[c, t % held].astype(jnp.float32) - gradient_ref[c, at]
                    parts += [value[:mode_count], value[mode_count:]]
                first = c * out_rows + 2 * (share * tiles + start)
                if len(parts) == SUBLANES:
                    whole = interleaved([part.reshape(mode_count // SUBLANES, SUBLANES, LANES) for part in parts])
                    for mode in range(mode_count):
                        here = pl.ds(pl.multiple_of(first + mode * stride, SUBLANES), SUBLANES)
                        total_ref[here, :] = whole[mode % SUBLANES][mode // SUBLANES]
                else:
                    for i, part in enumerate(parts):
                        total_ref[pl.ds(first + i, mode_count, stride=stride), :] = part
        done = pl.ds(c * out_rows, out_rows)
        copies.append(pltpu.make_async_copy(total_ref.at[done], out_ref.at[done], sems.at[c]))
        copies[c].start()
    for copy in copies:
        copy.wait()


def momentum_of(received, gradient, count):
    components, held, rows, _ = received[0].shape
    shape = (components * rows * len(received) * held, LANES)
    return pl.pallas_call(
        functools.partial(momentum_kernel, count, len(received)),
        in_specs=[vmem()] * (len(received) + 1),
        out_specs=pl.BlockSpec(memory_space=pl.ANY),
        out_shape=jax.ShapeDtypeStruct(shape, jnp.float32),
        scratch_shapes=[pltpu.VMEM(shape, jnp.float32), pltpu.SemaphoreType.DMA((components,))],
        compiler_params=params(),
        cost_estimate=cost(),
    )(*received, gradient)


def whole_output(value, mode_count, width):
    value = value.reshape(3, mode_count, width // LANES, 2, LANES)
    return value.transpose(0, 1, 3, 2, 4).reshape(3, mode_count, 2, width)


def body(mode_fields, radius, radial_blocks, axial_blocks, block_columns, interface_nodes):
    _, mode_count, _, width = mode_fields.shape
    count = lax.axis_size("mode")
    rows = 2 * mode_count
    inverse, forward = tables(M, THETA, count)
    inverse, forward = jnp.asarray(inverse), jnp.asarray(forward)

    def joined(pieces):
        return [piece.reshape(piece.shape[:-3] + (rows, LANES)) for piece in pieces]

    groups = groups_of(width // count // LANES)
    arrived = []
    for group in range(groups):
        arrived.append(exchange([pack(mode_fields, 0, 6, step, group, groups) for step in range(1, count)]))
    parcels = [(0, 6, 0, group, groups) for group in range(groups)]
    parcels += [(6, 12, step, 0, 1) for step in range(count)]
    *packed, inverse, forward = pack_rest(mode_fields, parcels, [inverse, forward])
    own, shares = packed[:groups], packed[groups:]
    local, physical = [], []
    for group in range(groups):
        *terms, velocity_magnetic = first_physics(joined([own[group]] + arrived[group]), inverse, forward)
        local += terms[:1] + exchange(terms[1:])
        physical.append(velocity_magnetic)
    local, shares = lax.optimization_barrier((local, shares))
    sources = shares[:1] + exchange(shares[1:])
    toward_prev, toward_next = interface(local, interface_nodes, count)
    from_prev = from_behind(toward_next, "mer", 1)
    from_next = from_behind(toward_prev, "mer", -1)
    induction, gradient = derive(
        local, from_prev, from_next, radial_blocks, axial_blocks, radius.reshape(1, width), block_columns.T, count
    )
    sources, gradient = lax.optimization_barrier((sources, gradient))
    lorentz = list(second_physics(joined(sources), physical, inverse, forward))
    lorentz = lorentz[:1] + exchange(lorentz[1:])
    momentum = momentum_of(lorentz, gradient, count)
    return (whole_output(induction, mode_count, width), whole_output(momentum, mode_count, width))


def solution(mesh):
    placed = (
        P(None, "mode", None, "mer"),
        P("mer"),
        P(None, None, "mer"),
        P(None, None, "mer"),
        P("mer", None),
        P("mer", None),
    )
    return jax.shard_map(
        body,
        mesh=mesh,
        in_specs=placed,
        out_specs=(P(None, "mode", None, "mer"), P(None, "mode", None, "mer")),
        check_vma=False,
    )
```

```python
import functools
import math

import jax
import jax.numpy as jnp
import ml_dtypes
import numpy as np
from jax import lax
from jax.experimental import pallas as pl
from jax.experimental.pallas import tpu as pltpu
from jax.sharding import PartitionSpec as P

M = 128
THETA = 256
BLK = 64
NNZB = 5
LANES = 128
VMEM_LIMIT = 24 * 1024 * 1024


def params(limit=VMEM_LIMIT):
    return pltpu.CompilerParams(vmem_limit_bytes=limit)


def vmem():
    return pl.BlockSpec(memory_space=pltpu.VMEM)


def cost():
    return pl.CostEstimate(flops=1024, bytes_accessed=1024, transcendentals=0)


def dest_of(me, step, count):
    if count & (count - 1) == 0:
        return jnp.bitwise_xor(me, step)
    return lax.rem(me + step, count)


def source_of(me, step, count):
    if count & (count - 1) == 0:
        return jnp.bitwise_xor(me, step)
    return lax.rem(me + count - step, count)


def send(piece, step):
    count = lax.axis_size("mode")
    power = count & (count - 1) == 0
    pairs = [(i, i ^ step if power else (i + step) % count) for i in range(count)]
    return lax.ppermute(piece, "mode", pairs)


def exchange(pieces):
    return [send(piece, step) for step, piece in enumerate(pieces, 1)]


def from_behind(value, axis, steps):
    count = lax.axis_size(axis)
    initial, last = (max(0, -steps), min(count, count - steps))
    return lax.ppermute(value, axis, [(source, source + steps) for source in range(initial, last)])


def tables(mode_total, angle_total, share_count):
    mode_ids = np.arange(mode_total)
    angle_ids = np.arange(angle_total)
    phase = angle_ids[:, None] * mode_ids[None, :] % angle_total
    angle = phase.astype(np.float32) * np.float32(2.0 * math.pi / angle_total)
    weight = np.where(mode_ids == 0, 1.0, 2.0).astype(np.float32)
    cosines = np.cos(angle)
    sines = np.sin(angle)
    inverse = np.stack([weight * cosines, -weight * sines], axis=-1).astype(ml_dtypes.bfloat16)
    forward = np.stack([cosines.T, -sines.T], axis=1) / np.float32(angle_total)
    forward = forward.reshape(share_count, mode_total // share_count, 2, angle_total)
    forward = forward.transpose(0, 2, 1, 3).reshape(2 * mode_total, angle_total).astype(ml_dtypes.bfloat16)
    return (inverse.reshape(angle_total, 2 * mode_total), forward)


def groups_of(tiles):
    return 2 if tiles % 2 == 0 else 1


def pieces_of(fields_ref, first, share, group, out_ref):
    count = lax.axis_size("mode")
    tiles = fields_ref.shape[3] // count // LANES
    components, held = out_ref.shape[:2]
    pairs = []
    for t in range(held):
        start = pl.multiple_of((share * tiles + group * held + t) * LANES, LANES)
        pairs.append((fields_ref.at[pl.ds(first, components), :, :, pl.ds(start, LANES)], out_ref.at[:, t]))
    return pairs


def run_copies(pairs, sems, beside=()):
    copies = [pltpu.make_async_copy(source, target, sems.at[i]) for i, (source, target) in enumerate(pairs)]
    for copy in copies:
        copy.start()
    for source, target in beside:
        target[...] = source[...]
    for copy in copies:
        copy.wait()


def packed_shape(fields, first, last, groups):
    _, mode_count, _, width = fields.shape
    return (last - first, width // lax.axis_size("mode") // LANES // groups, mode_count, 2, LANES)


def pack(fields, first, last, step, group, groups):
    count = lax.axis_size("mode")
    shape = packed_shape(fields, first, last, groups)

    def kernel(fields_ref, out_ref, sems):
        share = dest_of(lax.axis_index("mode"), step, count)
        run_copies(pieces_of(fields_ref, first, share, group, out_ref), sems)

    return pl.pallas_call(
        kernel,
        in_specs=[pl.BlockSpec(memory_space=pl.ANY)],
        out_specs=vmem(),
        out_shape=jax.ShapeDtypeStruct(shape, jnp.bfloat16),
        scratch_shapes=[pltpu.SemaphoreType.DMA((shape[1],))],
        compiler_params=params(),
        cost_estimate=cost(),
    )(fields)


def pack_rest(fields, parcels, carried):
    count = lax.axis_size("mode")
    shapes = [packed_shape(fields, first, last, groups) for first, last, _, _, groups in parcels]

    def kernel(fields_ref, *refs):
        inputs, refs = refs[: len(carried)], refs[len(carried) :]
        parcel_refs, outputs = refs[: len(parcels)], refs[len(parcels) : -1]
        me = lax.axis_index("mode")
        pairs = []
        for (first, _, step, group, _), parcel_ref in zip(parcels, parcel_refs):
            pairs += pieces_of(fields_ref, first, dest_of(me, step, count), group, parcel_ref)
        run_copies(pairs, refs[-1], zip(inputs, outputs))

    return pl.pallas_call(
        kernel,
        in_specs=[pl.BlockSpec(memory_space=pl.ANY)] + [vmem()] * len(carried),
        out_specs=[vmem()] * (len(parcels) + len(carried)),
        out_shape=[jax.ShapeDtypeStruct(shape, jnp.bfloat16) for shape in shapes]
        + [jax.ShapeDtypeStruct(value.shape, value.dtype) for value in carried],
        scratch_shapes=[pltpu.SemaphoreType.DMA((sum(shape[1] for shape in shapes),))],
        compiler_params=params(),
        cost_estimate=cost(),
    )(fields, *carried)


def cross(a, b):
    return [a[1] * b[2] - a[2] * b[1], a[2] * b[0] - a[0] * b[2], a[0] * b[1] - a[1] * b[0]]


def to_physical(count, in_refs, inverse, x_ref, store):
    me = lax.axis_index("mode")
    components, tiles, rows, _ = in_refs[0].shape
    for step in range(count):
        at = pl.multiple_of(source_of(me, step, count) * rows, rows)
        for c in range(components):
            for t in range(tiles):
                x_ref[c, pl.ds(at, rows), t * LANES : (t + 1) * LANES] = in_refs[step][c, t]
    for c in range(components):
        store(c, jnp.dot(inverse, x_ref[c], preferred_element_type=jnp.float32))


def to_modes(count, forward_ref, table_ref, product_ref, out_refs):
    me = lax.axis_index("mode")
    components, tiles, rows, _ = out_refs[0].shape
    for step in range(count):
        at = pl.multiple_of(dest_of(me, step, count) * rows, rows)
        table_ref[step * rows : (step + 1) * rows] = forward_ref[pl.ds(at, rows)]
    for c in range(components):
        terms = jnp.dot(table_ref[...], product_ref[c], preferred_element_type=jnp.float32)
        terms = terms.astype(jnp.bfloat16)
        for step in range(count):
            for t in range(tiles):
                out_refs[step][c, t] = terms[step * rows : (step + 1) * rows, t * LANES : (t + 1) * LANES]


CHUNK = 32


def first_kernel(count, *refs):
    in_refs, (inverse_ref, forward_ref) = refs[:count], refs[count : count + 2]
    out_refs, (physical_ref, x_ref, product_ref, table_ref) = refs[count + 2 : 2 * count + 2], refs[2 * count + 2 :]

    def store(c, value):
        physical_ref[c] = value

    to_physical(count, in_refs, inverse_ref[...], x_ref, store)
    for i in range(THETA // CHUNK):
        at = slice(i * CHUNK, (i + 1) * CHUNK)
        velocity = [physical_ref[c, at] for c in range(3)]
        magnetic = [physical_ref[c, at] for c in range(3, 6)]
        energy = 0.5 * (velocity[0] * velocity[0] + velocity[1] * velocity[1] + velocity[2] * velocity[2])
        for c, value in enumerate(cross(velocity, magnetic) + [energy]):
            product_ref[c, at] = value.astype(jnp.bfloat16)
    to_modes(count, forward_ref, table_ref, product_ref, out_refs)


def first_physics(received, inverse, forward):
    count = len(received)
    components, tiles, rows, _ = received[0].shape
    width = tiles * LANES
    return pl.pallas_call(
        functools.partial(first_kernel, count),
        in_specs=[vmem()] * (count + 2),
        out_specs=[vmem()] * (count + 1),
        out_shape=[jax.ShapeDtypeStruct((4, tiles, rows, LANES), jnp.bfloat16)] * count
        + [jax.ShapeDtypeStruct((components, THETA, width), jnp.float32)],
        scratch_shapes=[
            pltpu.VMEM((components, 2 * M, width), jnp.bfloat16),
            pltpu.VMEM((4, THETA, width), jnp.bfloat16),
            pltpu.VMEM((2 * M, THETA), jnp.bfloat16),
        ],
        compiler_params=params(),
        cost_estimate=cost(),
    )(*received, inverse, forward)


def second_kernel(count, groups, *refs):
    in_refs, refs = refs[:count], refs[count:]
    first_refs, (inverse_ref, forward_ref) = refs[:groups], refs[groups : groups + 2]
    out_refs, (physical_ref, x_ref, product_ref, table_ref) = refs[groups + 2 : groups + 2 + count], refs[groups + 2 + count :]
    width = first_refs[0].shape[2]

    def store(c, value):
        physical_ref[c] = value

    to_physical(count, in_refs, inverse_ref[...], x_ref, store)
    for group in range(groups):
        lanes = slice(group * width, (group + 1) * width)
        for i in range(THETA // CHUNK):
            at = slice(i * CHUNK, (i + 1) * CHUNK)
            velocity = [first_refs[group][c, at] for c in range(3)]
            magnetic = [first_refs[group][c, at] for c in range(3, 6)]
            current = [physical_ref[c, at, lanes] for c in range(3)]
            vorticity = [physical_ref[c, at, lanes] for c in range(3, 6)]
            lorentz = [a + b for a, b in zip(cross(current, magnetic), cross(velocity, vorticity))]
            for c, value in enumerate(lorentz):
                product_ref[c, at, lanes] = value.astype(jnp.bfloat16)
    to_modes(count, forward_ref, table_ref, product_ref, out_refs)


def second_physics(received, physical, inverse, forward):
    count, groups = len(received), len(physical)
    components, tiles, rows, _ = received[0].shape
    width = tiles * LANES
    return pl.pallas_call(
        functools.partial(second_kernel, count, groups),
        in_specs=[vmem()] * (count + groups + 2),
        out_specs=[vmem()] * count,
        out_shape=[jax.ShapeDtypeStruct((3, tiles, rows, LANES), jnp.bfloat16)] * count,
        scratch_shapes=[
            pltpu.VMEM((components, THETA, width), jnp.float32),
            pltpu.VMEM((components, 2 * M, width), jnp.bfloat16),
            pltpu.VMEM((3, THETA, width), jnp.bfloat16),
            pltpu.VMEM((2 * M, THETA), jnp.bfloat16),
        ],
        compiler_params=params(),
        cost_estimate=cost(),
    )(*received, *physical, inverse, forward)


def tiles_of(in_refs, count):
    me = lax.axis_index("mode")
    components, held, rows, _ = in_refs[0].shape
    groups = len(in_refs) // count
    for group in range(groups):
        for step in range(count):
            share = source_of(me, step, count)
            for t in range(held):
                at = share * (groups * held) + group * held + t
                yield at, in_refs[group * count + step][:, t].reshape(components * rows, LANES)


def interface_kernel(count, arrived, *refs):
    in_refs, (nodes_ref, prev_ref, next_ref) = refs[:arrived], refs[arrived:]
    components, _, rows, _ = in_refs[0].shape
    halo = nodes_ref.shape[1]
    totals = [jnp.zeros((components * rows, halo), jnp.float32) for _ in range(2)]
    inner = lax.broadcasted_iota(jnp.int32, (LANES, halo), 0)
    for at, values in tiles_of(in_refs, count):
        ids = inner + at * LANES
        for way in range(2):
            chosen = jnp.where(ids == nodes_ref[way : way + 1, :], 1.0, 0.0).astype(jnp.bfloat16)
            totals[way] += jnp.dot(values, chosen, preferred_element_type=jnp.float32)
    for out_ref, total in zip((prev_ref, next_ref), totals):
        picked = total.astype(jnp.bfloat16)
        for c in range(components):
            for t in range(halo // LANES):
                out_ref[c, t] = picked[c * rows : (c + 1) * rows, t * LANES : (t + 1) * LANES]


def interface(received, interface_nodes, count):
    components, _, rows, _ = received[0].shape
    halo = interface_nodes.shape[1]
    shape = jax.ShapeDtypeStruct((components, halo // LANES, rows, LANES), jnp.bfloat16)
    return pl.pallas_call(
        functools.partial(interface_kernel, count, len(received)),
        in_specs=[vmem()] * (len(received) + 1),
        out_specs=[vmem()] * 2,
        out_shape=[shape] * 2,
        compiler_params=params(),
        cost_estimate=cost(),
    )(*received, interface_nodes)


def derive_kernel(count, arrived, *refs):
    in_refs = refs[:arrived]
    prev_ref, next_ref, radial_ref, axial_ref, radius_ref, columns_ref = refs[arrived : arrived + 6]
    induction_ref, momentum_ref, extended_ref = refs[arrived + 6 :]
    me = lax.axis_index("mode")
    components, held, rows, _ = in_refs[0].shape
    mode_count = rows // 2
    node_tiles = arrived * held
    halo_tiles = prev_ref.shape[1]

    def extend(at, tile):
        extended_ref[0, at] = tile
        extended_ref[1, at] = jnp.concatenate([tile[:, BLK:], tile[:, :BLK]], axis=1)

    for at, tile in tiles_of(in_refs, count):
        extend(at, tile)
    for t in range(halo_tiles):
        extend(node_tiles + t, prev_ref[:, t].reshape(components * rows, LANES))
        extend(node_tiles + halo_tiles + t, next_ref[:, t].reshape(components * rows, LANES))
    modes = (lax.broadcasted_iota(jnp.int32, (mode_count, LANES), 0) + me * mode_count).astype(jnp.float32)
    low = lax.broadcasted_iota(jnp.int32, (components * rows, LANES), 1) < BLK
    lane = lax.broadcasted_iota(jnp.int32, (1, 2 * LANES), 1)
    in_first = jnp.where(lax.rem(lane, LANES) < BLK, 1.0, 0.0)
    in_half = [in_first.astype(jnp.bfloat16), (1.0 - in_first).astype(jnp.bfloat16)]

    def rotated(values):
        return jnp.concatenate([-modes * values[mode_count:], modes * values[:mode_count]], axis=0)

    def pair(b, carry):
        here = pl.ds(pl.multiple_of(b * LANES, LANES), LANES)
        left, right = [], []
        for k in range(NNZB):
            weights = jnp.concatenate([radial_ref[k, :, here], axial_ref[k, :, here]], axis=1)
            first, second = columns_ref[k, 2 * b], columns_ref[k, 2 * b + 1]
            first_tile = extended_ref[lax.rem(first, 2), lax.div(first, 2)]
            second_tile = extended_ref[1 - lax.rem(second, 2), lax.div(second, 2)]
            left.append(jnp.where(low, first_tile, second_tile))
            right += [weights * in_half[0], weights * in_half[1]]
        total = jnp.dot(
            jnp.concatenate(left, axis=1),
            jnp.concatenate(right, axis=0),
            preferred_element_type=jnp.float32,
        )
        along_r = [total[c * rows : (c + 1) * rows, :LANES] for c in range(components)]
        along_z = [total[c * rows : (c + 1) * rows, LANES:] for c in range(components)]
        values = [extended_ref[0, b, c * rows : (c + 1) * rows].astype(jnp.float32) for c in range(components)]
        inv_radius = 1.0 / radius_ref[:, here]
        induction = [
            rotated(values[2]) * inv_radius - along_z[1],
            along_z[0] - along_r[2],
            along_r[1] + values[1] * inv_radius - rotated(values[0]) * inv_radius,
        ]
        stride = 2 * node_tiles
        for i, value in enumerate(induction):
            for p in range(2):
                induction_ref[pl.ds(i * mode_count * stride + 2 * b + p, mode_count, stride=stride), :] = value[
                    p * mode_count : (p + 1) * mode_count
                ]
        momentum_ref[0, b] = along_r[3]
        momentum_ref[1, b] = rotated(values[3]) * inv_radius
        momentum_ref[2, b] = along_z[3]
        return carry

    lax.fori_loop(0, node_tiles, pair, 0, unroll=2)


def derive(received, from_prev, from_next, radial_blocks, axial_blocks, radius, columns, count):
    components, held, rows, _ = received[0].shape
    node_tiles = len(received) * held
    halo_tiles = from_prev.shape[1]
    out_rows = 3 * rows * node_tiles
    return pl.pallas_call(
        functools.partial(derive_kernel, count, len(received)),
        in_specs=[vmem()] * (len(received) + 5) + [pl.BlockSpec(memory_space=pltpu.SMEM)],
        out_specs=[vmem()] * 2,
        out_shape=[
            jax.ShapeDtypeStruct((out_rows, LANES), jnp.float32),
            jax.ShapeDtypeStruct((3, node_tiles, rows, LANES), jnp.float32),
        ],
        scratch_shapes=[pltpu.VMEM((2, node_tiles + 2 * halo_tiles, components * rows, LANES), jnp.bfloat16)],
        compiler_params=params(),
        cost_estimate=cost(),
    )(*received, from_prev, from_next, radial_blocks, axial_blocks, radius, columns)


SUBLANES = 8


def interleaved(parts):
    parts = list(parts)
    row = lax.broadcasted_iota(jnp.int32, parts[0].shape, 1)
    for distance in (1, 2, 4):
        upper = jnp.bitwise_and(row, distance) != 0
        for k in range(SUBLANES):
            if k & distance == 0:
                first, second = parts[k], parts[k + distance]
                parts[k] = jnp.where(upper, pltpu.roll(second, distance, 1), first)
                parts[k + distance] = jnp.where(upper, second, pltpu.roll(first, SUBLANES - distance, 1))
    return parts


def momentum_kernel(count, arrived, *refs):
    in_refs, (gradient_ref, out_ref, total_ref, sems) = refs[:arrived], refs[arrived:]
    me = lax.axis_index("mode")
    components, held, rows, _ = in_refs[0].shape
    mode_count = rows // 2
    tiles = arrived // count * held
    stride = 2 * count * tiles
    out_rows = mode_count * stride
    copies = []
    for c in range(components):
        for step in range(count):
            share = source_of(me, step, count)
            for start in range(0, tiles, SUBLANES // 2):
                parts = []
                for t in range(start, min(tiles, start + SUBLANES // 2)):
                    at = share * tiles + t
                    piece_ref = in_refs[t // held * count + step]
                    value = piece_ref[c, t % held].astype(jnp.float32) - gradient_ref[c, at]
                    parts += [value[:mode_count], value[mode_count:]]
                first = c * out_rows + 2 * (share * tiles + start)
                if len(parts) == SUBLANES:
                    whole = interleaved([part.reshape(mode_count // SUBLANES, SUBLANES, LANES) for part in parts])
                    for mode in range(mode_count):
                        here = pl.ds(pl.multiple_of(first + mode * stride, SUBLANES), SUBLANES)
                        total_ref[here, :] = whole[mode % SUBLANES][mode // SUBLANES]
                else:
                    for i, part in enumerate(parts):
                        total_ref[pl.ds(first + i, mode_count, stride=stride), :] = part
        done = pl.ds(c * out_rows, out_rows)
        copies.append(pltpu.make_async_copy(total_ref.at[done], out_ref.at[done], sems.at[c]))
        copies[c].start()
    for copy in copies:
        copy.wait()


def momentum_of(received, gradient, count):
    components, held, rows, _ = received[0].shape
    shape = (components * rows * len(received) * held, LANES)
    return pl.pallas_call(
        functools.partial(momentum_kernel, count, len(received)),
        in_specs=[vmem()] * (len(received) + 1),
        out_specs=pl.BlockSpec(memory_space=pl.ANY),
        out_shape=jax.ShapeDtypeStruct(shape, jnp.float32),
        scratch_shapes=[pltpu.VMEM(shape, jnp.float32), pltpu.SemaphoreType.DMA((components,))],
        compiler_params=params(),
        cost_estimate=cost(),
    )(*received, gradient)


def whole_output(value, mode_count, width):
    value = value.reshape(3, mode_count, width // LANES, 2, LANES)
    return value.transpose(0, 1, 3, 2, 4).reshape(3, mode_count, 2, width)


def body(mode_fields, radius, radial_blocks, axial_blocks, block_columns, interface_nodes):
    _, mode_count, _, width = mode_fields.shape
    count = lax.axis_size("mode")
    rows = 2 * mode_count
    inverse, forward = tables(M, THETA, count)
    inverse, forward = jnp.asarray(inverse), jnp.asarray(forward)

    def joined(pieces):
        return [piece.reshape(piece.shape[:-3] + (rows, LANES)) for piece in pieces]

    groups = groups_of(width // count // LANES)
    arrived = []
    for group in range(groups):
        arrived.append(exchange([pack(mode_fields, 0, 6, step, group, groups) for step in range(1, count)]))
    parcels = [(0, 6, 0, group, groups) for group in range(groups)]
    *own, inverse, forward = pack_rest(mode_fields, parcels, [inverse, forward])
    arrived[0][1:2], carried = lax.optimization_barrier((arrived[0][1:2], [inverse, forward]))
    parcels = [(6, 12, step, 0, 1) for step in range(count)]
    *shares, later_inverse, later_forward = pack_rest(mode_fields, parcels, carried)
    local, physical = [], []
    for group in range(groups):
        if group == 0:
            tables_here = (later_inverse, later_forward)
        else:
            tables_here = (inverse, forward)
        *terms, velocity_magnetic = first_physics(joined([own[group]] + arrived[group]), *tables_here)
        local += terms[:1] + exchange(terms[1:])
        physical.append(velocity_magnetic)
    local, shares = lax.optimization_barrier((local, shares))
    sources = shares[:1] + exchange(shares[1:])
    toward_prev, toward_next = interface(local, interface_nodes, count)
    halos = (from_behind(toward_next, "mer", 1), from_behind(toward_prev, "mer", -1))
    sources, halos = lax.optimization_barrier((sources, halos))
    lorentz = list(second_physics(joined(sources), physical, later_inverse, later_forward))
    lorentz, radius = lax.optimization_barrier((lorentz, radius))
    lorentz = lorentz[:1] + exchange(lorentz[1:])
    induction, gradient = derive(
        local, *halos, radial_blocks, axial_blocks, radius.reshape(1, width), block_columns.T, count
    )
    momentum = momentum_of(lorentz, gradient, count)
    return (whole_output(induction, mode_count, width), whole_output(momentum, mode_count, width))


def solution(mesh):
    placed = (
        P(None, "mode", None, "mer"),
        P("mer"),
        P(None, None, "mer"),
        P(None, None, "mer"),
        P("mer", None),
        P("mer", None),
    )
    return jax.shard_map(
        body,
        mesh=mesh,
        in_specs=placed,
        out_specs=(P(None, "mode", None, "mer"), P(None, "mode", None, "mer")),
        check_vma=False,
    )
```

```python
import functools
import math

import jax
import jax.numpy as jnp
import ml_dtypes
import numpy as np
from jax import lax
from jax.experimental import pallas as pl
from jax.experimental.pallas import tpu as pltpu
from jax.sharding import PartitionSpec as P

M = 128
THETA = 256
BLK = 64
NNZB = 5
LANES = 128
VMEM_LIMIT = 24 * 1024 * 1024


def params(limit=VMEM_LIMIT):
    return pltpu.CompilerParams(vmem_limit_bytes=limit)


def vmem():
    return pl.BlockSpec(memory_space=pltpu.VMEM)


def cost():
    return pl.CostEstimate(flops=1024, bytes_accessed=1024, transcendentals=0)


def dest_of(me, step, count):
    if count & (count - 1) == 0:
        return jnp.bitwise_xor(me, step)
    return lax.rem(me + step, count)


def source_of(me, step, count):
    if count & (count - 1) == 0:
        return jnp.bitwise_xor(me, step)
    return lax.rem(me + count - step, count)


def send(piece, step):
    count = lax.axis_size("mode")
    power = count & (count - 1) == 0
    pairs = [(i, i ^ step if power else (i + step) % count) for i in range(count)]
    return lax.ppermute(piece, "mode", pairs)


def exchange(pieces):
    return [send(piece, step) for step, piece in enumerate(pieces, 1)]


def swap(piece, step):
    count = lax.axis_size("mode")
    pairs = [[i, i ^ step] for i in range(count) if i < i ^ step]
    both = lax.all_gather(piece.reshape(-1, LANES), "mode", axis_index_groups=pairs)
    return both.reshape((2,) + piece.shape)


def from_behind(value, axis, steps):
    count = lax.axis_size(axis)
    initial, last = (max(0, -steps), min(count, count - steps))
    return lax.ppermute(value, axis, [(source, source + steps) for source in range(initial, last)])


def tables(mode_total, angle_total, share_count):
    mode_ids = np.arange(mode_total)
    angle_ids = np.arange(angle_total)
    phase = angle_ids[:, None] * mode_ids[None, :] % angle_total
    angle = phase.astype(np.float32) * np.float32(2.0 * math.pi / angle_total)
    weight = np.where(mode_ids == 0, 1.0, 2.0).astype(np.float32)
    cosines = np.cos(angle)
    sines = np.sin(angle)
    inverse = np.stack([weight * cosines, -weight * sines], axis=-1).astype(ml_dtypes.bfloat16)
    forward = np.stack([cosines.T, -sines.T], axis=1) / np.float32(angle_total)
    forward = forward.reshape(share_count, mode_total // share_count, 2, angle_total)
    forward = forward.transpose(0, 2, 1, 3).reshape(2 * mode_total, angle_total).astype(ml_dtypes.bfloat16)
    return (inverse.reshape(angle_total, 2 * mode_total), forward)


def groups_of(tiles):
    return 2 if tiles % 2 == 0 else 1


def pieces_of(fields_ref, first, share, group, out_ref):
    count = lax.axis_size("mode")
    tiles = fields_ref.shape[3] // count // LANES
    components, held = out_ref.shape[:2]
    pairs = []
    for t in range(held):
        start = pl.multiple_of((share * tiles + group * held + t) * LANES, LANES)
        pairs.append((fields_ref.at[pl.ds(first, components), :, :, pl.ds(start, LANES)], out_ref.at[:, t]))
    return pairs


def run_copies(pairs, sems, beside=()):
    copies = [pltpu.make_async_copy(source, target, sems.at[i]) for i, (source, target) in enumerate(pairs)]
    for copy in copies:
        copy.start()
    for source, target in beside:
        target[...] = source[...]
    for copy in copies:
        copy.wait()


def packed_shape(fields, first, last, groups):
    _, mode_count, _, width = fields.shape
    return (last - first, width // lax.axis_size("mode") // LANES // groups, mode_count, 2, LANES)


def pack(fields, first, last, step, group, groups):
    count = lax.axis_size("mode")
    shape = packed_shape(fields, first, last, groups)

    def kernel(fields_ref, out_ref, sems):
        share = dest_of(lax.axis_index("mode"), step, count)
        run_copies(pieces_of(fields_ref, first, share, group, out_ref), sems)

    return pl.pallas_call(
        kernel,
        in_specs=[pl.BlockSpec(memory_space=pl.ANY)],
        out_specs=vmem(),
        out_shape=jax.ShapeDtypeStruct(shape, jnp.bfloat16),
        scratch_shapes=[pltpu.SemaphoreType.DMA((shape[1],))],
        compiler_params=params(),
        cost_estimate=cost(),
    )(fields)


def pack_rest(fields, parcels, carried):
    count = lax.axis_size("mode")
    shapes = [packed_shape(fields, first, last, groups) for first, last, _, _, groups in parcels]

    def kernel(fields_ref, *refs):
        inputs, refs = refs[: len(carried)], refs[len(carried) :]
        parcel_refs, outputs = refs[: len(parcels)], refs[len(parcels) : -1]
        me = lax.axis_index("mode")
        pairs = []
        for (first, _, step, group, _), parcel_ref in zip(parcels, parcel_refs):
            pairs += pieces_of(fields_ref, first, dest_of(me, step, count), group, parcel_ref)
        run_copies(pairs, refs[-1], zip(inputs, outputs))

    return pl.pallas_call(
        kernel,
        in_specs=[pl.BlockSpec(memory_space=pl.ANY)] + [vmem()] * len(carried),
        out_specs=[vmem()] * (len(parcels) + len(carried)),
        out_shape=[jax.ShapeDtypeStruct(shape, jnp.bfloat16) for shape in shapes]
        + [jax.ShapeDtypeStruct(value.shape, value.dtype) for value in carried],
        scratch_shapes=[pltpu.SemaphoreType.DMA((sum(shape[1] for shape in shapes),))],
        compiler_params=params(),
        cost_estimate=cost(),
    )(fields, *carried)


def cross(a, b):
    return [a[1] * b[2] - a[2] * b[1], a[2] * b[0] - a[0] * b[2], a[0] * b[1] - a[1] * b[0]]


def to_physical(count, in_refs, inverse, x_ref, store):
    me = lax.axis_index("mode")
    components, tiles, rows, _ = in_refs[0].shape
    for step in range(count):
        at = pl.multiple_of(source_of(me, step, count) * rows, rows)
        for c in range(components):
            for t in range(tiles):
                x_ref[c, pl.ds(at, rows), t * LANES : (t + 1) * LANES] = in_refs[step][c, t]
    for c in range(components):
        store(c, jnp.dot(inverse, x_ref[c], preferred_element_type=jnp.float32))


def to_modes(count, forward_ref, table_ref, product_ref, out_refs):
    me = lax.axis_index("mode")
    components, tiles, rows, _ = out_refs[0].shape
    for step in range(count):
        at = pl.multiple_of(dest_of(me, step, count) * rows, rows)
        table_ref[step * rows : (step + 1) * rows] = forward_ref[pl.ds(at, rows)]
    for c in range(components):
        terms = jnp.dot(table_ref[...], product_ref[c], preferred_element_type=jnp.float32)
        terms = terms.astype(jnp.bfloat16)
        for step in range(count):
            for t in range(tiles):
                out_refs[step][c, t] = terms[step * rows : (step + 1) * rows, t * LANES : (t + 1) * LANES]


CHUNK = 32


def first_kernel(count, *refs):
    in_refs, (inverse_ref, forward_ref) = refs[:count], refs[count : count + 2]
    out_refs, (physical_ref, x_ref, product_ref, table_ref) = refs[count + 2 : 2 * count + 2], refs[2 * count + 2 :]

    def store(c, value):
        physical_ref[c] = value

    to_physical(count, in_refs, inverse_ref[...], x_ref, store)
    for i in range(THETA // CHUNK):
        at = slice(i * CHUNK, (i + 1) * CHUNK)
        velocity = [physical_ref[c, at] for c in range(3)]
        magnetic = [physical_ref[c, at] for c in range(3, 6)]
        energy = 0.5 * (velocity[0] * velocity[0] + velocity[1] * velocity[1] + velocity[2] * velocity[2])
        for c, value in enumerate(cross(velocity, magnetic) + [energy]):
            product_ref[c, at] = value.astype(jnp.bfloat16)
    to_modes(count, forward_ref, table_ref, product_ref, out_refs)


def first_physics(received, inverse, forward):
    count = len(received)
    components, tiles, rows, _ = received[0].shape
    width = tiles * LANES
    return pl.pallas_call(
        functools.partial(first_kernel, count),
        in_specs=[vmem()] * (count + 2),
        out_specs=[vmem()] * (count + 1),
        out_shape=[jax.ShapeDtypeStruct((4, tiles, rows, LANES), jnp.bfloat16)] * count
        + [jax.ShapeDtypeStruct((components, THETA, width), jnp.float32)],
        scratch_shapes=[
            pltpu.VMEM((components, 2 * M, width), jnp.bfloat16),
            pltpu.VMEM((4, THETA, width), jnp.bfloat16),
            pltpu.VMEM((2 * M, THETA), jnp.bfloat16),
        ],
        compiler_params=params(),
        cost_estimate=cost(),
    )(*received, inverse, forward)


def second_kernel(count, groups, *refs):
    me = lax.axis_index("mode")
    in_refs, refs = list(refs[:count]), refs[count:]
    for step in range(1, count):
        in_refs[step] = in_refs[step].at[(jnp.bitwise_xor(me, step) > me).astype(jnp.int32)]
    first_refs, (inverse_ref, forward_ref) = refs[:groups], refs[groups : groups + 2]
    out_refs, (physical_ref, x_ref, product_ref, table_ref) = refs[groups + 2 : groups + 2 + count], refs[groups + 2 + count :]
    width = first_refs[0].shape[2]

    def store(c, value):
        physical_ref[c] = value

    to_physical(count, in_refs, inverse_ref[...], x_ref, store)
    for group in range(groups):
        lanes = slice(group * width, (group + 1) * width)
        for i in range(THETA // CHUNK):
            at = slice(i * CHUNK, (i + 1) * CHUNK)
            velocity = [first_refs[group][c, at] for c in range(3)]
            magnetic = [first_refs[group][c, at] for c in range(3, 6)]
            current = [physical_ref[c, at, lanes] for c in range(3)]
            vorticity = [physical_ref[c, at, lanes] for c in range(3, 6)]
            lorentz = [a + b for a, b in zip(cross(current, magnetic), cross(velocity, vorticity))]
            for c, value in enumerate(lorentz):
                product_ref[c, at, lanes] = value.astype(jnp.bfloat16)
    to_modes(count, forward_ref, table_ref, product_ref, out_refs)


def second_physics(received, physical, inverse, forward):
    count, groups = len(received), len(physical)
    components, tiles, rows, _ = received[0].shape
    width = tiles * LANES
    return pl.pallas_call(
        functools.partial(second_kernel, count, groups),
        in_specs=[vmem()] * (count + groups + 2),
        out_specs=[vmem()] * count,
        out_shape=[jax.ShapeDtypeStruct((3, tiles, rows, LANES), jnp.bfloat16)] * count,
        scratch_shapes=[
            pltpu.VMEM((components, THETA, width), jnp.float32),
            pltpu.VMEM((components, 2 * M, width), jnp.bfloat16),
            pltpu.VMEM((3, THETA, width), jnp.bfloat16),
            pltpu.VMEM((2 * M, THETA), jnp.bfloat16),
        ],
        compiler_params=params(),
        cost_estimate=cost(),
    )(*received, *physical, inverse, forward)


def tiles_of(in_refs, count):
    me = lax.axis_index("mode")
    components, held, rows, _ = in_refs[0].shape
    groups = len(in_refs) // count
    for group in range(groups):
        for step in range(count):
            share = source_of(me, step, count)
            for t in range(held):
                at = share * (groups * held) + group * held + t
                yield at, in_refs[group * count + step][:, t].reshape(components * rows, LANES)


def interface_kernel(count, arrived, *refs):
    in_refs, (nodes_ref, prev_ref, next_ref) = refs[:arrived], refs[arrived:]
    components, _, rows, _ = in_refs[0].shape
    halo = nodes_ref.shape[1]
    totals = [jnp.zeros((components * rows, halo), jnp.float32) for _ in range(2)]
    inner = lax.broadcasted_iota(jnp.int32, (LANES, halo), 0)
    for at, values in tiles_of(in_refs, count):
        ids = inner + at * LANES
        for way in range(2):
            chosen = jnp.where(ids == nodes_ref[way : way + 1, :], 1.0, 0.0).astype(jnp.bfloat16)
            totals[way] += jnp.dot(values, chosen, preferred_element_type=jnp.float32)
    for out_ref, total in zip((prev_ref, next_ref), totals):
        picked = total.astype(jnp.bfloat16)
        for c in range(components):
            for t in range(halo // LANES):
                out_ref[c, t] = picked[c * rows : (c + 1) * rows, t * LANES : (t + 1) * LANES]


def interface(received, interface_nodes, count):
    components, _, rows, _ = received[0].shape
    halo = interface_nodes.shape[1]
    shape = jax.ShapeDtypeStruct((components, halo // LANES, rows, LANES), jnp.bfloat16)
    return pl.pallas_call(
        functools.partial(interface_kernel, count, len(received)),
        in_specs=[vmem()] * (len(received) + 1),
        out_specs=[vmem()] * 2,
        out_shape=[shape] * 2,
        compiler_params=params(),
        cost_estimate=cost(),
    )(*received, interface_nodes)


def derive_kernel(count, arrived, *refs):
    in_refs = refs[:arrived]
    prev_ref, next_ref, radial_ref, axial_ref, radius_ref, columns_ref = refs[arrived : arrived + 6]
    induction_ref, momentum_ref, extended_ref = refs[arrived + 6 :]
    me = lax.axis_index("mode")
    components, held, rows, _ = in_refs[0].shape
    mode_count = rows // 2
    node_tiles = arrived * held
    halo_tiles = prev_ref.shape[1]

    def extend(at, tile):
        extended_ref[0, at] = tile
        extended_ref[1, at] = jnp.concatenate([tile[:, BLK:], tile[:, :BLK]], axis=1)

    for at, tile in tiles_of(in_refs, count):
        extend(at, tile)
    for t in range(halo_tiles):
        extend(node_tiles + t, prev_ref[:, t].reshape(components * rows, LANES))
        extend(node_tiles + halo_tiles + t, next_ref[:, t].reshape(components * rows, LANES))
    modes = (lax.broadcasted_iota(jnp.int32, (mode_count, LANES), 0) + me * mode_count).astype(jnp.float32)
    low = lax.broadcasted_iota(jnp.int32, (components * rows, LANES), 1) < BLK
    lane = lax.broadcasted_iota(jnp.int32, (1, 2 * LANES), 1)
    in_first = jnp.where(lax.rem(lane, LANES) < BLK, 1.0, 0.0)
    in_half = [in_first.astype(jnp.bfloat16), (1.0 - in_first).astype(jnp.bfloat16)]

    def rotated(values):
        return jnp.concatenate([-modes * values[mode_count:], modes * values[:mode_count]], axis=0)

    def pair(b, carry):
        here = pl.ds(pl.multiple_of(b * LANES, LANES), LANES)
        left, right = [], []
        for k in range(NNZB):
            weights = jnp.concatenate([radial_ref[k, :, here], axial_ref[k, :, here]], axis=1)
            first, second = columns_ref[k, 2 * b], columns_ref[k, 2 * b + 1]
            first_tile = extended_ref[lax.rem(first, 2), lax.div(first, 2)]
            second_tile = extended_ref[1 - lax.rem(second, 2), lax.div(second, 2)]
            left.append(jnp.where(low, first_tile, second_tile))
            right += [weights * in_half[0], weights * in_half[1]]
        total = jnp.dot(
            jnp.concatenate(left, axis=1),
            jnp.concatenate(right, axis=0),
            preferred_element_type=jnp.float32,
        )
        along_r = [total[c * rows : (c + 1) * rows, :LANES] for c in range(components)]
        along_z = [total[c * rows : (c + 1) * rows, LANES:] for c in range(components)]
        values = [extended_ref[0, b, c * rows : (c + 1) * rows].astype(jnp.float32) for c in range(components)]
        inv_radius = 1.0 / radius_ref[:, here]
        induction = [
            rotated(values[2]) * inv_radius - along_z[1],
            along_z[0] - along_r[2],
            along_r[1] + values[1] * inv_radius - rotated(values[0]) * inv_radius,
        ]
        stride = 2 * node_tiles
        for i, value in enumerate(induction):
            for p in range(2):
                induction_ref[pl.ds(i * mode_count * stride + 2 * b + p, mode_count, stride=stride), :] = value[
                    p * mode_count : (p + 1) * mode_count
                ]
        momentum_ref[0, b] = along_r[3]
        momentum_ref[1, b] = rotated(values[3]) * inv_radius
        momentum_ref[2, b] = along_z[3]
        return carry

    lax.fori_loop(0, node_tiles, pair, 0, unroll=2)


def derive(received, from_prev, from_next, radial_blocks, axial_blocks, radius, columns, count):
    components, held, rows, _ = received[0].shape
    node_tiles = len(received) * held
    halo_tiles = from_prev.shape[1]
    out_rows = 3 * rows * node_tiles
    return pl.pallas_call(
        functools.partial(derive_kernel, count, len(received)),
        in_specs=[vmem()] * (len(received) + 5) + [pl.BlockSpec(memory_space=pltpu.SMEM)],
        out_specs=[vmem()] * 2,
        out_shape=[
            jax.ShapeDtypeStruct((out_rows, LANES), jnp.float32),
            jax.ShapeDtypeStruct((3, node_tiles, rows, LANES), jnp.float32),
        ],
        scratch_shapes=[pltpu.VMEM((2, node_tiles + 2 * halo_tiles, components * rows, LANES), jnp.bfloat16)],
        compiler_params=params(),
        cost_estimate=cost(),
    )(*received, from_prev, from_next, radial_blocks, axial_blocks, radius, columns)


SUBLANES = 8


def interleaved(parts):
    parts = list(parts)
    row = lax.broadcasted_iota(jnp.int32, parts[0].shape, 1)
    for distance in (1, 2, 4):
        upper = jnp.bitwise_and(row, distance) != 0
        for k in range(SUBLANES):
            if k & distance == 0:
                first, second = parts[k], parts[k + distance]
                parts[k] = jnp.where(upper, pltpu.roll(second, distance, 1), first)
                parts[k + distance] = jnp.where(upper, second, pltpu.roll(first, SUBLANES - distance, 1))
    return parts


def momentum_kernel(count, arrived, *refs):
    in_refs, (gradient_ref, out_ref, total_ref, sems) = refs[:arrived], refs[arrived:]
    me = lax.axis_index("mode")
    components, held, rows, _ = in_refs[0].shape
    mode_count = rows // 2
    tiles = arrived // count * held
    stride = 2 * count * tiles
    out_rows = mode_count * stride
    copies = []
    for c in range(components):
        for step in range(count):
            share = source_of(me, step, count)
            for start in range(0, tiles, SUBLANES // 2):
                parts = []
                for t in range(start, min(tiles, start + SUBLANES // 2)):
                    at = share * tiles + t
                    piece_ref = in_refs[t // held * count + step]
                    value = piece_ref[c, t % held].astype(jnp.float32) - gradient_ref[c, at]
                    parts += [value[:mode_count], value[mode_count:]]
                first = c * out_rows + 2 * (share * tiles + start)
                if len(parts) == SUBLANES:
                    whole = interleaved([part.reshape(mode_count // SUBLANES, SUBLANES, LANES) for part in parts])
                    for mode in range(mode_count):
                        here = pl.ds(pl.multiple_of(first + mode * stride, SUBLANES), SUBLANES)
                        total_ref[here, :] = whole[mode % SUBLANES][mode // SUBLANES]
                else:
                    for i, part in enumerate(parts):
                        total_ref[pl.ds(first + i, mode_count, stride=stride), :] = part
        done = pl.ds(c * out_rows, out_rows)
        copies.append(pltpu.make_async_copy(total_ref.at[done], out_ref.at[done], sems.at[c]))
        copies[c].start()
    for copy in copies:
        copy.wait()


def momentum_of(received, gradient, count):
    components, held, rows, _ = received[0].shape
    shape = (components * rows * len(received) * held, LANES)
    return pl.pallas_call(
        functools.partial(momentum_kernel, count, len(received)),
        in_specs=[vmem()] * (len(received) + 1),
        out_specs=pl.BlockSpec(memory_space=pl.ANY),
        out_shape=jax.ShapeDtypeStruct(shape, jnp.float32),
        scratch_shapes=[pltpu.VMEM(shape, jnp.float32), pltpu.SemaphoreType.DMA((components,))],
        compiler_params=params(),
        cost_estimate=cost(),
    )(*received, gradient)


def whole_output(value, mode_count, width):
    value = value.reshape(3, mode_count, width // LANES, 2, LANES)
    return value.transpose(0, 1, 3, 2, 4).reshape(3, mode_count, 2, width)


def body(mode_fields, radius, radial_blocks, axial_blocks, block_columns, interface_nodes):
    _, mode_count, _, width = mode_fields.shape
    count = lax.axis_size("mode")
    rows = 2 * mode_count
    inverse, forward = tables(M, THETA, count)
    inverse, forward = jnp.asarray(inverse), jnp.asarray(forward)

    def joined(pieces):
        return [piece.reshape(piece.shape[:-3] + (rows, LANES)) for piece in pieces]

    groups = groups_of(width // count // LANES)
    arrived = []
    for group in range(groups):
        arrived.append(exchange([pack(mode_fields, 0, 6, step, group, groups) for step in range(1, count)]))
    parcels = [(0, 6, 0, group, groups) for group in range(groups)]
    *own, inverse, forward = pack_rest(mode_fields, parcels, [inverse, forward])
    arrived[0][1:2], carried = lax.optimization_barrier((arrived[0][1:2], [inverse, forward]))
    parcels = [(6, 12, step, 0, 1) for step in range(count)]
    *shares, later_inverse, later_forward = pack_rest(mode_fields, parcels, carried)
    local, physical = [], []
    for group in range(groups):
        if group == 0:
            tables_here = (later_inverse, later_forward)
        else:
            tables_here = (inverse, forward)
        *terms, velocity_magnetic = first_physics(joined([own[group]] + arrived[group]), *tables_here)
        local += terms[:1] + exchange(terms[1:])
        physical.append(velocity_magnetic)
    local, shares = lax.optimization_barrier((local, shares))
    sources = shares[:1] + [swap(share, step) for step, share in enumerate(shares[1:], 1)]
    toward_prev, toward_next = interface(local, interface_nodes, count)
    halos = (from_behind(toward_next, "mer", 1), from_behind(toward_prev, "mer", -1))
    sources, halos = lax.optimization_barrier((sources, halos))
    lorentz = list(second_physics(joined(sources), physical, later_inverse, later_forward))
    lorentz, radius = lax.optimization_barrier((lorentz, radius))
    lorentz = lorentz[:1] + exchange(lorentz[1:])
    induction, gradient = derive(
        local, *halos, radial_blocks, axial_blocks, radius.reshape(1, width), block_columns.T, count
    )
    momentum = momentum_of(lorentz, gradient, count)
    return (whole_output(induction, mode_count, width), whole_output(momentum, mode_count, width))


def solution(mesh):
    placed = (
        P(None, "mode", None, "mer"),
        P("mer"),
        P(None, None, "mer"),
        P(None, None, "mer"),
        P("mer", None),
        P("mer", None),
    )
    return jax.shard_map(
        body,
        mesh=mesh,
        in_specs=placed,
        out_specs=(P(None, "mode", None, "mer"), P(None, "mode", None, "mer")),
        check_vma=False,
    )
```

```python
import functools
import math

import jax
import jax.numpy as jnp
import ml_dtypes
import numpy as np
from jax import lax
from jax.experimental import pallas as pl
from jax.experimental.pallas import tpu as pltpu
from jax.sharding import PartitionSpec as P

M = 128
THETA = 256
BLK = 64
NNZB = 5
LANES = 128
VMEM_LIMIT = 24 * 1024 * 1024


def params(limit=VMEM_LIMIT):
    return pltpu.CompilerParams(vmem_limit_bytes=limit)


def vmem():
    return pl.BlockSpec(memory_space=pltpu.VMEM)


def cost():
    return pl.CostEstimate(flops=1024, bytes_accessed=1024, transcendentals=0)


def offsets(count, place):
    order = list(range(count - 1))
    order.insert(place, count - 1)
    return order if place < count else list(range(count))


def dest_of(me, offset, count):
    if count & (count - 1) == 0:
        return jnp.bitwise_xor(me, offset)
    return lax.rem(me + offset, count)


def source_of(me, offset, count):
    if count & (count - 1) == 0:
        return jnp.bitwise_xor(me, offset)
    return lax.rem(me + count - offset, count)


def exchange(pieces, order):
    count = lax.axis_size("mode")
    power = count & (count - 1) == 0
    received = []
    for piece, offset in zip(pieces, order):
        if offset == 0:
            received.append(piece)
            continue
        pairs = [(i, i ^ offset if power else (i + offset) % count) for i in range(count)]
        received.append(lax.ppermute(piece, "mode", pairs))
    return received


def from_behind(value, axis, steps):
    count = lax.axis_size(axis)
    initial, last = (max(0, -steps), min(count, count - steps))
    return lax.ppermute(value, axis, [(source, source + steps) for source in range(initial, last)])


def tables(mode_total, angle_total, share_count):
    mode_ids = np.arange(mode_total)
    angle_ids = np.arange(angle_total)
    phase = angle_ids[:, None] * mode_ids[None, :] % angle_total
    angle = phase.astype(np.float32) * np.float32(2.0 * math.pi / angle_total)
    weight = np.where(mode_ids == 0, 1.0, 2.0).astype(np.float32)
    cosines = np.cos(angle)
    sines = np.sin(angle)
    inverse = np.stack([weight * cosines, -weight * sines], axis=-1).astype(ml_dtypes.bfloat16)
    forward = np.stack([cosines.T, -sines.T], axis=1) / np.float32(angle_total)
    forward = forward.reshape(share_count, mode_total // share_count, 2, angle_total)
    forward = forward.transpose(0, 2, 1, 3).reshape(2 * mode_total, angle_total).astype(ml_dtypes.bfloat16)
    return (inverse.reshape(angle_total, 2 * mode_total), forward)


def groups_of(tiles):
    return 2 if tiles % 2 == 0 else 1


def pieces_of(fields_ref, first, share, group, out_ref):
    count = lax.axis_size("mode")
    tiles = fields_ref.shape[3] // count // LANES
    components, held = out_ref.shape[:2]
    pairs = []
    for t in range(held):
        start = pl.multiple_of((share * tiles + group * held + t) * LANES, LANES)
        pairs.append((fields_ref.at[pl.ds(first, components), :, :, pl.ds(start, LANES)], out_ref.at[:, t]))
    return pairs


def run_copies(pairs, sems, beside=()):
    copies = [pltpu.make_async_copy(source, target, sems.at[i]) for i, (source, target) in enumerate(pairs)]
    for copy in copies:
        copy.start()
    for source, target in beside:
        target[...] = source[...]
    for copy in copies:
        copy.wait()


def packed_shape(fields, first, last, groups):
    _, mode_count, _, width = fields.shape
    return (last - first, width // lax.axis_size("mode") // LANES // groups, mode_count, 2, LANES)


def pack(fields, first, last, offset, group, groups):
    count = lax.axis_size("mode")
    shape = packed_shape(fields, first, last, groups)

    def kernel(fields_ref, out_ref, sems):
        share = dest_of(lax.axis_index("mode"), offset, count)
        run_copies(pieces_of(fields_ref, first, share, group, out_ref), sems)

    return pl.pallas_call(
        kernel,
        in_specs=[pl.BlockSpec(memory_space=pl.ANY)],
        out_specs=vmem(),
        out_shape=jax.ShapeDtypeStruct(shape, jnp.bfloat16),
        scratch_shapes=[pltpu.SemaphoreType.DMA((shape[1],))],
        compiler_params=params(),
        cost_estimate=cost(),
    )(fields)


def pack_rest(fields, parcels, carried):
    count = lax.axis_size("mode")
    shapes = [packed_shape(fields, first, last, groups) for first, last, _, _, groups in parcels]

    def kernel(fields_ref, *refs):
        inputs, refs = refs[: len(carried)], refs[len(carried) :]
        parcel_refs, outputs = refs[: len(parcels)], refs[len(parcels) : -1]
        me = lax.axis_index("mode")
        pairs = []
        for (first, _, offset, group, _), parcel_ref in zip(parcels, parcel_refs):
            pairs += pieces_of(fields_ref, first, dest_of(me, offset, count), group, parcel_ref)
        run_copies(pairs, refs[-1], zip(inputs, outputs))

    return pl.pallas_call(
        kernel,
        in_specs=[pl.BlockSpec(memory_space=pl.ANY)] + [vmem()] * len(carried),
        out_specs=[vmem()] * (len(parcels) + len(carried)),
        out_shape=[jax.ShapeDtypeStruct(shape, jnp.bfloat16) for shape in shapes]
        + [jax.ShapeDtypeStruct(value.shape, value.dtype) for value in carried],
        scratch_shapes=[pltpu.SemaphoreType.DMA((sum(shape[1] for shape in shapes),))],
        compiler_params=params(),
        cost_estimate=cost(),
    )(fields, *carried)


def cross(a, b):
    return [a[1] * b[2] - a[2] * b[1], a[2] * b[0] - a[0] * b[2], a[0] * b[1] - a[1] * b[0]]


def to_physical(order, in_refs, inverse, x_ref, store):
    me = lax.axis_index("mode")
    components, tiles, rows, _ = in_refs[0].shape
    for in_ref, offset in zip(in_refs, order):
        at = pl.multiple_of(source_of(me, offset, len(order)) * rows, rows)
        for c in range(components):
            for t in range(tiles):
                x_ref[c, pl.ds(at, rows), t * LANES : (t + 1) * LANES] = in_ref[c, t]
    for c in range(components):
        store(c, jnp.dot(inverse, x_ref[c], preferred_element_type=jnp.float32))


def to_modes(order, forward_ref, table_ref, product_ref, out_refs):
    count = len(order)
    me = lax.axis_index("mode")
    components, tiles, rows, _ = out_refs[0].shape
    for step, offset in enumerate(order):
        at = pl.multiple_of(dest_of(me, offset, count) * rows, rows)
        table_ref[step * rows : (step + 1) * rows] = forward_ref[pl.ds(at, rows)]
    for c in range(components):
        terms = jnp.dot(table_ref[...], product_ref[c], preferred_element_type=jnp.float32)
        terms = terms.astype(jnp.bfloat16)
        for step in range(count):
            for t in range(tiles):
                out_refs[step][c, t] = terms[step * rows : (step + 1) * rows, t * LANES : (t + 1) * LANES]


CHUNK = 32


def first_kernel(count, *refs):
    in_refs, (inverse_ref, forward_ref) = refs[:count], refs[count : count + 2]
    out_refs, (physical_ref, x_ref, product_ref, table_ref) = refs[count + 2 : 2 * count + 2], refs[2 * count + 2 :]

    def store(c, value):
        physical_ref[c] = value

    to_physical(offsets(count, 2), in_refs, inverse_ref[...], x_ref, store)
    for i in range(THETA // CHUNK):
        at = slice(i * CHUNK, (i + 1) * CHUNK)
        velocity = [physical_ref[c, at] for c in range(3)]
        magnetic = [physical_ref[c, at] for c in range(3, 6)]
        energy = 0.5 * (velocity[0] * velocity[0] + velocity[1] * velocity[1] + velocity[2] * velocity[2])
        for c, value in enumerate(cross(velocity, magnetic) + [energy]):
            product_ref[c, at] = value.astype(jnp.bfloat16)
    to_modes(offsets(count, 1), forward_ref, table_ref, product_ref, out_refs)


def first_physics(received, inverse, forward):
    count = len(received)
    components, tiles, rows, _ = received[0].shape
    width = tiles * LANES
    return pl.pallas_call(
        functools.partial(first_kernel, count),
        in_specs=[vmem()] * (count + 2),
        out_specs=[vmem()] * (count + 1),
        out_shape=[jax.ShapeDtypeStruct((4, tiles, rows, LANES), jnp.bfloat16)] * count
        + [jax.ShapeDtypeStruct((components, THETA, width), jnp.float32)],
        scratch_shapes=[
            pltpu.VMEM((components, 2 * M, width), jnp.bfloat16),
            pltpu.VMEM((4, THETA, width), jnp.bfloat16),
            pltpu.VMEM((2 * M, THETA), jnp.bfloat16),
        ],
        compiler_params=params(),
        cost_estimate=cost(),
    )(*received, inverse, forward)


def second_kernel(count, groups, *refs):
    in_refs, refs = refs[:count], refs[count:]
    first_refs, (inverse_ref, forward_ref) = refs[:groups], refs[groups : groups + 2]
    out_refs, (physical_ref, x_ref, product_ref, table_ref) = refs[groups + 2 : groups + 2 + count], refs[groups + 2 + count :]
    width = first_refs[0].shape[2]

    def store(c, value):
        physical_ref[c] = value

    to_physical(offsets(count, 1), in_refs, inverse_ref[...], x_ref, store)
    for group in range(groups):
        lanes = slice(group * width, (group + 1) * width)
        for i in range(THETA // CHUNK):
            at = slice(i * CHUNK, (i + 1) * CHUNK)
            velocity = [first_refs[group][c, at] for c in range(3)]
            magnetic = [first_refs[group][c, at] for c in range(3, 6)]
            current = [physical_ref[c, at, lanes] for c in range(3)]
            vorticity = [physical_ref[c, at, lanes] for c in range(3, 6)]
            lorentz = [a + b for a, b in zip(cross(current, magnetic), cross(velocity, vorticity))]
            for c, value in enumerate(lorentz):
                product_ref[c, at, lanes] = value.astype(jnp.bfloat16)
    to_modes(offsets(count, 1), forward_ref, table_ref, product_ref, out_refs)


def second_physics(received, physical, inverse, forward):
    count, groups = len(received), len(physical)
    components, tiles, rows, _ = received[0].shape
    width = tiles * LANES
    return pl.pallas_call(
        functools.partial(second_kernel, count, groups),
        in_specs=[vmem()] * (count + groups + 2),
        out_specs=[vmem()] * count,
        out_shape=[jax.ShapeDtypeStruct((3, tiles, rows, LANES), jnp.bfloat16)] * count,
        scratch_shapes=[
            pltpu.VMEM((components, THETA, width), jnp.float32),
            pltpu.VMEM((components, 2 * M, width), jnp.bfloat16),
            pltpu.VMEM((3, THETA, width), jnp.bfloat16),
            pltpu.VMEM((2 * M, THETA), jnp.bfloat16),
        ],
        compiler_params=params(),
        cost_estimate=cost(),
    )(*received, *physical, inverse, forward)


def tiles_of(in_refs, count):
    me = lax.axis_index("mode")
    components, held, rows, _ = in_refs[0].shape
    groups = len(in_refs) // count
    for group in range(groups):
        for step, offset in enumerate(offsets(count, 1)):
            share = source_of(me, offset, count)
            for t in range(held):
                at = share * (groups * held) + group * held + t
                yield at, in_refs[group * count + step][:, t].reshape(components * rows, LANES)


def interface_kernel(count, arrived, *refs):
    in_refs, (nodes_ref, prev_ref, next_ref) = refs[:arrived], refs[arrived:]
    components, _, rows, _ = in_refs[0].shape
    halo = nodes_ref.shape[1]
    totals = [jnp.zeros((components * rows, halo), jnp.float32) for _ in range(2)]
    inner = lax.broadcasted_iota(jnp.int32, (LANES, halo), 0)
    for at, values in tiles_of(in_refs, count):
        ids = inner + at * LANES
        for way in range(2):
            chosen = jnp.where(ids == nodes_ref[way : way + 1, :], 1.0, 0.0).astype(jnp.bfloat16)
            totals[way] += jnp.dot(values, chosen, preferred_element_type=jnp.float32)
    for out_ref, total in zip((prev_ref, next_ref), totals):
        picked = total.astype(jnp.bfloat16)
        for c in range(components):
            for t in range(halo // LANES):
                out_ref[c, t] = picked[c * rows : (c + 1) * rows, t * LANES : (t + 1) * LANES]


def interface(received, interface_nodes, count):
    components, _, rows, _ = received[0].shape
    halo = interface_nodes.shape[1]
    shape = jax.ShapeDtypeStruct((components, halo // LANES, rows, LANES), jnp.bfloat16)
    return pl.pallas_call(
        functools.partial(interface_kernel, count, len(received)),
        in_specs=[vmem()] * (len(received) + 1),
        out_specs=[vmem()] * 2,
        out_shape=[shape] * 2,
        compiler_params=params(),
        cost_estimate=cost(),
    )(*received, interface_nodes)


SUBLANES = 8


def interleaved(parts):
    parts = list(parts)
    row = lax.broadcasted_iota(jnp.int32, parts[0].shape, 1)
    for distance in (1, 2, 4):
        upper = jnp.bitwise_and(row, distance) != 0
        for k in range(SUBLANES):
            if k & distance == 0:
                first, second = parts[k], parts[k + distance]
                parts[k] = jnp.where(upper, pltpu.roll(second, distance, 1), first)
                parts[k + distance] = jnp.where(upper, second, pltpu.roll(first, SUBLANES - distance, 1))
    return parts


def put_rows(out_ref, first, stride, tiles):
    modes = tiles[0].shape[0] // 2
    parts = [part for tile in tiles for part in (tile[:modes], tile[modes:])]
    if len(parts) == SUBLANES:
        whole = interleaved([part.reshape(modes // SUBLANES, SUBLANES, LANES) for part in parts])
        for mode in range(modes):
            here = pl.ds(pl.multiple_of(first + mode * stride, SUBLANES), SUBLANES)
            out_ref[here, :] = whole[mode % SUBLANES][mode // SUBLANES]
    else:
        for i, part in enumerate(parts):
            out_ref[pl.ds(first + i, modes, stride=stride), :] = part


def derive_kernel(count, arrived, *refs):
    in_refs = refs[:arrived]
    prev_ref, next_ref, radial_ref, axial_ref, radius_ref, columns_ref = refs[arrived : arrived + 6]
    induction_ref, momentum_ref, extended_ref = refs[arrived + 6 :]
    me = lax.axis_index("mode")
    components, held, rows, _ = in_refs[0].shape
    mode_count = rows // 2
    node_tiles = arrived * held
    halo_tiles = prev_ref.shape[1]

    def extend(at, tile):
        extended_ref[0, at] = tile
        extended_ref[1, at] = jnp.concatenate([tile[:, BLK:], tile[:, :BLK]], axis=1)

    for at, tile in tiles_of(in_refs, count):
        extend(at, tile)
    for t in range(halo_tiles):
        extend(node_tiles + t, prev_ref[:, t].reshape(components * rows, LANES))
        extend(node_tiles + halo_tiles + t, next_ref[:, t].reshape(components * rows, LANES))
    modes = (lax.broadcasted_iota(jnp.int32, (mode_count, LANES), 0) + me * mode_count).astype(jnp.float32)
    low = lax.broadcasted_iota(jnp.int32, (components * rows, LANES), 1) < BLK
    lane = lax.broadcasted_iota(jnp.int32, (1, 2 * LANES), 1)
    in_first = jnp.where(lax.rem(lane, LANES) < BLK, 1.0, 0.0)
    in_half = [in_first.astype(jnp.bfloat16), (1.0 - in_first).astype(jnp.bfloat16)]

    def rotated(values):
        return jnp.concatenate([-modes * values[mode_count:], modes * values[:mode_count]], axis=0)

    def tile_of(b):
        here = pl.ds(pl.multiple_of(b * LANES, LANES), LANES)
        left, right = [], []
        for k in range(NNZB):
            weights = jnp.concatenate([radial_ref[k, :, here], axial_ref[k, :, here]], axis=1)
            first, second = columns_ref[k, 2 * b], columns_ref[k, 2 * b + 1]
            first_tile = extended_ref[lax.rem(first, 2), lax.div(first, 2)]
            second_tile = extended_ref[1 - lax.rem(second, 2), lax.div(second, 2)]
            left.append(jnp.where(low, first_tile, second_tile))
            right += [weights * in_half[0], weights * in_half[1]]
        total = jnp.dot(
            jnp.concatenate(left, axis=1),
            jnp.concatenate(right, axis=0),
            preferred_element_type=jnp.float32,
        )
        along_r = [total[c * rows : (c + 1) * rows, :LANES] for c in range(components)]
        along_z = [total[c * rows : (c + 1) * rows, LANES:] for c in range(components)]
        values = [extended_ref[0, b, c * rows : (c + 1) * rows].astype(jnp.float32) for c in range(components)]
        inv_radius = 1.0 / radius_ref[:, here]
        momentum_ref[0, b] = along_r[3]
        momentum_ref[1, b] = rotated(values[3]) * inv_radius
        momentum_ref[2, b] = along_z[3]
        return [
            rotated(values[2]) * inv_radius - along_z[1],
            along_z[0] - along_r[2],
            along_r[1] + values[1] * inv_radius - rotated(values[0]) * inv_radius,
        ]

    stride = 2 * node_tiles
    together = SUBLANES // 2 if node_tiles % (SUBLANES // 2) == 0 else 1

    def tiles_at(q, carry):
        induction = [tile_of(q * together + i) for i in range(together)]
        for i in range(3):
            put_rows(induction_ref, i * mode_count * stride + 2 * q * together, stride, [tile[i] for tile in induction])
        return carry

    lax.fori_loop(0, node_tiles // together, tiles_at, 0)


def derive(received, from_prev, from_next, radial_blocks, axial_blocks, radius, columns, count):
    components, held, rows, _ = received[0].shape
    node_tiles = len(received) * held
    halo_tiles = from_prev.shape[1]
    out_rows = 3 * rows * node_tiles
    return pl.pallas_call(
        functools.partial(derive_kernel, count, len(received)),
        in_specs=[vmem()] * (len(received) + 5) + [pl.BlockSpec(memory_space=pltpu.SMEM)],
        out_specs=[vmem()] * 2,
        out_shape=[
            jax.ShapeDtypeStruct((out_rows, LANES), jnp.float32),
            jax.ShapeDtypeStruct((3, node_tiles, rows, LANES), jnp.float32),
        ],
        scratch_shapes=[pltpu.VMEM((2, node_tiles + 2 * halo_tiles, components * rows, LANES), jnp.bfloat16)],
        compiler_params=params(),
        cost_estimate=cost(),
    )(*received, from_prev, from_next, radial_blocks, axial_blocks, radius, columns)


def momentum_kernel(count, arrived, *refs):
    in_refs, (gradient_ref, out_ref, total_ref, sems) = refs[:arrived], refs[arrived:]
    me = lax.axis_index("mode")
    components, held, rows, _ = in_refs[0].shape
    mode_count = rows // 2
    tiles = arrived // count * held
    stride = 2 * count * tiles
    out_rows = mode_count * stride
    copies = []
    for c in range(components):
        for step, offset in enumerate(offsets(count, 1)):
            share = source_of(me, offset, count)
            for start in range(0, tiles, SUBLANES // 2):
                values = []
                for t in range(start, min(tiles, start + SUBLANES // 2)):
                    piece = in_refs[t // held * count + step][c, t % held].astype(jnp.float32)
                    values.append(piece - gradient_ref[c, share * tiles + t])
                put_rows(total_ref, c * out_rows + 2 * (share * tiles + start), stride, values)
        done = pl.ds(c * out_rows, out_rows)
        copies.append(pltpu.make_async_copy(total_ref.at[done], out_ref.at[done], sems.at[c]))
        copies[c].start()
    for copy in copies:
        copy.wait()


def momentum_of(received, gradient, count):
    components, held, rows, _ = received[0].shape
    shape = (components * rows * len(received) * held, LANES)
    return pl.pallas_call(
        functools.partial(momentum_kernel, count, len(received)),
        in_specs=[vmem()] * (len(received) + 1),
        out_specs=pl.BlockSpec(memory_space=pl.ANY),
        out_shape=jax.ShapeDtypeStruct(shape, jnp.float32),
        scratch_shapes=[pltpu.VMEM(shape, jnp.float32), pltpu.SemaphoreType.DMA((components,))],
        compiler_params=params(),
        cost_estimate=cost(),
    )(*received, gradient)


def whole_output(value, mode_count, width):
    value = value.reshape(3, mode_count, width // LANES, 2, LANES)
    return value.transpose(0, 1, 3, 2, 4).reshape(3, mode_count, 2, width)


def body(mode_fields, radius, radial_blocks, axial_blocks, block_columns, interface_nodes):
    _, mode_count, _, width = mode_fields.shape
    count = lax.axis_size("mode")
    rows = 2 * mode_count
    inverse, forward = tables(M, THETA, count)
    inverse, forward = jnp.asarray(inverse), jnp.asarray(forward)

    def joined(pieces):
        return [piece.reshape(piece.shape[:-3] + (rows, LANES)) for piece in pieces]

    groups = groups_of(width // count // LANES)
    arrived = []
    for group in range(groups):
        order = offsets(count, 2)
        arrived.append(exchange([pack(mode_fields, 0, 6, offset, group, groups) for offset in order[1:]], order[1:]))
    parcels = [(0, 6, 0, group, groups) for group in range(groups)]
    *own, inverse, forward = pack_rest(mode_fields, parcels, [inverse, forward])
    arrived[0][1:2], carried = lax.optimization_barrier((arrived[0][1:2], [inverse, forward]))
    order = offsets(count, 1)
    parcels = [(6, 12, offset, 0, 1) for offset in order]
    *shares, later_inverse, later_forward = pack_rest(mode_fields, parcels, carried)
    local, physical = [], []
    for group in range(groups):
        if group == 0:
            tables_here = (later_inverse, later_forward)
        else:
            tables_here = (inverse, forward)
        *terms, velocity_magnetic = first_physics(joined([own[group]] + arrived[group]), *tables_here)
        local += exchange(terms, order)
        physical.append(velocity_magnetic)
    local, shares = lax.optimization_barrier((local, shares))
    sources = exchange(shares, order)
    toward_prev, toward_next = interface(local, interface_nodes, count)
    halos = (from_behind(toward_next, "mer", 1), from_behind(toward_prev, "mer", -1))
    sources, halos = lax.optimization_barrier((sources, halos))
    lorentz = list(second_physics(joined(sources), physical, later_inverse, later_forward))
    lorentz, radius = lax.optimization_barrier((lorentz, radius))
    lorentz = exchange(lorentz, order)
    induction, gradient = derive(
        local, *halos, radial_blocks, axial_blocks, radius.reshape(1, width), block_columns.T, count
    )
    momentum = momentum_of(lorentz, gradient, count)
    return (whole_output(induction, mode_count, width), whole_output(momentum, mode_count, width))


def solution(mesh):
    placed = (
        P(None, "mode", None, "mer"),
        P("mer"),
        P(None, None, "mer"),
        P(None, None, "mer"),
        P("mer", None),
        P("mer", None),
    )
    return jax.shard_map(
        body,
        mesh=mesh,
        in_specs=placed,
        out_specs=(P(None, "mode", None, "mer"), P(None, "mode", None, "mer")),
        check_vma=False,
    )
```

```python
import functools
import math

import jax
import jax.numpy as jnp
import ml_dtypes
import numpy as np
from jax import lax
from jax.experimental import pallas as pl
from jax.experimental.pallas import tpu as pltpu
from jax.sharding import PartitionSpec as P

M = 128
THETA = 256
BLK = 64
NNZB = 5
LANES = 128
VMEM_LIMIT = 24 * 1024 * 1024


def params(limit=VMEM_LIMIT):
    return pltpu.CompilerParams(vmem_limit_bytes=limit)


def vmem():
    return pl.BlockSpec(memory_space=pltpu.VMEM)


def cost():
    return pl.CostEstimate(flops=1024, bytes_accessed=1024, transcendentals=0)


FIRST_SEND, FIRST_RETURN, SECOND = 2, 1, None


def offsets(count, place):
    order = list(range(count - 1))
    order.insert(count - 1 if place is None else min(place, count - 1), count - 1)
    return order


def dest_of(me, offset, count):
    if count & (count - 1) == 0:
        return jnp.bitwise_xor(me, offset)
    return lax.rem(me + offset, count)


def source_of(me, offset, count):
    if count & (count - 1) == 0:
        return jnp.bitwise_xor(me, offset)
    return lax.rem(me + count - offset, count)


def exchange(pieces, order):
    count = lax.axis_size("mode")
    power = count & (count - 1) == 0
    received = []
    for piece, offset in zip(pieces, order):
        if offset == 0:
            received.append(piece)
            continue
        pairs = [(i, i ^ offset if power else (i + offset) % count) for i in range(count)]
        received.append(lax.ppermute(piece, "mode", pairs))
    return received


def from_behind(value, axis, steps):
    count = lax.axis_size(axis)
    initial, last = (max(0, -steps), min(count, count - steps))
    return lax.ppermute(value, axis, [(source, source + steps) for source in range(initial, last)])


def tables(mode_total, angle_total, share_count):
    mode_ids = np.arange(mode_total)
    angle_ids = np.arange(angle_total)
    phase = angle_ids[:, None] * mode_ids[None, :] % angle_total
    angle = phase.astype(np.float32) * np.float32(2.0 * math.pi / angle_total)
    weight = np.where(mode_ids == 0, 1.0, 2.0).astype(np.float32)
    cosines = np.cos(angle)
    sines = np.sin(angle)
    inverse = np.stack([weight * cosines, -weight * sines], axis=-1).astype(ml_dtypes.bfloat16)
    forward = np.stack([cosines.T, -sines.T], axis=1) / np.float32(angle_total)
    forward = forward.reshape(share_count, mode_total // share_count, 2, angle_total)
    forward = forward.transpose(0, 2, 1, 3).reshape(2 * mode_total, angle_total).astype(ml_dtypes.bfloat16)
    return (inverse.reshape(angle_total, 2 * mode_total), forward)


def groups_of(tiles):
    return 2 if tiles % 2 == 0 else 1


def pieces_of(fields_ref, first, share, group, out_ref):
    count = lax.axis_size("mode")
    tiles = fields_ref.shape[3] // count // LANES
    components, held = out_ref.shape[:2]
    pairs = []
    for t in range(held):
        start = pl.multiple_of((share * tiles + group * held + t) * LANES, LANES)
        pairs.append((fields_ref.at[pl.ds(first, components), :, :, pl.ds(start, LANES)], out_ref.at[:, t]))
    return pairs


def run_copies(pairs, sems, beside=()):
    copies = [pltpu.make_async_copy(source, target, sems.at[i]) for i, (source, target) in enumerate(pairs)]
    for copy in copies:
        copy.start()
    for source, target in beside:
        target[...] = source[...]
    for copy in copies:
        copy.wait()


def packed_shape(fields, first, last, groups):
    _, mode_count, _, width = fields.shape
    return (last - first, width // lax.axis_size("mode") // LANES // groups, mode_count, 2, LANES)


def pack(fields, first, last, offset, group, groups):
    count = lax.axis_size("mode")
    shape = packed_shape(fields, first, last, groups)

    def kernel(fields_ref, out_ref, sems):
        share = dest_of(lax.axis_index("mode"), offset, count)
        run_copies(pieces_of(fields_ref, first, share, group, out_ref), sems)

    return pl.pallas_call(
        kernel,
        in_specs=[pl.BlockSpec(memory_space=pl.ANY)],
        out_specs=vmem(),
        out_shape=jax.ShapeDtypeStruct(shape, jnp.bfloat16),
        scratch_shapes=[pltpu.SemaphoreType.DMA((shape[1],))],
        compiler_params=params(),
        cost_estimate=cost(),
    )(fields)


def pack_rest(fields, parcels, carried):
    count = lax.axis_size("mode")
    shapes = [packed_shape(fields, first, last, groups) for first, last, _, _, groups in parcels]

    def kernel(fields_ref, *refs):
        inputs, refs = refs[: len(carried)], refs[len(carried) :]
        parcel_refs, outputs = refs[: len(parcels)], refs[len(parcels) : -1]
        me = lax.axis_index("mode")
        pairs = []
        for (first, _, offset, group, _), parcel_ref in zip(parcels, parcel_refs):
            pairs += pieces_of(fields_ref, first, dest_of(me, offset, count), group, parcel_ref)
        run_copies(pairs, refs[-1], zip(inputs, outputs))

    return pl.pallas_call(
        kernel,
        in_specs=[pl.BlockSpec(memory_space=pl.ANY)] + [vmem()] * len(carried),
        out_specs=[vmem()] * (len(parcels) + len(carried)),
        out_shape=[jax.ShapeDtypeStruct(shape, jnp.bfloat16) for shape in shapes]
        + [jax.ShapeDtypeStruct(value.shape, value.dtype) for value in carried],
        scratch_shapes=[pltpu.SemaphoreType.DMA((sum(shape[1] for shape in shapes),))],
        compiler_params=params(),
        cost_estimate=cost(),
    )(fields, *carried)


def cross(a, b):
    return [a[1] * b[2] - a[2] * b[1], a[2] * b[0] - a[0] * b[2], a[0] * b[1] - a[1] * b[0]]


def to_physical(order, in_refs, inverse, x_ref, store):
    me = lax.axis_index("mode")
    components, tiles, rows, _ = in_refs[0].shape
    for in_ref, offset in zip(in_refs, order):
        at = pl.multiple_of(source_of(me, offset, len(order)) * rows, rows)
        for c in range(components):
            for t in range(tiles):
                x_ref[c, pl.ds(at, rows), t * LANES : (t + 1) * LANES] = in_ref[c, t]
    for c in range(components):
        store(c, jnp.dot(inverse, x_ref[c], preferred_element_type=jnp.float32))


def to_modes(order, forward_ref, table_ref, product_ref, out_refs):
    count = len(order)
    me = lax.axis_index("mode")
    components, tiles, rows, _ = out_refs[0].shape
    for step, offset in enumerate(order):
        at = pl.multiple_of(dest_of(me, offset, count) * rows, rows)
        table_ref[step * rows : (step + 1) * rows] = forward_ref[pl.ds(at, rows)]
    for c in range(components):
        terms = jnp.dot(table_ref[...], product_ref[c], preferred_element_type=jnp.float32)
        terms = terms.astype(jnp.bfloat16)
        for step in range(count):
            for t in range(tiles):
                out_refs[step][c, t] = terms[step * rows : (step + 1) * rows, t * LANES : (t + 1) * LANES]


CHUNK = 32


def first_kernel(count, *refs):
    in_refs, (inverse_ref, forward_ref) = refs[:count], refs[count : count + 2]
    out_refs, (physical_ref, x_ref, product_ref, table_ref) = refs[count + 2 : 2 * count + 2], refs[2 * count + 2 :]

    def store(c, value):
        physical_ref[c] = value

    to_physical(offsets(count, FIRST_SEND), in_refs, inverse_ref[...], x_ref, store)
    for i in range(THETA // CHUNK):
        at = slice(i * CHUNK, (i + 1) * CHUNK)
        velocity = [physical_ref[c, at] for c in range(3)]
        magnetic = [physical_ref[c, at] for c in range(3, 6)]
        energy = 0.5 * (velocity[0] * velocity[0] + velocity[1] * velocity[1] + velocity[2] * velocity[2])
        for c, value in enumerate(cross(velocity, magnetic) + [energy]):
            product_ref[c, at] = value.astype(jnp.bfloat16)
    to_modes(offsets(count, FIRST_RETURN), forward_ref, table_ref, product_ref, out_refs)


def first_physics(received, inverse, forward):
    count = len(received)
    components, tiles, rows, _ = received[0].shape
    width = tiles * LANES
    return pl.pallas_call(
        functools.partial(first_kernel, count),
        in_specs=[vmem()] * (count + 2),
        out_specs=[vmem()] * (count + 1),
        out_shape=[jax.ShapeDtypeStruct((4, tiles, rows, LANES), jnp.bfloat16)] * count
        + [jax.ShapeDtypeStruct((components, THETA, width), jnp.float32)],
        scratch_shapes=[
            pltpu.VMEM((components, 2 * M, width), jnp.bfloat16),
            pltpu.VMEM((4, THETA, width), jnp.bfloat16),
            pltpu.VMEM((2 * M, THETA), jnp.bfloat16),
        ],
        compiler_params=params(),
        cost_estimate=cost(),
    )(*received, inverse, forward)


def second_kernel(count, groups, *refs):
    in_refs, refs = refs[:count], refs[count:]
    first_refs, (inverse_ref, forward_ref) = refs[:groups], refs[groups : groups + 2]
    out_refs, (physical_ref, x_ref, product_ref, table_ref) = refs[groups + 2 : groups + 2 + count], refs[groups + 2 + count :]
    width = first_refs[0].shape[2]

    def store(c, value):
        physical_ref[c] = value

    to_physical(offsets(count, SECOND), in_refs, inverse_ref[...], x_ref, store)
    for group in range(groups):
        lanes = slice(group * width, (group + 1) * width)
        for i in range(THETA // CHUNK):
            at = slice(i * CHUNK, (i + 1) * CHUNK)
            velocity = [first_refs[group][c, at] for c in range(3)]
            magnetic = [first_refs[group][c, at] for c in range(3, 6)]
            current = [physical_ref[c, at, lanes] for c in range(3)]
            vorticity = [physical_ref[c, at, lanes] for c in range(3, 6)]
            lorentz = [a + b for a, b in zip(cross(current, magnetic), cross(velocity, vorticity))]
            for c, value in enumerate(lorentz):
                product_ref[c, at, lanes] = value.astype(jnp.bfloat16)
    to_modes(offsets(count, SECOND), forward_ref, table_ref, product_ref, out_refs)


def second_physics(received, physical, inverse, forward):
    count, groups = len(received), len(physical)
    components, tiles, rows, _ = received[0].shape
    width = tiles * LANES
    return pl.pallas_call(
        functools.partial(second_kernel, count, groups),
        in_specs=[vmem()] * (count + groups + 2),
        out_specs=[vmem()] * count,
        out_shape=[jax.ShapeDtypeStruct((3, tiles, rows, LANES), jnp.bfloat16)] * count,
        scratch_shapes=[
            pltpu.VMEM((components, THETA, width), jnp.float32),
            pltpu.VMEM((components, 2 * M, width), jnp.bfloat16),
            pltpu.VMEM((3, THETA, width), jnp.bfloat16),
            pltpu.VMEM((2 * M, THETA), jnp.bfloat16),
        ],
        compiler_params=params(),
        cost_estimate=cost(),
    )(*received, *physical, inverse, forward)


def tiles_of(in_refs, count):
    me = lax.axis_index("mode")
    components, held, rows, _ = in_refs[0].shape
    groups = len(in_refs) // count
    for group in range(groups):
        for step, offset in enumerate(offsets(count, FIRST_RETURN)):
            share = source_of(me, offset, count)
            for t in range(held):
                at = share * (groups * held) + group * held + t
                yield at, in_refs[group * count + step][:, t].reshape(components * rows, LANES)


def interface_kernel(count, arrived, *refs):
    in_refs, (nodes_ref, prev_ref, next_ref) = refs[:arrived], refs[arrived:]
    components, _, rows, _ = in_refs[0].shape
    halo = nodes_ref.shape[1]
    totals = [jnp.zeros((components * rows, halo), jnp.float32) for _ in range(2)]
    inner = lax.broadcasted_iota(jnp.int32, (LANES, halo), 0)
    for at, values in tiles_of(in_refs, count):
        ids = inner + at * LANES
        for way in range(2):
            chosen = jnp.where(ids == nodes_ref[way : way + 1, :], 1.0, 0.0).astype(jnp.bfloat16)
            totals[way] += jnp.dot(values, chosen, preferred_element_type=jnp.float32)
    for out_ref, total in zip((prev_ref, next_ref), totals):
        picked = total.astype(jnp.bfloat16)
        for c in range(components):
            for t in range(halo // LANES):
                out_ref[c, t] = picked[c * rows : (c + 1) * rows, t * LANES : (t + 1) * LANES]


def interface(received, interface_nodes, count):
    components, _, rows, _ = received[0].shape
    halo = interface_nodes.shape[1]
    shape = jax.ShapeDtypeStruct((components, halo // LANES, rows, LANES), jnp.bfloat16)
    return pl.pallas_call(
        functools.partial(interface_kernel, count, len(received)),
        in_specs=[vmem()] * (len(received) + 1),
        out_specs=[vmem()] * 2,
        out_shape=[shape] * 2,
        compiler_params=params(),
        cost_estimate=cost(),
    )(*received, interface_nodes)


SUBLANES = 8


def interleaved(parts):
    parts = list(parts)
    row = lax.broadcasted_iota(jnp.int32, parts[0].shape, 1)
    for distance in (1, 2, 4):
        upper = jnp.bitwise_and(row, distance) != 0
        for k in range(SUBLANES):
            if k & distance == 0:
                first, second = parts[k], parts[k + distance]
                parts[k] = jnp.where(upper, pltpu.roll(second, distance, 1), first)
                parts[k + distance] = jnp.where(upper, second, pltpu.roll(first, SUBLANES - distance, 1))
    return parts


def put_rows(out_ref, first, stride, tiles):
    modes = tiles[0].shape[0] // 2
    parts = [part for tile in tiles for part in (tile[:modes], tile[modes:])]
    if len(parts) == SUBLANES:
        whole = interleaved([part.reshape(modes // SUBLANES, SUBLANES, LANES) for part in parts])
        for mode in range(modes):
            here = pl.ds(pl.multiple_of(first + mode * stride, SUBLANES), SUBLANES)
            out_ref[here, :] = whole[mode % SUBLANES][mode // SUBLANES]
    else:
        for i, part in enumerate(parts):
            out_ref[pl.ds(first + i, modes, stride=stride), :] = part


def derive_kernel(count, arrived, *refs):
    in_refs = refs[:arrived]
    prev_ref, next_ref, radial_ref, axial_ref, radius_ref, columns_ref = refs[arrived : arrived + 6]
    induction_ref, momentum_ref, extended_ref = refs[arrived + 6 :]
    me = lax.axis_index("mode")
    components, held, rows, _ = in_refs[0].shape
    mode_count = rows // 2
    node_tiles = arrived * held
    halo_tiles = prev_ref.shape[1]

    def extend(at, tile):
        extended_ref[0, at] = tile
        extended_ref[1, at] = jnp.concatenate([tile[:, BLK:], tile[:, :BLK]], axis=1)

    for at, tile in tiles_of(in_refs, count):
        extend(at, tile)
    for t in range(halo_tiles):
        extend(node_tiles + t, prev_ref[:, t].reshape(components * rows, LANES))
        extend(node_tiles + halo_tiles + t, next_ref[:, t].reshape(components * rows, LANES))
    modes = (lax.broadcasted_iota(jnp.int32, (mode_count, LANES), 0) + me * mode_count).astype(jnp.float32)
    low = lax.broadcasted_iota(jnp.int32, (components * rows, LANES), 1) < BLK
    lane = lax.broadcasted_iota(jnp.int32, (1, 2 * LANES), 1)
    in_first = jnp.where(lax.rem(lane, LANES) < BLK, 1.0, 0.0)
    in_half = [in_first.astype(jnp.bfloat16), (1.0 - in_first).astype(jnp.bfloat16)]

    def rotated(values):
        return jnp.concatenate([-modes * values[mode_count:], modes * values[:mode_count]], axis=0)

    def tile_of(b):
        here = pl.ds(pl.multiple_of(b * LANES, LANES), LANES)
        left, right = [], []
        for k in range(NNZB):
            weights = jnp.concatenate([radial_ref[k, :, here], axial_ref[k, :, here]], axis=1)
            first, second = columns_ref[k, 2 * b], columns_ref[k, 2 * b + 1]
            first_tile = extended_ref[lax.rem(first, 2), lax.div(first, 2)]
            second_tile = extended_ref[1 - lax.rem(second, 2), lax.div(second, 2)]
            left.append(jnp.where(low, first_tile, second_tile))
            right += [weights * in_half[0], weights * in_half[1]]
        total = jnp.dot(
            jnp.concatenate(left, axis=1),
            jnp.concatenate(right, axis=0),
            preferred_element_type=jnp.float32,
        )
        along_r = [total[c * rows : (c + 1) * rows, :LANES] for c in range(components)]
        along_z = [total[c * rows : (c + 1) * rows, LANES:] for c in range(components)]
        values = [extended_ref[0, b, c * rows : (c + 1) * rows].astype(jnp.float32) for c in range(components)]
        inv_radius = 1.0 / radius_ref[:, here]
        momentum_ref[0, b] = along_r[3]
        momentum_ref[1, b] = rotated(values[3]) * inv_radius
        momentum_ref[2, b] = along_z[3]
        return [
            rotated(values[2]) * inv_radius - along_z[1],
            along_z[0] - along_r[2],
            along_r[1] + values[1] * inv_radius - rotated(values[0]) * inv_radius,
        ]

    stride = 2 * node_tiles
    together = SUBLANES // 2 if node_tiles % (SUBLANES // 2) == 0 else 1

    def tiles_at(q, carry):
        induction = [tile_of(q * together + i) for i in range(together)]
        for i in range(3):
            put_rows(induction_ref, i * mode_count * stride + 2 * q * together, stride, [tile[i] for tile in induction])
        return carry

    lax.fori_loop(0, node_tiles // together, tiles_at, 0)


def derive(received, from_prev, from_next, radial_blocks, axial_blocks, radius, columns, count):
    components, held, rows, _ = received[0].shape
    node_tiles = len(received) * held
    halo_tiles = from_prev.shape[1]
    out_rows = 3 * rows * node_tiles
    return pl.pallas_call(
        functools.partial(derive_kernel, count, len(received)),
        in_specs=[vmem()] * (len(received) + 5) + [pl.BlockSpec(memory_space=pltpu.SMEM)],
        out_specs=[vmem()] * 2,
        out_shape=[
            jax.ShapeDtypeStruct((out_rows, LANES), jnp.float32),
            jax.ShapeDtypeStruct((3, node_tiles, rows, LANES), jnp.float32),
        ],
        scratch_shapes=[pltpu.VMEM((2, node_tiles + 2 * halo_tiles, components * rows, LANES), jnp.bfloat16)],
        compiler_params=params(),
        cost_estimate=cost(),
    )(*received, from_prev, from_next, radial_blocks, axial_blocks, radius, columns)


def momentum_kernel(count, arrived, *refs):
    in_refs, (gradient_ref, out_ref, total_ref, sems) = refs[:arrived], refs[arrived:]
    me = lax.axis_index("mode")
    components, held, rows, _ = in_refs[0].shape
    mode_count = rows // 2
    tiles = arrived // count * held
    stride = 2 * count * tiles
    out_rows = mode_count * stride
    copies = []
    for c in range(components):
        for step, offset in enumerate(offsets(count, SECOND)):
            share = source_of(me, offset, count)
            for start in range(0, tiles, SUBLANES // 2):
                values = []
                for t in range(start, min(tiles, start + SUBLANES // 2)):
                    piece = in_refs[t // held * count + step][c, t % held].astype(jnp.float32)
                    values.append(piece - gradient_ref[c, share * tiles + t])
                put_rows(total_ref, c * out_rows + 2 * (share * tiles + start), stride, values)
        done = pl.ds(c * out_rows, out_rows)
        copies.append(pltpu.make_async_copy(total_ref.at[done], out_ref.at[done], sems.at[c]))
        copies[c].start()
    for copy in copies:
        copy.wait()


def momentum_of(received, gradient, count):
    components, held, rows, _ = received[0].shape
    shape = (components * rows * len(received) * held, LANES)
    return pl.pallas_call(
        functools.partial(momentum_kernel, count, len(received)),
        in_specs=[vmem()] * (len(received) + 1),
        out_specs=pl.BlockSpec(memory_space=pl.ANY),
        out_shape=jax.ShapeDtypeStruct(shape, jnp.float32),
        scratch_shapes=[pltpu.VMEM(shape, jnp.float32), pltpu.SemaphoreType.DMA((components,))],
        compiler_params=params(),
        cost_estimate=cost(),
    )(*received, gradient)


def whole_output(value, mode_count, width):
    value = value.reshape(3, mode_count, width // LANES, 2, LANES)
    return value.transpose(0, 1, 3, 2, 4).reshape(3, mode_count, 2, width)


def body(mode_fields, radius, radial_blocks, axial_blocks, block_columns, interface_nodes):
    _, mode_count, _, width = mode_fields.shape
    count = lax.axis_size("mode")
    rows = 2 * mode_count
    inverse, forward = tables(M, THETA, count)
    inverse, forward = jnp.asarray(inverse), jnp.asarray(forward)

    def joined(pieces):
        return [piece.reshape(piece.shape[:-3] + (rows, LANES)) for piece in pieces]

    groups = groups_of(width // count // LANES)
    arrived = []
    for group in range(groups):
        order = offsets(count, FIRST_SEND)
        arrived.append(exchange([pack(mode_fields, 0, 6, offset, group, groups) for offset in order[1:]], order[1:]))
    parcels = [(0, 6, 0, group, groups) for group in range(groups)]
    *own, inverse, forward = pack_rest(mode_fields, parcels, [inverse, forward])
    arrived[0][1:2], carried = lax.optimization_barrier((arrived[0][1:2], [inverse, forward]))
    order = offsets(count, SECOND)
    parcels = [(6, 12, offset, 0, 1) for offset in order]
    *shares, later_inverse, later_forward = pack_rest(mode_fields, parcels, carried)
    local, physical = [], []
    for group in range(groups):
        if group == 0:
            tables_here = (later_inverse, later_forward)
        else:
            tables_here = (inverse, forward)
        *terms, velocity_magnetic = first_physics(joined([own[group]] + arrived[group]), *tables_here)
        local += exchange(terms, offsets(count, FIRST_RETURN))
        physical.append(velocity_magnetic)
    local, shares = lax.optimization_barrier((local, shares))
    sources = exchange(shares, order)
    toward_prev, toward_next = interface(local, interface_nodes, count)
    halos = (from_behind(toward_next, "mer", 1), from_behind(toward_prev, "mer", -1))
    sources, halos = lax.optimization_barrier((sources, halos))
    lorentz = list(second_physics(joined(sources), physical, later_inverse, later_forward))
    lorentz, radius = lax.optimization_barrier((lorentz, radius))
    lorentz = exchange(lorentz, order)
    induction, gradient = derive(
        local, *halos, radial_blocks, axial_blocks, radius.reshape(1, width), block_columns.T, count
    )
    momentum = momentum_of(lorentz, gradient, count)
    return (whole_output(induction, mode_count, width), whole_output(momentum, mode_count, width))


def solution(mesh):
    placed = (
        P(None, "mode", None, "mer"),
        P("mer"),
        P(None, None, "mer"),
        P(None, None, "mer"),
        P("mer", None),
        P("mer", None),
    )
    return jax.shard_map(
        body,
        mesh=mesh,
        in_specs=placed,
        out_specs=(P(None, "mode", None, "mer"), P(None, "mode", None, "mer")),
        check_vma=False,
    )
```

```python
import functools
import math

import jax
import jax.numpy as jnp
import ml_dtypes
import numpy as np
from jax import lax
from jax.experimental import pallas as pl
from jax.experimental.pallas import tpu as pltpu
from jax.sharding import PartitionSpec as P

M = 128
THETA = 256
BLK = 64
NNZB = 5
LANES = 128
VMEM_LIMIT = 24 * 1024 * 1024


def params(limit=VMEM_LIMIT):
    return pltpu.CompilerParams(vmem_limit_bytes=limit)


def vmem():
    return pl.BlockSpec(memory_space=pltpu.VMEM)


def cost():
    return pl.CostEstimate(flops=1024, bytes_accessed=1024, transcendentals=0)


FIRST_SEND, FIRST_RETURN, SECOND = 2, 1, None


def offsets(count, place):
    order = list(range(count - 1))
    order.insert(count - 1 if place is None else min(place, count - 1), count - 1)
    return order


def dest_of(me, offset, count):
    if count & (count - 1) == 0:
        return jnp.bitwise_xor(me, offset)
    return lax.rem(me + offset, count)


def source_of(me, offset, count):
    if count & (count - 1) == 0:
        return jnp.bitwise_xor(me, offset)
    return lax.rem(me + count - offset, count)


def exchange(pieces, order):
    count = lax.axis_size("mode")
    power = count & (count - 1) == 0
    received = []
    for piece, offset in zip(pieces, order):
        if offset == 0:
            received.append(piece)
            continue
        pairs = [(i, i ^ offset if power else (i + offset) % count) for i in range(count)]
        received.append(lax.ppermute(piece, "mode", pairs))
    return received


def from_behind(value, axis, steps):
    count = lax.axis_size(axis)
    initial, last = (max(0, -steps), min(count, count - steps))
    return lax.ppermute(value, axis, [(source, source + steps) for source in range(initial, last)])


def tables(mode_total, angle_total, share_count):
    mode_ids = np.arange(mode_total)
    angle_ids = np.arange(angle_total)
    phase = angle_ids[:, None] * mode_ids[None, :] % angle_total
    angle = phase.astype(np.float32) * np.float32(2.0 * math.pi / angle_total)
    weight = np.where(mode_ids == 0, 1.0, 2.0).astype(np.float32)
    cosines = np.cos(angle)
    sines = np.sin(angle)
    inverse = np.stack([weight * cosines, -weight * sines], axis=-1).astype(ml_dtypes.bfloat16)
    forward = np.stack([cosines.T, -sines.T], axis=1) / np.float32(angle_total)
    forward = forward.reshape(share_count, mode_total // share_count, 2, angle_total)
    forward = forward.transpose(0, 2, 1, 3).reshape(2 * mode_total, angle_total).astype(ml_dtypes.bfloat16)
    return (inverse.reshape(angle_total, 2 * mode_total), forward)


def groups_of(tiles):
    return 2 if tiles % 2 == 0 else 1


def pieces_of(fields_ref, first, share, group, out_ref):
    count = lax.axis_size("mode")
    tiles = fields_ref.shape[3] // count // LANES
    components, held = out_ref.shape[:2]
    pairs = []
    for t in range(held):
        start = pl.multiple_of((share * tiles + group * held + t) * LANES, LANES)
        pairs.append((fields_ref.at[pl.ds(first, components), :, :, pl.ds(start, LANES)], out_ref.at[:, t]))
    return pairs


def run_copies(pairs, sems, beside=()):
    copies = [pltpu.make_async_copy(source, target, sems.at[i]) for i, (source, target) in enumerate(pairs)]
    for copy in copies:
        copy.start()
    for source, target in beside:
        target[...] = source[...]
    for copy in copies:
        copy.wait()


def packed_shape(fields, first, last, groups):
    _, mode_count, _, width = fields.shape
    return (last - first, width // lax.axis_size("mode") // LANES // groups, mode_count, 2, LANES)


def pack(fields, first, last, offset, group, groups):
    count = lax.axis_size("mode")
    shape = packed_shape(fields, first, last, groups)

    def kernel(fields_ref, out_ref, sems):
        share = dest_of(lax.axis_index("mode"), offset, count)
        run_copies(pieces_of(fields_ref, first, share, group, out_ref), sems)

    return pl.pallas_call(
        kernel,
        in_specs=[pl.BlockSpec(memory_space=pl.ANY)],
        out_specs=vmem(),
        out_shape=jax.ShapeDtypeStruct(shape, jnp.bfloat16),
        scratch_shapes=[pltpu.SemaphoreType.DMA((shape[1],))],
        compiler_params=params(),
        cost_estimate=cost(),
    )(fields)


def pack_rest(fields, parcels, carried):
    count = lax.axis_size("mode")
    shapes = [packed_shape(fields, first, last, groups) for first, last, _, _, groups in parcels]

    def kernel(fields_ref, *refs):
        inputs, refs = refs[: len(carried)], refs[len(carried) :]
        parcel_refs, outputs = refs[: len(parcels)], refs[len(parcels) : -1]
        me = lax.axis_index("mode")
        pairs = []
        for (first, _, offset, group, _), parcel_ref in zip(parcels, parcel_refs):
            pairs += pieces_of(fields_ref, first, dest_of(me, offset, count), group, parcel_ref)
        run_copies(pairs, refs[-1], zip(inputs, outputs))

    return pl.pallas_call(
        kernel,
        in_specs=[pl.BlockSpec(memory_space=pl.ANY)] + [vmem()] * len(carried),
        out_specs=[vmem()] * (len(parcels) + len(carried)),
        out_shape=[jax.ShapeDtypeStruct(shape, jnp.bfloat16) for shape in shapes]
        + [jax.ShapeDtypeStruct(value.shape, value.dtype) for value in carried],
        scratch_shapes=[pltpu.SemaphoreType.DMA((sum(shape[1] for shape in shapes),))],
        compiler_params=params(),
        cost_estimate=cost(),
    )(fields, *carried)


def cross(a, b):
    return [a[1] * b[2] - a[2] * b[1], a[2] * b[0] - a[0] * b[2], a[0] * b[1] - a[1] * b[0]]


def to_physical(order, in_refs, inverse, x_ref, store):
    me = lax.axis_index("mode")
    components, tiles, rows, _ = in_refs[0].shape
    for in_ref, offset in zip(in_refs, order):
        at = pl.multiple_of(source_of(me, offset, len(order)) * rows, rows)
        for c in range(components):
            for t in range(tiles):
                x_ref[c, pl.ds(at, rows), t * LANES : (t + 1) * LANES] = in_ref[c, t]
    for c in range(components):
        store(c, jnp.dot(inverse, x_ref[c], preferred_element_type=jnp.float32))


def to_modes(order, forward_ref, table_ref, product_ref, out_refs):
    count = len(order)
    me = lax.axis_index("mode")
    components, tiles, rows, _ = out_refs[0].shape
    for step, offset in enumerate(order):
        at = pl.multiple_of(dest_of(me, offset, count) * rows, rows)
        table_ref[step * rows : (step + 1) * rows] = forward_ref[pl.ds(at, rows)]
    for c in range(components):
        terms = jnp.dot(table_ref[...], product_ref[c], preferred_element_type=jnp.float32)
        terms = terms.astype(jnp.bfloat16)
        for step in range(count):
            for t in range(tiles):
                out_refs[step][c, t] = terms[step * rows : (step + 1) * rows, t * LANES : (t + 1) * LANES]


CHUNK = 32


def first_kernel(count, *refs):
    in_refs, (inverse_ref, forward_ref) = refs[:count], refs[count : count + 2]
    out_refs, (physical_ref, x_ref, product_ref, table_ref) = refs[count + 2 : 2 * count + 2], refs[2 * count + 2 :]

    def store(c, value):
        physical_ref[c] = value

    to_physical(offsets(count, FIRST_SEND), in_refs, inverse_ref[...], x_ref, store)
    for i in range(THETA // CHUNK):
        at = slice(i * CHUNK, (i + 1) * CHUNK)
        velocity = [physical_ref[c, at] for c in range(3)]
        magnetic = [physical_ref[c, at] for c in range(3, 6)]
        energy = 0.5 * (velocity[0] * velocity[0] + velocity[1] * velocity[1] + velocity[2] * velocity[2])
        for c, value in enumerate(cross(velocity, magnetic) + [energy]):
            product_ref[c, at] = value.astype(jnp.bfloat16)
    to_modes(offsets(count, FIRST_RETURN), forward_ref, table_ref, product_ref, out_refs)


def first_physics(received, inverse, forward):
    count = len(received)
    components, tiles, rows, _ = received[0].shape
    width = tiles * LANES
    return pl.pallas_call(
        functools.partial(first_kernel, count),
        in_specs=[vmem()] * (count + 2),
        out_specs=[vmem()] * (count + 1),
        out_shape=[jax.ShapeDtypeStruct((4, tiles, rows, LANES), jnp.bfloat16)] * count
        + [jax.ShapeDtypeStruct((components, THETA, width), jnp.float32)],
        scratch_shapes=[
            pltpu.VMEM((components, 2 * M, width), jnp.bfloat16),
            pltpu.VMEM((4, THETA, width), jnp.bfloat16),
            pltpu.VMEM((2 * M, THETA), jnp.bfloat16),
        ],
        compiler_params=params(),
        cost_estimate=cost(),
    )(*received, inverse, forward)


def second_kernel(count, groups, *refs):
    in_refs, refs = refs[:count], refs[count:]
    first_refs, (inverse_ref, forward_ref) = refs[:groups], refs[groups : groups + 2]
    out_refs, (physical_ref, x_ref, product_ref, table_ref) = refs[groups + 2 : groups + 2 + count], refs[groups + 2 + count :]
    width = first_refs[0].shape[2]

    def store(c, value):
        physical_ref[c] = value

    to_physical(offsets(count, SECOND), in_refs, inverse_ref[...], x_ref, store)
    for group in range(groups):
        lanes = slice(group * width, (group + 1) * width)
        for i in range(THETA // CHUNK):
            at = slice(i * CHUNK, (i + 1) * CHUNK)
            velocity = [first_refs[group][c, at] for c in range(3)]
            magnetic = [first_refs[group][c, at] for c in range(3, 6)]
            current = [physical_ref[c, at, lanes] for c in range(3)]
            vorticity = [physical_ref[c, at, lanes] for c in range(3, 6)]
            lorentz = [a + b for a, b in zip(cross(current, magnetic), cross(velocity, vorticity))]
            for c, value in enumerate(lorentz):
                product_ref[c, at, lanes] = value.astype(jnp.bfloat16)
    to_modes(offsets(count, SECOND), forward_ref, table_ref, product_ref, out_refs)


def second_physics(received, physical, inverse, forward):
    count, groups = len(received), len(physical)
    components, tiles, rows, _ = received[0].shape
    width = tiles * LANES
    return pl.pallas_call(
        functools.partial(second_kernel, count, groups),
        in_specs=[vmem()] * (count + groups + 2),
        out_specs=[vmem()] * count,
        out_shape=[jax.ShapeDtypeStruct((3, tiles, rows, LANES), jnp.bfloat16)] * count,
        scratch_shapes=[
            pltpu.VMEM((components, THETA, width), jnp.float32),
            pltpu.VMEM((components, 2 * M, width), jnp.bfloat16),
            pltpu.VMEM((3, THETA, width), jnp.bfloat16),
            pltpu.VMEM((2 * M, THETA), jnp.bfloat16),
        ],
        compiler_params=params(),
        cost_estimate=cost(),
    )(*received, *physical, inverse, forward)


def tiles_of(in_refs, count):
    me = lax.axis_index("mode")
    components, held, rows, _ = in_refs[0].shape
    groups = len(in_refs) // count
    for group in range(groups):
        for step, offset in enumerate(offsets(count, FIRST_RETURN)):
            share = source_of(me, offset, count)
            for t in range(held):
                at = share * (groups * held) + group * held + t
                yield at, in_refs[group * count + step][:, t].reshape(components * rows, LANES)


def interface_kernel(count, arrived, *refs):
    in_refs, (nodes_ref, prev_ref, next_ref) = refs[:arrived], refs[arrived:]
    components, _, rows, _ = in_refs[0].shape
    halo = nodes_ref.shape[1]
    totals = [jnp.zeros((components * rows, halo), jnp.float32) for _ in range(2)]
    inner = lax.broadcasted_iota(jnp.int32, (LANES, halo), 0)
    for at, values in tiles_of(in_refs, count):
        ids = inner + at * LANES
        for way in range(2):
            chosen = jnp.where(ids == nodes_ref[way : way + 1, :], 1.0, 0.0).astype(jnp.bfloat16)
            totals[way] += jnp.dot(values, chosen, preferred_element_type=jnp.float32)
    for out_ref, total in zip((prev_ref, next_ref), totals):
        picked = total.astype(jnp.bfloat16)
        for c in range(components):
            for t in range(halo // LANES):
                out_ref[c, t] = picked[c * rows : (c + 1) * rows, t * LANES : (t + 1) * LANES]


def interface(received, interface_nodes, count):
    components, _, rows, _ = received[0].shape
    halo = interface_nodes.shape[1]
    shape = jax.ShapeDtypeStruct((components, halo // LANES, rows, LANES), jnp.bfloat16)
    return pl.pallas_call(
        functools.partial(interface_kernel, count, len(received)),
        in_specs=[vmem()] * (len(received) + 1),
        out_specs=[vmem()] * 2,
        out_shape=[shape] * 2,
        compiler_params=params(),
        cost_estimate=cost(),
    )(*received, interface_nodes)


SUBLANES = 8


def interleaved(parts):
    parts = list(parts)
    row = lax.broadcasted_iota(jnp.int32, parts[0].shape, 1)
    for distance in (1, 2, 4):
        upper = jnp.bitwise_and(row, distance) != 0
        for k in range(SUBLANES):
            if k & distance == 0:
                first, second = parts[k], parts[k + distance]
                parts[k] = jnp.where(upper, pltpu.roll(second, distance, 1), first)
                parts[k + distance] = jnp.where(upper, second, pltpu.roll(first, SUBLANES - distance, 1))
    return parts


def put_rows(out_ref, first, stride, tiles):
    modes = tiles[0].shape[0] // 2
    parts = [part for tile in tiles for part in (tile[:modes], tile[modes:])]
    if len(parts) == SUBLANES:
        whole = interleaved([part.reshape(modes // SUBLANES, SUBLANES, LANES) for part in parts])
        for mode in range(modes):
            here = pl.ds(pl.multiple_of(first + mode * stride, SUBLANES), SUBLANES)
            out_ref[here, :] = whole[mode % SUBLANES][mode // SUBLANES]
    else:
        for i, part in enumerate(parts):
            out_ref[pl.ds(first + i, modes, stride=stride), :] = part


def derive_kernel(count, arrived, *refs):
    in_refs = refs[:arrived]
    prev_ref, next_ref, radial_ref, axial_ref, radius_ref, columns_ref = refs[arrived : arrived + 6]
    induction_ref, momentum_ref, extended_ref = refs[arrived + 6 :]
    me = lax.axis_index("mode")
    components, held, rows, _ = in_refs[0].shape
    mode_count = rows // 2
    node_tiles = arrived * held
    halo_tiles = prev_ref.shape[1]

    def extend(at, tile):
        extended_ref[0, at] = tile
        extended_ref[1, at] = jnp.concatenate([tile[:, BLK:], tile[:, :BLK]], axis=1)

    for at, tile in tiles_of(in_refs, count):
        extend(at, tile)
    for t in range(halo_tiles):
        extend(node_tiles + t, prev_ref[:, t].reshape(components * rows, LANES))
        extend(node_tiles + halo_tiles + t, next_ref[:, t].reshape(components * rows, LANES))
    modes = (lax.broadcasted_iota(jnp.int32, (mode_count, LANES), 0) + me * mode_count).astype(jnp.float32)
    low = lax.broadcasted_iota(jnp.int32, (components * rows, LANES), 1) < BLK
    lane = lax.broadcasted_iota(jnp.int32, (1, 2 * LANES), 1)
    in_first = jnp.where(lax.rem(lane, LANES) < BLK, 1.0, 0.0)
    in_half = [in_first.astype(jnp.bfloat16), (1.0 - in_first).astype(jnp.bfloat16)]

    def rotated(values):
        return jnp.concatenate([-modes * values[mode_count:], modes * values[:mode_count]], axis=0)

    def tile_of(b):
        here = pl.ds(pl.multiple_of(b * LANES, LANES), LANES)
        left, right = [], []
        for k in range(NNZB):
            weights = jnp.concatenate([radial_ref[k, :, here], axial_ref[k, :, here]], axis=1)
            first, second = columns_ref[k, 2 * b], columns_ref[k, 2 * b + 1]
            first_tile = extended_ref[lax.rem(first, 2), lax.div(first, 2)]
            second_tile = extended_ref[1 - lax.rem(second, 2), lax.div(second, 2)]
            left.append(jnp.where(low, first_tile, second_tile))
            right += [weights * in_half[0], weights * in_half[1]]
        total = jnp.dot(
            jnp.concatenate(left, axis=1),
            jnp.concatenate(right, axis=0),
            preferred_element_type=jnp.float32,
        )
        along_r = [total[c * rows : (c + 1) * rows, :LANES] for c in range(components)]
        along_z = [total[c * rows : (c + 1) * rows, LANES:] for c in range(components)]
        values = [extended_ref[0, b, c * rows : (c + 1) * rows].astype(jnp.float32) for c in range(components)]
        inv_radius = 1.0 / radius_ref[:, here]
        momentum_ref[0, b] = along_r[3]
        momentum_ref[1, b] = rotated(values[3]) * inv_radius
        momentum_ref[2, b] = along_z[3]
        return [
            rotated(values[2]) * inv_radius - along_z[1],
            along_z[0] - along_r[2],
            along_r[1] + values[1] * inv_radius - rotated(values[0]) * inv_radius,
        ]

    stride = 2 * node_tiles
    together = SUBLANES // 2 if node_tiles % (SUBLANES // 2) == 0 else 1

    def tiles_at(q, carry):
        induction = [tile_of(q * together + i) for i in range(together)]
        for i in range(3):
            put_rows(induction_ref, i * mode_count * stride + 2 * q * together, stride, [tile[i] for tile in induction])
        return carry

    lax.fori_loop(0, node_tiles // together, tiles_at, 0)


def derive(received, from_prev, from_next, radial_blocks, axial_blocks, radius, columns, count):
    components, held, rows, _ = received[0].shape
    node_tiles = len(received) * held
    halo_tiles = from_prev.shape[1]
    out_rows = 3 * rows * node_tiles
    return pl.pallas_call(
        functools.partial(derive_kernel, count, len(received)),
        in_specs=[vmem()] * (len(received) + 5) + [pl.BlockSpec(memory_space=pltpu.SMEM)],
        out_specs=[vmem()] * 2,
        out_shape=[
            jax.ShapeDtypeStruct((out_rows, LANES), jnp.float32),
            jax.ShapeDtypeStruct((3, node_tiles, rows, LANES), jnp.float32),
        ],
        scratch_shapes=[pltpu.VMEM((2, node_tiles + 2 * halo_tiles, components * rows, LANES), jnp.bfloat16)],
        compiler_params=params(),
        cost_estimate=cost(),
    )(*received, from_prev, from_next, radial_blocks, axial_blocks, radius, columns)


def momentum_kernel(count, arrived, *refs):
    in_refs, (gradient_ref, out_ref, total_ref, sems) = refs[:arrived], refs[arrived:]
    me = lax.axis_index("mode")
    components, held, rows, _ = in_refs[0].shape
    mode_count = rows // 2
    tiles = arrived // count * held
    stride = 2 * count * tiles
    out_rows = mode_count * stride
    copies = []
    for c in range(components):
        for step, offset in enumerate(offsets(count, SECOND)):
            share = source_of(me, offset, count)
            for start in range(0, tiles, SUBLANES // 2):
                values = []
                for t in range(start, min(tiles, start + SUBLANES // 2)):
                    piece = in_refs[t // held * count + step][c, t % held].astype(jnp.float32)
                    values.append(piece - gradient_ref[c, share * tiles + t])
                put_rows(total_ref, c * out_rows + 2 * (share * tiles + start), stride, values)
        done = pl.ds(c * out_rows, out_rows)
        copies.append(pltpu.make_async_copy(total_ref.at[done], out_ref.at[done], sems.at[c]))
        copies[c].start()
    for copy in copies:
        copy.wait()


def momentum_of(received, gradient, count):
    components, held, rows, _ = received[0].shape
    shape = (components * rows * len(received) * held, LANES)
    return pl.pallas_call(
        functools.partial(momentum_kernel, count, len(received)),
        in_specs=[vmem()] * (len(received) + 1),
        out_specs=pl.BlockSpec(memory_space=pl.ANY),
        out_shape=jax.ShapeDtypeStruct(shape, jnp.float32),
        scratch_shapes=[pltpu.VMEM(shape, jnp.float32), pltpu.SemaphoreType.DMA((components,))],
        compiler_params=params(),
        cost_estimate=cost(),
    )(*received, gradient)


def whole_output(value, mode_count, width):
    value = value.reshape(3, mode_count, width // LANES, 2, LANES)
    return value.transpose(0, 1, 3, 2, 4).reshape(3, mode_count, 2, width)


def body(mode_fields, radius, radial_blocks, axial_blocks, block_columns, interface_nodes):
    _, mode_count, _, width = mode_fields.shape
    count = lax.axis_size("mode")
    rows = 2 * mode_count
    inverse, forward = tables(M, THETA, count)
    inverse, forward = jnp.asarray(inverse), jnp.asarray(forward)

    def joined(pieces):
        return [piece.reshape(piece.shape[:-3] + (rows, LANES)) for piece in pieces]

    groups = groups_of(width // count // LANES)
    arrived = []
    for group in range(groups):
        order = offsets(count, FIRST_SEND)
        arrived.append(exchange([pack(mode_fields, 0, 6, offset, group, groups) for offset in order[1:]], order[1:]))
    parcels = [(0, 6, 0, group, groups) for group in range(groups)]
    *own, inverse, forward = pack_rest(mode_fields, parcels, [inverse, forward])
    arrived[0][1:2], carried = lax.optimization_barrier((arrived[0][1:2], [inverse, forward]))
    order = offsets(count, SECOND)
    parcels = [(6, 12, offset, 0, 1) for offset in order]
    *shares, later_inverse, later_forward = pack_rest(mode_fields, parcels, carried)
    local, physical = [], []
    for group in range(groups):
        if group == 0:
            tables_here = (later_inverse, later_forward)
        else:
            tables_here = (inverse, forward)
        *terms, velocity_magnetic = first_physics(joined([own[group]] + arrived[group]), *tables_here)
        local += exchange(terms, offsets(count, FIRST_RETURN))
        physical.append(velocity_magnetic)
    for group in range(groups):
        held, sent = slice(count if group == 0 else 0, None), slice(1, 2) if group == 0 else slice(2, None)
        local[held], shares[sent] = lax.optimization_barrier((local[held], shares[sent]))
    sources = exchange(shares, order)
    toward_prev, toward_next = interface(local, interface_nodes, count)
    halos = (from_behind(toward_next, "mer", 1), from_behind(toward_prev, "mer", -1))
    sources, halos = lax.optimization_barrier((sources, halos))
    lorentz = list(second_physics(joined(sources), physical, later_inverse, later_forward))
    lorentz, radius = lax.optimization_barrier((lorentz, radius))
    lorentz = exchange(lorentz, order)
    induction, gradient = derive(
        local, *halos, radial_blocks, axial_blocks, radius.reshape(1, width), block_columns.T, count
    )
    momentum = momentum_of(lorentz, gradient, count)
    return (whole_output(induction, mode_count, width), whole_output(momentum, mode_count, width))


def solution(mesh):
    placed = (
        P(None, "mode", None, "mer"),
        P("mer"),
        P(None, None, "mer"),
        P(None, None, "mer"),
        P("mer", None),
        P("mer", None),
    )
    return jax.shard_map(
        body,
        mesh=mesh,
        in_specs=placed,
        out_specs=(P(None, "mode", None, "mer"), P(None, "mode", None, "mer")),
        check_vma=False,
    )
```

```python
import functools
import math

import jax
import jax.numpy as jnp
import ml_dtypes
import numpy as np
from jax import lax
from jax.experimental import pallas as pl
from jax.experimental.pallas import tpu as pltpu
from jax.sharding import PartitionSpec as P

M = 128
THETA = 256
BLK = 64
NNZB = 5
LANES = 128
VMEM_LIMIT = 24 * 1024 * 1024


def params(limit=VMEM_LIMIT):
    return pltpu.CompilerParams(vmem_limit_bytes=limit)


def vmem():
    return pl.BlockSpec(memory_space=pltpu.VMEM)


def cost():
    return pl.CostEstimate(flops=1024, bytes_accessed=1024, transcendentals=0)


FIRST_SEND, FIRST_RETURN, SECOND = 2, 1, None


def offsets(count, place):
    order = list(range(count - 1))
    order.insert(count - 1 if place is None else min(place, count - 1), count - 1)
    return order


def dest_of(me, offset, count):
    if count & (count - 1) == 0:
        return jnp.bitwise_xor(me, offset)
    return lax.rem(me + offset, count)


def source_of(me, offset, count):
    if count & (count - 1) == 0:
        return jnp.bitwise_xor(me, offset)
    return lax.rem(me + count - offset, count)


def exchange(pieces, order):
    count = lax.axis_size("mode")
    power = count & (count - 1) == 0
    received = []
    for piece, offset in zip(pieces, order):
        if offset == 0:
            received.append(piece)
            continue
        pairs = [(i, i ^ offset if power else (i + offset) % count) for i in range(count)]
        received.append(lax.ppermute(piece, "mode", pairs))
    return received


def from_behind(value, axis, steps):
    count = lax.axis_size(axis)
    initial, last = (max(0, -steps), min(count, count - steps))
    return lax.ppermute(value, axis, [(source, source + steps) for source in range(initial, last)])


def tables(mode_total, angle_total, share_count):
    mode_ids = np.arange(mode_total)
    angle_ids = np.arange(angle_total)
    phase = angle_ids[:, None] * mode_ids[None, :] % angle_total
    angle = phase.astype(np.float32) * np.float32(2.0 * math.pi / angle_total)
    weight = np.where(mode_ids == 0, 1.0, 2.0).astype(np.float32)
    cosines = np.cos(angle)
    sines = np.sin(angle)
    inverse = np.stack([weight * cosines, -weight * sines], axis=-1).astype(ml_dtypes.bfloat16)
    forward = np.stack([cosines.T, -sines.T], axis=1) / np.float32(angle_total)
    forward = forward.reshape(share_count, mode_total // share_count, 2, angle_total)
    forward = forward.transpose(0, 2, 1, 3).reshape(2 * mode_total, angle_total).astype(ml_dtypes.bfloat16)
    return (inverse.reshape(angle_total, 2 * mode_total), forward)


def groups_of(tiles):
    return 2 if tiles % 2 == 0 else 1


def pieces_of(fields_ref, first, share, group, out_ref):
    count = lax.axis_size("mode")
    tiles = fields_ref.shape[3] // count // LANES
    components, held = out_ref.shape[:2]
    pairs = []
    for t in range(held):
        start = pl.multiple_of((share * tiles + group * held + t) * LANES, LANES)
        pairs.append((fields_ref.at[pl.ds(first, components), :, :, pl.ds(start, LANES)], out_ref.at[:, t]))
    return pairs


def run_copies(pairs, sems, beside=()):
    copies = [pltpu.make_async_copy(source, target, sems.at[i]) for i, (source, target) in enumerate(pairs)]
    for copy in copies:
        copy.start()
    for source, target in beside:
        target[...] = source[...]
    for copy in copies:
        copy.wait()


def packed_shape(fields, first, last, groups):
    _, mode_count, _, width = fields.shape
    return (last - first, width // lax.axis_size("mode") // LANES // groups, mode_count, 2, LANES)


def pack(fields, first, last, offset, group, groups):
    count = lax.axis_size("mode")
    shape = packed_shape(fields, first, last, groups)

    def kernel(fields_ref, out_ref, sems):
        share = dest_of(lax.axis_index("mode"), offset, count)
        run_copies(pieces_of(fields_ref, first, share, group, out_ref), sems)

    return pl.pallas_call(
        kernel,
        in_specs=[pl.BlockSpec(memory_space=pl.ANY)],
        out_specs=vmem(),
        out_shape=jax.ShapeDtypeStruct(shape, jnp.bfloat16),
        scratch_shapes=[pltpu.SemaphoreType.DMA((shape[1],))],
        compiler_params=params(),
        cost_estimate=cost(),
    )(fields)


def pack_rest(fields, parcels, carried):
    count = lax.axis_size("mode")
    shapes = [packed_shape(fields, first, last, groups) for first, last, _, _, groups in parcels]

    def kernel(fields_ref, *refs):
        inputs, refs = refs[: len(carried)], refs[len(carried) :]
        parcel_refs, outputs = refs[: len(parcels)], refs[len(parcels) : -1]
        me = lax.axis_index("mode")
        pairs = []
        for (first, _, offset, group, _), parcel_ref in zip(parcels, parcel_refs):
            pairs += pieces_of(fields_ref, first, dest_of(me, offset, count), group, parcel_ref)
        run_copies(pairs, refs[-1], zip(inputs, outputs))

    return pl.pallas_call(
        kernel,
        in_specs=[pl.BlockSpec(memory_space=pl.ANY)] + [vmem()] * len(carried),
        out_specs=[vmem()] * (len(parcels) + len(carried)),
        out_shape=[jax.ShapeDtypeStruct(shape, jnp.bfloat16) for shape in shapes]
        + [jax.ShapeDtypeStruct(value.shape, value.dtype) for value in carried],
        scratch_shapes=[pltpu.SemaphoreType.DMA((sum(shape[1] for shape in shapes),))],
        compiler_params=params(),
        cost_estimate=cost(),
    )(fields, *carried)


def cross(a, b):
    return [a[1] * b[2] - a[2] * b[1], a[2] * b[0] - a[0] * b[2], a[0] * b[1] - a[1] * b[0]]


def to_physical(order, in_refs, inverse, x_ref, store):
    me = lax.axis_index("mode")
    components, tiles, rows, _ = in_refs[0].shape
    for in_ref, offset in zip(in_refs, order):
        at = pl.multiple_of(source_of(me, offset, len(order)) * rows, rows)
        for c in range(components):
            for t in range(tiles):
                x_ref[c, pl.ds(at, rows), t * LANES : (t + 1) * LANES] = in_ref[c, t]
    for c in range(components):
        store(c, jnp.dot(inverse, x_ref[c], preferred_element_type=jnp.float32))


def to_modes(order, forward_ref, table_ref, product_ref, out_refs):
    count = len(order)
    me = lax.axis_index("mode")
    components, tiles, rows, _ = out_refs[0].shape
    for step, offset in enumerate(order):
        at = pl.multiple_of(dest_of(me, offset, count) * rows, rows)
        table_ref[step * rows : (step + 1) * rows] = forward_ref[pl.ds(at, rows)]
    for c in range(components):
        terms = jnp.dot(table_ref[...], product_ref[c], preferred_element_type=jnp.float32)
        terms = terms.astype(jnp.bfloat16)
        for step in range(count):
            for t in range(tiles):
                out_refs[step][c, t] = terms[step * rows : (step + 1) * rows, t * LANES : (t + 1) * LANES]


CHUNK = 32


def first_kernel(count, *refs):
    in_refs, (inverse_ref, forward_ref) = refs[:count], refs[count : count + 2]
    out_refs, (physical_ref, x_ref, product_ref, table_ref) = refs[count + 2 : 2 * count + 2], refs[2 * count + 2 :]

    def store(c, value):
        physical_ref[c] = value

    to_physical(offsets(count, FIRST_SEND), in_refs, inverse_ref[...], x_ref, store)
    for i in range(THETA // CHUNK):
        at = slice(i * CHUNK, (i + 1) * CHUNK)
        velocity = [physical_ref[c, at] for c in range(3)]
        magnetic = [physical_ref[c, at] for c in range(3, 6)]
        energy = 0.5 * (velocity[0] * velocity[0] + velocity[1] * velocity[1] + velocity[2] * velocity[2])
        for c, value in enumerate(cross(velocity, magnetic) + [energy]):
            product_ref[c, at] = value.astype(jnp.bfloat16)
    to_modes(offsets(count, FIRST_RETURN), forward_ref, table_ref, product_ref, out_refs)


def first_physics(received, inverse, forward):
    count = len(received)
    components, tiles, rows, _ = received[0].shape
    width = tiles * LANES
    return pl.pallas_call(
        functools.partial(first_kernel, count),
        in_specs=[vmem()] * (count + 2),
        out_specs=[vmem()] * (count + 1),
        out_shape=[jax.ShapeDtypeStruct((4, tiles, rows, LANES), jnp.bfloat16)] * count
        + [jax.ShapeDtypeStruct((components, THETA, width), jnp.float32)],
        scratch_shapes=[
            pltpu.VMEM((components, 2 * M, width), jnp.bfloat16),
            pltpu.VMEM((4, THETA, width), jnp.bfloat16),
            pltpu.VMEM((2 * M, THETA), jnp.bfloat16),
        ],
        compiler_params=params(),
        cost_estimate=cost(),
    )(*received, inverse, forward)


def second_kernel(count, groups, *refs):
    in_refs, refs = refs[:count], refs[count:]
    first_refs, (inverse_ref, forward_ref) = refs[:groups], refs[groups : groups + 2]
    out_refs, (physical_ref, x_ref, product_ref, table_ref) = refs[groups + 2 : groups + 2 + count], refs[groups + 2 + count :]
    width = first_refs[0].shape[2]

    def store(c, value):
        physical_ref[c] = value

    to_physical(offsets(count, SECOND), in_refs, inverse_ref[...], x_ref, store)
    for group in range(groups):
        lanes = slice(group * width, (group + 1) * width)
        for i in range(THETA // CHUNK):
            at = slice(i * CHUNK, (i + 1) * CHUNK)
            velocity = [first_refs[group][c, at] for c in range(3)]
            magnetic = [first_refs[group][c, at] for c in range(3, 6)]
            current = [physical_ref[c, at, lanes] for c in range(3)]
            vorticity = [physical_ref[c, at, lanes] for c in range(3, 6)]
            lorentz = [a + b for a, b in zip(cross(current, magnetic), cross(velocity, vorticity))]
            for c, value in enumerate(lorentz):
                product_ref[c, at, lanes] = value.astype(jnp.bfloat16)
    to_modes(offsets(count, SECOND), forward_ref, table_ref, product_ref, out_refs)


def second_physics(received, physical, inverse, forward):
    count, groups = len(received), len(physical)
    components, tiles, rows, _ = received[0].shape
    width = tiles * LANES
    return pl.pallas_call(
        functools.partial(second_kernel, count, groups),
        in_specs=[vmem()] * (count + groups + 2),
        out_specs=[vmem()] * count,
        out_shape=[jax.ShapeDtypeStruct((3, tiles, rows, LANES), jnp.bfloat16)] * count,
        scratch_shapes=[
            pltpu.VMEM((components, THETA, width), jnp.float32),
            pltpu.VMEM((components, 2 * M, width), jnp.bfloat16),
            pltpu.VMEM((3, THETA, width), jnp.bfloat16),
            pltpu.VMEM((2 * M, THETA), jnp.bfloat16),
        ],
        compiler_params=params(),
        cost_estimate=cost(),
    )(*received, *physical, inverse, forward)


def tiles_of(in_refs, count):
    me = lax.axis_index("mode")
    components, held, rows, _ = in_refs[0].shape
    groups = len(in_refs) // count
    for group in range(groups):
        for step, offset in enumerate(offsets(count, FIRST_RETURN)):
            share = source_of(me, offset, count)
            for t in range(held):
                at = share * (groups * held) + group * held + t
                yield at, in_refs[group * count + step][:, t].reshape(components * rows, LANES)


def interface_kernel(count, arrived, *refs):
    in_refs, (nodes_ref, prev_ref, next_ref) = refs[:arrived], refs[arrived:]
    components, _, rows, _ = in_refs[0].shape
    halo = nodes_ref.shape[1]
    totals = [jnp.zeros((components * rows, halo), jnp.float32) for _ in range(2)]
    inner = lax.broadcasted_iota(jnp.int32, (LANES, halo), 0)
    for at, values in tiles_of(in_refs, count):
        ids = inner + at * LANES
        for way in range(2):
            chosen = jnp.where(ids == nodes_ref[way : way + 1, :], 1.0, 0.0).astype(jnp.bfloat16)
            totals[way] += jnp.dot(values, chosen, preferred_element_type=jnp.float32)
    for out_ref, total in zip((prev_ref, next_ref), totals):
        picked = total.astype(jnp.bfloat16)
        for c in range(components):
            for t in range(halo // LANES):
                out_ref[c, t] = picked[c * rows : (c + 1) * rows, t * LANES : (t + 1) * LANES]


def interface(received, interface_nodes, count):
    components, _, rows, _ = received[0].shape
    halo = interface_nodes.shape[1]
    shape = jax.ShapeDtypeStruct((components, halo // LANES, rows, LANES), jnp.bfloat16)
    return pl.pallas_call(
        functools.partial(interface_kernel, count, len(received)),
        in_specs=[vmem()] * (len(received) + 1),
        out_specs=[vmem()] * 2,
        out_shape=[shape] * 2,
        compiler_params=params(),
        cost_estimate=cost(),
    )(*received, interface_nodes)


SUBLANES = 8


def interleaved(parts):
    parts = list(parts)
    row = lax.broadcasted_iota(jnp.int32, parts[0].shape, 1)
    for distance in (1, 2, 4):
        upper = jnp.bitwise_and(row, distance) != 0
        for k in range(SUBLANES):
            if k & distance == 0:
                first, second = parts[k], parts[k + distance]
                parts[k] = jnp.where(upper, pltpu.roll(second, distance, 1), first)
                parts[k + distance] = jnp.where(upper, second, pltpu.roll(first, SUBLANES - distance, 1))
    return parts


def put_rows(out_ref, first, stride, tiles):
    modes = tiles[0].shape[0] // 2
    parts = [part for tile in tiles for part in (tile[:modes], tile[modes:])]
    if len(parts) == SUBLANES:
        whole = interleaved([part.reshape(modes // SUBLANES, SUBLANES, LANES) for part in parts])
        for mode in range(modes):
            here = pl.ds(pl.multiple_of(first + mode * stride, SUBLANES), SUBLANES)
            out_ref[here, :] = whole[mode % SUBLANES][mode // SUBLANES]
    else:
        for i, part in enumerate(parts):
            out_ref[pl.ds(first + i, modes, stride=stride), :] = part


def derive_kernel(count, arrived, *refs):
    in_refs = refs[:arrived]
    prev_ref, next_ref, radial_ref, axial_ref, radius_ref, columns_ref = refs[arrived : arrived + 6]
    induction_ref, momentum_ref, extended_ref = refs[arrived + 6 :]
    me = lax.axis_index("mode")
    components, held, rows, _ = in_refs[0].shape
    mode_count = rows // 2
    node_tiles = arrived * held
    halo_tiles = prev_ref.shape[1]

    def extend(at, tile):
        extended_ref[0, at] = tile
        extended_ref[1, at] = jnp.concatenate([tile[:, BLK:], tile[:, :BLK]], axis=1)

    for at, tile in tiles_of(in_refs, count):
        extend(at, tile)
    for t in range(halo_tiles):
        extend(node_tiles + t, prev_ref[:, t].reshape(components * rows, LANES))
        extend(node_tiles + halo_tiles + t, next_ref[:, t].reshape(components * rows, LANES))
    modes = (lax.broadcasted_iota(jnp.int32, (mode_count, LANES), 0) + me * mode_count).astype(jnp.float32)
    low = lax.broadcasted_iota(jnp.int32, (components * rows, LANES), 1) < BLK
    lane = lax.broadcasted_iota(jnp.int32, (1, 2 * LANES), 1)
    in_first = jnp.where(lax.rem(lane, LANES) < BLK, 1.0, 0.0)
    in_half = [in_first.astype(jnp.bfloat16), (1.0 - in_first).astype(jnp.bfloat16)]

    def rotated(values):
        return jnp.concatenate([-modes * values[mode_count:], modes * values[:mode_count]], axis=0)

    def tile_of(b):
        here = pl.ds(pl.multiple_of(b * LANES, LANES), LANES)
        left, right = [], []
        for k in range(NNZB):
            weights = jnp.concatenate([radial_ref[k, :, here], axial_ref[k, :, here]], axis=1)
            first, second = columns_ref[k, 2 * b], columns_ref[k, 2 * b + 1]
            first_tile = extended_ref[lax.rem(first, 2), lax.div(first, 2)]
            second_tile = extended_ref[1 - lax.rem(second, 2), lax.div(second, 2)]
            left.append(jnp.where(low, first_tile, second_tile))
            right += [weights * in_half[0], weights * in_half[1]]
        total = jnp.dot(
            jnp.concatenate(left, axis=1),
            jnp.concatenate(right, axis=0),
            preferred_element_type=jnp.float32,
        )
        along_r = [total[c * rows : (c + 1) * rows, :LANES] for c in range(components)]
        along_z = [total[c * rows : (c + 1) * rows, LANES:] for c in range(components)]
        values = [extended_ref[0, b, c * rows : (c + 1) * rows].astype(jnp.float32) for c in range(components)]
        inv_radius = 1.0 / radius_ref[:, here]
        momentum_ref[0, b] = along_r[3]
        momentum_ref[1, b] = rotated(values[3]) * inv_radius
        momentum_ref[2, b] = along_z[3]
        return [
            rotated(values[2]) * inv_radius - along_z[1],
            along_z[0] - along_r[2],
            along_r[1] + values[1] * inv_radius - rotated(values[0]) * inv_radius,
        ]

    stride = 2 * node_tiles
    together = SUBLANES // 2 if node_tiles % (SUBLANES // 2) == 0 else 1

    def tiles_at(q, carry):
        induction = [tile_of(q * together + i) for i in range(together)]
        for i in range(3):
            put_rows(induction_ref, i * mode_count * stride + 2 * q * together, stride, [tile[i] for tile in induction])
        return carry

    lax.fori_loop(0, node_tiles // together, tiles_at, 0)


def derive(received, from_prev, from_next, radial_blocks, axial_blocks, radius, columns, count):
    components, held, rows, _ = received[0].shape
    node_tiles = len(received) * held
    halo_tiles = from_prev.shape[1]
    out_rows = 3 * rows * node_tiles
    return pl.pallas_call(
        functools.partial(derive_kernel, count, len(received)),
        in_specs=[vmem()] * (len(received) + 5) + [pl.BlockSpec(memory_space=pltpu.SMEM)],
        out_specs=[vmem()] * 2,
        out_shape=[
            jax.ShapeDtypeStruct((out_rows, LANES), jnp.float32),
            jax.ShapeDtypeStruct((3, node_tiles, rows, LANES), jnp.float32),
        ],
        scratch_shapes=[pltpu.VMEM((2, node_tiles + 2 * halo_tiles, components * rows, LANES), jnp.bfloat16)],
        compiler_params=params(),
        cost_estimate=cost(),
    )(*received, from_prev, from_next, radial_blocks, axial_blocks, radius, columns)


def momentum_kernel(count, arrived, *refs):
    in_refs, (gradient_ref, out_ref, total_ref, sems) = refs[:arrived], refs[arrived:]
    me = lax.axis_index("mode")
    components, held, rows, _ = in_refs[0].shape
    mode_count = rows // 2
    tiles = arrived // count * held
    stride = 2 * count * tiles
    out_rows = mode_count * stride
    copies = []
    for c in range(components):
        for step, offset in enumerate(offsets(count, SECOND)):
            share = source_of(me, offset, count)
            for start in range(0, tiles, SUBLANES // 2):
                values = []
                for t in range(start, min(tiles, start + SUBLANES // 2)):
                    piece = in_refs[t // held * count + step][c, t % held].astype(jnp.float32)
                    values.append(piece - gradient_ref[c, share * tiles + t])
                put_rows(total_ref, c * out_rows + 2 * (share * tiles + start), stride, values)
        done = pl.ds(c * out_rows, out_rows)
        copies.append(pltpu.make_async_copy(total_ref.at[done], out_ref.at[done], sems.at[c]))
        copies[c].start()
    for copy in copies:
        copy.wait()


def momentum_of(received, gradient, count):
    components, held, rows, _ = received[0].shape
    shape = (components * rows * len(received) * held, LANES)
    return pl.pallas_call(
        functools.partial(momentum_kernel, count, len(received)),
        in_specs=[vmem()] * (len(received) + 1),
        out_specs=pl.BlockSpec(memory_space=pl.ANY),
        out_shape=jax.ShapeDtypeStruct(shape, jnp.float32),
        scratch_shapes=[pltpu.VMEM(shape, jnp.float32), pltpu.SemaphoreType.DMA((components,))],
        compiler_params=params(),
        cost_estimate=cost(),
    )(*received, gradient)


def whole_output(value, mode_count, width):
    value = value.reshape(3, mode_count, width // LANES, 2, LANES)
    return value.transpose(0, 1, 3, 2, 4).reshape(3, mode_count, 2, width)


def body(mode_fields, radius, radial_blocks, axial_blocks, block_columns, interface_nodes):
    _, mode_count, _, width = mode_fields.shape
    count = lax.axis_size("mode")
    rows = 2 * mode_count
    inverse, forward = tables(M, THETA, count)
    inverse, forward = jnp.asarray(inverse), jnp.asarray(forward)

    def joined(pieces):
        return [piece.reshape(piece.shape[:-3] + (rows, LANES)) for piece in pieces]

    groups = groups_of(width // count // LANES)
    arrived = []
    for group in range(groups):
        order = offsets(count, FIRST_SEND)
        arrived.append(exchange([pack(mode_fields, 0, 6, offset, group, groups) for offset in order[1:]], order[1:]))
    parcels = [(0, 6, 0, group, groups) for group in range(groups)]
    *own, inverse, forward = pack_rest(mode_fields, parcels, [inverse, forward])
    arrived[0][1:2], carried = lax.optimization_barrier((arrived[0][1:2], [inverse, forward]))
    order = offsets(count, SECOND)
    parcels = [(6, 12, offset, 0, 1) for offset in order]
    *shares, later_inverse, later_forward = pack_rest(mode_fields, parcels, carried)
    local, physical = [], []
    for group in range(groups):
        if group == 0:
            tables_here = (later_inverse, later_forward)
        else:
            tables_here = (inverse, forward)
        *terms, velocity_magnetic = first_physics(joined([own[group]] + arrived[group]), *tables_here)
        local += exchange(terms, offsets(count, FIRST_RETURN))
        physical.append(velocity_magnetic)
    early = min(3, count)
    arrived[0][0], shares[:early] = lax.optimization_barrier((arrived[0][0], shares[:early]))
    sources = exchange(shares[:early], order[:early])
    local, shares[early:] = lax.optimization_barrier((local, shares[early:]))
    sources += exchange(shares[early:], order[early:])
    local, sources[:early] = lax.optimization_barrier((local, sources[:early]))
    toward_prev, toward_next = interface(local, interface_nodes, count)
    halos = (from_behind(toward_next, "mer", 1), from_behind(toward_prev, "mer", -1))
    sources, halos = lax.optimization_barrier((sources, halos))
    lorentz = list(second_physics(joined(sources), physical, later_inverse, later_forward))
    lorentz, radius = lax.optimization_barrier((lorentz, radius))
    lorentz = exchange(lorentz, order)
    induction, gradient = derive(
        local, *halos, radial_blocks, axial_blocks, radius.reshape(1, width), block_columns.T, count
    )
    momentum = momentum_of(lorentz, gradient, count)
    return (whole_output(induction, mode_count, width), whole_output(momentum, mode_count, width))


def solution(mesh):
    placed = (
        P(None, "mode", None, "mer"),
        P("mer"),
        P(None, None, "mer"),
        P(None, None, "mer"),
        P("mer", None),
        P("mer", None),
    )
    return jax.shard_map(
        body,
        mesh=mesh,
        in_specs=placed,
        out_specs=(P(None, "mode", None, "mer"), P(None, "mode", None, "mer")),
        check_vma=False,
    )
```

```python
import functools
import math

import jax
import jax.numpy as jnp
import ml_dtypes
import numpy as np
from jax import lax
from jax.experimental import pallas as pl
from jax.experimental.pallas import tpu as pltpu
from jax.sharding import PartitionSpec as P

M = 128
THETA = 256
BLK = 64
NNZB = 5
LANES = 128
VMEM_LIMIT = 24 * 1024 * 1024


def params(limit=VMEM_LIMIT):
    return pltpu.CompilerParams(vmem_limit_bytes=limit)


def vmem():
    return pl.BlockSpec(memory_space=pltpu.VMEM)


def cost():
    return pl.CostEstimate(flops=1024, bytes_accessed=1024, transcendentals=0)


FIRST_SEND, FIRST_RETURN, SECOND_SEND, SECOND_RETURN = 2, 1, None, 1


def offsets(count, place):
    order = list(range(count - 1))
    order.insert(count - 1 if place is None else min(place, count - 1), count - 1)
    return order


def dest_of(me, offset, count):
    if count & (count - 1) == 0:
        return jnp.bitwise_xor(me, offset)
    return lax.rem(me + offset, count)


def source_of(me, offset, count):
    if count & (count - 1) == 0:
        return jnp.bitwise_xor(me, offset)
    return lax.rem(me + count - offset, count)


def exchange(pieces, order):
    count = lax.axis_size("mode")
    power = count & (count - 1) == 0
    received = []
    for piece, offset in zip(pieces, order):
        if offset == 0:
            received.append(piece)
            continue
        pairs = [(i, i ^ offset if power else (i + offset) % count) for i in range(count)]
        received.append(lax.ppermute(piece, "mode", pairs))
    return received


def from_behind(value, axis, steps):
    count = lax.axis_size(axis)
    initial, last = (max(0, -steps), min(count, count - steps))
    return lax.ppermute(value, axis, [(source, source + steps) for source in range(initial, last)])


def tables(mode_total, angle_total, share_count):
    mode_ids = np.arange(mode_total)
    angle_ids = np.arange(angle_total)
    phase = angle_ids[:, None] * mode_ids[None, :] % angle_total
    angle = phase.astype(np.float32) * np.float32(2.0 * math.pi / angle_total)
    weight = np.where(mode_ids == 0, 1.0, 2.0).astype(np.float32)
    cosines = np.cos(angle)
    sines = np.sin(angle)
    inverse = np.stack([weight * cosines, -weight * sines], axis=-1).astype(ml_dtypes.bfloat16)
    forward = np.stack([cosines.T, -sines.T], axis=1) / np.float32(angle_total)
    forward = forward.reshape(share_count, mode_total // share_count, 2, angle_total)
    forward = forward.transpose(0, 2, 1, 3).reshape(2 * mode_total, angle_total).astype(ml_dtypes.bfloat16)
    return (inverse.reshape(angle_total, 2 * mode_total), forward)


def groups_of(tiles):
    return 2 if tiles % 2 == 0 else 1


def pieces_of(fields_ref, first, share, group, out_ref):
    count = lax.axis_size("mode")
    tiles = fields_ref.shape[3] // count // LANES
    components, held = out_ref.shape[:2]
    pairs = []
    for t in range(held):
        start = pl.multiple_of((share * tiles + group * held + t) * LANES, LANES)
        pairs.append((fields_ref.at[pl.ds(first, components), :, :, pl.ds(start, LANES)], out_ref.at[:, t]))
    return pairs


def run_copies(pairs, sems, beside=()):
    copies = [pltpu.make_async_copy(source, target, sems.at[i]) for i, (source, target) in enumerate(pairs)]
    for copy in copies:
        copy.start()
    for source, target in beside:
        target[...] = source[...]
    for copy in copies:
        copy.wait()


def packed_shape(fields, first, last, groups):
    _, mode_count, _, width = fields.shape
    return (last - first, width // lax.axis_size("mode") // LANES // groups, mode_count, 2, LANES)


def pack(fields, first, last, offset, group, groups):
    count = lax.axis_size("mode")
    shape = packed_shape(fields, first, last, groups)

    def kernel(fields_ref, out_ref, sems):
        share = dest_of(lax.axis_index("mode"), offset, count)
        run_copies(pieces_of(fields_ref, first, share, group, out_ref), sems)

    return pl.pallas_call(
        kernel,
        in_specs=[pl.BlockSpec(memory_space=pl.ANY)],
        out_specs=vmem(),
        out_shape=jax.ShapeDtypeStruct(shape, jnp.bfloat16),
        scratch_shapes=[pltpu.SemaphoreType.DMA((shape[1],))],
        compiler_params=params(),
        cost_estimate=cost(),
    )(fields)


def pack_rest(fields, parcels, carried):
    count = lax.axis_size("mode")
    shapes = [packed_shape(fields, first, last, groups) for first, last, _, _, groups in parcels]

    def kernel(fields_ref, *refs):
        inputs, refs = refs[: len(carried)], refs[len(carried) :]
        parcel_refs, outputs = refs[: len(parcels)], refs[len(parcels) : -1]
        me = lax.axis_index("mode")
        pairs = []
        for (first, _, offset, group, _), parcel_ref in zip(parcels, parcel_refs):
            pairs += pieces_of(fields_ref, first, dest_of(me, offset, count), group, parcel_ref)
        run_copies(pairs, refs[-1], zip(inputs, outputs))

    return pl.pallas_call(
        kernel,
        in_specs=[pl.BlockSpec(memory_space=pl.ANY)] + [vmem()] * len(carried),
        out_specs=[vmem()] * (len(parcels) + len(carried)),
        out_shape=[jax.ShapeDtypeStruct(shape, jnp.bfloat16) for shape in shapes]
        + [jax.ShapeDtypeStruct(value.shape, value.dtype) for value in carried],
        scratch_shapes=[pltpu.SemaphoreType.DMA((sum(shape[1] for shape in shapes),))],
        compiler_params=params(),
        cost_estimate=cost(),
    )(fields, *carried)


def cross(a, b):
    return [a[1] * b[2] - a[2] * b[1], a[2] * b[0] - a[0] * b[2], a[0] * b[1] - a[1] * b[0]]


def to_physical(order, in_refs, inverse, x_ref, store):
    me = lax.axis_index("mode")
    components, tiles, rows, _ = in_refs[0].shape
    for in_ref, offset in zip(in_refs, order):
        at = pl.multiple_of(source_of(me, offset, len(order)) * rows, rows)
        for c in range(components):
            for t in range(tiles):
                x_ref[c, pl.ds(at, rows), t * LANES : (t + 1) * LANES] = in_ref[c, t]
    for c in range(components):
        store(c, jnp.dot(inverse, x_ref[c], preferred_element_type=jnp.float32))


def to_modes(order, forward_ref, table_ref, product_ref, out_refs):
    count = len(order)
    me = lax.axis_index("mode")
    components, tiles, rows, _ = out_refs[0].shape
    for step, offset in enumerate(order):
        at = pl.multiple_of(dest_of(me, offset, count) * rows, rows)
        table_ref[step * rows : (step + 1) * rows] = forward_ref[pl.ds(at, rows)]
    for c in range(components):
        terms = jnp.dot(table_ref[...], product_ref[c], preferred_element_type=jnp.float32)
        terms = terms.astype(jnp.bfloat16)
        for step in range(count):
            for t in range(tiles):
                out_refs[step][c, t] = terms[step * rows : (step + 1) * rows, t * LANES : (t + 1) * LANES]


CHUNK = 32


def first_kernel(count, *refs):
    in_refs, (inverse_ref, forward_ref) = refs[:count], refs[count : count + 2]
    out_refs, (physical_ref, x_ref, product_ref, table_ref) = refs[count + 2 : 2 * count + 2], refs[2 * count + 2 :]

    def store(c, value):
        physical_ref[c] = value

    to_physical(offsets(count, FIRST_SEND), in_refs, inverse_ref[...], x_ref, store)
    for i in range(THETA // CHUNK):
        at = slice(i * CHUNK, (i + 1) * CHUNK)
        velocity = [physical_ref[c, at] for c in range(3)]
        magnetic = [physical_ref[c, at] for c in range(3, 6)]
        energy = 0.5 * (velocity[0] * velocity[0] + velocity[1] * velocity[1] + velocity[2] * velocity[2])
        for c, value in enumerate(cross(velocity, magnetic) + [energy]):
            product_ref[c, at] = value.astype(jnp.bfloat16)
    to_modes(offsets(count, FIRST_RETURN), forward_ref, table_ref, product_ref, out_refs)


def first_physics(received, inverse, forward):
    count = len(received)
    components, tiles, rows, _ = received[0].shape
    width = tiles * LANES
    return pl.pallas_call(
        functools.partial(first_kernel, count),
        in_specs=[vmem()] * (count + 2),
        out_specs=[vmem()] * (count + 1),
        out_shape=[jax.ShapeDtypeStruct((4, tiles, rows, LANES), jnp.bfloat16)] * count
        + [jax.ShapeDtypeStruct((components, THETA, width), jnp.float32)],
        scratch_shapes=[
            pltpu.VMEM((components, 2 * M, width), jnp.bfloat16),
            pltpu.VMEM((4, THETA, width), jnp.bfloat16),
            pltpu.VMEM((2 * M, THETA), jnp.bfloat16),
        ],
        compiler_params=params(),
        cost_estimate=cost(),
    )(*received, inverse, forward)


def second_kernel(count, groups, *refs):
    in_refs, refs = refs[:count], refs[count:]
    first_refs, (inverse_ref, forward_ref) = refs[:groups], refs[groups : groups + 2]
    out_refs, (physical_ref, x_ref, product_ref, table_ref) = refs[groups + 2 : groups + 2 + count], refs[groups + 2 + count :]
    width = first_refs[0].shape[2]

    def store(c, value):
        physical_ref[c] = value

    to_physical(offsets(count, SECOND_SEND), in_refs, inverse_ref[...], x_ref, store)
    for group in range(groups):
        lanes = slice(group * width, (group + 1) * width)
        for i in range(THETA // CHUNK):
            at = slice(i * CHUNK, (i + 1) * CHUNK)
            velocity = [first_refs[group][c, at] for c in range(3)]
            magnetic = [first_refs[group][c, at] for c in range(3, 6)]
            current = [physical_ref[c, at, lanes] for c in range(3)]
            vorticity = [physical_ref[c, at, lanes] for c in range(3, 6)]
            lorentz = [a + b for a, b in zip(cross(current, magnetic), cross(velocity, vorticity))]
            for c, value in enumerate(lorentz):
                product_ref[c, at, lanes] = value.astype(jnp.bfloat16)
    to_modes(offsets(count, SECOND_RETURN), forward_ref, table_ref, product_ref, out_refs)


def second_physics(received, physical, inverse, forward):
    count, groups = len(received), len(physical)
    components, tiles, rows, _ = received[0].shape
    width = tiles * LANES
    return pl.pallas_call(
        functools.partial(second_kernel, count, groups),
        in_specs=[vmem()] * (count + groups + 2),
        out_specs=[vmem()] * count,
        out_shape=[jax.ShapeDtypeStruct((3, tiles, rows, LANES), jnp.bfloat16)] * count,
        scratch_shapes=[
            pltpu.VMEM((components, THETA, width), jnp.float32),
            pltpu.VMEM((components, 2 * M, width), jnp.bfloat16),
            pltpu.VMEM((3, THETA, width), jnp.bfloat16),
            pltpu.VMEM((2 * M, THETA), jnp.bfloat16),
        ],
        compiler_params=params(),
        cost_estimate=cost(),
    )(*received, *physical, inverse, forward)


def tiles_of(in_refs, count):
    me = lax.axis_index("mode")
    components, held, rows, _ = in_refs[0].shape
    groups = len(in_refs) // count
    for group in range(groups):
        for step, offset in enumerate(offsets(count, FIRST_RETURN)):
            share = source_of(me, offset, count)
            for t in range(held):
                at = share * (groups * held) + group * held + t
                yield at, in_refs[group * count + step][:, t].reshape(components * rows, LANES)


def interface_kernel(count, arrived, *refs):
    in_refs, (nodes_ref, prev_ref, next_ref) = refs[:arrived], refs[arrived:]
    components, _, rows, _ = in_refs[0].shape
    halo = nodes_ref.shape[1]
    totals = [jnp.zeros((components * rows, halo), jnp.float32) for _ in range(2)]
    inner = lax.broadcasted_iota(jnp.int32, (LANES, halo), 0)
    for at, values in tiles_of(in_refs, count):
        ids = inner + at * LANES
        for way in range(2):
            chosen = jnp.where(ids == nodes_ref[way : way + 1, :], 1.0, 0.0).astype(jnp.bfloat16)
            totals[way] += jnp.dot(values, chosen, preferred_element_type=jnp.float32)
    for out_ref, total in zip((prev_ref, next_ref), totals):
        picked = total.astype(jnp.bfloat16)
        for c in range(components):
            for t in range(halo // LANES):
                out_ref[c, t] = picked[c * rows : (c + 1) * rows, t * LANES : (t + 1) * LANES]


def interface(received, interface_nodes, count):
    components, _, rows, _ = received[0].shape
    halo = interface_nodes.shape[1]
    shape = jax.ShapeDtypeStruct((components, halo // LANES, rows, LANES), jnp.bfloat16)
    return pl.pallas_call(
        functools.partial(interface_kernel, count, len(received)),
        in_specs=[vmem()] * (len(received) + 1),
        out_specs=[vmem()] * 2,
        out_shape=[shape] * 2,
        compiler_params=params(),
        cost_estimate=cost(),
    )(*received, interface_nodes)


SUBLANES = 8


def interleaved(parts):
    parts = list(parts)
    row = lax.broadcasted_iota(jnp.int32, parts[0].shape, 1)
    for distance in (1, 2, 4):
        upper = jnp.bitwise_and(row, distance) != 0
        for k in range(SUBLANES):
            if k & distance == 0:
                first, second = parts[k], parts[k + distance]
                parts[k] = jnp.where(upper, pltpu.roll(second, distance, 1), first)
                parts[k + distance] = jnp.where(upper, second, pltpu.roll(first, SUBLANES - distance, 1))
    return parts


def put_rows(out_ref, first, stride, tiles):
    modes = tiles[0].shape[0] // 2
    parts = [part for tile in tiles for part in (tile[:modes], tile[modes:])]
    if len(parts) == SUBLANES:
        whole = interleaved([part.reshape(modes // SUBLANES, SUBLANES, LANES) for part in parts])
        for mode in range(modes):
            here = pl.ds(pl.multiple_of(first + mode * stride, SUBLANES), SUBLANES)
            out_ref[here, :] = whole[mode % SUBLANES][mode // SUBLANES]
    else:
        for i, part in enumerate(parts):
            out_ref[pl.ds(first + i, modes, stride=stride), :] = part


def derive_kernel(count, arrived, *refs):
    in_refs = refs[:arrived]
    prev_ref, next_ref, radial_ref, axial_ref, radius_ref, columns_ref = refs[arrived : arrived + 6]
    induction_ref, momentum_ref, extended_ref = refs[arrived + 6 :]
    me = lax.axis_index("mode")
    components, held, rows, _ = in_refs[0].shape
    mode_count = rows // 2
    node_tiles = arrived * held
    halo_tiles = prev_ref.shape[1]

    def extend(at, tile):
        extended_ref[0, at] = tile
        extended_ref[1, at] = jnp.concatenate([tile[:, BLK:], tile[:, :BLK]], axis=1)

    for at, tile in tiles_of(in_refs, count):
        extend(at, tile)
    for t in range(halo_tiles):
        extend(node_tiles + t, prev_ref[:, t].reshape(components * rows, LANES))
        extend(node_tiles + halo_tiles + t, next_ref[:, t].reshape(components * rows, LANES))
    modes = (lax.broadcasted_iota(jnp.int32, (mode_count, LANES), 0) + me * mode_count).astype(jnp.float32)
    low = lax.broadcasted_iota(jnp.int32, (components * rows, LANES), 1) < BLK
    lane = lax.broadcasted_iota(jnp.int32, (1, 2 * LANES), 1)
    in_first = jnp.where(lax.rem(lane, LANES) < BLK, 1.0, 0.0)
    in_half = [in_first.astype(jnp.bfloat16), (1.0 - in_first).astype(jnp.bfloat16)]

    def rotated(values):
        return jnp.concatenate([-modes * values[mode_count:], modes * values[:mode_count]], axis=0)

    def tile_of(b):
        here = pl.ds(pl.multiple_of(b * LANES, LANES), LANES)
        left, right = [], []
        for k in range(NNZB):
            weights = jnp.concatenate([radial_ref[k, :, here], axial_ref[k, :, here]], axis=1)
            first, second = columns_ref[k, 2 * b], columns_ref[k, 2 * b + 1]
            first_tile = extended_ref[lax.rem(first, 2), lax.div(first, 2)]
            second_tile = extended_ref[1 - lax.rem(second, 2), lax.div(second, 2)]
            left.append(jnp.where(low, first_tile, second_tile))
            right += [weights * in_half[0], weights * in_half[1]]
        total = jnp.dot(
            jnp.concatenate(left, axis=1),
            jnp.concatenate(right, axis=0),
            preferred_element_type=jnp.float32,
        )
        along_r = [total[c * rows : (c + 1) * rows, :LANES] for c in range(components)]
        along_z = [total[c * rows : (c + 1) * rows, LANES:] for c in range(components)]
        values = [extended_ref[0, b, c * rows : (c + 1) * rows].astype(jnp.float32) for c in range(components)]
        inv_radius = 1.0 / radius_ref[:, here]
        momentum_ref[0, b] = along_r[3]
        momentum_ref[1, b] = rotated(values[3]) * inv_radius
        momentum_ref[2, b] = along_z[3]
        return [
            rotated(values[2]) * inv_radius - along_z[1],
            along_z[0] - along_r[2],
            along_r[1] + values[1] * inv_radius - rotated(values[0]) * inv_radius,
        ]

    stride = 2 * node_tiles
    together = SUBLANES // 2 if node_tiles % (SUBLANES // 2) == 0 else 1

    def tiles_at(q, carry):
        induction = [tile_of(q * together + i) for i in range(together)]
        for i in range(3):
            put_rows(induction_ref, i * mode_count * stride + 2 * q * together, stride, [tile[i] for tile in induction])
        return carry

    lax.fori_loop(0, node_tiles // together, tiles_at, 0)


def derive(received, from_prev, from_next, radial_blocks, axial_blocks, radius, columns, count):
    components, held, rows, _ = received[0].shape
    node_tiles = len(received) * held
    halo_tiles = from_prev.shape[1]
    out_rows = 3 * rows * node_tiles
    return pl.pallas_call(
        functools.partial(derive_kernel, count, len(received)),
        in_specs=[vmem()] * (len(received) + 5) + [pl.BlockSpec(memory_space=pltpu.SMEM)],
        out_specs=[vmem()] * 2,
        out_shape=[
            jax.ShapeDtypeStruct((out_rows, LANES), jnp.float32),
            jax.ShapeDtypeStruct((3, node_tiles, rows, LANES), jnp.float32),
        ],
        scratch_shapes=[pltpu.VMEM((2, node_tiles + 2 * halo_tiles, components * rows, LANES), jnp.bfloat16)],
        compiler_params=params(),
        cost_estimate=cost(),
    )(*received, from_prev, from_next, radial_blocks, axial_blocks, radius, columns)


def momentum_kernel(places, *refs):
    count = lax.axis_size("mode")
    in_refs, gradient_ref = refs[: len(places)], refs[len(places)]
    out_ref, total_ref, sems = refs[-3:]
    me = lax.axis_index("mode")
    components, tiles, rows, _ = in_refs[0].shape
    mode_count = rows // 2
    copies = []
    for i, place in enumerate(places):
        share = source_of(me, offsets(count, SECOND_RETURN)[place], count)
        for c in range(components):
            for start in range(0, tiles, SUBLANES // 2):
                values = []
                for t in range(start, min(tiles, start + SUBLANES // 2)):
                    values.append(in_refs[i][c, t].astype(jnp.float32) - gradient_ref[c, share * tiles + t])
                put_rows(total_ref.at[i], c * mode_count * 2 * tiles + 2 * start, 2 * tiles, values)
        here = pl.ds(pl.multiple_of(share * 2 * tiles, 2 * tiles), 2 * tiles)
        source = total_ref.at[i].reshape(components * mode_count, 2 * tiles, LANES)
        copies.append(pltpu.make_async_copy(source, out_ref.at[:, here, :], sems.at[i]))
        copies[i].start()
    for copy in copies:
        copy.wait()


def momentum_of(received, gradient, places, before):
    components, tiles, rows, _ = received[0].shape
    shape = (components * rows // 2, 2 * gradient.shape[1], LANES)
    anywhere = pl.BlockSpec(memory_space=pl.ANY)
    return pl.pallas_call(
        functools.partial(momentum_kernel, places),
        in_specs=[vmem()] * (len(received) + 1) + [anywhere] * len(before),
        out_specs=anywhere,
        out_shape=jax.ShapeDtypeStruct(shape, jnp.float32),
        scratch_shapes=[
            pltpu.VMEM((len(places), components * rows * tiles, LANES), jnp.float32),
            pltpu.SemaphoreType.DMA((len(places),)),
        ],
        input_output_aliases={len(received) + 1: 0} if before else {},
        compiler_params=params(),
        cost_estimate=cost(),
    )(*received, gradient, *before)


def whole_output(value, mode_count, width):
    value = value.reshape(3, mode_count, width // LANES, 2, LANES)
    return value.transpose(0, 1, 3, 2, 4).reshape(3, mode_count, 2, width)


def body(mode_fields, radius, radial_blocks, axial_blocks, block_columns, interface_nodes):
    _, mode_count, _, width = mode_fields.shape
    count = lax.axis_size("mode")
    rows = 2 * mode_count
    inverse, forward = tables(M, THETA, count)
    inverse, forward = jnp.asarray(inverse), jnp.asarray(forward)

    def joined(pieces):
        return [piece.reshape(piece.shape[:-3] + (rows, LANES)) for piece in pieces]

    groups = groups_of(width // count // LANES)
    arrived = []
    for group in range(groups):
        order = offsets(count, FIRST_SEND)
        arrived.append(exchange([pack(mode_fields, 0, 6, offset, group, groups) for offset in order[1:]], order[1:]))
    parcels = [(0, 6, 0, group, groups) for group in range(groups)]
    *own, inverse, forward = pack_rest(mode_fields, parcels, [inverse, forward])
    arrived[0][1:2], carried = lax.optimization_barrier((arrived[0][1:2], [inverse, forward]))
    order = offsets(count, SECOND_SEND)
    parcels = [(6, 12, offset, 0, 1) for offset in order]
    *shares, later_inverse, later_forward = pack_rest(mode_fields, parcels, carried)
    local, physical = [], []
    for group in range(groups):
        if group == 0:
            tables_here = (later_inverse, later_forward)
        else:
            tables_here = (inverse, forward)
        *terms, velocity_magnetic = first_physics(joined([own[group]] + arrived[group]), *tables_here)
        local += exchange(terms, offsets(count, FIRST_RETURN))
        physical.append(velocity_magnetic)
    for group in range(groups):
        held, sent = slice(count if group == 0 else 0, None), slice(1, 2) if group == 0 else slice(2, None)
        local[held], shares[sent] = lax.optimization_barrier((local[held], shares[sent]))
    sources = exchange(shares, order)
    toward_prev, toward_next = interface(local, interface_nodes, count)
    halos = (from_behind(toward_next, "mer", 1), from_behind(toward_prev, "mer", -1))
    sources, halos = lax.optimization_barrier((sources, halos))
    lorentz = list(second_physics(joined(sources), physical, later_inverse, later_forward))
    lorentz, radius = lax.optimization_barrier((lorentz, radius))
    lorentz = exchange(lorentz, offsets(count, SECOND_RETURN))
    induction, gradient = derive(
        local, *halos, radial_blocks, axial_blocks, radius.reshape(1, width), block_columns.T, count
    )
    late = count - 1
    places = [place for place in range(count) if place != late]
    momentum = momentum_of([lorentz[place] for place in places], gradient, places, [])
    momentum = momentum_of([lorentz[late]], gradient, [late], [momentum])
    return (whole_output(induction, mode_count, width), whole_output(momentum, mode_count, width))


def solution(mesh):
    placed = (
        P(None, "mode", None, "mer"),
        P("mer"),
        P(None, None, "mer"),
        P(None, None, "mer"),
        P("mer", None),
        P("mer", None),
    )
    return jax.shard_map(
        body,
        mesh=mesh,
        in_specs=placed,
        out_specs=(P(None, "mode", None, "mer"), P(None, "mode", None, "mer")),
        check_vma=False,
    )
```

```python
import functools
import math

import jax
import jax.numpy as jnp
import ml_dtypes
import numpy as np
from jax import lax
from jax.experimental import pallas as pl
from jax.experimental.pallas import tpu as pltpu
from jax.sharding import PartitionSpec as P

M = 128
THETA = 256
BLK = 64
NNZB = 5
LANES = 128
VMEM_LIMIT = 24 * 1024 * 1024


def params(limit=VMEM_LIMIT):
    return pltpu.CompilerParams(vmem_limit_bytes=limit)


def vmem():
    return pl.BlockSpec(memory_space=pltpu.VMEM)


def cost():
    return pl.CostEstimate(flops=1024, bytes_accessed=1024, transcendentals=0)


FIRST_SEND, FIRST_RETURN, SECOND = 1, 1, None


def offsets(count, place):
    order = list(range(count - 1))
    order.insert(count - 1 if place is None else min(place, count - 1), count - 1)
    return order


def dest_of(me, offset, count):
    if count & (count - 1) == 0:
        return jnp.bitwise_xor(me, offset)
    return lax.rem(me + offset, count)


def source_of(me, offset, count):
    if count & (count - 1) == 0:
        return jnp.bitwise_xor(me, offset)
    return lax.rem(me + count - offset, count)


def exchange(pieces, order):
    count = lax.axis_size("mode")
    power = count & (count - 1) == 0
    received = []
    for piece, offset in zip(pieces, order):
        if offset == 0:
            received.append(piece)
            continue
        pairs = [(i, i ^ offset if power else (i + offset) % count) for i in range(count)]
        received.append(lax.ppermute(piece, "mode", pairs))
    return received


def from_behind(value, axis, steps):
    count = lax.axis_size(axis)
    initial, last = (max(0, -steps), min(count, count - steps))
    return lax.ppermute(value, axis, [(source, source + steps) for source in range(initial, last)])


def tables(mode_total, angle_total, share_count):
    mode_ids = np.arange(mode_total)
    angle_ids = np.arange(angle_total)
    phase = angle_ids[:, None] * mode_ids[None, :] % angle_total
    angle = phase.astype(np.float32) * np.float32(2.0 * math.pi / angle_total)
    weight = np.where(mode_ids == 0, 1.0, 2.0).astype(np.float32)
    cosines = np.cos(angle)
    sines = np.sin(angle)
    inverse = np.stack([weight * cosines, -weight * sines], axis=-1).astype(ml_dtypes.bfloat16)
    forward = np.stack([cosines.T, -sines.T], axis=1) / np.float32(angle_total)
    forward = forward.reshape(share_count, mode_total // share_count, 2, angle_total)
    forward = forward.transpose(0, 2, 1, 3).reshape(2 * mode_total, angle_total).astype(ml_dtypes.bfloat16)
    return (inverse.reshape(angle_total, 2 * mode_total), forward)


def groups_of(tiles):
    return 2 if tiles % 2 == 0 else 1


def pieces_of(fields_ref, first, share, group, out_ref):
    count = lax.axis_size("mode")
    tiles = fields_ref.shape[3] // count // LANES
    components, held = out_ref.shape[:2]
    pairs = []
    for t in range(held):
        start = pl.multiple_of((share * tiles + group * held + t) * LANES, LANES)
        pairs.append((fields_ref.at[pl.ds(first, components), :, :, pl.ds(start, LANES)], out_ref.at[:, t]))
    return pairs


def run_copies(pairs, sems, beside=()):
    copies = [pltpu.make_async_copy(source, target, sems.at[i]) for i, (source, target) in enumerate(pairs)]
    for copy in copies:
        copy.start()
    for source, target in beside:
        target[...] = source[...]
    for copy in copies:
        copy.wait()


def load(fields, components):
    shape = (components,) + fields.shape[1:]

    def kernel(fields_ref, out_ref, sems):
        run_copies([(fields_ref.at[c], out_ref.at[c]) for c in range(components)], sems)

    return pl.pallas_call(
        kernel,
        in_specs=[pl.BlockSpec(memory_space=pltpu.HBM)],
        out_specs=vmem(),
        out_shape=jax.ShapeDtypeStruct(shape, fields.dtype),
        scratch_shapes=[pltpu.SemaphoreType.DMA((components,))],
        compiler_params=params(),
        cost_estimate=cost(),
    )(pltpu.with_memory_space_constraint(fields, pltpu.HBM))


def packed_shape(fields, first, last, groups):
    _, mode_count, _, width = fields.shape
    return (last - first, width // lax.axis_size("mode") // LANES // groups, mode_count, 2, LANES)


def pack(fields, first, last, offset, group, groups):
    count = lax.axis_size("mode")
    shape = packed_shape(fields, first, last, groups)

    def kernel(fields_ref, out_ref, sems):
        share = dest_of(lax.axis_index("mode"), offset, count)
        run_copies(pieces_of(fields_ref, first, share, group, out_ref), sems)

    return pl.pallas_call(
        kernel,
        in_specs=[pl.BlockSpec(memory_space=pl.ANY)],
        out_specs=vmem(),
        out_shape=jax.ShapeDtypeStruct(shape, jnp.bfloat16),
        scratch_shapes=[pltpu.SemaphoreType.DMA((shape[1],))],
        compiler_params=params(),
        cost_estimate=cost(),
    )(fields)


def pack_rest(fields, parcels, carried):
    count = lax.axis_size("mode")
    shapes = [packed_shape(fields, first, last, groups) for first, last, _, _, groups in parcels]

    def kernel(fields_ref, *refs):
        inputs, refs = refs[: len(carried)], refs[len(carried) :]
        parcel_refs, outputs = refs[: len(parcels)], refs[len(parcels) : -1]
        me = lax.axis_index("mode")
        pairs = []
        for (first, _, offset, group, _), parcel_ref in zip(parcels, parcel_refs):
            pairs += pieces_of(fields_ref, first, dest_of(me, offset, count), group, parcel_ref)
        run_copies(pairs, refs[-1], zip(inputs, outputs))

    return pl.pallas_call(
        kernel,
        in_specs=[pl.BlockSpec(memory_space=pl.ANY)] + [vmem()] * len(carried),
        out_specs=[vmem()] * (len(parcels) + len(carried)),
        out_shape=[jax.ShapeDtypeStruct(shape, jnp.bfloat16) for shape in shapes]
        + [jax.ShapeDtypeStruct(value.shape, value.dtype) for value in carried],
        scratch_shapes=[pltpu.SemaphoreType.DMA((sum(shape[1] for shape in shapes),))],
        compiler_params=params(),
        cost_estimate=cost(),
    )(fields, *carried)


def cross(a, b):
    return [a[1] * b[2] - a[2] * b[1], a[2] * b[0] - a[0] * b[2], a[0] * b[1] - a[1] * b[0]]


def to_physical(order, in_refs, inverse, x_ref, store):
    me = lax.axis_index("mode")
    components, tiles, rows, _ = in_refs[0].shape
    for in_ref, offset in zip(in_refs, order):
        at = pl.multiple_of(source_of(me, offset, len(order)) * rows, rows)
        for c in range(components):
            for t in range(tiles):
                x_ref[c, pl.ds(at, rows), t * LANES : (t + 1) * LANES] = in_ref[c, t]
    for c in range(components):
        store(c, jnp.dot(inverse, x_ref[c], preferred_element_type=jnp.float32))


def to_modes(order, forward_ref, table_ref, product_ref, out_refs):
    count = len(order)
    me = lax.axis_index("mode")
    components, tiles, rows, _ = out_refs[0].shape
    for step, offset in enumerate(order):
        at = pl.multiple_of(dest_of(me, offset, count) * rows, rows)
        table_ref[step * rows : (step + 1) * rows] = forward_ref[pl.ds(at, rows)]
    for c in range(components):
        terms = jnp.dot(table_ref[...], product_ref[c], preferred_element_type=jnp.float32)
        terms = terms.astype(jnp.bfloat16)
        for step in range(count):
            for t in range(tiles):
                out_refs[step][c, t] = terms[step * rows : (step + 1) * rows, t * LANES : (t + 1) * LANES]


CHUNK = 32


def first_kernel(count, *refs):
    in_refs, (inverse_ref, forward_ref) = refs[:count], refs[count : count + 2]
    out_refs, (physical_ref, x_ref, product_ref, table_ref) = refs[count + 2 : 2 * count + 2], refs[2 * count + 2 :]

    def store(c, value):
        physical_ref[c] = value

    to_physical(offsets(count, FIRST_SEND), in_refs, inverse_ref[...], x_ref, store)
    for i in range(THETA // CHUNK):
        at = slice(i * CHUNK, (i + 1) * CHUNK)
        velocity = [physical_ref[c, at] for c in range(3)]
        magnetic = [physical_ref[c, at] for c in range(3, 6)]
        energy = 0.5 * (velocity[0] * velocity[0] + velocity[1] * velocity[1] + velocity[2] * velocity[2])
        for c, value in enumerate(cross(velocity, magnetic) + [energy]):
            product_ref[c, at] = value.astype(jnp.bfloat16)
    to_modes(offsets(count, FIRST_RETURN), forward_ref, table_ref, product_ref, out_refs)


def first_physics(received, inverse, forward):
    count = len(received)
    components, tiles, rows, _ = received[0].shape
    width = tiles * LANES
    return pl.pallas_call(
        functools.partial(first_kernel, count),
        in_specs=[vmem()] * (count + 2),
        out_specs=[vmem()] * (count + 1),
        out_shape=[jax.ShapeDtypeStruct((4, tiles, rows, LANES), jnp.bfloat16)] * count
        + [jax.ShapeDtypeStruct((components, THETA, width), jnp.float32)],
        scratch_shapes=[
            pltpu.VMEM((components, 2 * M, width), jnp.bfloat16),
            pltpu.VMEM((4, THETA, width), jnp.bfloat16),
            pltpu.VMEM((2 * M, THETA), jnp.bfloat16),
        ],
        compiler_params=params(),
        cost_estimate=cost(),
    )(*received, inverse, forward)


def second_kernel(count, groups, *refs):
    in_refs, refs = refs[:count], refs[count:]
    first_refs, (inverse_ref, forward_ref) = refs[:groups], refs[groups : groups + 2]
    out_refs, (physical_ref, x_ref, product_ref, table_ref) = refs[groups + 2 : groups + 2 + count], refs[groups + 2 + count :]
    width = first_refs[0].shape[2]

    def store(c, value):
        physical_ref[c] = value

    to_physical(offsets(count, SECOND), in_refs, inverse_ref[...], x_ref, store)
    for group in range(groups):
        lanes = slice(group * width, (group + 1) * width)
        for i in range(THETA // CHUNK):
            at = slice(i * CHUNK, (i + 1) * CHUNK)
            velocity = [first_refs[group][c, at] for c in range(3)]
            magnetic = [first_refs[group][c, at] for c in range(3, 6)]
            current = [physical_ref[c, at, lanes] for c in range(3)]
            vorticity = [physical_ref[c, at, lanes] for c in range(3, 6)]
            lorentz = [a + b for a, b in zip(cross(current, magnetic), cross(velocity, vorticity))]
            for c, value in enumerate(lorentz):
                product_ref[c, at, lanes] = value.astype(jnp.bfloat16)
    to_modes(offsets(count, SECOND), forward_ref, table_ref, product_ref, out_refs)


def second_physics(received, physical, inverse, forward):
    count, groups = len(received), len(physical)
    components, tiles, rows, _ = received[0].shape
    width = tiles * LANES
    return pl.pallas_call(
        functools.partial(second_kernel, count, groups),
        in_specs=[vmem()] * (count + groups + 2),
        out_specs=[vmem()] * count,
        out_shape=[jax.ShapeDtypeStruct((3, tiles, rows, LANES), jnp.bfloat16)] * count,
        scratch_shapes=[
            pltpu.VMEM((components, THETA, width), jnp.float32),
            pltpu.VMEM((components, 2 * M, width), jnp.bfloat16),
            pltpu.VMEM((3, THETA, width), jnp.bfloat16),
            pltpu.VMEM((2 * M, THETA), jnp.bfloat16),
        ],
        compiler_params=params(),
        cost_estimate=cost(),
    )(*received, *physical, inverse, forward)


def tiles_of(in_refs, count):
    me = lax.axis_index("mode")
    components, held, rows, _ = in_refs[0].shape
    groups = len(in_refs) // count
    for group in range(groups):
        for step, offset in enumerate(offsets(count, FIRST_RETURN)):
            share = source_of(me, offset, count)
            for t in range(held):
                at = share * (groups * held) + group * held + t
                yield at, in_refs[group * count + step][:, t].reshape(components * rows, LANES)


def interface_kernel(count, arrived, *refs):
    in_refs, (nodes_ref, prev_ref, next_ref) = refs[:arrived], refs[arrived:]
    components, _, rows, _ = in_refs[0].shape
    halo = nodes_ref.shape[1]
    totals = [jnp.zeros((components * rows, halo), jnp.float32) for _ in range(2)]
    inner = lax.broadcasted_iota(jnp.int32, (LANES, halo), 0)
    for at, values in tiles_of(in_refs, count):
        ids = inner + at * LANES
        for way in range(2):
            chosen = jnp.where(ids == nodes_ref[way : way + 1, :], 1.0, 0.0).astype(jnp.bfloat16)
            totals[way] += jnp.dot(values, chosen, preferred_element_type=jnp.float32)
    for out_ref, total in zip((prev_ref, next_ref), totals):
        picked = total.astype(jnp.bfloat16)
        for c in range(components):
            for t in range(halo // LANES):
                out_ref[c, t] = picked[c * rows : (c + 1) * rows, t * LANES : (t + 1) * LANES]


def interface(received, interface_nodes, count):
    components, _, rows, _ = received[0].shape
    halo = interface_nodes.shape[1]
    shape = jax.ShapeDtypeStruct((components, halo // LANES, rows, LANES), jnp.bfloat16)
    return pl.pallas_call(
        functools.partial(interface_kernel, count, len(received)),
        in_specs=[vmem()] * (len(received) + 1),
        out_specs=[vmem()] * 2,
        out_shape=[shape] * 2,
        compiler_params=params(),
        cost_estimate=cost(),
    )(*received, interface_nodes)


SUBLANES = 8


def interleaved(parts):
    parts = list(parts)
    row = lax.broadcasted_iota(jnp.int32, parts[0].shape, 1)
    for distance in (1, 2, 4):
        upper = jnp.bitwise_and(row, distance) != 0
        for k in range(SUBLANES):
            if k & distance == 0:
                first, second = parts[k], parts[k + distance]
                parts[k] = jnp.where(upper, pltpu.roll(second, distance, 1), first)
                parts[k + distance] = jnp.where(upper, second, pltpu.roll(first, SUBLANES - distance, 1))
    return parts


def put_rows(out_ref, first, stride, tiles):
    modes = tiles[0].shape[0] // 2
    parts = [part for tile in tiles for part in (tile[:modes], tile[modes:])]
    if len(parts) == SUBLANES:
        whole = interleaved([part.reshape(modes // SUBLANES, SUBLANES, LANES) for part in parts])
        for mode in range(modes):
            here = pl.ds(pl.multiple_of(first + mode * stride, SUBLANES), SUBLANES)
            out_ref[here, :] = whole[mode % SUBLANES][mode // SUBLANES]
    else:
        for i, part in enumerate(parts):
            out_ref[pl.ds(first + i, modes, stride=stride), :] = part


def derive_kernel(count, arrived, *refs):
    in_refs = refs[:arrived]
    prev_ref, next_ref, radial_ref, axial_ref, radius_ref, columns_ref = refs[arrived : arrived + 6]
    induction_ref, momentum_ref, extended_ref = refs[arrived + 6 :]
    me = lax.axis_index("mode")
    components, held, rows, _ = in_refs[0].shape
    mode_count = rows // 2
    node_tiles = arrived * held
    halo_tiles = prev_ref.shape[1]

    def extend(at, tile):
        extended_ref[0, at] = tile
        extended_ref[1, at] = jnp.concatenate([tile[:, BLK:], tile[:, :BLK]], axis=1)

    for at, tile in tiles_of(in_refs, count):
        extend(at, tile)
    for t in range(halo_tiles):
        extend(node_tiles + t, prev_ref[:, t].reshape(components * rows, LANES))
        extend(node_tiles + halo_tiles + t, next_ref[:, t].reshape(components * rows, LANES))
    modes = (lax.broadcasted_iota(jnp.int32, (mode_count, LANES), 0) + me * mode_count).astype(jnp.float32)
    low = lax.broadcasted_iota(jnp.int32, (components * rows, LANES), 1) < BLK
    lane = lax.broadcasted_iota(jnp.int32, (1, 2 * LANES), 1)
    in_first = jnp.where(lax.rem(lane, LANES) < BLK, 1.0, 0.0)
    in_half = [in_first.astype(jnp.bfloat16), (1.0 - in_first).astype(jnp.bfloat16)]

    def rotated(values):
        return jnp.concatenate([-modes * values[mode_count:], modes * values[:mode_count]], axis=0)

    def tile_of(b):
        here = pl.ds(pl.multiple_of(b * LANES, LANES), LANES)
        left, right = [], []
        for k in range(NNZB):
            weights = jnp.concatenate([radial_ref[k, :, here], axial_ref[k, :, here]], axis=1)
            first, second = columns_ref[k, 2 * b], columns_ref[k, 2 * b + 1]
            first_tile = extended_ref[lax.rem(first, 2), lax.div(first, 2)]
            second_tile = extended_ref[1 - lax.rem(second, 2), lax.div(second, 2)]
            left.append(jnp.where(low, first_tile, second_tile))
            right += [weights * in_half[0], weights * in_half[1]]
        total = jnp.dot(
            jnp.concatenate(left, axis=1),
            jnp.concatenate(right, axis=0),
            preferred_element_type=jnp.float32,
        )
        along_r = [total[c * rows : (c + 1) * rows, :LANES] for c in range(components)]
        along_z = [total[c * rows : (c + 1) * rows, LANES:] for c in range(components)]
        values = [extended_ref[0, b, c * rows : (c + 1) * rows].astype(jnp.float32) for c in range(components)]
        inv_radius = 1.0 / radius_ref[:, here]
        momentum_ref[0, b] = along_r[3]
        momentum_ref[1, b] = rotated(values[3]) * inv_radius
        momentum_ref[2, b] = along_z[3]
        return [
            rotated(values[2]) * inv_radius - along_z[1],
            along_z[0] - along_r[2],
            along_r[1] + values[1] * inv_radius - rotated(values[0]) * inv_radius,
        ]

    stride = 2 * node_tiles
    together = SUBLANES // 2 if node_tiles % (SUBLANES // 2) == 0 else 1

    def tiles_at(q, carry):
        induction = [tile_of(q * together + i) for i in range(together)]
        for i in range(3):
            put_rows(induction_ref, i * mode_count * stride + 2 * q * together, stride, [tile[i] for tile in induction])
        return carry

    lax.fori_loop(0, node_tiles // together, tiles_at, 0)


def derive(received, from_prev, from_next, radial_blocks, axial_blocks, radius, columns, count):
    components, held, rows, _ = received[0].shape
    node_tiles = len(received) * held
    halo_tiles = from_prev.shape[1]
    out_rows = 3 * rows * node_tiles
    return pl.pallas_call(
        functools.partial(derive_kernel, count, len(received)),
        in_specs=[vmem()] * (len(received) + 5) + [pl.BlockSpec(memory_space=pltpu.SMEM)],
        out_specs=[vmem()] * 2,
        out_shape=[
            jax.ShapeDtypeStruct((out_rows, LANES), jnp.float32),
            jax.ShapeDtypeStruct((3, node_tiles, rows, LANES), jnp.float32),
        ],
        scratch_shapes=[pltpu.VMEM((2, node_tiles + 2 * halo_tiles, components * rows, LANES), jnp.bfloat16)],
        compiler_params=params(),
        cost_estimate=cost(),
    )(*received, from_prev, from_next, radial_blocks, axial_blocks, radius, columns)


def momentum_kernel(count, arrived, *refs):
    in_refs, (gradient_ref, out_ref, total_ref, sems) = refs[:arrived], refs[arrived:]
    me = lax.axis_index("mode")
    components, held, rows, _ = in_refs[0].shape
    mode_count = rows // 2
    tiles = arrived // count * held
    stride = 2 * count * tiles
    out_rows = mode_count * stride
    copies = []
    for c in range(components):
        for step, offset in enumerate(offsets(count, SECOND)):
            share = source_of(me, offset, count)
            for start in range(0, tiles, SUBLANES // 2):
                values = []
                for t in range(start, min(tiles, start + SUBLANES // 2)):
                    piece = in_refs[t // held * count + step][c, t % held].astype(jnp.float32)
                    values.append(piece - gradient_ref[c, share * tiles + t])
                put_rows(total_ref, c * out_rows + 2 * (share * tiles + start), stride, values)
        done = pl.ds(c * out_rows, out_rows)
        copies.append(pltpu.make_async_copy(total_ref.at[done], out_ref.at[done], sems.at[c]))
        copies[c].start()
    for copy in copies:
        copy.wait()


def momentum_of(received, gradient, count):
    components, held, rows, _ = received[0].shape
    shape = (components * rows * len(received) * held, LANES)
    return pl.pallas_call(
        functools.partial(momentum_kernel, count, len(received)),
        in_specs=[vmem()] * (len(received) + 1),
        out_specs=pl.BlockSpec(memory_space=pl.ANY),
        out_shape=jax.ShapeDtypeStruct(shape, jnp.float32),
        scratch_shapes=[pltpu.VMEM(shape, jnp.float32), pltpu.SemaphoreType.DMA((components,))],
        compiler_params=params(),
        cost_estimate=cost(),
    )(*received, gradient)


def whole_output(value, mode_count, width):
    value = value.reshape(3, mode_count, width // LANES, 2, LANES)
    return value.transpose(0, 1, 3, 2, 4).reshape(3, mode_count, 2, width)


def body(mode_fields, radius, radial_blocks, axial_blocks, block_columns, interface_nodes):
    _, mode_count, _, width = mode_fields.shape
    count = lax.axis_size("mode")
    rows = 2 * mode_count
    inverse, forward = tables(M, THETA, count)
    inverse, forward = jnp.asarray(inverse), jnp.asarray(forward)

    def joined(pieces):
        return [piece.reshape(piece.shape[:-3] + (rows, LANES)) for piece in pieces]

    groups = groups_of(width // count // LANES)
    flow = load(mode_fields, 6)
    arrived = []
    for group in range(groups):
        order = offsets(count, FIRST_SEND)
        arrived.append(exchange([pack(flow, 0, 6, offset, group, groups) for offset in order[1:]], order[1:]))
    parcels = [(0, 6, 0, group, groups) for group in range(groups)]
    *own, inverse, forward = pack_rest(flow, parcels, [inverse, forward])
    arrived[0][1:2], carried = lax.optimization_barrier((arrived[0][1:2], [inverse, forward]))
    order = offsets(count, SECOND)
    parcels = [(6, 12, offset, 0, 1) for offset in order]
    *shares, later_inverse, later_forward = pack_rest(mode_fields, parcels, carried)
    local, physical = [], []
    for group in range(groups):
        if group == 0:
            tables_here = (later_inverse, later_forward)
        else:
            tables_here = (inverse, forward)
        *terms, velocity_magnetic = first_physics(joined([own[group]] + arrived[group]), *tables_here)
        local += exchange(terms, offsets(count, FIRST_RETURN))
        physical.append(velocity_magnetic)
    for group in range(groups):
        held, sent = slice(count if group == 0 else 0, None), slice(1, 2) if group == 0 else slice(2, None)
        local[held], shares[sent] = lax.optimization_barrier((local[held], shares[sent]))
    sources = exchange(shares, order)
    toward_prev, toward_next = interface(local, interface_nodes, count)
    halos = (from_behind(toward_next, "mer", 1), from_behind(toward_prev, "mer", -1))
    sources, halos = lax.optimization_barrier((sources, halos))
    lorentz = list(second_physics(joined(sources), physical, later_inverse, later_forward))
    lorentz, radius = lax.optimization_barrier((lorentz, radius))
    lorentz = exchange(lorentz, order)
    induction, gradient = derive(
        local, *halos, radial_blocks, axial_blocks, radius.reshape(1, width), block_columns.T, count
    )
    momentum = momentum_of(lorentz, gradient, count)
    return (whole_output(induction, mode_count, width), whole_output(momentum, mode_count, width))


def solution(mesh):
    placed = (
        P(None, "mode", None, "mer"),
        P("mer"),
        P(None, None, "mer"),
        P(None, None, "mer"),
        P("mer", None),
        P("mer", None),
    )
    return jax.shard_map(
        body,
        mesh=mesh,
        in_specs=placed,
        out_specs=(P(None, "mode", None, "mer"), P(None, "mode", None, "mer")),
        check_vma=False,
    )
```

```python
import functools
import math

import jax
import jax.numpy as jnp
import ml_dtypes
import numpy as np
from jax import lax
from jax.experimental import pallas as pl
from jax.experimental.pallas import tpu as pltpu
from jax.sharding import PartitionSpec as P

M = 128
THETA = 256
BLK = 64
NNZB = 5
LANES = 128
VMEM_LIMIT = 24 * 1024 * 1024


def params(limit=VMEM_LIMIT):
    return pltpu.CompilerParams(vmem_limit_bytes=limit)


def vmem():
    return pl.BlockSpec(memory_space=pltpu.VMEM)


def cost():
    return pl.CostEstimate(flops=1024, bytes_accessed=1024, transcendentals=0)


FIRST_SEND, FIRST_RETURN, SECOND_SEND, SECOND_RETURN = 1, 1, 1, None


def offsets(count, place):
    order = list(range(count - 1))
    order.insert(count - 1 if place is None else min(place, count - 1), count - 1)
    return order


def dest_of(me, offset, count):
    if count & (count - 1) == 0:
        return jnp.bitwise_xor(me, offset)
    return lax.rem(me + offset, count)


def source_of(me, offset, count):
    if count & (count - 1) == 0:
        return jnp.bitwise_xor(me, offset)
    return lax.rem(me + count - offset, count)


def exchange(pieces, order):
    count = lax.axis_size("mode")
    power = count & (count - 1) == 0
    received = []
    for piece, offset in zip(pieces, order):
        if offset == 0:
            received.append(piece)
            continue
        pairs = [(i, i ^ offset if power else (i + offset) % count) for i in range(count)]
        received.append(lax.ppermute(piece, "mode", pairs))
    return received


def from_behind(value, axis, steps):
    count = lax.axis_size(axis)
    initial, last = (max(0, -steps), min(count, count - steps))
    return lax.ppermute(value, axis, [(source, source + steps) for source in range(initial, last)])


def tables(mode_total, angle_total, share_count):
    mode_ids = np.arange(mode_total)
    angle_ids = np.arange(angle_total)
    phase = angle_ids[:, None] * mode_ids[None, :] % angle_total
    angle = phase.astype(np.float32) * np.float32(2.0 * math.pi / angle_total)
    weight = np.where(mode_ids == 0, 1.0, 2.0).astype(np.float32)
    cosines = np.cos(angle)
    sines = np.sin(angle)
    inverse = np.stack([weight * cosines, -weight * sines], axis=-1).astype(ml_dtypes.bfloat16)
    forward = np.stack([cosines.T, -sines.T], axis=1) / np.float32(angle_total)
    forward = forward.reshape(share_count, mode_total // share_count, 2, angle_total)
    forward = forward.transpose(0, 2, 1, 3).reshape(2 * mode_total, angle_total).astype(ml_dtypes.bfloat16)
    return (inverse.reshape(angle_total, 2 * mode_total), forward)


def groups_of(tiles):
    return 2 if tiles % 2 == 0 else 1


def pieces_of(fields_ref, first, share, group, out_ref):
    count = lax.axis_size("mode")
    tiles = fields_ref.shape[3] // count // LANES
    components, held = out_ref.shape[:2]
    pairs = []
    for t in range(held):
        start = pl.multiple_of((share * tiles + group * held + t) * LANES, LANES)
        pairs.append((fields_ref.at[pl.ds(first, components), :, :, pl.ds(start, LANES)], out_ref.at[:, t]))
    return pairs


def run_copies(pairs, sems, beside=()):
    copies = [pltpu.make_async_copy(source, target, sems.at[i]) for i, (source, target) in enumerate(pairs)]
    for copy in copies:
        copy.start()
    for source, target in beside:
        target[...] = source[...]
    for copy in copies:
        copy.wait()


def load(fields, components):
    shape = (components,) + fields.shape[1:]

    def kernel(fields_ref, out_ref, sems):
        run_copies([(fields_ref.at[c], out_ref.at[c]) for c in range(components)], sems)

    return pl.pallas_call(
        kernel,
        in_specs=[pl.BlockSpec(memory_space=pltpu.HBM)],
        out_specs=vmem(),
        out_shape=jax.ShapeDtypeStruct(shape, fields.dtype),
        scratch_shapes=[pltpu.SemaphoreType.DMA((components,))],
        compiler_params=params(),
        cost_estimate=cost(),
    )(pltpu.with_memory_space_constraint(fields, pltpu.HBM))


def packed_shape(fields, first, last, groups):
    _, mode_count, _, width = fields.shape
    return (last - first, width // lax.axis_size("mode") // LANES // groups, mode_count, 2, LANES)


def pack(fields, first, last, offset, group, groups):
    count = lax.axis_size("mode")
    shape = packed_shape(fields, first, last, groups)

    def kernel(fields_ref, out_ref, sems):
        share = dest_of(lax.axis_index("mode"), offset, count)
        run_copies(pieces_of(fields_ref, first, share, group, out_ref), sems)

    return pl.pallas_call(
        kernel,
        in_specs=[pl.BlockSpec(memory_space=pl.ANY)],
        out_specs=vmem(),
        out_shape=jax.ShapeDtypeStruct(shape, jnp.bfloat16),
        scratch_shapes=[pltpu.SemaphoreType.DMA((shape[1],))],
        compiler_params=params(),
        cost_estimate=cost(),
    )(fields)


def pack_rest(fields, parcels, carried):
    count = lax.axis_size("mode")
    shapes = [packed_shape(fields, first, last, groups) for first, last, _, _, groups in parcels]

    def kernel(fields_ref, *refs):
        inputs, refs = refs[: len(carried)], refs[len(carried) :]
        parcel_refs, outputs = refs[: len(parcels)], refs[len(parcels) : -1]
        me = lax.axis_index("mode")
        pairs = []
        for (first, _, offset, group, _), parcel_ref in zip(parcels, parcel_refs):
            pairs += pieces_of(fields_ref, first, dest_of(me, offset, count), group, parcel_ref)
        run_copies(pairs, refs[-1], zip(inputs, outputs))

    return pl.pallas_call(
        kernel,
        in_specs=[pl.BlockSpec(memory_space=pl.ANY)] + [vmem()] * len(carried),
        out_specs=[vmem()] * (len(parcels) + len(carried)),
        out_shape=[jax.ShapeDtypeStruct(shape, jnp.bfloat16) for shape in shapes]
        + [jax.ShapeDtypeStruct(value.shape, value.dtype) for value in carried],
        scratch_shapes=[pltpu.SemaphoreType.DMA((sum(shape[1] for shape in shapes),))],
        compiler_params=params(),
        cost_estimate=cost(),
    )(fields, *carried)


def cross(a, b):
    return [a[1] * b[2] - a[2] * b[1], a[2] * b[0] - a[0] * b[2], a[0] * b[1] - a[1] * b[0]]


def to_physical(order, in_refs, inverse, x_ref, store):
    me = lax.axis_index("mode")
    components, tiles, rows, _ = in_refs[0].shape
    for in_ref, offset in zip(in_refs, order):
        at = pl.multiple_of(source_of(me, offset, len(order)) * rows, rows)
        for c in range(components):
            for t in range(tiles):
                x_ref[c, pl.ds(at, rows), t * LANES : (t + 1) * LANES] = in_ref[c, t]
    for c in range(components):
        store(c, jnp.dot(inverse, x_ref[c], preferred_element_type=jnp.float32))


def to_modes(order, forward_ref, table_ref, product_ref, out_refs):
    count = len(order)
    me = lax.axis_index("mode")
    components, tiles, rows, _ = out_refs[0].shape
    for step, offset in enumerate(order):
        at = pl.multiple_of(dest_of(me, offset, count) * rows, rows)
        table_ref[step * rows : (step + 1) * rows] = forward_ref[pl.ds(at, rows)]
    for c in range(components):
        terms = jnp.dot(table_ref[...], product_ref[c], preferred_element_type=jnp.float32)
        terms = terms.astype(jnp.bfloat16)
        for step in range(count):
            for t in range(tiles):
                out_refs[step][c, t] = terms[step * rows : (step + 1) * rows, t * LANES : (t + 1) * LANES]


CHUNK = 32


def first_kernel(count, *refs):
    in_refs, (inverse_ref, forward_ref) = refs[:count], refs[count : count + 2]
    out_refs, (physical_ref, x_ref, product_ref, table_ref) = refs[count + 2 : 2 * count + 2], refs[2 * count + 2 :]

    def store(c, value):
        physical_ref[c] = value

    to_physical(offsets(count, FIRST_SEND), in_refs, inverse_ref[...], x_ref, store)
    for i in range(THETA // CHUNK):
        at = slice(i * CHUNK, (i + 1) * CHUNK)
        velocity = [physical_ref[c, at] for c in range(3)]
        magnetic = [physical_ref[c, at] for c in range(3, 6)]
        energy = 0.5 * (velocity[0] * velocity[0] + velocity[1] * velocity[1] + velocity[2] * velocity[2])
        for c, value in enumerate(cross(velocity, magnetic) + [energy]):
            product_ref[c, at] = value.astype(jnp.bfloat16)
    to_modes(offsets(count, FIRST_RETURN), forward_ref, table_ref, product_ref, out_refs)


def first_physics(received, inverse, forward):
    count = len(received)
    components, tiles, rows, _ = received[0].shape
    width = tiles * LANES
    return pl.pallas_call(
        functools.partial(first_kernel, count),
        in_specs=[vmem()] * (count + 2),
        out_specs=[vmem()] * (count + 1),
        out_shape=[jax.ShapeDtypeStruct((4, tiles, rows, LANES), jnp.bfloat16)] * count
        + [jax.ShapeDtypeStruct((components, THETA, width), jnp.float32)],
        scratch_shapes=[
            pltpu.VMEM((components, 2 * M, width), jnp.bfloat16),
            pltpu.VMEM((4, THETA, width), jnp.bfloat16),
            pltpu.VMEM((2 * M, THETA), jnp.bfloat16),
        ],
        compiler_params=params(),
        cost_estimate=cost(),
    )(*received, inverse, forward)


def second_kernel(count, groups, *refs):
    in_refs, refs = refs[:count], refs[count:]
    first_refs, (inverse_ref, forward_ref) = refs[:groups], refs[groups : groups + 2]
    out_refs, (physical_ref, x_ref, product_ref, table_ref) = refs[groups + 2 : groups + 2 + count], refs[groups + 2 + count :]
    width = first_refs[0].shape[2]

    def store(c, value):
        physical_ref[c] = value

    to_physical(offsets(count, SECOND_SEND), in_refs, inverse_ref[...], x_ref, store)
    for group in range(groups):
        lanes = slice(group * width, (group + 1) * width)
        for i in range(THETA // CHUNK):
            at = slice(i * CHUNK, (i + 1) * CHUNK)
            velocity = [first_refs[group][c, at] for c in range(3)]
            magnetic = [first_refs[group][c, at] for c in range(3, 6)]
            current = [physical_ref[c, at, lanes] for c in range(3)]
            vorticity = [physical_ref[c, at, lanes] for c in range(3, 6)]
            lorentz = [a + b for a, b in zip(cross(current, magnetic), cross(velocity, vorticity))]
            for c, value in enumerate(lorentz):
                product_ref[c, at, lanes] = value.astype(jnp.bfloat16)
    to_modes(offsets(count, SECOND_RETURN), forward_ref, table_ref, product_ref, out_refs)


def second_physics(received, physical, inverse, forward):
    count, groups = len(received), len(physical)
    components, tiles, rows, _ = received[0].shape
    width = tiles * LANES
    return pl.pallas_call(
        functools.partial(second_kernel, count, groups),
        in_specs=[vmem()] * (count + groups + 2),
        out_specs=[vmem()] * count,
        out_shape=[jax.ShapeDtypeStruct((3, tiles, rows, LANES), jnp.bfloat16)] * count,
        scratch_shapes=[
            pltpu.VMEM((components, THETA, width), jnp.float32),
            pltpu.VMEM((components, 2 * M, width), jnp.bfloat16),
            pltpu.VMEM((3, THETA, width), jnp.bfloat16),
            pltpu.VMEM((2 * M, THETA), jnp.bfloat16),
        ],
        compiler_params=params(),
        cost_estimate=cost(),
    )(*received, *physical, inverse, forward)


def tiles_of(in_refs, count):
    me = lax.axis_index("mode")
    components, held, rows, _ = in_refs[0].shape
    groups = len(in_refs) // count
    for group in range(groups):
        for step, offset in enumerate(offsets(count, FIRST_RETURN)):
            share = source_of(me, offset, count)
            for t in range(held):
                at = share * (groups * held) + group * held + t
                yield at, in_refs[group * count + step][:, t].reshape(components * rows, LANES)


def interface_kernel(count, arrived, *refs):
    in_refs, (nodes_ref, prev_ref, next_ref) = refs[:arrived], refs[arrived:]
    components, _, rows, _ = in_refs[0].shape
    halo = nodes_ref.shape[1]
    totals = [jnp.zeros((components * rows, halo), jnp.float32) for _ in range(2)]
    inner = lax.broadcasted_iota(jnp.int32, (LANES, halo), 0)
    for at, values in tiles_of(in_refs, count):
        ids = inner + at * LANES
        for way in range(2):
            chosen = jnp.where(ids == nodes_ref[way : way + 1, :], 1.0, 0.0).astype(jnp.bfloat16)
            totals[way] += jnp.dot(values, chosen, preferred_element_type=jnp.float32)
    for out_ref, total in zip((prev_ref, next_ref), totals):
        picked = total.astype(jnp.bfloat16)
        for c in range(components):
            for t in range(halo // LANES):
                out_ref[c, t] = picked[c * rows : (c + 1) * rows, t * LANES : (t + 1) * LANES]


def interface(received, interface_nodes, count):
    components, _, rows, _ = received[0].shape
    halo = interface_nodes.shape[1]
    shape = jax.ShapeDtypeStruct((components, halo // LANES, rows, LANES), jnp.bfloat16)
    return pl.pallas_call(
        functools.partial(interface_kernel, count, len(received)),
        in_specs=[vmem()] * (len(received) + 1),
        out_specs=[vmem()] * 2,
        out_shape=[shape] * 2,
        compiler_params=params(),
        cost_estimate=cost(),
    )(*received, interface_nodes)


SUBLANES = 8


def interleaved(parts):
    parts = list(parts)
    row = lax.broadcasted_iota(jnp.int32, parts[0].shape, 1)
    for distance in (1, 2, 4):
        upper = jnp.bitwise_and(row, distance) != 0
        for k in range(SUBLANES):
            if k & distance == 0:
                first, second = parts[k], parts[k + distance]
                parts[k] = jnp.where(upper, pltpu.roll(second, distance, 1), first)
                parts[k + distance] = jnp.where(upper, second, pltpu.roll(first, SUBLANES - distance, 1))
    return parts


def put_rows(out_ref, first, stride, tiles):
    modes = tiles[0].shape[0] // 2
    parts = [part for tile in tiles for part in (tile[:modes], tile[modes:])]
    if len(parts) == SUBLANES:
        whole = interleaved([part.reshape(modes // SUBLANES, SUBLANES, LANES) for part in parts])
        for mode in range(modes):
            here = pl.ds(pl.multiple_of(first + mode * stride, SUBLANES), SUBLANES)
            out_ref[here, :] = whole[mode % SUBLANES][mode // SUBLANES]
    else:
        for i, part in enumerate(parts):
            out_ref[pl.ds(first + i, modes, stride=stride), :] = part


def derive_kernel(count, arrived, *refs):
    in_refs = refs[:arrived]
    prev_ref, next_ref, radial_ref, axial_ref, radius_ref, columns_ref = refs[arrived : arrived + 6]
    induction_ref, momentum_ref, extended_ref = refs[arrived + 6 :]
    me = lax.axis_index("mode")
    components, held, rows, _ = in_refs[0].shape
    mode_count = rows // 2
    node_tiles = arrived * held
    halo_tiles = prev_ref.shape[1]

    def extend(at, tile):
        extended_ref[0, at] = tile
        extended_ref[1, at] = jnp.concatenate([tile[:, BLK:], tile[:, :BLK]], axis=1)

    for at, tile in tiles_of(in_refs, count):
        extend(at, tile)
    for t in range(halo_tiles):
        extend(node_tiles + t, prev_ref[:, t].reshape(components * rows, LANES))
        extend(node_tiles + halo_tiles + t, next_ref[:, t].reshape(components * rows, LANES))
    modes = (lax.broadcasted_iota(jnp.int32, (mode_count, LANES), 0) + me * mode_count).astype(jnp.float32)
    low = lax.broadcasted_iota(jnp.int32, (components * rows, LANES), 1) < BLK
    lane = lax.broadcasted_iota(jnp.int32, (1, 2 * LANES), 1)
    in_first = jnp.where(lax.rem(lane, LANES) < BLK, 1.0, 0.0)
    in_half = [in_first.astype(jnp.bfloat16), (1.0 - in_first).astype(jnp.bfloat16)]

    def rotated(values):
        return jnp.concatenate([-modes * values[mode_count:], modes * values[:mode_count]], axis=0)

    def tile_of(b):
        here = pl.ds(pl.multiple_of(b * LANES, LANES), LANES)
        left, right = [], []
        for k in range(NNZB):
            weights = jnp.concatenate([radial_ref[k, :, here], axial_ref[k, :, here]], axis=1)
            first, second = columns_ref[k, 2 * b], columns_ref[k, 2 * b + 1]
            first_tile = extended_ref[lax.rem(first, 2), lax.div(first, 2)]
            second_tile = extended_ref[1 - lax.rem(second, 2), lax.div(second, 2)]
            left.append(jnp.where(low, first_tile, second_tile))
            right += [weights * in_half[0], weights * in_half[1]]
        total = jnp.dot(
            jnp.concatenate(left, axis=1),
            jnp.concatenate(right, axis=0),
            preferred_element_type=jnp.float32,
        )
        along_r = [total[c * rows : (c + 1) * rows, :LANES] for c in range(components)]
        along_z = [total[c * rows : (c + 1) * rows, LANES:] for c in range(components)]
        values = [extended_ref[0, b, c * rows : (c + 1) * rows].astype(jnp.float32) for c in range(components)]
        inv_radius = 1.0 / radius_ref[:, here]
        momentum_ref[0, b] = along_r[3]
        momentum_ref[1, b] = rotated(values[3]) * inv_radius
        momentum_ref[2, b] = along_z[3]
        return [
            rotated(values[2]) * inv_radius - along_z[1],
            along_z[0] - along_r[2],
            along_r[1] + values[1] * inv_radius - rotated(values[0]) * inv_radius,
        ]

    stride = 2 * node_tiles
    together = SUBLANES // 2 if node_tiles % (SUBLANES // 2) == 0 else 1

    def tiles_at(q, carry):
        induction = [tile_of(q * together + i) for i in range(together)]
        for i in range(3):
            put_rows(induction_ref, i * mode_count * stride + 2 * q * together, stride, [tile[i] for tile in induction])
        return carry

    lax.fori_loop(0, node_tiles // together, tiles_at, 0)


def derive(received, from_prev, from_next, radial_blocks, axial_blocks, radius, columns, count):
    components, held, rows, _ = received[0].shape
    node_tiles = len(received) * held
    halo_tiles = from_prev.shape[1]
    out_rows = 3 * rows * node_tiles
    return pl.pallas_call(
        functools.partial(derive_kernel, count, len(received)),
        in_specs=[vmem()] * (len(received) + 5) + [pl.BlockSpec(memory_space=pltpu.SMEM)],
        out_specs=[vmem()] * 2,
        out_shape=[
            jax.ShapeDtypeStruct((out_rows, LANES), jnp.float32),
            jax.ShapeDtypeStruct((3, node_tiles, rows, LANES), jnp.float32),
        ],
        scratch_shapes=[pltpu.VMEM((2, node_tiles + 2 * halo_tiles, components * rows, LANES), jnp.bfloat16)],
        compiler_params=params(),
        cost_estimate=cost(),
    )(*received, from_prev, from_next, radial_blocks, axial_blocks, radius, columns)


def momentum_kernel(count, arrived, *refs):
    in_refs, (gradient_ref, out_ref, total_ref, sems) = refs[:arrived], refs[arrived:]
    me = lax.axis_index("mode")
    components, held, rows, _ = in_refs[0].shape
    mode_count = rows // 2
    tiles = arrived // count * held
    stride = 2 * count * tiles
    out_rows = mode_count * stride
    copies = []
    for c in range(components):
        for step, offset in enumerate(offsets(count, SECOND_RETURN)):
            share = source_of(me, offset, count)
            for start in range(0, tiles, SUBLANES // 2):
                values = []
                for t in range(start, min(tiles, start + SUBLANES // 2)):
                    piece = in_refs[t // held * count + step][c, t % held].astype(jnp.float32)
                    values.append(piece - gradient_ref[c, share * tiles + t])
                put_rows(total_ref, c * out_rows + 2 * (share * tiles + start), stride, values)
        done = pl.ds(c * out_rows, out_rows)
        copies.append(pltpu.make_async_copy(total_ref.at[done], out_ref.at[done], sems.at[c]))
        copies[c].start()
    for copy in copies:
        copy.wait()


def momentum_of(received, gradient, count):
    components, held, rows, _ = received[0].shape
    shape = (components * rows * len(received) * held, LANES)
    return pl.pallas_call(
        functools.partial(momentum_kernel, count, len(received)),
        in_specs=[vmem()] * (len(received) + 1),
        out_specs=pl.BlockSpec(memory_space=pl.ANY),
        out_shape=jax.ShapeDtypeStruct(shape, jnp.float32),
        scratch_shapes=[pltpu.VMEM(shape, jnp.float32), pltpu.SemaphoreType.DMA((components,))],
        compiler_params=params(),
        cost_estimate=cost(),
    )(*received, gradient)


def whole_output(value, mode_count, width):
    value = value.reshape(3, mode_count, width // LANES, 2, LANES)
    return value.transpose(0, 1, 3, 2, 4).reshape(3, mode_count, 2, width)


def body(mode_fields, radius, radial_blocks, axial_blocks, block_columns, interface_nodes):
    _, mode_count, _, width = mode_fields.shape
    count = lax.axis_size("mode")
    rows = 2 * mode_count
    inverse, forward = tables(M, THETA, count)
    inverse, forward = jnp.asarray(inverse), jnp.asarray(forward)

    def joined(pieces):
        return [piece.reshape(piece.shape[:-3] + (rows, LANES)) for piece in pieces]

    groups = groups_of(width // count // LANES)
    flow = load(mode_fields, 6)
    arrived = []
    for group in range(groups):
        order = offsets(count, FIRST_SEND)
        arrived.append(exchange([pack(flow, 0, 6, offset, group, groups) for offset in order[1:]], order[1:]))
    parcels = [(0, 6, 0, group, groups) for group in range(groups)]
    *own, inverse, forward = pack_rest(flow, parcels, [inverse, forward])
    arrived[0][1:2], carried = lax.optimization_barrier((arrived[0][1:2], [inverse, forward]))
    order = offsets(count, SECOND_SEND)
    parcels = [(6, 12, offset, 0, 1) for offset in order]
    *shares, later_inverse, later_forward = pack_rest(mode_fields, parcels, carried)
    local, physical = [], []
    for group in range(groups):
        if group == 0:
            tables_here = (later_inverse, later_forward)
        else:
            tables_here = (inverse, forward)
        *terms, velocity_magnetic = first_physics(joined([own[group]] + arrived[group]), *tables_here)
        local += exchange(terms, offsets(count, FIRST_RETURN))
        physical.append(velocity_magnetic)
    for group in range(groups):
        held, sent = slice(count if group == 0 else 0, None), slice(1, 2) if group == 0 else slice(2, None)
        local[held], shares[sent] = lax.optimization_barrier((local[held], shares[sent]))
    sources = exchange(shares, order)
    toward_prev, toward_next = interface(local, interface_nodes, count)
    halos = (from_behind(toward_next, "mer", 1), from_behind(toward_prev, "mer", -1))
    sources, halos = lax.optimization_barrier((sources, halos))
    lorentz = list(second_physics(joined(sources), physical, later_inverse, later_forward))
    lorentz, radius = lax.optimization_barrier((lorentz, radius))
    lorentz = exchange(lorentz, offsets(count, SECOND_RETURN))
    induction, gradient = derive(
        local, *halos, radial_blocks, axial_blocks, radius.reshape(1, width), block_columns.T, count
    )
    momentum = momentum_of(lorentz, gradient, count)
    return (whole_output(induction, mode_count, width), whole_output(momentum, mode_count, width))


def solution(mesh):
    placed = (
        P(None, "mode", None, "mer"),
        P("mer"),
        P(None, None, "mer"),
        P(None, None, "mer"),
        P("mer", None),
        P("mer", None),
    )
    return jax.shard_map(
        body,
        mesh=mesh,
        in_specs=placed,
        out_specs=(P(None, "mode", None, "mer"), P(None, "mode", None, "mer")),
        check_vma=False,
    )
```

```python
import functools
import math

import jax
import jax.numpy as jnp
import ml_dtypes
import numpy as np
from jax import lax
from jax.experimental import pallas as pl
from jax.experimental.pallas import tpu as pltpu
from jax.sharding import PartitionSpec as P

M = 128
THETA = 256
BLK = 64
NNZB = 5
LANES = 128
VMEM_LIMIT = 24 * 1024 * 1024


def params(limit=VMEM_LIMIT):
    return pltpu.CompilerParams(vmem_limit_bytes=limit)


def vmem():
    return pl.BlockSpec(memory_space=pltpu.VMEM)


def cost():
    return pl.CostEstimate(flops=1024, bytes_accessed=1024, transcendentals=0)


FIRST_SEND, FIRST_RETURN, SECOND_SEND, SECOND_RETURN = 1, 1, 1, None


def offsets(count, place):
    order = list(range(count - 1))
    order.insert(count - 1 if place is None else min(place, count - 1), count - 1)
    return order


def dest_of(me, offset, count):
    if count & (count - 1) == 0:
        return jnp.bitwise_xor(me, offset)
    return lax.rem(me + offset, count)


def source_of(me, offset, count):
    if count & (count - 1) == 0:
        return jnp.bitwise_xor(me, offset)
    return lax.rem(me + count - offset, count)


def exchange(pieces, order):
    count = lax.axis_size("mode")
    power = count & (count - 1) == 0
    received = []
    for piece, offset in zip(pieces, order):
        if offset == 0:
            received.append(piece)
            continue
        pairs = [(i, i ^ offset if power else (i + offset) % count) for i in range(count)]
        received.append(lax.ppermute(piece, "mode", pairs))
    return received


def from_behind(value, axis, steps):
    count = lax.axis_size(axis)
    initial, last = (max(0, -steps), min(count, count - steps))
    return lax.ppermute(value, axis, [(source, source + steps) for source in range(initial, last)])


def tables(mode_total, angle_total, share_count):
    mode_ids = np.arange(mode_total)
    angle_ids = np.arange(angle_total)
    phase = angle_ids[:, None] * mode_ids[None, :] % angle_total
    angle = phase.astype(np.float32) * np.float32(2.0 * math.pi / angle_total)
    weight = np.where(mode_ids == 0, 1.0, 2.0).astype(np.float32)
    cosines = np.cos(angle)
    sines = np.sin(angle)
    inverse = np.stack([weight * cosines, -weight * sines], axis=-1).astype(ml_dtypes.bfloat16)
    forward = np.stack([cosines.T, -sines.T], axis=1) / np.float32(angle_total)
    forward = forward.reshape(share_count, mode_total // share_count, 2, angle_total)
    forward = forward.transpose(0, 2, 1, 3).reshape(2 * mode_total, angle_total).astype(ml_dtypes.bfloat16)
    return (inverse.reshape(angle_total, 2 * mode_total), forward)


def groups_of(tiles):
    return 2 if tiles % 2 == 0 else 1


def spans_of(tiles):
    return [(0, tiles - 1), (tiles - 1, 1)] if tiles > 2 else [(0, tiles)]


def pieces_of(fields_ref, first, share, begin, out_ref):
    count = lax.axis_size("mode")
    tiles = fields_ref.shape[3] // count // LANES
    components, held = out_ref.shape[:2]
    pairs = []
    for t in range(held):
        start = pl.multiple_of((share * tiles + begin + t) * LANES, LANES)
        pairs.append((fields_ref.at[pl.ds(first, components), :, :, pl.ds(start, LANES)], out_ref.at[:, t]))
    return pairs


def run_copies(pairs, sems, beside=()):
    copies = [pltpu.make_async_copy(source, target, sems.at[i]) for i, (source, target) in enumerate(pairs)]
    for copy in copies:
        copy.start()
    for source, target in beside:
        target[...] = source[...]
    for copy in copies:
        copy.wait()


def load(fields, components):
    shape = (components,) + fields.shape[1:]

    def kernel(fields_ref, out_ref, sems):
        run_copies([(fields_ref.at[c], out_ref.at[c]) for c in range(components)], sems)

    return pl.pallas_call(
        kernel,
        in_specs=[pl.BlockSpec(memory_space=pltpu.HBM)],
        out_specs=vmem(),
        out_shape=jax.ShapeDtypeStruct(shape, fields.dtype),
        scratch_shapes=[pltpu.SemaphoreType.DMA((components,))],
        compiler_params=params(),
        cost_estimate=cost(),
    )(pltpu.with_memory_space_constraint(fields, pltpu.HBM))


def packed_shape(fields, first, last, held):
    return (last - first, held, fields.shape[1], 2, LANES)


def pack(fields, first, last, offset, begin, held):
    count = lax.axis_size("mode")
    shape = packed_shape(fields, first, last, held)

    def kernel(fields_ref, out_ref, sems):
        share = dest_of(lax.axis_index("mode"), offset, count)
        run_copies(pieces_of(fields_ref, first, share, begin, out_ref), sems)

    return pl.pallas_call(
        kernel,
        in_specs=[pl.BlockSpec(memory_space=pl.ANY)],
        out_specs=vmem(),
        out_shape=jax.ShapeDtypeStruct(shape, jnp.bfloat16),
        scratch_shapes=[pltpu.SemaphoreType.DMA((shape[1],))],
        compiler_params=params(),
        cost_estimate=cost(),
    )(fields)


def pack_rest(fields, parcels, carried):
    count = lax.axis_size("mode")
    shapes = [packed_shape(fields, first, last, held) for first, last, _, _, held in parcels]

    def kernel(fields_ref, *refs):
        inputs, refs = refs[: len(carried)], refs[len(carried) :]
        parcel_refs, outputs = refs[: len(parcels)], refs[len(parcels) : -1]
        me = lax.axis_index("mode")
        pairs = []
        for (first, _, offset, begin, _), parcel_ref in zip(parcels, parcel_refs):
            pairs += pieces_of(fields_ref, first, dest_of(me, offset, count), begin, parcel_ref)
        run_copies(pairs, refs[-1], zip(inputs, outputs))

    return pl.pallas_call(
        kernel,
        in_specs=[pl.BlockSpec(memory_space=pl.ANY)] + [vmem()] * len(carried),
        out_specs=[vmem()] * (len(parcels) + len(carried)),
        out_shape=[jax.ShapeDtypeStruct(shape, jnp.bfloat16) for shape in shapes]
        + [jax.ShapeDtypeStruct(value.shape, value.dtype) for value in carried],
        scratch_shapes=[pltpu.SemaphoreType.DMA((sum(shape[1] for shape in shapes),))],
        compiler_params=params(),
        cost_estimate=cost(),
    )(fields, *carried)


def cross(a, b):
    return [a[1] * b[2] - a[2] * b[1], a[2] * b[0] - a[0] * b[2], a[0] * b[1] - a[1] * b[0]]


def to_physical(order, in_refs, inverse, x_ref, store):
    me = lax.axis_index("mode")
    components, tiles, rows, _ = in_refs[0].shape
    for in_ref, offset in zip(in_refs, order):
        at = pl.multiple_of(source_of(me, offset, len(order)) * rows, rows)
        for c in range(components):
            for t in range(tiles):
                x_ref[c, pl.ds(at, rows), t * LANES : (t + 1) * LANES] = in_ref[c, t]
    for c in range(components):
        store(c, jnp.dot(inverse, x_ref[c], preferred_element_type=jnp.float32))


def to_modes(order, forward_ref, table_ref, product_ref, out_refs):
    count = len(order)
    me = lax.axis_index("mode")
    components, tiles, rows, _ = out_refs[0].shape
    for step, offset in enumerate(order):
        at = pl.multiple_of(dest_of(me, offset, count) * rows, rows)
        table_ref[step * rows : (step + 1) * rows] = forward_ref[pl.ds(at, rows)]
    for c in range(components):
        terms = jnp.dot(table_ref[...], product_ref[c], preferred_element_type=jnp.float32)
        terms = terms.astype(jnp.bfloat16)
        for step in range(count):
            for t in range(tiles):
                out_refs[step][c, t] = terms[step * rows : (step + 1) * rows, t * LANES : (t + 1) * LANES]


CHUNK = 32


def first_kernel(count, *refs):
    in_refs, (inverse_ref, forward_ref) = refs[:count], refs[count : count + 2]
    out_refs, (physical_ref, x_ref, product_ref, table_ref) = refs[count + 2 : 2 * count + 2], refs[2 * count + 2 :]

    def store(c, value):
        physical_ref[c] = value

    to_physical(offsets(count, FIRST_SEND), in_refs, inverse_ref[...], x_ref, store)
    for i in range(THETA // CHUNK):
        at = slice(i * CHUNK, (i + 1) * CHUNK)
        velocity = [physical_ref[c, at] for c in range(3)]
        magnetic = [physical_ref[c, at] for c in range(3, 6)]
        energy = 0.5 * (velocity[0] * velocity[0] + velocity[1] * velocity[1] + velocity[2] * velocity[2])
        for c, value in enumerate(cross(velocity, magnetic) + [energy]):
            product_ref[c, at] = value.astype(jnp.bfloat16)
    to_modes(offsets(count, FIRST_RETURN), forward_ref, table_ref, product_ref, out_refs)


def first_physics(received, inverse, forward):
    count = len(received)
    components, tiles, rows, _ = received[0].shape
    width = tiles * LANES
    return pl.pallas_call(
        functools.partial(first_kernel, count),
        in_specs=[vmem()] * (count + 2),
        out_specs=[vmem()] * (count + 1),
        out_shape=[jax.ShapeDtypeStruct((4, tiles, rows, LANES), jnp.bfloat16)] * count
        + [jax.ShapeDtypeStruct((components, THETA, width), jnp.float32)],
        scratch_shapes=[
            pltpu.VMEM((components, 2 * M, width), jnp.bfloat16),
            pltpu.VMEM((4, THETA, width), jnp.bfloat16),
            pltpu.VMEM((2 * M, THETA), jnp.bfloat16),
        ],
        compiler_params=params(),
        cost_estimate=cost(),
    )(*received, inverse, forward)


def second_kernel(count, groups, begin, *refs):
    in_refs, refs = refs[:count], refs[count:]
    first_refs, (inverse_ref, forward_ref) = refs[:groups], refs[groups : groups + 2]
    out_refs, (physical_ref, x_ref, product_ref, table_ref) = refs[groups + 2 : groups + 2 + count], refs[groups + 2 + count :]
    in_group = first_refs[0].shape[2] // LANES

    def store(c, value):
        physical_ref[c] = value

    to_physical(offsets(count, SECOND_SEND), in_refs, inverse_ref[...], x_ref, store)
    for t in range(in_refs[0].shape[1]):
        lanes = slice(t * LANES, (t + 1) * LANES)
        first_ref, place = first_refs[(begin + t) // in_group], (begin + t) % in_group
        first_lanes = slice(place * LANES, (place + 1) * LANES)
        for i in range(THETA // CHUNK):
            at = slice(i * CHUNK, (i + 1) * CHUNK)
            velocity = [first_ref[c, at, first_lanes] for c in range(3)]
            magnetic = [first_ref[c, at, first_lanes] for c in range(3, 6)]
            current = [physical_ref[c, at, lanes] for c in range(3)]
            vorticity = [physical_ref[c, at, lanes] for c in range(3, 6)]
            lorentz = [a + b for a, b in zip(cross(current, magnetic), cross(velocity, vorticity))]
            for c, value in enumerate(lorentz):
                product_ref[c, at, lanes] = value.astype(jnp.bfloat16)
    to_modes(offsets(count, SECOND_RETURN), forward_ref, table_ref, product_ref, out_refs)


def second_physics(received, physical, begin, inverse, forward):
    count, groups = len(received), len(physical)
    components, tiles, rows, _ = received[0].shape
    width = tiles * LANES
    return pl.pallas_call(
        functools.partial(second_kernel, count, groups, begin),
        in_specs=[vmem()] * (count + groups + 2),
        out_specs=[vmem()] * count,
        out_shape=[jax.ShapeDtypeStruct((3, tiles, rows, LANES), jnp.bfloat16)] * count,
        scratch_shapes=[
            pltpu.VMEM((components, THETA, width), jnp.float32),
            pltpu.VMEM((components, 2 * M, width), jnp.bfloat16),
            pltpu.VMEM((3, THETA, width), jnp.bfloat16),
            pltpu.VMEM((2 * M, THETA), jnp.bfloat16),
        ],
        compiler_params=params(),
        cost_estimate=cost(),
    )(*received, *physical, inverse, forward)


def tiles_of(in_refs, count):
    me = lax.axis_index("mode")
    components, held, rows, _ = in_refs[0].shape
    groups = len(in_refs) // count
    for group in range(groups):
        for step, offset in enumerate(offsets(count, FIRST_RETURN)):
            share = source_of(me, offset, count)
            for t in range(held):
                at = share * (groups * held) + group * held + t
                yield at, in_refs[group * count + step][:, t].reshape(components * rows, LANES)


def interface_kernel(count, arrived, *refs):
    in_refs, (nodes_ref, prev_ref, next_ref) = refs[:arrived], refs[arrived:]
    components, _, rows, _ = in_refs[0].shape
    halo = nodes_ref.shape[1]
    totals = [jnp.zeros((components * rows, halo), jnp.float32) for _ in range(2)]
    inner = lax.broadcasted_iota(jnp.int32, (LANES, halo), 0)
    for at, values in tiles_of(in_refs, count):
        ids = inner + at * LANES
        for way in range(2):
            chosen = jnp.where(ids == nodes_ref[way : way + 1, :], 1.0, 0.0).astype(jnp.bfloat16)
            totals[way] += jnp.dot(values, chosen, preferred_element_type=jnp.float32)
    for out_ref, total in zip((prev_ref, next_ref), totals):
        picked = total.astype(jnp.bfloat16)
        for c in range(components):
            for t in range(halo // LANES):
                out_ref[c, t] = picked[c * rows : (c + 1) * rows, t * LANES : (t + 1) * LANES]


def interface(received, interface_nodes, count):
    components, _, rows, _ = received[0].shape
    halo = interface_nodes.shape[1]
    shape = jax.ShapeDtypeStruct((components, halo // LANES, rows, LANES), jnp.bfloat16)
    return pl.pallas_call(
        functools.partial(interface_kernel, count, len(received)),
        in_specs=[vmem()] * (len(received) + 1),
        out_specs=[vmem()] * 2,
        out_shape=[shape] * 2,
        compiler_params=params(),
        cost_estimate=cost(),
    )(*received, interface_nodes)


SUBLANES = 8


def interleaved(parts):
    parts = list(parts)
    row = lax.broadcasted_iota(jnp.int32, parts[0].shape, 1)
    for distance in (1, 2, 4):
        upper = jnp.bitwise_and(row, distance) != 0
        for k in range(SUBLANES):
            if k & distance == 0:
                first, second = parts[k], parts[k + distance]
                parts[k] = jnp.where(upper, pltpu.roll(second, distance, 1), first)
                parts[k + distance] = jnp.where(upper, second, pltpu.roll(first, SUBLANES - distance, 1))
    return parts


def put_rows(out_ref, first, stride, tiles):
    modes = tiles[0].shape[0] // 2
    parts = [part for tile in tiles for part in (tile[:modes], tile[modes:])]
    if len(parts) == SUBLANES:
        whole = interleaved([part.reshape(modes // SUBLANES, SUBLANES, LANES) for part in parts])
        for mode in range(modes):
            here = pl.ds(pl.multiple_of(first + mode * stride, SUBLANES), SUBLANES)
            out_ref[here, :] = whole[mode % SUBLANES][mode // SUBLANES]
    else:
        for i, part in enumerate(parts):
            out_ref[pl.ds(first + i, modes, stride=stride), :] = part


def derive_kernel(count, arrived, *refs):
    in_refs = refs[:arrived]
    prev_ref, next_ref, radial_ref, axial_ref, radius_ref, columns_ref = refs[arrived : arrived + 6]
    induction_ref, momentum_ref, extended_ref = refs[arrived + 6 :]
    me = lax.axis_index("mode")
    components, held, rows, _ = in_refs[0].shape
    mode_count = rows // 2
    node_tiles = arrived * held
    halo_tiles = prev_ref.shape[1]

    def extend(at, tile):
        extended_ref[0, at] = tile
        extended_ref[1, at] = jnp.concatenate([tile[:, BLK:], tile[:, :BLK]], axis=1)

    for at, tile in tiles_of(in_refs, count):
        extend(at, tile)
    for t in range(halo_tiles):
        extend(node_tiles + t, prev_ref[:, t].reshape(components * rows, LANES))
        extend(node_tiles + halo_tiles + t, next_ref[:, t].reshape(components * rows, LANES))
    modes = (lax.broadcasted_iota(jnp.int32, (mode_count, LANES), 0) + me * mode_count).astype(jnp.float32)
    low = lax.broadcasted_iota(jnp.int32, (components * rows, LANES), 1) < BLK
    lane = lax.broadcasted_iota(jnp.int32, (1, 2 * LANES), 1)
    in_first = jnp.where(lax.rem(lane, LANES) < BLK, 1.0, 0.0)
    in_half = [in_first.astype(jnp.bfloat16), (1.0 - in_first).astype(jnp.bfloat16)]

    def rotated(values):
        return jnp.concatenate([-modes * values[mode_count:], modes * values[:mode_count]], axis=0)

    def tile_of(b):
        here = pl.ds(pl.multiple_of(b * LANES, LANES), LANES)
        left, right = [], []
        for k in range(NNZB):
            weights = jnp.concatenate([radial_ref[k, :, here], axial_ref[k, :, here]], axis=1)
            first, second = columns_ref[k, 2 * b], columns_ref[k, 2 * b + 1]
            first_tile = extended_ref[lax.rem(first, 2), lax.div(first, 2)]
            second_tile = extended_ref[1 - lax.rem(second, 2), lax.div(second, 2)]
            left.append(jnp.where(low, first_tile, second_tile))
            right += [weights * in_half[0], weights * in_half[1]]
        total = jnp.dot(
            jnp.concatenate(left, axis=1),
            jnp.concatenate(right, axis=0),
            preferred_element_type=jnp.float32,
        )
        along_r = [total[c * rows : (c + 1) * rows, :LANES] for c in range(components)]
        along_z = [total[c * rows : (c + 1) * rows, LANES:] for c in range(components)]
        values = [extended_ref[0, b, c * rows : (c + 1) * rows].astype(jnp.float32) for c in range(components)]
        inv_radius = 1.0 / radius_ref[:, here]
        momentum_ref[0, b] = along_r[3]
        momentum_ref[1, b] = rotated(values[3]) * inv_radius
        momentum_ref[2, b] = along_z[3]
        return [
            rotated(values[2]) * inv_radius - along_z[1],
            along_z[0] - along_r[2],
            along_r[1] + values[1] * inv_radius - rotated(values[0]) * inv_radius,
        ]

    stride = 2 * node_tiles
    together = SUBLANES // 2 if node_tiles % (SUBLANES // 2) == 0 else 1

    def tiles_at(q, carry):
        induction = [tile_of(q * together + i) for i in range(together)]
        for i in range(3):
            put_rows(induction_ref, i * mode_count * stride + 2 * q * together, stride, [tile[i] for tile in induction])
        return carry

    lax.fori_loop(0, node_tiles // together, tiles_at, 0)


def derive(received, from_prev, from_next, radial_blocks, axial_blocks, radius, columns, count):
    components, held, rows, _ = received[0].shape
    node_tiles = len(received) * held
    halo_tiles = from_prev.shape[1]
    out_rows = 3 * rows * node_tiles
    return pl.pallas_call(
        functools.partial(derive_kernel, count, len(received)),
        in_specs=[vmem()] * (len(received) + 5) + [pl.BlockSpec(memory_space=pltpu.SMEM)],
        out_specs=[vmem()] * 2,
        out_shape=[
            jax.ShapeDtypeStruct((out_rows, LANES), jnp.float32),
            jax.ShapeDtypeStruct((3, node_tiles, rows, LANES), jnp.float32),
        ],
        scratch_shapes=[pltpu.VMEM((2, node_tiles + 2 * halo_tiles, components * rows, LANES), jnp.bfloat16)],
        compiler_params=params(),
        cost_estimate=cost(),
    )(*received, from_prev, from_next, radial_blocks, axial_blocks, radius, columns)


def momentum_kernel(count, arrived, *refs):
    in_refs, (gradient_ref, out_ref, total_ref, sems) = refs[:arrived], refs[arrived:]
    me = lax.axis_index("mode")
    components, _, rows, _ = in_refs[0].shape
    tiles = gradient_ref.shape[1] // count
    holders = [(part, t) for part in range(arrived // count) for t in range(in_refs[part * count].shape[1])]
    mode_count = rows // 2
    stride = 2 * count * tiles
    out_rows = mode_count * stride
    copies = []
    for c in range(components):
        for step, offset in enumerate(offsets(count, SECOND_RETURN)):
            share = source_of(me, offset, count)
            for start in range(0, tiles, SUBLANES // 2):
                values = []
                for t in range(start, min(tiles, start + SUBLANES // 2)):
                    part, at = holders[t]
                    piece = in_refs[part * count + step][c, at].astype(jnp.float32)
                    values.append(piece - gradient_ref[c, share * tiles + t])
                put_rows(total_ref, c * out_rows + 2 * (share * tiles + start), stride, values)
        done = pl.ds(c * out_rows, out_rows)
        copies.append(pltpu.make_async_copy(total_ref.at[done], out_ref.at[done], sems.at[c]))
        copies[c].start()
    for copy in copies:
        copy.wait()


def momentum_of(received, gradient, count):
    components, _, rows, _ = received[0].shape
    shape = (components * rows * gradient.shape[1], LANES)
    return pl.pallas_call(
        functools.partial(momentum_kernel, count, len(received)),
        in_specs=[vmem()] * (len(received) + 1),
        out_specs=pl.BlockSpec(memory_space=pl.ANY),
        out_shape=jax.ShapeDtypeStruct(shape, jnp.float32),
        scratch_shapes=[pltpu.VMEM(shape, jnp.float32), pltpu.SemaphoreType.DMA((components,))],
        compiler_params=params(),
        cost_estimate=cost(),
    )(*received, gradient)


def whole_output(value, mode_count, width):
    value = value.reshape(3, mode_count, width // LANES, 2, LANES)
    return value.transpose(0, 1, 3, 2, 4).reshape(3, mode_count, 2, width)


def body(mode_fields, radius, radial_blocks, axial_blocks, block_columns, interface_nodes):
    _, mode_count, _, width = mode_fields.shape
    count = lax.axis_size("mode")
    rows = 2 * mode_count
    inverse, forward = tables(M, THETA, count)
    inverse, forward = jnp.asarray(inverse), jnp.asarray(forward)

    def joined(pieces):
        return [piece.reshape(piece.shape[:-3] + (rows, LANES)) for piece in pieces]

    tiles = width // count // LANES
    groups, spans = groups_of(tiles), spans_of(tiles)
    held = tiles // groups
    flow = load(mode_fields, 6)
    arrived = []
    for group in range(groups):
        order = offsets(count, FIRST_SEND)
        parcels = [pack(flow, 0, 6, offset, group * held, held) for offset in order[1:]]
        arrived.append(exchange(parcels, order[1:]))
    parcels = [(0, 6, 0, group * held, held) for group in range(groups)]
    *own, inverse, forward = pack_rest(flow, parcels, [inverse, forward])
    arrived[0][1:2], carried = lax.optimization_barrier((arrived[0][1:2], [inverse, forward]))
    order = offsets(count, SECOND_SEND)
    parcels = [(6, 12, offset) + span for span in spans for offset in order]
    *shares, later_inverse, later_forward = pack_rest(mode_fields, parcels, carried)
    local, physical = [], []
    for group in range(groups):
        if group == 0:
            tables_here = (later_inverse, later_forward)
        else:
            tables_here = (inverse, forward)
        *terms, velocity_magnetic = first_physics(joined([own[group]] + arrived[group]), *tables_here)
        local += exchange(terms, offsets(count, FIRST_RETURN))
        physical.append(velocity_magnetic)
    for group in range(groups):
        back, sent = slice(count if group == 0 else 0, None), slice(1, 2) if group == 0 else slice(2, count)
        local[back], shares[sent] = lax.optimization_barrier((local[back], shares[sent]))
    toward_prev, toward_next = interface(local, interface_nodes, count)
    halos = (from_behind(toward_next, "mer", 1), from_behind(toward_prev, "mer", -1))
    halos, shares[count:] = lax.optimization_barrier((halos, shares[count:]))
    lorentz = []
    for part, (begin, _) in enumerate(spans):
        sources = exchange(shares[part * count : (part + 1) * count], order)
        terms = list(second_physics(joined(sources), physical, begin, later_inverse, later_forward))
        if part == len(spans) - 1:
            terms, radius = lax.optimization_barrier((terms, radius))
        lorentz += exchange(terms, offsets(count, SECOND_RETURN))
    induction, gradient = derive(
        local, *halos, radial_blocks, axial_blocks, radius.reshape(1, width), block_columns.T, count
    )
    momentum = momentum_of(lorentz, gradient, count)
    return (whole_output(induction, mode_count, width), whole_output(momentum, mode_count, width))


def solution(mesh):
    placed = (
        P(None, "mode", None, "mer"),
        P("mer"),
        P(None, None, "mer"),
        P(None, None, "mer"),
        P("mer", None),
        P("mer", None),
    )
    return jax.shard_map(
        body,
        mesh=mesh,
        in_specs=placed,
        out_specs=(P(None, "mode", None, "mer"), P(None, "mode", None, "mer")),
        check_vma=False,
    )
```

```python
import functools
import math

import jax
import jax.numpy as jnp
import ml_dtypes
import numpy as np
from jax import lax
from jax.experimental import pallas as pl
from jax.experimental.pallas import tpu as pltpu
from jax.sharding import PartitionSpec as P

M = 128
THETA = 256
BLK = 64
NNZB = 5
LANES = 128
VMEM_LIMIT = 24 * 1024 * 1024


def params(limit=VMEM_LIMIT):
    return pltpu.CompilerParams(vmem_limit_bytes=limit)


def vmem():
    return pl.BlockSpec(memory_space=pltpu.VMEM)


def cost():
    return pl.CostEstimate(flops=1024, bytes_accessed=1024, transcendentals=0)


FIRST_SEND, FIRST_RETURN, SECOND_SEND, SECOND_RETURN = 1, 1, 1, None


def offsets(count, place):
    order = list(range(count - 1))
    order.insert(count - 1 if place is None else min(place, count - 1), count - 1)
    return order


def dest_of(me, offset, count):
    if count & (count - 1) == 0:
        return jnp.bitwise_xor(me, offset)
    return lax.rem(me + offset, count)


def source_of(me, offset, count):
    if count & (count - 1) == 0:
        return jnp.bitwise_xor(me, offset)
    return lax.rem(me + count - offset, count)


def exchange(pieces, order):
    count = lax.axis_size("mode")
    power = count & (count - 1) == 0
    received = []
    for piece, offset in zip(pieces, order):
        if offset == 0:
            received.append(piece)
            continue
        pairs = [(i, i ^ offset if power else (i + offset) % count) for i in range(count)]
        received.append(lax.ppermute(piece, "mode", pairs))
    return received


def from_behind(value, axis, steps):
    count = lax.axis_size(axis)
    initial, last = (max(0, -steps), min(count, count - steps))
    return lax.ppermute(value, axis, [(source, source + steps) for source in range(initial, last)])


def tables(mode_total, angle_total, share_count):
    mode_ids = np.arange(mode_total)
    angle_ids = np.arange(angle_total)
    phase = angle_ids[:, None] * mode_ids[None, :] % angle_total
    angle = phase.astype(np.float32) * np.float32(2.0 * math.pi / angle_total)
    weight = np.where(mode_ids == 0, 1.0, 2.0).astype(np.float32)
    cosines = np.cos(angle)
    sines = np.sin(angle)
    inverse = np.stack([weight * cosines, -weight * sines], axis=-1).astype(ml_dtypes.bfloat16)
    forward = np.stack([cosines.T, -sines.T], axis=1) / np.float32(angle_total)
    forward = forward.reshape(share_count, mode_total // share_count, 2, angle_total)
    forward = forward.transpose(0, 2, 1, 3).reshape(2 * mode_total, angle_total).astype(ml_dtypes.bfloat16)
    return (inverse.reshape(angle_total, 2 * mode_total), forward)


def groups_of(tiles):
    return 2 if tiles % 2 == 0 else 1


def pieces_of(fields_ref, first, share, group, out_ref):
    count = lax.axis_size("mode")
    tiles = fields_ref.shape[3] // count // LANES
    components, held = out_ref.shape[:2]
    pairs = []
    for t in range(held):
        start = pl.multiple_of((share * tiles + group * held + t) * LANES, LANES)
        pairs.append((fields_ref.at[pl.ds(first, components), :, :, pl.ds(start, LANES)], out_ref.at[:, t]))
    return pairs


def run_copies(pairs, sems, beside=()):
    copies = [pltpu.make_async_copy(source, target, sems.at[i]) for i, (source, target) in enumerate(pairs)]
    for copy in copies:
        copy.start()
    for source, target in beside:
        target[...] = source[...]
    for copy in copies:
        copy.wait()


def load(fields, components):
    shape = (components,) + fields.shape[1:]

    def kernel(fields_ref, out_ref, sems):
        run_copies([(fields_ref.at[c], out_ref.at[c]) for c in range(components)], sems)

    return pl.pallas_call(
        kernel,
        in_specs=[pl.BlockSpec(memory_space=pltpu.HBM)],
        out_specs=vmem(),
        out_shape=jax.ShapeDtypeStruct(shape, fields.dtype),
        scratch_shapes=[pltpu.SemaphoreType.DMA((components,))],
        compiler_params=params(),
        cost_estimate=cost(),
    )(pltpu.with_memory_space_constraint(fields, pltpu.HBM))


def packed_shape(fields, first, last, groups):
    _, mode_count, _, width = fields.shape
    return (last - first, width // lax.axis_size("mode") // LANES // groups, mode_count, 2, LANES)


def pack(fields, first, last, offset, group, groups):
    count = lax.axis_size("mode")
    shape = packed_shape(fields, first, last, groups)

    def kernel(fields_ref, out_ref, sems):
        share = dest_of(lax.axis_index("mode"), offset, count)
        run_copies(pieces_of(fields_ref, first, share, group, out_ref), sems)

    return pl.pallas_call(
        kernel,
        in_specs=[pl.BlockSpec(memory_space=pl.ANY)],
        out_specs=vmem(),
        out_shape=jax.ShapeDtypeStruct(shape, jnp.bfloat16),
        scratch_shapes=[pltpu.SemaphoreType.DMA((shape[1],))],
        compiler_params=params(),
        cost_estimate=cost(),
    )(fields)


def pack_rest(fields, parcels, carried):
    count = lax.axis_size("mode")
    shapes = [packed_shape(fields, first, last, groups) for first, last, _, _, groups in parcels]

    def kernel(fields_ref, *refs):
        inputs, refs = refs[: len(carried)], refs[len(carried) :]
        parcel_refs, outputs = refs[: len(parcels)], refs[len(parcels) : -1]
        me = lax.axis_index("mode")
        pairs = []
        for (first, _, offset, group, _), parcel_ref in zip(parcels, parcel_refs):
            pairs += pieces_of(fields_ref, first, dest_of(me, offset, count), group, parcel_ref)
        run_copies(pairs, refs[-1], zip(inputs, outputs))

    return pl.pallas_call(
        kernel,
        in_specs=[pl.BlockSpec(memory_space=pl.ANY)] + [vmem()] * len(carried),
        out_specs=[vmem()] * (len(parcels) + len(carried)),
        out_shape=[jax.ShapeDtypeStruct(shape, jnp.bfloat16) for shape in shapes]
        + [jax.ShapeDtypeStruct(value.shape, value.dtype) for value in carried],
        scratch_shapes=[pltpu.SemaphoreType.DMA((sum(shape[1] for shape in shapes),))],
        compiler_params=params(),
        cost_estimate=cost(),
    )(fields, *carried)


def cross(a, b):
    return [a[1] * b[2] - a[2] * b[1], a[2] * b[0] - a[0] * b[2], a[0] * b[1] - a[1] * b[0]]


def to_physical(order, in_refs, inverse, x_ref, store):
    me = lax.axis_index("mode")
    components, tiles, rows, _ = in_refs[0].shape
    for in_ref, offset in zip(in_refs, order):
        at = pl.multiple_of(source_of(me, offset, len(order)) * rows, rows)
        for c in range(components):
            for t in range(tiles):
                x_ref[c, pl.ds(at, rows), t * LANES : (t + 1) * LANES] = in_ref[c, t]
    for c in range(components):
        store(c, jnp.dot(inverse, x_ref[c], preferred_element_type=jnp.float32))


def to_modes(order, forward_ref, table_ref, product_ref, out_refs):
    count = len(order)
    me = lax.axis_index("mode")
    components, tiles, rows, _ = out_refs[0].shape
    for step, offset in enumerate(order):
        at = pl.multiple_of(dest_of(me, offset, count) * rows, rows)
        table_ref[step * rows : (step + 1) * rows] = forward_ref[pl.ds(at, rows)]
    for c in range(components):
        terms = jnp.dot(table_ref[...], product_ref[c], preferred_element_type=jnp.float32)
        terms = terms.astype(jnp.bfloat16)
        for step in range(count):
            for t in range(tiles):
                out_refs[step][c, t] = terms[step * rows : (step + 1) * rows, t * LANES : (t + 1) * LANES]


CHUNK = 32


def first_kernel(count, *refs):
    in_refs, (inverse_ref, forward_ref) = refs[:count], refs[count : count + 2]
    out_refs, (physical_ref, x_ref, product_ref, table_ref) = refs[count + 2 : 2 * count + 2], refs[2 * count + 2 :]

    def store(c, value):
        physical_ref[c] = value

    to_physical(offsets(count, FIRST_SEND), in_refs, inverse_ref[...], x_ref, store)
    for i in range(THETA // CHUNK):
        at = slice(i * CHUNK, (i + 1) * CHUNK)
        velocity = [physical_ref[c, at] for c in range(3)]
        magnetic = [physical_ref[c, at] for c in range(3, 6)]
        energy = 0.5 * (velocity[0] * velocity[0] + velocity[1] * velocity[1] + velocity[2] * velocity[2])
        for c, value in enumerate(cross(velocity, magnetic) + [energy]):
            product_ref[c, at] = value.astype(jnp.bfloat16)
    to_modes(offsets(count, FIRST_RETURN), forward_ref, table_ref, product_ref, out_refs)


def first_physics(received, inverse, forward):
    count = len(received)
    components, tiles, rows, _ = received[0].shape
    width = tiles * LANES
    return pl.pallas_call(
        functools.partial(first_kernel, count),
        in_specs=[vmem()] * (count + 2),
        out_specs=[vmem()] * (count + 1),
        out_shape=[jax.ShapeDtypeStruct((4, tiles, rows, LANES), jnp.bfloat16)] * count
        + [jax.ShapeDtypeStruct((components, THETA, width), jnp.float32)],
        scratch_shapes=[
            pltpu.VMEM((components, 2 * M, width), jnp.bfloat16),
            pltpu.VMEM((4, THETA, width), jnp.bfloat16),
            pltpu.VMEM((2 * M, THETA), jnp.bfloat16),
        ],
        compiler_params=params(),
        cost_estimate=cost(),
    )(*received, inverse, forward)


def second_kernel(count, groups, *refs):
    in_refs, refs = refs[:count], refs[count:]
    first_refs, (inverse_ref, forward_ref) = refs[:groups], refs[groups : groups + 2]
    out_refs, (physical_ref, x_ref, product_ref, table_ref) = refs[groups + 2 : groups + 2 + count], refs[groups + 2 + count :]
    width = first_refs[0].shape[2]

    def store(c, value):
        physical_ref[c] = value

    to_physical(offsets(count, SECOND_SEND), in_refs, inverse_ref[...], x_ref, store)
    for group in range(groups):
        lanes = slice(group * width, (group + 1) * width)
        for i in range(THETA // CHUNK):
            at = slice(i * CHUNK, (i + 1) * CHUNK)
            velocity = [first_refs[group][c, at] for c in range(3)]
            magnetic = [first_refs[group][c, at] for c in range(3, 6)]
            current = [physical_ref[c, at, lanes] for c in range(3)]
            vorticity = [physical_ref[c, at, lanes] for c in range(3, 6)]
            lorentz = [a + b for a, b in zip(cross(current, magnetic), cross(velocity, vorticity))]
            for c, value in enumerate(lorentz):
                product_ref[c, at, lanes] = value.astype(jnp.bfloat16)
    to_modes(offsets(count, SECOND_RETURN), forward_ref, table_ref, product_ref, out_refs)


def second_physics(received, physical, inverse, forward):
    count, groups = len(received), len(physical)
    components, tiles, rows, _ = received[0].shape
    width = tiles * LANES
    return pl.pallas_call(
        functools.partial(second_kernel, count, groups),
        in_specs=[vmem()] * (count + groups + 2),
        out_specs=[vmem()] * count,
        out_shape=[jax.ShapeDtypeStruct((3, tiles, rows, LANES), jnp.bfloat16)] * count,
        scratch_shapes=[
            pltpu.VMEM((components, THETA, width), jnp.float32),
            pltpu.VMEM((components, 2 * M, width), jnp.bfloat16),
            pltpu.VMEM((3, THETA, width), jnp.bfloat16),
            pltpu.VMEM((2 * M, THETA), jnp.bfloat16),
        ],
        compiler_params=params(),
        cost_estimate=cost(),
    )(*received, *physical, inverse, forward)


def tiles_of(in_refs, count):
    me = lax.axis_index("mode")
    components, held, rows, _ = in_refs[0].shape
    groups = len(in_refs) // count
    for group in range(groups):
        for step, offset in enumerate(offsets(count, FIRST_RETURN)):
            share = source_of(me, offset, count)
            for t in range(held):
                at = share * (groups * held) + group * held + t
                yield at, in_refs[group * count + step][:, t].reshape(components * rows, LANES)


def interface_kernel(count, arrived, *refs):
    in_refs, (nodes_ref, prev_ref, next_ref) = refs[:arrived], refs[arrived:]
    components, _, rows, _ = in_refs[0].shape
    halo = nodes_ref.shape[1]
    totals = [jnp.zeros((components * rows, halo), jnp.float32) for _ in range(2)]
    inner = lax.broadcasted_iota(jnp.int32, (LANES, halo), 0)
    for at, values in tiles_of(in_refs, count):
        ids = inner + at * LANES
        for way in range(2):
            chosen = jnp.where(ids == nodes_ref[way : way + 1, :], 1.0, 0.0).astype(jnp.bfloat16)
            totals[way] += jnp.dot(values, chosen, preferred_element_type=jnp.float32)
    for out_ref, total in zip((prev_ref, next_ref), totals):
        picked = total.astype(jnp.bfloat16)
        for c in range(components):
            for t in range(halo // LANES):
                out_ref[c, t] = picked[c * rows : (c + 1) * rows, t * LANES : (t + 1) * LANES]


def interface(received, interface_nodes, count):
    components, _, rows, _ = received[0].shape
    halo = interface_nodes.shape[1]
    shape = jax.ShapeDtypeStruct((components, halo // LANES, rows, LANES), jnp.bfloat16)
    return pl.pallas_call(
        functools.partial(interface_kernel, count, len(received)),
        in_specs=[vmem()] * (len(received) + 1),
        out_specs=[vmem()] * 2,
        out_shape=[shape] * 2,
        compiler_params=params(),
        cost_estimate=cost(),
    )(*received, interface_nodes)


SUBLANES = 8


def interleaved(parts):
    parts = list(parts)
    row = lax.broadcasted_iota(jnp.int32, parts[0].shape, 1)
    for distance in (1, 2, 4):
        upper = jnp.bitwise_and(row, distance) != 0
        for k in range(SUBLANES):
            if k & distance == 0:
                first, second = parts[k], parts[k + distance]
                parts[k] = jnp.where(upper, pltpu.roll(second, distance, 1), first)
                parts[k + distance] = jnp.where(upper, second, pltpu.roll(first, SUBLANES - distance, 1))
    return parts


def put_rows(out_ref, first, stride, tiles):
    modes = tiles[0].shape[0] // 2
    parts = [part for tile in tiles for part in (tile[:modes], tile[modes:])]
    if len(parts) == SUBLANES:
        whole = interleaved([part.reshape(modes // SUBLANES, SUBLANES, LANES) for part in parts])
        for mode in range(modes):
            here = pl.ds(pl.multiple_of(first + mode * stride, SUBLANES), SUBLANES)
            out_ref[here, :] = whole[mode % SUBLANES][mode // SUBLANES]
    else:
        for i, part in enumerate(parts):
            out_ref[pl.ds(first + i, modes, stride=stride), :] = part


def derive_kernel(count, arrived, *refs):
    in_refs = refs[:arrived]
    prev_ref, next_ref, radial_ref, axial_ref, radius_ref, columns_ref = refs[arrived : arrived + 6]
    induction_ref, momentum_ref, extended_ref = refs[arrived + 6 :]
    me = lax.axis_index("mode")
    components, held, rows, _ = in_refs[0].shape
    mode_count = rows // 2
    node_tiles = arrived * held
    halo_tiles = prev_ref.shape[1]

    def extend(at, tile):
        extended_ref[0, at] = tile
        extended_ref[1, at] = jnp.concatenate([tile[:, BLK:], tile[:, :BLK]], axis=1)

    for at, tile in tiles_of(in_refs, count):
        extend(at, tile)
    for t in range(halo_tiles):
        extend(node_tiles + t, prev_ref[:, t].reshape(components * rows, LANES))
        extend(node_tiles + halo_tiles + t, next_ref[:, t].reshape(components * rows, LANES))
    modes = (lax.broadcasted_iota(jnp.int32, (mode_count, LANES), 0) + me * mode_count).astype(jnp.float32)
    low = lax.broadcasted_iota(jnp.int32, (components * rows, LANES), 1) < BLK
    lane = lax.broadcasted_iota(jnp.int32, (1, 2 * LANES), 1)
    in_first = jnp.where(lax.rem(lane, LANES) < BLK, 1.0, 0.0)
    in_half = [in_first.astype(jnp.bfloat16), (1.0 - in_first).astype(jnp.bfloat16)]

    def rotated(values):
        return jnp.concatenate([-modes * values[mode_count:], modes * values[:mode_count]], axis=0)

    def tile_of(b):
        here = pl.ds(pl.multiple_of(b * LANES, LANES), LANES)
        left, right = [], []
        for k in range(NNZB):
            weights = jnp.concatenate([radial_ref[k, :, here], axial_ref[k, :, here]], axis=1)
            first, second = columns_ref[k, 2 * b], columns_ref[k, 2 * b + 1]
            first_tile = extended_ref[lax.rem(first, 2), lax.div(first, 2)]
            second_tile = extended_ref[1 - lax.rem(second, 2), lax.div(second, 2)]
            left.append(jnp.where(low, first_tile, second_tile))
            right += [weights * in_half[0], weights * in_half[1]]
        total = jnp.dot(
            jnp.concatenate(left, axis=1),
            jnp.concatenate(right, axis=0),
            preferred_element_type=jnp.float32,
        )
        along_r = [total[c * rows : (c + 1) * rows, :LANES] for c in range(components)]
        along_z = [total[c * rows : (c + 1) * rows, LANES:] for c in range(components)]
        values = [extended_ref[0, b, c * rows : (c + 1) * rows].astype(jnp.float32) for c in range(components)]
        inv_radius = 1.0 / radius_ref[:, here]
        momentum_ref[0, b] = along_r[3]
        momentum_ref[1, b] = rotated(values[3]) * inv_radius
        momentum_ref[2, b] = along_z[3]
        return [
            rotated(values[2]) * inv_radius - along_z[1],
            along_z[0] - along_r[2],
            along_r[1] + values[1] * inv_radius - rotated(values[0]) * inv_radius,
        ]

    stride = 2 * node_tiles
    together = SUBLANES // 2 if node_tiles % (SUBLANES // 2) == 0 else 1

    def tiles_at(q, carry):
        induction = [tile_of(q * together + i) for i in range(together)]
        for i in range(3):
            put_rows(induction_ref, i * mode_count * stride + 2 * q * together, stride, [tile[i] for tile in induction])
        return carry

    lax.fori_loop(0, node_tiles // together, tiles_at, 0)


def derive(received, from_prev, from_next, radial_blocks, axial_blocks, radius, columns, count):
    components, held, rows, _ = received[0].shape
    node_tiles = len(received) * held
    halo_tiles = from_prev.shape[1]
    out_rows = 3 * rows * node_tiles
    return pl.pallas_call(
        functools.partial(derive_kernel, count, len(received)),
        in_specs=[vmem()] * (len(received) + 5) + [pl.BlockSpec(memory_space=pltpu.SMEM)],
        out_specs=[vmem()] * 2,
        out_shape=[
            jax.ShapeDtypeStruct((out_rows, LANES), jnp.float32),
            jax.ShapeDtypeStruct((3, node_tiles, rows, LANES), jnp.float32),
        ],
        scratch_shapes=[pltpu.VMEM((2, node_tiles + 2 * halo_tiles, components * rows, LANES), jnp.bfloat16)],
        compiler_params=params(),
        cost_estimate=cost(),
    )(*received, from_prev, from_next, radial_blocks, axial_blocks, radius, columns)


def momentum_kernel(count, arrived, *refs):
    in_refs, (gradient_ref, out_ref, total_ref, sems) = refs[:arrived], refs[arrived:]
    me = lax.axis_index("mode")
    components, held, rows, _ = in_refs[0].shape
    mode_count = rows // 2
    tiles = arrived // count * held
    stride = 2 * count * tiles
    out_rows = mode_count * stride
    copies = []
    for c in range(components):
        for step, offset in enumerate(offsets(count, SECOND_RETURN)):
            share = source_of(me, offset, count)
            for start in range(0, tiles, SUBLANES // 2):
                values = []
                for t in range(start, min(tiles, start + SUBLANES // 2)):
                    piece = in_refs[t // held * count + step][c, t % held].astype(jnp.float32)
                    values.append(piece - gradient_ref[c, share * tiles + t])
                put_rows(total_ref, c * out_rows + 2 * (share * tiles + start), stride, values)
        done = pl.ds(c * out_rows, out_rows)
        copies.append(pltpu.make_async_copy(total_ref.at[done], out_ref.at[done], sems.at[c]))
        copies[c].start()
    for copy in copies:
        copy.wait()


def momentum_of(received, gradient, count):
    components, held, rows, _ = received[0].shape
    shape = (components * rows * len(received) * held, LANES)
    return pl.pallas_call(
        functools.partial(momentum_kernel, count, len(received)),
        in_specs=[vmem()] * (len(received) + 1),
        out_specs=pl.BlockSpec(memory_space=pl.ANY),
        out_shape=jax.ShapeDtypeStruct(shape, jnp.float32),
        scratch_shapes=[pltpu.VMEM(shape, jnp.float32), pltpu.SemaphoreType.DMA((components,))],
        compiler_params=params(),
        cost_estimate=cost(),
    )(*received, gradient)


def whole_output(value, mode_count, width):
    value = value.reshape(3, mode_count, width // LANES, 2, LANES)
    return value.transpose(0, 1, 3, 2, 4).reshape(3, mode_count, 2, width)


def body(mode_fields, radius, radial_blocks, axial_blocks, block_columns, interface_nodes):
    _, mode_count, _, width = mode_fields.shape
    count = lax.axis_size("mode")
    rows = 2 * mode_count
    inverse, forward = tables(M, THETA, count)
    inverse, forward = jnp.asarray(inverse), jnp.asarray(forward)

    def joined(pieces):
        return [piece.reshape(piece.shape[:-3] + (rows, LANES)) for piece in pieces]

    groups = groups_of(width // count // LANES)
    flow = load(mode_fields, 6)
    arrived = []
    for group in range(groups):
        order = offsets(count, FIRST_SEND)
        arrived.append(exchange([pack(flow, 0, 6, offset, group, groups) for offset in order[1:]], order[1:]))
    parcels = [(0, 6, 0, group, groups) for group in range(groups)]
    *own, inverse, forward = pack_rest(flow, parcels, [inverse, forward])
    arrived[0][1:2], carried = lax.optimization_barrier((arrived[0][1:2], [inverse, forward]))
    order = offsets(count, SECOND_SEND)
    parcels = [(6, 12, offset, 0, 1) for offset in order]
    *shares, later_inverse, later_forward = pack_rest(mode_fields, parcels, carried)
    local, physical = [], []
    for group in range(groups):
        if group == 0:
            tables_here = (later_inverse, later_forward)
        else:
            tables_here = (inverse, forward)
        *terms, velocity_magnetic = first_physics(joined([own[group]] + arrived[group]), *tables_here)
        local += exchange(terms, offsets(count, FIRST_RETURN))
        physical.append(velocity_magnetic)
    arrived[0][0], shares[1] = lax.optimization_barrier((arrived[0][0], shares[1]))
    sources = exchange(shares[:2], order[:2])
    local, shares[2:] = lax.optimization_barrier((local, shares[2:]))
    sources += exchange(shares[2:], order[2:])
    local, sources[1] = lax.optimization_barrier((local, sources[1]))
    toward_prev, toward_next = interface(local, interface_nodes, count)
    halos = (from_behind(toward_next, "mer", 1), from_behind(toward_prev, "mer", -1))
    sources, halos = lax.optimization_barrier((sources, halos))
    lorentz = list(second_physics(joined(sources), physical, later_inverse, later_forward))
    lorentz, radius = lax.optimization_barrier((lorentz, radius))
    lorentz = exchange(lorentz, offsets(count, SECOND_RETURN))
    induction, gradient = derive(
        local, *halos, radial_blocks, axial_blocks, radius.reshape(1, width), block_columns.T, count
    )
    momentum = momentum_of(lorentz, gradient, count)
    return (whole_output(induction, mode_count, width), whole_output(momentum, mode_count, width))


def solution(mesh):
    placed = (
        P(None, "mode", None, "mer"),
        P("mer"),
        P(None, None, "mer"),
        P(None, None, "mer"),
        P("mer", None),
        P("mer", None),
    )
    return jax.shard_map(
        body,
        mesh=mesh,
        in_specs=placed,
        out_specs=(P(None, "mode", None, "mer"), P(None, "mode", None, "mer")),
        check_vma=False,
    )
```

```python
import functools
import math

import jax
import jax.numpy as jnp
import ml_dtypes
import numpy as np
from jax import lax
from jax.experimental import pallas as pl
from jax.experimental.pallas import tpu as pltpu
from jax.sharding import PartitionSpec as P

M = 128
THETA = 256
BLK = 64
NNZB = 5
LANES = 128
VMEM_LIMIT = 24 * 1024 * 1024


def params(limit=VMEM_LIMIT):
    return pltpu.CompilerParams(vmem_limit_bytes=limit)


def vmem():
    return pl.BlockSpec(memory_space=pltpu.VMEM)


def cost():
    return pl.CostEstimate(flops=1024, bytes_accessed=1024, transcendentals=0)


FIRST_SEND, FIRST_RETURN, SECOND_SEND, SECOND_RETURN = 1, 1, 1, 1


def offsets(count, place):
    order = list(range(count - 1))
    order.insert(count - 1 if place is None else min(place, count - 1), count - 1)
    return order


def dest_of(me, offset, count):
    if count & (count - 1) == 0:
        return jnp.bitwise_xor(me, offset)
    return lax.rem(me + offset, count)


def source_of(me, offset, count):
    if count & (count - 1) == 0:
        return jnp.bitwise_xor(me, offset)
    return lax.rem(me + count - offset, count)


def exchange(pieces, order):
    count = lax.axis_size("mode")
    power = count & (count - 1) == 0
    received = []
    for piece, offset in zip(pieces, order):
        if offset == 0:
            received.append(piece)
            continue
        pairs = [(i, i ^ offset if power else (i + offset) % count) for i in range(count)]
        received.append(lax.ppermute(piece, "mode", pairs))
    return received


def from_behind(value, axis, steps):
    count = lax.axis_size(axis)
    initial, last = (max(0, -steps), min(count, count - steps))
    return lax.ppermute(value, axis, [(source, source + steps) for source in range(initial, last)])


def tables(mode_total, angle_total, share_count):
    mode_ids = np.arange(mode_total)
    angle_ids = np.arange(angle_total)
    phase = angle_ids[:, None] * mode_ids[None, :] % angle_total
    angle = phase.astype(np.float32) * np.float32(2.0 * math.pi / angle_total)
    weight = np.where(mode_ids == 0, 1.0, 2.0).astype(np.float32)
    cosines = np.cos(angle)
    sines = np.sin(angle)
    inverse = np.stack([weight * cosines, -weight * sines], axis=-1).astype(ml_dtypes.bfloat16)
    forward = np.stack([cosines.T, -sines.T], axis=1) / np.float32(angle_total)
    forward = forward.reshape(share_count, mode_total // share_count, 2, angle_total)
    forward = forward.transpose(0, 2, 1, 3).reshape(2 * mode_total, angle_total).astype(ml_dtypes.bfloat16)
    return (inverse.reshape(angle_total, 2 * mode_total), forward)


def groups_of(tiles):
    return 2 if tiles % 2 == 0 else 1


def pieces_of(fields_ref, first, share, group, out_ref):
    count = lax.axis_size("mode")
    tiles = fields_ref.shape[3] // count // LANES
    components, held = out_ref.shape[:2]
    pairs = []
    for t in range(held):
        start = pl.multiple_of((share * tiles + group * held + t) * LANES, LANES)
        pairs.append((fields_ref.at[pl.ds(first, components), :, :, pl.ds(start, LANES)], out_ref.at[:, t]))
    return pairs


def run_copies(pairs, sems, beside=()):
    copies = [pltpu.make_async_copy(source, target, sems.at[i]) for i, (source, target) in enumerate(pairs)]
    for copy in copies:
        copy.start()
    for source, target in beside:
        target[...] = source[...]
    for copy in copies:
        copy.wait()


def load(fields, components):
    shape = (components,) + fields.shape[1:]

    def kernel(fields_ref, out_ref, sems):
        run_copies([(fields_ref.at[c], out_ref.at[c]) for c in range(components)], sems)

    return pl.pallas_call(
        kernel,
        in_specs=[pl.BlockSpec(memory_space=pltpu.HBM)],
        out_specs=vmem(),
        out_shape=jax.ShapeDtypeStruct(shape, fields.dtype),
        scratch_shapes=[pltpu.SemaphoreType.DMA((components,))],
        compiler_params=params(),
        cost_estimate=cost(),
    )(pltpu.with_memory_space_constraint(fields, pltpu.HBM))


def packed_shape(fields, first, last, groups):
    _, mode_count, _, width = fields.shape
    return (last - first, width // lax.axis_size("mode") // LANES // groups, mode_count, 2, LANES)


def pack(fields, first, last, offset, group, groups):
    count = lax.axis_size("mode")
    shape = packed_shape(fields, first, last, groups)

    def kernel(fields_ref, out_ref, sems):
        share = dest_of(lax.axis_index("mode"), offset, count)
        run_copies(pieces_of(fields_ref, first, share, group, out_ref), sems)

    return pl.pallas_call(
        kernel,
        in_specs=[pl.BlockSpec(memory_space=pl.ANY)],
        out_specs=vmem(),
        out_shape=jax.ShapeDtypeStruct(shape, jnp.bfloat16),
        scratch_shapes=[pltpu.SemaphoreType.DMA((shape[1],))],
        compiler_params=params(),
        cost_estimate=cost(),
    )(fields)


def pack_rest(fields, parcels, carried):
    count = lax.axis_size("mode")
    shapes = [packed_shape(fields, first, last, groups) for first, last, _, _, groups in parcels]

    def kernel(fields_ref, *refs):
        inputs, refs = refs[: len(carried)], refs[len(carried) :]
        parcel_refs, outputs = refs[: len(parcels)], refs[len(parcels) : -1]
        me = lax.axis_index("mode")
        pairs = []
        for (first, _, offset, group, _), parcel_ref in zip(parcels, parcel_refs):
            pairs += pieces_of(fields_ref, first, dest_of(me, offset, count), group, parcel_ref)
        run_copies(pairs, refs[-1], zip(inputs, outputs))

    return pl.pallas_call(
        kernel,
        in_specs=[pl.BlockSpec(memory_space=pl.ANY)] + [vmem()] * len(carried),
        out_specs=[vmem()] * (len(parcels) + len(carried)),
        out_shape=[jax.ShapeDtypeStruct(shape, jnp.bfloat16) for shape in shapes]
        + [jax.ShapeDtypeStruct(value.shape, value.dtype) for value in carried],
        scratch_shapes=[pltpu.SemaphoreType.DMA((sum(shape[1] for shape in shapes),))],
        compiler_params=params(),
        cost_estimate=cost(),
    )(fields, *carried)


def cross(a, b):
    return [a[1] * b[2] - a[2] * b[1], a[2] * b[0] - a[0] * b[2], a[0] * b[1] - a[1] * b[0]]


def to_physical(order, in_refs, inverse, x_ref, store):
    me = lax.axis_index("mode")
    components, tiles, rows, _ = in_refs[0].shape
    for in_ref, offset in zip(in_refs, order):
        at = pl.multiple_of(source_of(me, offset, len(order)) * rows, rows)
        for c in range(components):
            for t in range(tiles):
                x_ref[c, pl.ds(at, rows), t * LANES : (t + 1) * LANES] = in_ref[c, t]
    for c in range(components):
        store(c, jnp.dot(inverse, x_ref[c], preferred_element_type=jnp.float32))


def to_modes(order, forward_ref, table_ref, product_ref, out_refs):
    count = len(order)
    me = lax.axis_index("mode")
    components, tiles, rows, _ = out_refs[0].shape
    for step, offset in enumerate(order):
        at = pl.multiple_of(dest_of(me, offset, count) * rows, rows)
        table_ref[step * rows : (step + 1) * rows] = forward_ref[pl.ds(at, rows)]
    for c in range(components):
        terms = jnp.dot(table_ref[...], product_ref[c], preferred_element_type=jnp.float32)
        terms = terms.astype(jnp.bfloat16)
        for step in range(count):
            for t in range(tiles):
                out_refs[step][c, t] = terms[step * rows : (step + 1) * rows, t * LANES : (t + 1) * LANES]


CHUNK = 32


def first_kernel(count, *refs):
    in_refs, (inverse_ref, forward_ref) = refs[:count], refs[count : count + 2]
    out_refs, (physical_ref, x_ref, product_ref, table_ref) = refs[count + 2 : 2 * count + 2], refs[2 * count + 2 :]

    def store(c, value):
        physical_ref[c] = value

    to_physical(offsets(count, FIRST_SEND), in_refs, inverse_ref[...], x_ref, store)
    for i in range(THETA // CHUNK):
        at = slice(i * CHUNK, (i + 1) * CHUNK)
        velocity = [physical_ref[c, at] for c in range(3)]
        magnetic = [physical_ref[c, at] for c in range(3, 6)]
        energy = 0.5 * (velocity[0] * velocity[0] + velocity[1] * velocity[1] + velocity[2] * velocity[2])
        for c, value in enumerate(cross(velocity, magnetic) + [energy]):
            product_ref[c, at] = value.astype(jnp.bfloat16)
    to_modes(offsets(count, FIRST_RETURN), forward_ref, table_ref, product_ref, out_refs)


def first_physics(received, inverse, forward):
    count = len(received)
    components, tiles, rows, _ = received[0].shape
    width = tiles * LANES
    return pl.pallas_call(
        functools.partial(first_kernel, count),
        in_specs=[vmem()] * (count + 2),
        out_specs=[vmem()] * (count + 1),
        out_shape=[jax.ShapeDtypeStruct((4, tiles, rows, LANES), jnp.bfloat16)] * count
        + [jax.ShapeDtypeStruct((components, THETA, width), jnp.float32)],
        scratch_shapes=[
            pltpu.VMEM((components, 2 * M, width), jnp.bfloat16),
            pltpu.VMEM((4, THETA, width), jnp.bfloat16),
            pltpu.VMEM((2 * M, THETA), jnp.bfloat16),
        ],
        compiler_params=params(),
        cost_estimate=cost(),
    )(*received, inverse, forward)


def second_kernel(count, groups, *refs):
    in_refs, refs = refs[:count], refs[count:]
    first_refs, (inverse_ref, forward_ref) = refs[:groups], refs[groups : groups + 2]
    out_refs, (physical_ref, x_ref, product_ref, table_ref) = refs[groups + 2 : groups + 2 + count], refs[groups + 2 + count :]
    width = first_refs[0].shape[2]

    def store(c, value):
        physical_ref[c] = value

    to_physical(offsets(count, SECOND_SEND), in_refs, inverse_ref[...], x_ref, store)
    for group in range(groups):
        lanes = slice(group * width, (group + 1) * width)
        for i in range(THETA // CHUNK):
            at = slice(i * CHUNK, (i + 1) * CHUNK)
            velocity = [first_refs[group][c, at] for c in range(3)]
            magnetic = [first_refs[group][c, at] for c in range(3, 6)]
            current = [physical_ref[c, at, lanes] for c in range(3)]
            vorticity = [physical_ref[c, at, lanes] for c in range(3, 6)]
            lorentz = [a + b for a, b in zip(cross(current, magnetic), cross(velocity, vorticity))]
            for c, value in enumerate(lorentz):
                product_ref[c, at, lanes] = value.astype(jnp.bfloat16)
    to_modes(offsets(count, SECOND_RETURN), forward_ref, table_ref, product_ref, out_refs)


def second_physics(received, physical, inverse, forward):
    count, groups = len(received), len(physical)
    components, tiles, rows, _ = received[0].shape
    width = tiles * LANES
    return pl.pallas_call(
        functools.partial(second_kernel, count, groups),
        in_specs=[vmem()] * (count + groups + 2),
        out_specs=[vmem()] * count,
        out_shape=[jax.ShapeDtypeStruct((3, tiles, rows, LANES), jnp.bfloat16)] * count,
        scratch_shapes=[
            pltpu.VMEM((components, THETA, width), jnp.float32),
            pltpu.VMEM((components, 2 * M, width), jnp.bfloat16),
            pltpu.VMEM((3, THETA, width), jnp.bfloat16),
            pltpu.VMEM((2 * M, THETA), jnp.bfloat16),
        ],
        compiler_params=params(),
        cost_estimate=cost(),
    )(*received, *physical, inverse, forward)


def tiles_of(in_refs, count):
    me = lax.axis_index("mode")
    components, held, rows, _ = in_refs[0].shape
    groups = len(in_refs) // count
    for group in range(groups):
        for step, offset in enumerate(offsets(count, FIRST_RETURN)):
            share = source_of(me, offset, count)
            for t in range(held):
                at = share * (groups * held) + group * held + t
                yield at, in_refs[group * count + step][:, t].reshape(components * rows, LANES)


def interface_kernel(count, arrived, *refs):
    in_refs, (nodes_ref, prev_ref, next_ref) = refs[:arrived], refs[arrived:]
    components, _, rows, _ = in_refs[0].shape
    halo = nodes_ref.shape[1]
    totals = [jnp.zeros((components * rows, halo), jnp.float32) for _ in range(2)]
    inner = lax.broadcasted_iota(jnp.int32, (LANES, halo), 0)
    for at, values in tiles_of(in_refs, count):
        ids = inner + at * LANES
        for way in range(2):
            chosen = jnp.where(ids == nodes_ref[way : way + 1, :], 1.0, 0.0).astype(jnp.bfloat16)
            totals[way] += jnp.dot(values, chosen, preferred_element_type=jnp.float32)
    for out_ref, total in zip((prev_ref, next_ref), totals):
        picked = total.astype(jnp.bfloat16)
        for c in range(components):
            for t in range(halo // LANES):
                out_ref[c, t] = picked[c * rows : (c + 1) * rows, t * LANES : (t + 1) * LANES]


def interface(received, interface_nodes, count):
    components, _, rows, _ = received[0].shape
    halo = interface_nodes.shape[1]
    shape = jax.ShapeDtypeStruct((components, halo // LANES, rows, LANES), jnp.bfloat16)
    return pl.pallas_call(
        functools.partial(interface_kernel, count, len(received)),
        in_specs=[vmem()] * (len(received) + 1),
        out_specs=[vmem()] * 2,
        out_shape=[shape] * 2,
        compiler_params=params(),
        cost_estimate=cost(),
    )(*received, interface_nodes)


SUBLANES = 8


def interleaved(parts):
    parts = list(parts)
    row = lax.broadcasted_iota(jnp.int32, parts[0].shape, 1)
    for distance in (1, 2, 4):
        upper = jnp.bitwise_and(row, distance) != 0
        for k in range(SUBLANES):
            if k & distance == 0:
                first, second = parts[k], parts[k + distance]
                parts[k] = jnp.where(upper, pltpu.roll(second, distance, 1), first)
                parts[k + distance] = jnp.where(upper, second, pltpu.roll(first, SUBLANES - distance, 1))
    return parts


def put_rows(out_ref, first, stride, tiles):
    modes = tiles[0].shape[0] // 2
    parts = [part for tile in tiles for part in (tile[:modes], tile[modes:])]
    if len(parts) == SUBLANES:
        whole = interleaved([part.reshape(modes // SUBLANES, SUBLANES, LANES) for part in parts])
        for mode in range(modes):
            here = pl.ds(pl.multiple_of(first + mode * stride, SUBLANES), SUBLANES)
            out_ref[here, :] = whole[mode % SUBLANES][mode // SUBLANES]
    else:
        for i, part in enumerate(parts):
            out_ref[pl.ds(first + i, modes, stride=stride), :] = part


def derive_kernel(count, arrived, *refs):
    in_refs = refs[:arrived]
    prev_ref, next_ref, radial_ref, axial_ref, radius_ref, columns_ref = refs[arrived : arrived + 6]
    induction_ref, momentum_ref, extended_ref = refs[arrived + 6 :]
    me = lax.axis_index("mode")
    components, held, rows, _ = in_refs[0].shape
    mode_count = rows // 2
    node_tiles = arrived * held
    halo_tiles = prev_ref.shape[1]

    def extend(at, tile):
        extended_ref[0, at] = tile
        extended_ref[1, at] = jnp.concatenate([tile[:, BLK:], tile[:, :BLK]], axis=1)

    for at, tile in tiles_of(in_refs, count):
        extend(at, tile)
    for t in range(halo_tiles):
        extend(node_tiles + t, prev_ref[:, t].reshape(components * rows, LANES))
        extend(node_tiles + halo_tiles + t, next_ref[:, t].reshape(components * rows, LANES))
    modes = (lax.broadcasted_iota(jnp.int32, (mode_count, LANES), 0) + me * mode_count).astype(jnp.float32)
    low = lax.broadcasted_iota(jnp.int32, (components * rows, LANES), 1) < BLK
    lane = lax.broadcasted_iota(jnp.int32, (1, 2 * LANES), 1)
    in_first = jnp.where(lax.rem(lane, LANES) < BLK, 1.0, 0.0)
    in_half = [in_first.astype(jnp.bfloat16), (1.0 - in_first).astype(jnp.bfloat16)]

    def rotated(values):
        return jnp.concatenate([-modes * values[mode_count:], modes * values[:mode_count]], axis=0)

    def tile_of(b):
        here = pl.ds(pl.multiple_of(b * LANES, LANES), LANES)
        left, right = [], []
        for k in range(NNZB):
            weights = jnp.concatenate([radial_ref[k, :, here], axial_ref[k, :, here]], axis=1)
            first, second = columns_ref[k, 2 * b], columns_ref[k, 2 * b + 1]
            first_tile = extended_ref[lax.rem(first, 2), lax.div(first, 2)]
            second_tile = extended_ref[1 - lax.rem(second, 2), lax.div(second, 2)]
            left.append(jnp.where(low, first_tile, second_tile))
            right += [weights * in_half[0], weights * in_half[1]]
        total = jnp.dot(
            jnp.concatenate(left, axis=1),
            jnp.concatenate(right, axis=0),
            preferred_element_type=jnp.float32,
        )
        along_r = [total[c * rows : (c + 1) * rows, :LANES] for c in range(components)]
        along_z = [total[c * rows : (c + 1) * rows, LANES:] for c in range(components)]
        values = [extended_ref[0, b, c * rows : (c + 1) * rows].astype(jnp.float32) for c in range(components)]
        inv_radius = 1.0 / radius_ref[:, here]
        momentum_ref[0, b] = along_r[3]
        momentum_ref[1, b] = rotated(values[3]) * inv_radius
        momentum_ref[2, b] = along_z[3]
        return [
            rotated(values[2]) * inv_radius - along_z[1],
            along_z[0] - along_r[2],
            along_r[1] + values[1] * inv_radius - rotated(values[0]) * inv_radius,
        ]

    stride = 2 * node_tiles
    together = SUBLANES // 2 if node_tiles % (SUBLANES // 2) == 0 else 1

    def tiles_at(q, carry):
        induction = [tile_of(q * together + i) for i in range(together)]
        for i in range(3):
            put_rows(induction_ref, i * mode_count * stride + 2 * q * together, stride, [tile[i] for tile in induction])
        return carry

    lax.fori_loop(0, node_tiles // together, tiles_at, 0)


def derive(received, from_prev, from_next, radial_blocks, axial_blocks, radius, columns, count):
    components, held, rows, _ = received[0].shape
    node_tiles = len(received) * held
    halo_tiles = from_prev.shape[1]
    out_rows = 3 * rows * node_tiles
    return pl.pallas_call(
        functools.partial(derive_kernel, count, len(received)),
        in_specs=[vmem()] * (len(received) + 5) + [pl.BlockSpec(memory_space=pltpu.SMEM)],
        out_specs=[vmem()] * 2,
        out_shape=[
            jax.ShapeDtypeStruct((out_rows, LANES), jnp.float32),
            jax.ShapeDtypeStruct((3, node_tiles, rows, LANES), jnp.float32),
        ],
        scratch_shapes=[pltpu.VMEM((2, node_tiles + 2 * halo_tiles, components * rows, LANES), jnp.bfloat16)],
        compiler_params=params(),
        cost_estimate=cost(),
    )(*received, from_prev, from_next, radial_blocks, axial_blocks, radius, columns)


def momentum_kernel(count, arrived, *refs):
    in_refs, (gradient_ref, out_ref, total_ref, sems) = refs[:arrived], refs[arrived:]
    me = lax.axis_index("mode")
    components, held, rows, _ = in_refs[0].shape
    mode_count = rows // 2
    tiles = arrived // count * held
    stride = 2 * count * tiles
    out_rows = mode_count * stride
    copies = []
    for c in range(components):
        for step, offset in enumerate(offsets(count, SECOND_RETURN)):
            share = source_of(me, offset, count)
            for start in range(0, tiles, SUBLANES // 2):
                values = []
                for t in range(start, min(tiles, start + SUBLANES // 2)):
                    piece = in_refs[t // held * count + step][c, t % held].astype(jnp.float32)
                    values.append(piece - gradient_ref[c, share * tiles + t])
                put_rows(total_ref, c * out_rows + 2 * (share * tiles + start), stride, values)
        done = pl.ds(c * out_rows, out_rows)
        copies.append(pltpu.make_async_copy(total_ref.at[done], out_ref.at[done], sems.at[c]))
        copies[c].start()
    for copy in copies:
        copy.wait()


def momentum_of(received, gradient, count):
    components, held, rows, _ = received[0].shape
    shape = (components * rows * len(received) * held, LANES)
    return pl.pallas_call(
        functools.partial(momentum_kernel, count, len(received)),
        in_specs=[vmem()] * (len(received) + 1),
        out_specs=pl.BlockSpec(memory_space=pl.ANY),
        out_shape=jax.ShapeDtypeStruct(shape, jnp.float32),
        scratch_shapes=[pltpu.VMEM(shape, jnp.float32), pltpu.SemaphoreType.DMA((components,))],
        compiler_params=params(),
        cost_estimate=cost(),
    )(*received, gradient)


def whole_output(value, mode_count, width):
    value = value.reshape(3, mode_count, width // LANES, 2, LANES)
    return value.transpose(0, 1, 3, 2, 4).reshape(3, mode_count, 2, width)


def body(mode_fields, radius, radial_blocks, axial_blocks, block_columns, interface_nodes):
    _, mode_count, _, width = mode_fields.shape
    count = lax.axis_size("mode")
    rows = 2 * mode_count
    inverse, forward = tables(M, THETA, count)
    inverse, forward = jnp.asarray(inverse), jnp.asarray(forward)

    def joined(pieces):
        return [piece.reshape(piece.shape[:-3] + (rows, LANES)) for piece in pieces]

    groups = groups_of(width // count // LANES)
    flow = load(mode_fields, 6)
    arrived = []
    for group in range(groups):
        order = offsets(count, FIRST_SEND)
        arrived.append(exchange([pack(flow, 0, 6, offset, group, groups) for offset in order[1:]], order[1:]))
    parcels = [(0, 6, 0, group, groups) for group in range(groups)]
    *own, inverse, forward = pack_rest(flow, parcels, [inverse, forward])
    arrived[0][1:2], carried = lax.optimization_barrier((arrived[0][1:2], [inverse, forward]))
    order = offsets(count, SECOND_SEND)
    parcels = [(6, 12, offset, 0, 1) for offset in order]
    *shares, later_inverse, later_forward = pack_rest(mode_fields, parcels, carried)
    local, physical = [], []
    for group in range(groups):
        if group == 0:
            tables_here = (later_inverse, later_forward)
        else:
            tables_here = (inverse, forward)
        *terms, velocity_magnetic = first_physics(joined([own[group]] + arrived[group]), *tables_here)
        local += exchange(terms, offsets(count, FIRST_RETURN))
        physical.append(velocity_magnetic)
    for group in range(groups):
        held, sent = slice(count if group == 0 else 0, None), slice(1, 2) if group == 0 else slice(2, None)
        local[held], shares[sent] = lax.optimization_barrier((local[held], shares[sent]))
    sources = exchange(shares, order)
    toward_prev, toward_next = interface(local, interface_nodes, count)
    halos = (from_behind(toward_next, "mer", 1), from_behind(toward_prev, "mer", -1))
    sources, halos = lax.optimization_barrier((sources, halos))
    lorentz = list(second_physics(joined(sources), physical, later_inverse, later_forward))
    lorentz, radius = lax.optimization_barrier((lorentz, radius))
    lorentz = exchange(lorentz, offsets(count, SECOND_RETURN))
    induction, gradient = derive(
        local, *halos, radial_blocks, axial_blocks, radius.reshape(1, width), block_columns.T, count
    )
    momentum = momentum_of(lorentz, gradient, count)
    return (whole_output(induction, mode_count, width), whole_output(momentum, mode_count, width))


def solution(mesh):
    placed = (
        P(None, "mode", None, "mer"),
        P("mer"),
        P(None, None, "mer"),
        P(None, None, "mer"),
        P("mer", None),
        P("mer", None),
    )
    return jax.shard_map(
        body,
        mesh=mesh,
        in_specs=placed,
        out_specs=(P(None, "mode", None, "mer"), P(None, "mode", None, "mer")),
        check_vma=False,
    )
```

```python
import functools
import math

import jax
import jax.numpy as jnp
import ml_dtypes
import numpy as np
from jax import lax
from jax.experimental import pallas as pl
from jax.experimental.pallas import tpu as pltpu
from jax.sharding import PartitionSpec as P

M = 128
THETA = 256
BLK = 64
NNZB = 5
LANES = 128
VMEM_LIMIT = 24 * 1024 * 1024


def params(limit=VMEM_LIMIT):
    return pltpu.CompilerParams(vmem_limit_bytes=limit)


def vmem():
    return pl.BlockSpec(memory_space=pltpu.VMEM)


def cost():
    return pl.CostEstimate(flops=1024, bytes_accessed=1024, transcendentals=0)


FIRST_SEND, FIRST_RETURN, SECOND_SEND, SECOND_RETURN = 1, 1, 1, 1


def offsets(count, place):
    order = list(range(count - 1))
    order.insert(count - 1 if place is None else min(place, count - 1), count - 1)
    return order


def dest_of(me, offset, count):
    if count & (count - 1) == 0:
        return jnp.bitwise_xor(me, offset)
    return lax.rem(me + offset, count)


def source_of(me, offset, count):
    if count & (count - 1) == 0:
        return jnp.bitwise_xor(me, offset)
    return lax.rem(me + count - offset, count)


def exchange(pieces, order):
    count = lax.axis_size("mode")
    power = count & (count - 1) == 0
    received = []
    for piece, offset in zip(pieces, order):
        if offset == 0:
            received.append(piece)
            continue
        pairs = [(i, i ^ offset if power else (i + offset) % count) for i in range(count)]
        received.append(lax.ppermute(piece, "mode", pairs))
    return received


def from_behind(value, axis, steps):
    count = lax.axis_size(axis)
    initial, last = (max(0, -steps), min(count, count - steps))
    return lax.ppermute(value, axis, [(source, source + steps) for source in range(initial, last)])


def tables(mode_total, angle_total, share_count):
    mode_ids = np.arange(mode_total)
    angle_ids = np.arange(angle_total)
    phase = angle_ids[:, None] * mode_ids[None, :] % angle_total
    angle = phase.astype(np.float32) * np.float32(2.0 * math.pi / angle_total)
    weight = np.where(mode_ids == 0, 1.0, 2.0).astype(np.float32)
    cosines = np.cos(angle)
    sines = np.sin(angle)
    inverse = np.stack([weight * cosines, -weight * sines], axis=-1).astype(ml_dtypes.bfloat16)
    forward = np.stack([cosines.T, -sines.T], axis=1) / np.float32(angle_total)
    forward = forward.reshape(share_count, mode_total // share_count, 2, angle_total)
    forward = forward.transpose(0, 2, 1, 3).reshape(2 * mode_total, angle_total).astype(ml_dtypes.bfloat16)
    return (inverse.reshape(angle_total, 2 * mode_total), forward)


def groups_of(tiles):
    return 2 if tiles % 2 == 0 else 1


def spans_of(tiles):
    return [(0, tiles // 2), (tiles // 2, tiles - tiles // 2)] if tiles > 1 else [(0, tiles)]


def pieces_of(fields_ref, first, share, begin, out_ref):
    count = lax.axis_size("mode")
    tiles = fields_ref.shape[3] // count // LANES
    components, held = out_ref.shape[:2]
    pairs = []
    for t in range(held):
        start = pl.multiple_of((share * tiles + begin + t) * LANES, LANES)
        pairs.append((fields_ref.at[pl.ds(first, components), :, :, pl.ds(start, LANES)], out_ref.at[:, t]))
    return pairs


def run_copies(pairs, sems, beside=()):
    copies = [pltpu.make_async_copy(source, target, sems.at[i]) for i, (source, target) in enumerate(pairs)]
    for copy in copies:
        copy.start()
    for source, target in beside:
        target[...] = source[...]
    for copy in copies:
        copy.wait()


def load(fields, components):
    shape = (components,) + fields.shape[1:]

    def kernel(fields_ref, out_ref, sems):
        run_copies([(fields_ref.at[c], out_ref.at[c]) for c in range(components)], sems)

    return pl.pallas_call(
        kernel,
        in_specs=[pl.BlockSpec(memory_space=pltpu.HBM)],
        out_specs=vmem(),
        out_shape=jax.ShapeDtypeStruct(shape, fields.dtype),
        scratch_shapes=[pltpu.SemaphoreType.DMA((components,))],
        compiler_params=params(),
        cost_estimate=cost(),
    )(pltpu.with_memory_space_constraint(fields, pltpu.HBM))


def packed_shape(fields, first, last, held):
    return (last - first, held, fields.shape[1], 2, LANES)


def pack(fields, first, last, offset, begin, held):
    count = lax.axis_size("mode")
    shape = packed_shape(fields, first, last, held)

    def kernel(fields_ref, out_ref, sems):
        share = dest_of(lax.axis_index("mode"), offset, count)
        run_copies(pieces_of(fields_ref, first, share, begin, out_ref), sems)

    return pl.pallas_call(
        kernel,
        in_specs=[pl.BlockSpec(memory_space=pl.ANY)],
        out_specs=vmem(),
        out_shape=jax.ShapeDtypeStruct(shape, jnp.bfloat16),
        scratch_shapes=[pltpu.SemaphoreType.DMA((shape[1],))],
        compiler_params=params(),
        cost_estimate=cost(),
    )(fields)


def pack_rest(fields, parcels, carried):
    count = lax.axis_size("mode")
    shapes = [packed_shape(fields, first, last, held) for first, last, _, _, held in parcels]

    def kernel(fields_ref, *refs):
        inputs, refs = refs[: len(carried)], refs[len(carried) :]
        parcel_refs, outputs = refs[: len(parcels)], refs[len(parcels) : -1]
        me = lax.axis_index("mode")
        pairs = []
        for (first, _, offset, begin, _), parcel_ref in zip(parcels, parcel_refs):
            pairs += pieces_of(fields_ref, first, dest_of(me, offset, count), begin, parcel_ref)
        run_copies(pairs, refs[-1], zip(inputs, outputs))

    return pl.pallas_call(
        kernel,
        in_specs=[pl.BlockSpec(memory_space=pl.ANY)] + [vmem()] * len(carried),
        out_specs=[vmem()] * (len(parcels) + len(carried)),
        out_shape=[jax.ShapeDtypeStruct(shape, jnp.bfloat16) for shape in shapes]
        + [jax.ShapeDtypeStruct(value.shape, value.dtype) for value in carried],
        scratch_shapes=[pltpu.SemaphoreType.DMA((sum(shape[1] for shape in shapes),))],
        compiler_params=params(),
        cost_estimate=cost(),
    )(fields, *carried)


def cross(a, b):
    return [a[1] * b[2] - a[2] * b[1], a[2] * b[0] - a[0] * b[2], a[0] * b[1] - a[1] * b[0]]


def to_physical(order, in_refs, inverse, x_ref, store):
    me = lax.axis_index("mode")
    components, tiles, rows, _ = in_refs[0].shape
    for in_ref, offset in zip(in_refs, order):
        at = pl.multiple_of(source_of(me, offset, len(order)) * rows, rows)
        for c in range(components):
            for t in range(tiles):
                x_ref[c, pl.ds(at, rows), t * LANES : (t + 1) * LANES] = in_ref[c, t]
    for c in range(components):
        store(c, jnp.dot(inverse, x_ref[c], preferred_element_type=jnp.float32))


def to_modes(order, forward_ref, table_ref, product_ref, out_refs):
    count = len(order)
    me = lax.axis_index("mode")
    components, tiles, rows, _ = out_refs[0].shape
    for step, offset in enumerate(order):
        at = pl.multiple_of(dest_of(me, offset, count) * rows, rows)
        table_ref[step * rows : (step + 1) * rows] = forward_ref[pl.ds(at, rows)]
    for c in range(components):
        terms = jnp.dot(table_ref[...], product_ref[c], preferred_element_type=jnp.float32)
        terms = terms.astype(jnp.bfloat16)
        for step in range(count):
            for t in range(tiles):
                out_refs[step][c, t] = terms[step * rows : (step + 1) * rows, t * LANES : (t + 1) * LANES]


CHUNK = 32


def first_kernel(count, *refs):
    in_refs, (inverse_ref, forward_ref) = refs[:count], refs[count : count + 2]
    out_refs, (physical_ref, x_ref, product_ref, table_ref) = refs[count + 2 : 2 * count + 2], refs[2 * count + 2 :]

    def store(c, value):
        physical_ref[c] = value

    to_physical(offsets(count, FIRST_SEND), in_refs, inverse_ref[...], x_ref, store)
    for i in range(THETA // CHUNK):
        at = slice(i * CHUNK, (i + 1) * CHUNK)
        velocity = [physical_ref[c, at] for c in range(3)]
        magnetic = [physical_ref[c, at] for c in range(3, 6)]
        energy = 0.5 * (velocity[0] * velocity[0] + velocity[1] * velocity[1] + velocity[2] * velocity[2])
        for c, value in enumerate(cross(velocity, magnetic) + [energy]):
            product_ref[c, at] = value.astype(jnp.bfloat16)
    to_modes(offsets(count, FIRST_RETURN), forward_ref, table_ref, product_ref, out_refs)


def first_physics(received, inverse, forward):
    count = len(received)
    components, tiles, rows, _ = received[0].shape
    width = tiles * LANES
    return pl.pallas_call(
        functools.partial(first_kernel, count),
        in_specs=[vmem()] * (count + 2),
        out_specs=[vmem()] * (count + 1),
        out_shape=[jax.ShapeDtypeStruct((4, tiles, rows, LANES), jnp.bfloat16)] * count
        + [jax.ShapeDtypeStruct((components, THETA, width), jnp.float32)],
        scratch_shapes=[
            pltpu.VMEM((components, 2 * M, width), jnp.bfloat16),
            pltpu.VMEM((4, THETA, width), jnp.bfloat16),
            pltpu.VMEM((2 * M, THETA), jnp.bfloat16),
        ],
        compiler_params=params(),
        cost_estimate=cost(),
    )(*received, inverse, forward)


def second_kernel(count, groups, begin, *refs):
    in_refs, refs = refs[:count], refs[count:]
    first_refs, (inverse_ref, forward_ref) = refs[:groups], refs[groups : groups + 2]
    out_refs, (physical_ref, x_ref, product_ref, table_ref) = refs[groups + 2 : groups + 2 + count], refs[groups + 2 + count :]
    in_group = first_refs[0].shape[2] // LANES

    def store(c, value):
        physical_ref[c] = value

    to_physical(offsets(count, SECOND_SEND), in_refs, inverse_ref[...], x_ref, store)
    for t in range(in_refs[0].shape[1]):
        lanes = slice(t * LANES, (t + 1) * LANES)
        first_ref, place = first_refs[(begin + t) // in_group], (begin + t) % in_group
        first_lanes = slice(place * LANES, (place + 1) * LANES)
        for i in range(THETA // CHUNK):
            at = slice(i * CHUNK, (i + 1) * CHUNK)
            velocity = [first_ref[c, at, first_lanes] for c in range(3)]
            magnetic = [first_ref[c, at, first_lanes] for c in range(3, 6)]
            current = [physical_ref[c, at, lanes] for c in range(3)]
            vorticity = [physical_ref[c, at, lanes] for c in range(3, 6)]
            lorentz = [a + b for a, b in zip(cross(current, magnetic), cross(velocity, vorticity))]
            for c, value in enumerate(lorentz):
                product_ref[c, at, lanes] = value.astype(jnp.bfloat16)
    to_modes(offsets(count, SECOND_RETURN), forward_ref, table_ref, product_ref, out_refs)


def second_physics(received, physical, begin, inverse, forward):
    count, groups = len(received), len(physical)
    components, tiles, rows, _ = received[0].shape
    width = tiles * LANES
    return pl.pallas_call(
        functools.partial(second_kernel, count, groups, begin),
        in_specs=[vmem()] * (count + groups + 2),
        out_specs=[vmem()] * count,
        out_shape=[jax.ShapeDtypeStruct((3, tiles, rows, LANES), jnp.bfloat16)] * count,
        scratch_shapes=[
            pltpu.VMEM((components, THETA, width), jnp.float32),
            pltpu.VMEM((components, 2 * M, width), jnp.bfloat16),
            pltpu.VMEM((3, THETA, width), jnp.bfloat16),
            pltpu.VMEM((2 * M, THETA), jnp.bfloat16),
        ],
        compiler_params=params(),
        cost_estimate=cost(),
    )(*received, *physical, inverse, forward)


def tiles_of(in_refs, count):
    me = lax.axis_index("mode")
    components, held, rows, _ = in_refs[0].shape
    groups = len(in_refs) // count
    for group in range(groups):
        for step, offset in enumerate(offsets(count, FIRST_RETURN)):
            share = source_of(me, offset, count)
            for t in range(held):
                at = share * (groups * held) + group * held + t
                yield at, in_refs[group * count + step][:, t].reshape(components * rows, LANES)


def interface_kernel(count, arrived, *refs):
    in_refs, (nodes_ref, prev_ref, next_ref) = refs[:arrived], refs[arrived:]
    components, _, rows, _ = in_refs[0].shape
    halo = nodes_ref.shape[1]
    totals = [jnp.zeros((components * rows, halo), jnp.float32) for _ in range(2)]
    inner = lax.broadcasted_iota(jnp.int32, (LANES, halo), 0)
    for at, values in tiles_of(in_refs, count):
        ids = inner + at * LANES
        for way in range(2):
            chosen = jnp.where(ids == nodes_ref[way : way + 1, :], 1.0, 0.0).astype(jnp.bfloat16)
            totals[way] += jnp.dot(values, chosen, preferred_element_type=jnp.float32)
    for out_ref, total in zip((prev_ref, next_ref), totals):
        picked = total.astype(jnp.bfloat16)
        for c in range(components):
            for t in range(halo // LANES):
                out_ref[c, t] = picked[c * rows : (c + 1) * rows, t * LANES : (t + 1) * LANES]


def interface(received, interface_nodes, count):
    components, _, rows, _ = received[0].shape
    halo = interface_nodes.shape[1]
    shape = jax.ShapeDtypeStruct((components, halo // LANES, rows, LANES), jnp.bfloat16)
    return pl.pallas_call(
        functools.partial(interface_kernel, count, len(received)),
        in_specs=[vmem()] * (len(received) + 1),
        out_specs=[vmem()] * 2,
        out_shape=[shape] * 2,
        compiler_params=params(),
        cost_estimate=cost(),
    )(*received, interface_nodes)


SUBLANES = 8


def interleaved(parts):
    parts = list(parts)
    row = lax.broadcasted_iota(jnp.int32, parts[0].shape, 1)
    for distance in (1, 2, 4):
        upper = jnp.bitwise_and(row, distance) != 0
        for k in range(SUBLANES):
            if k & distance == 0:
                first, second = parts[k], parts[k + distance]
                parts[k] = jnp.where(upper, pltpu.roll(second, distance, 1), first)
                parts[k + distance] = jnp.where(upper, second, pltpu.roll(first, SUBLANES - distance, 1))
    return parts


def put_rows(out_ref, first, stride, tiles):
    modes = tiles[0].shape[0] // 2
    parts = [part for tile in tiles for part in (tile[:modes], tile[modes:])]
    if len(parts) == SUBLANES:
        whole = interleaved([part.reshape(modes // SUBLANES, SUBLANES, LANES) for part in parts])
        for mode in range(modes):
            here = pl.ds(pl.multiple_of(first + mode * stride, SUBLANES), SUBLANES)
            out_ref[here, :] = whole[mode % SUBLANES][mode // SUBLANES]
    else:
        for i, part in enumerate(parts):
            out_ref[pl.ds(first + i, modes, stride=stride), :] = part


def derive_kernel(count, arrived, *refs):
    in_refs = refs[:arrived]
    prev_ref, next_ref, radial_ref, axial_ref, radius_ref, columns_ref = refs[arrived : arrived + 6]
    induction_ref, momentum_ref, extended_ref = refs[arrived + 6 :]
    me = lax.axis_index("mode")
    components, held, rows, _ = in_refs[0].shape
    mode_count = rows // 2
    node_tiles = arrived * held
    halo_tiles = prev_ref.shape[1]

    def extend(at, tile):
        extended_ref[0, at] = tile
        extended_ref[1, at] = jnp.concatenate([tile[:, BLK:], tile[:, :BLK]], axis=1)

    for at, tile in tiles_of(in_refs, count):
        extend(at, tile)
    for t in range(halo_tiles):
        extend(node_tiles + t, prev_ref[:, t].reshape(components * rows, LANES))
        extend(node_tiles + halo_tiles + t, next_ref[:, t].reshape(components * rows, LANES))
    modes = (lax.broadcasted_iota(jnp.int32, (mode_count, LANES), 0) + me * mode_count).astype(jnp.float32)
    low = lax.broadcasted_iota(jnp.int32, (components * rows, LANES), 1) < BLK
    lane = lax.broadcasted_iota(jnp.int32, (1, 2 * LANES), 1)
    in_first = jnp.where(lax.rem(lane, LANES) < BLK, 1.0, 0.0)
    in_half = [in_first.astype(jnp.bfloat16), (1.0 - in_first).astype(jnp.bfloat16)]

    def rotated(values):
        return jnp.concatenate([-modes * values[mode_count:], modes * values[:mode_count]], axis=0)

    def tile_of(b):
        here = pl.ds(pl.multiple_of(b * LANES, LANES), LANES)
        left, right = [], []
        for k in range(NNZB):
            weights = jnp.concatenate([radial_ref[k, :, here], axial_ref[k, :, here]], axis=1)
            first, second = columns_ref[k, 2 * b], columns_ref[k, 2 * b + 1]
            first_tile = extended_ref[lax.rem(first, 2), lax.div(first, 2)]
            second_tile = extended_ref[1 - lax.rem(second, 2), lax.div(second, 2)]
            left.append(jnp.where(low, first_tile, second_tile))
            right += [weights * in_half[0], weights * in_half[1]]
        total = jnp.dot(
            jnp.concatenate(left, axis=1),
            jnp.concatenate(right, axis=0),
            preferred_element_type=jnp.float32,
        )
        along_r = [total[c * rows : (c + 1) * rows, :LANES] for c in range(components)]
        along_z = [total[c * rows : (c + 1) * rows, LANES:] for c in range(components)]
        values = [extended_ref[0, b, c * rows : (c + 1) * rows].astype(jnp.float32) for c in range(components)]
        inv_radius = 1.0 / radius_ref[:, here]
        momentum_ref[0, b] = along_r[3]
        momentum_ref[1, b] = rotated(values[3]) * inv_radius
        momentum_ref[2, b] = along_z[3]
        return [
            rotated(values[2]) * inv_radius - along_z[1],
            along_z[0] - along_r[2],
            along_r[1] + values[1] * inv_radius - rotated(values[0]) * inv_radius,
        ]

    stride = 2 * node_tiles
    together = SUBLANES // 2 if node_tiles % (SUBLANES // 2) == 0 else 1

    def tiles_at(q, carry):
        induction = [tile_of(q * together + i) for i in range(together)]
        for i in range(3):
            put_rows(induction_ref, i * mode_count * stride + 2 * q * together, stride, [tile[i] for tile in induction])
        return carry

    lax.fori_loop(0, node_tiles // together, tiles_at, 0)


def derive(received, from_prev, from_next, radial_blocks, axial_blocks, radius, columns, count):
    components, held, rows, _ = received[0].shape
    node_tiles = len(received) * held
    halo_tiles = from_prev.shape[1]
    out_rows = 3 * rows * node_tiles
    return pl.pallas_call(
        functools.partial(derive_kernel, count, len(received)),
        in_specs=[vmem()] * (len(received) + 5) + [pl.BlockSpec(memory_space=pltpu.SMEM)],
        out_specs=[vmem()] * 2,
        out_shape=[
            jax.ShapeDtypeStruct((out_rows, LANES), jnp.float32),
            jax.ShapeDtypeStruct((3, node_tiles, rows, LANES), jnp.float32),
        ],
        scratch_shapes=[pltpu.VMEM((2, node_tiles + 2 * halo_tiles, components * rows, LANES), jnp.bfloat16)],
        compiler_params=params(),
        cost_estimate=cost(),
    )(*received, from_prev, from_next, radial_blocks, axial_blocks, radius, columns)


def momentum_kernel(count, arrived, *refs):
    in_refs, (gradient_ref, out_ref, total_ref, sems) = refs[:arrived], refs[arrived:]
    me = lax.axis_index("mode")
    components, _, rows, _ = in_refs[0].shape
    tiles = gradient_ref.shape[1] // count
    holders = [(part, t) for part in range(arrived // count) for t in range(in_refs[part * count].shape[1])]
    mode_count = rows // 2
    stride = 2 * count * tiles
    out_rows = mode_count * stride
    copies = []
    for c in range(components):
        for step, offset in enumerate(offsets(count, SECOND_RETURN)):
            share = source_of(me, offset, count)
            for start in range(0, tiles, SUBLANES // 2):
                values = []
                for t in range(start, min(tiles, start + SUBLANES // 2)):
                    part, at = holders[t]
                    piece = in_refs[part * count + step][c, at].astype(jnp.float32)
                    values.append(piece - gradient_ref[c, share * tiles + t])
                put_rows(total_ref, c * out_rows + 2 * (share * tiles + start), stride, values)
        done = pl.ds(c * out_rows, out_rows)
        copies.append(pltpu.make_async_copy(total_ref.at[done], out_ref.at[done], sems.at[c]))
        copies[c].start()
    for copy in copies:
        copy.wait()


def momentum_of(received, gradient, count):
    components, _, rows, _ = received[0].shape
    shape = (components * rows * gradient.shape[1], LANES)
    return pl.pallas_call(
        functools.partial(momentum_kernel, count, len(received)),
        in_specs=[vmem()] * (len(received) + 1),
        out_specs=pl.BlockSpec(memory_space=pl.ANY),
        out_shape=jax.ShapeDtypeStruct(shape, jnp.float32),
        scratch_shapes=[pltpu.VMEM(shape, jnp.float32), pltpu.SemaphoreType.DMA((components,))],
        compiler_params=params(),
        cost_estimate=cost(),
    )(*received, gradient)


def whole_output(value, mode_count, width):
    value = value.reshape(3, mode_count, width // LANES, 2, LANES)
    return value.transpose(0, 1, 3, 2, 4).reshape(3, mode_count, 2, width)


def body(mode_fields, radius, radial_blocks, axial_blocks, block_columns, interface_nodes):
    _, mode_count, _, width = mode_fields.shape
    count = lax.axis_size("mode")
    rows = 2 * mode_count
    inverse, forward = tables(M, THETA, count)
    inverse, forward = jnp.asarray(inverse), jnp.asarray(forward)

    def joined(pieces):
        return [piece.reshape(piece.shape[:-3] + (rows, LANES)) for piece in pieces]

    tiles = width // count // LANES
    groups, spans = groups_of(tiles), spans_of(tiles)
    held = tiles // groups
    flow = load(mode_fields, 6)
    arrived = []
    for group in range(groups):
        order = offsets(count, FIRST_SEND)
        parcels = [pack(flow, 0, 6, offset, group * held, held) for offset in order[1:]]
        arrived.append(exchange(parcels, order[1:]))
    parcels = [(0, 6, 0, group * held, held) for group in range(groups)]
    *own, inverse, forward = pack_rest(flow, parcels, [inverse, forward])
    arrived[0][1:2], carried = lax.optimization_barrier((arrived[0][1:2], [inverse, forward]))
    order = offsets(count, SECOND_SEND)
    parcels = [(6, 12, offset) + span for span in spans for offset in order]
    *shares, later_inverse, later_forward = pack_rest(mode_fields, parcels, carried)
    local, physical = [], []
    for group in range(groups):
        if group == 0:
            tables_here = (later_inverse, later_forward)
        else:
            tables_here = (inverse, forward)
        *terms, velocity_magnetic = first_physics(joined([own[group]] + arrived[group]), *tables_here)
        local += exchange(terms, offsets(count, FIRST_RETURN))
        physical.append(velocity_magnetic)
    for group in range(groups):
        back, sent = slice(count if group == 0 else 0, None), slice(1, 2) if group == 0 else slice(2, count)
        local[back], shares[sent] = lax.optimization_barrier((local[back], shares[sent]))
    toward_prev, toward_next = interface(local, interface_nodes, count)
    halos = (from_behind(toward_next, "mer", 1), from_behind(toward_prev, "mer", -1))
    local, shares[count:] = lax.optimization_barrier((local, shares[count:]))
    lorentz = []
    for part, (begin, _) in enumerate(spans):
        sources = exchange(shares[part * count : (part + 1) * count], order)
        if part == len(spans) - 1:
            sources, halos = lax.optimization_barrier((sources, halos))
        terms = list(second_physics(joined(sources), physical, begin, later_inverse, later_forward))
        if part == len(spans) - 1:
            terms, radius = lax.optimization_barrier((terms, radius))
        lorentz += exchange(terms, offsets(count, SECOND_RETURN))
    induction, gradient = derive(
        local, *halos, radial_blocks, axial_blocks, radius.reshape(1, width), block_columns.T, count
    )
    momentum = momentum_of(lorentz, gradient, count)
    return (whole_output(induction, mode_count, width), whole_output(momentum, mode_count, width))


def solution(mesh):
    placed = (
        P(None, "mode", None, "mer"),
        P("mer"),
        P(None, None, "mer"),
        P(None, None, "mer"),
        P("mer", None),
        P("mer", None),
    )
    return jax.shard_map(
        body,
        mesh=mesh,
        in_specs=placed,
        out_specs=(P(None, "mode", None, "mer"), P(None, "mode", None, "mer")),
        check_vma=False,
    )
```

```python
import functools
import math

import jax
import jax.numpy as jnp
import ml_dtypes
import numpy as np
from jax import lax
from jax.experimental import pallas as pl
from jax.experimental.pallas import tpu as pltpu
from jax.sharding import PartitionSpec as P

M = 128
THETA = 256
BLK = 64
NNZB = 5
LANES = 128
VMEM_LIMIT = 24 * 1024 * 1024


def params(limit=VMEM_LIMIT):
    return pltpu.CompilerParams(vmem_limit_bytes=limit)


def vmem():
    return pl.BlockSpec(memory_space=pltpu.VMEM)


def cost():
    return pl.CostEstimate(flops=1024, bytes_accessed=1024, transcendentals=0)


FIRST_SEND, FIRST_RETURN, SECOND_SEND, SECOND_RETURN = 1, 1, 1, 1


def offsets(count, place):
    order = list(range(count - 1))
    order.insert(count - 1 if place is None else min(place, count - 1), count - 1)
    return order


def dest_of(me, offset, count):
    if count & (count - 1) == 0:
        return jnp.bitwise_xor(me, offset)
    return lax.rem(me + offset, count)


def source_of(me, offset, count):
    if count & (count - 1) == 0:
        return jnp.bitwise_xor(me, offset)
    return lax.rem(me + count - offset, count)


def exchange(pieces, order):
    count = lax.axis_size("mode")
    power = count & (count - 1) == 0
    received = []
    for piece, offset in zip(pieces, order):
        if offset == 0:
            received.append(piece)
            continue
        pairs = [(i, i ^ offset if power else (i + offset) % count) for i in range(count)]
        received.append(lax.ppermute(piece, "mode", pairs))
    return received


def from_behind(value, axis, steps):
    count = lax.axis_size(axis)
    initial, last = (max(0, -steps), min(count, count - steps))
    return lax.ppermute(value, axis, [(source, source + steps) for source in range(initial, last)])


def tables(mode_total, angle_total, share_count):
    mode_ids = np.arange(mode_total)
    angle_ids = np.arange(angle_total)
    phase = angle_ids[:, None] * mode_ids[None, :] % angle_total
    angle = phase.astype(np.float32) * np.float32(2.0 * math.pi / angle_total)
    weight = np.where(mode_ids == 0, 1.0, 2.0).astype(np.float32)
    cosines = np.cos(angle)
    sines = np.sin(angle)
    inverse = np.stack([weight * cosines, -weight * sines], axis=-1).astype(ml_dtypes.bfloat16)
    forward = np.stack([cosines.T, -sines.T], axis=1) / np.float32(angle_total)
    forward = forward.reshape(share_count, mode_total // share_count, 2, angle_total)
    forward = forward.transpose(0, 2, 1, 3).reshape(2 * mode_total, angle_total).astype(ml_dtypes.bfloat16)
    return (inverse.reshape(angle_total, 2 * mode_total), forward)


def groups_of(tiles):
    return 2 if tiles % 2 == 0 else 1


def spans_of(tiles):
    return [(0, tiles // 2), (tiles // 2, tiles - tiles // 2)] if tiles > 1 else [(0, tiles)]


def pieces_of(fields_ref, first, share, begin, out_ref):
    count = lax.axis_size("mode")
    tiles = fields_ref.shape[3] // count // LANES
    components, held = out_ref.shape[:2]
    pairs = []
    for t in range(held):
        start = pl.multiple_of((share * tiles + begin + t) * LANES, LANES)
        pairs.append((fields_ref.at[pl.ds(first, components), :, :, pl.ds(start, LANES)], out_ref.at[:, t]))
    return pairs


def run_copies(pairs, sems, beside=()):
    copies = [pltpu.make_async_copy(source, target, sems.at[i]) for i, (source, target) in enumerate(pairs)]
    for copy in copies:
        copy.start()
    for source, target in beside:
        target[...] = source[...]
    for copy in copies:
        copy.wait()


def load(fields, components):
    shape = (components,) + fields.shape[1:]

    def kernel(fields_ref, out_ref, sems):
        run_copies([(fields_ref.at[c], out_ref.at[c]) for c in range(components)], sems)

    return pl.pallas_call(
        kernel,
        in_specs=[pl.BlockSpec(memory_space=pltpu.HBM)],
        out_specs=vmem(),
        out_shape=jax.ShapeDtypeStruct(shape, fields.dtype),
        scratch_shapes=[pltpu.SemaphoreType.DMA((components,))],
        compiler_params=params(),
        cost_estimate=cost(),
    )(pltpu.with_memory_space_constraint(fields, pltpu.HBM))


def packed_shape(fields, first, last, held):
    return (last - first, held, fields.shape[1], 2, LANES)


def pack(fields, first, last, offset, begin, held):
    count = lax.axis_size("mode")
    shape = packed_shape(fields, first, last, held)

    def kernel(fields_ref, out_ref, sems):
        share = dest_of(lax.axis_index("mode"), offset, count)
        run_copies(pieces_of(fields_ref, first, share, begin, out_ref), sems)

    return pl.pallas_call(
        kernel,
        in_specs=[pl.BlockSpec(memory_space=pl.ANY)],
        out_specs=vmem(),
        out_shape=jax.ShapeDtypeStruct(shape, jnp.bfloat16),
        scratch_shapes=[pltpu.SemaphoreType.DMA((shape[1],))],
        compiler_params=params(),
        cost_estimate=cost(),
    )(fields)


def pack_rest(fields, parcels, carried):
    count = lax.axis_size("mode")
    shapes = [packed_shape(fields, first, last, held) for first, last, _, _, held in parcels]

    def kernel(fields_ref, *refs):
        inputs, refs = refs[: len(carried)], refs[len(carried) :]
        parcel_refs, outputs = refs[: len(parcels)], refs[len(parcels) : -1]
        me = lax.axis_index("mode")
        pairs = []
        for (first, _, offset, begin, _), parcel_ref in zip(parcels, parcel_refs):
            pairs += pieces_of(fields_ref, first, dest_of(me, offset, count), begin, parcel_ref)
        run_copies(pairs, refs[-1], zip(inputs, outputs))

    return pl.pallas_call(
        kernel,
        in_specs=[pl.BlockSpec(memory_space=pl.ANY)] + [vmem()] * len(carried),
        out_specs=[vmem()] * (len(parcels) + len(carried)),
        out_shape=[jax.ShapeDtypeStruct(shape, jnp.bfloat16) for shape in shapes]
        + [jax.ShapeDtypeStruct(value.shape, value.dtype) for value in carried],
        scratch_shapes=[pltpu.SemaphoreType.DMA((sum(shape[1] for shape in shapes),))],
        compiler_params=params(),
        cost_estimate=cost(),
    )(fields, *carried)


def cross(a, b):
    return [a[1] * b[2] - a[2] * b[1], a[2] * b[0] - a[0] * b[2], a[0] * b[1] - a[1] * b[0]]


def to_physical(order, in_refs, inverse, x_ref, store):
    me = lax.axis_index("mode")
    components, tiles, rows, _ = in_refs[0].shape
    for in_ref, offset in zip(in_refs, order):
        at = pl.multiple_of(source_of(me, offset, len(order)) * rows, rows)
        for c in range(components):
            for t in range(tiles):
                x_ref[c, pl.ds(at, rows), t * LANES : (t + 1) * LANES] = in_ref[c, t]
    for c in range(components):
        store(c, jnp.dot(inverse, x_ref[c], preferred_element_type=jnp.float32))


def to_modes(order, forward_ref, table_ref, product_ref, out_refs):
    count = len(order)
    me = lax.axis_index("mode")
    components, tiles, rows, _ = out_refs[0].shape
    for step, offset in enumerate(order):
        at = pl.multiple_of(dest_of(me, offset, count) * rows, rows)
        table_ref[step * rows : (step + 1) * rows] = forward_ref[pl.ds(at, rows)]
    for c in range(components):
        terms = jnp.dot(table_ref[...], product_ref[c], preferred_element_type=jnp.float32)
        terms = terms.astype(jnp.bfloat16)
        for step in range(count):
            for t in range(tiles):
                out_refs[step][c, t] = terms[step * rows : (step + 1) * rows, t * LANES : (t + 1) * LANES]


CHUNK = 32


def first_kernel(count, *refs):
    in_refs, (inverse_ref, forward_ref) = refs[:count], refs[count : count + 2]
    out_refs, (physical_ref, x_ref, product_ref, table_ref) = refs[count + 2 : 2 * count + 2], refs[2 * count + 2 :]

    def store(c, value):
        physical_ref[c] = value

    to_physical(offsets(count, FIRST_SEND), in_refs, inverse_ref[...], x_ref, store)
    for i in range(THETA // CHUNK):
        at = slice(i * CHUNK, (i + 1) * CHUNK)
        velocity = [physical_ref[c, at] for c in range(3)]
        magnetic = [physical_ref[c, at] for c in range(3, 6)]
        energy = 0.5 * (velocity[0] * velocity[0] + velocity[1] * velocity[1] + velocity[2] * velocity[2])
        for c, value in enumerate(cross(velocity, magnetic) + [energy]):
            product_ref[c, at] = value.astype(jnp.bfloat16)
    to_modes(offsets(count, FIRST_RETURN), forward_ref, table_ref, product_ref, out_refs)


def first_physics(received, inverse, forward):
    count = len(received)
    components, tiles, rows, _ = received[0].shape
    width = tiles * LANES
    return pl.pallas_call(
        functools.partial(first_kernel, count),
        in_specs=[vmem()] * (count + 2),
        out_specs=[vmem()] * (count + 1),
        out_shape=[jax.ShapeDtypeStruct((4, tiles, rows, LANES), jnp.bfloat16)] * count
        + [jax.ShapeDtypeStruct((components, THETA, width), jnp.float32)],
        scratch_shapes=[
            pltpu.VMEM((components, 2 * M, width), jnp.bfloat16),
            pltpu.VMEM((4, THETA, width), jnp.bfloat16),
            pltpu.VMEM((2 * M, THETA), jnp.bfloat16),
        ],
        compiler_params=params(),
        cost_estimate=cost(),
    )(*received, inverse, forward)


def second_kernel(count, groups, begin, *refs):
    in_refs, refs = refs[:count], refs[count:]
    first_refs, (inverse_ref, forward_ref) = refs[:groups], refs[groups : groups + 2]
    out_refs, (physical_ref, x_ref, product_ref, table_ref) = refs[groups + 2 : groups + 2 + count], refs[groups + 2 + count :]
    in_group = first_refs[0].shape[2] // LANES

    def store(c, value):
        physical_ref[c] = value

    to_physical(offsets(count, SECOND_SEND), in_refs, inverse_ref[...], x_ref, store)
    for t in range(in_refs[0].shape[1]):
        lanes = slice(t * LANES, (t + 1) * LANES)
        first_ref, place = first_refs[(begin + t) // in_group], (begin + t) % in_group
        first_lanes = slice(place * LANES, (place + 1) * LANES)
        for i in range(THETA // CHUNK):
            at = slice(i * CHUNK, (i + 1) * CHUNK)
            velocity = [first_ref[c, at, first_lanes] for c in range(3)]
            magnetic = [first_ref[c, at, first_lanes] for c in range(3, 6)]
            current = [physical_ref[c, at, lanes] for c in range(3)]
            vorticity = [physical_ref[c, at, lanes] for c in range(3, 6)]
            lorentz = [a + b for a, b in zip(cross(current, magnetic), cross(velocity, vorticity))]
            for c, value in enumerate(lorentz):
                product_ref[c, at, lanes] = value.astype(jnp.bfloat16)
    to_modes(offsets(count, SECOND_RETURN), forward_ref, table_ref, product_ref, out_refs)


def second_physics(received, physical, begin, inverse, forward):
    count, groups = len(received), len(physical)
    components, tiles, rows, _ = received[0].shape
    width = tiles * LANES
    return pl.pallas_call(
        functools.partial(second_kernel, count, groups, begin),
        in_specs=[vmem()] * (count + groups + 2),
        out_specs=[vmem()] * count,
        out_shape=[jax.ShapeDtypeStruct((3, tiles, rows, LANES), jnp.bfloat16)] * count,
        scratch_shapes=[
            pltpu.VMEM((components, THETA, width), jnp.float32),
            pltpu.VMEM((components, 2 * M, width), jnp.bfloat16),
            pltpu.VMEM((3, THETA, width), jnp.bfloat16),
            pltpu.VMEM((2 * M, THETA), jnp.bfloat16),
        ],
        compiler_params=params(),
        cost_estimate=cost(),
    )(*received, *physical, inverse, forward)


def tiles_of(in_refs, count):
    me = lax.axis_index("mode")
    components, held, rows, _ = in_refs[0].shape
    groups = len(in_refs) // count
    for group in range(groups):
        for step, offset in enumerate(offsets(count, FIRST_RETURN)):
            share = source_of(me, offset, count)
            for t in range(held):
                at = share * (groups * held) + group * held + t
                yield at, in_refs[group * count + step][:, t].reshape(components * rows, LANES)


def interface_kernel(count, arrived, *refs):
    in_refs, (nodes_ref, prev_ref, next_ref) = refs[:arrived], refs[arrived:]
    components, _, rows, _ = in_refs[0].shape
    halo = nodes_ref.shape[1]
    totals = [jnp.zeros((components * rows, halo), jnp.float32) for _ in range(2)]
    inner = lax.broadcasted_iota(jnp.int32, (LANES, halo), 0)
    for at, values in tiles_of(in_refs, count):
        ids = inner + at * LANES
        for way in range(2):
            chosen = jnp.where(ids == nodes_ref[way : way + 1, :], 1.0, 0.0).astype(jnp.bfloat16)
            totals[way] += jnp.dot(values, chosen, preferred_element_type=jnp.float32)
    for out_ref, total in zip((prev_ref, next_ref), totals):
        picked = total.astype(jnp.bfloat16)
        for c in range(components):
            for t in range(halo // LANES):
                out_ref[c, t] = picked[c * rows : (c + 1) * rows, t * LANES : (t + 1) * LANES]


def interface(received, interface_nodes, count):
    components, _, rows, _ = received[0].shape
    halo = interface_nodes.shape[1]
    shape = jax.ShapeDtypeStruct((components, halo // LANES, rows, LANES), jnp.bfloat16)
    return pl.pallas_call(
        functools.partial(interface_kernel, count, len(received)),
        in_specs=[vmem()] * (len(received) + 1),
        out_specs=[vmem()] * 2,
        out_shape=[shape] * 2,
        compiler_params=params(),
        cost_estimate=cost(),
    )(*received, interface_nodes)


SUBLANES = 8


def interleaved(parts):
    parts = list(parts)
    row = lax.broadcasted_iota(jnp.int32, parts[0].shape, 1)
    for distance in (1, 2, 4):
        upper = jnp.bitwise_and(row, distance) != 0
        for k in range(SUBLANES):
            if k & distance == 0:
                first, second = parts[k], parts[k + distance]
                parts[k] = jnp.where(upper, pltpu.roll(second, distance, 1), first)
                parts[k + distance] = jnp.where(upper, second, pltpu.roll(first, SUBLANES - distance, 1))
    return parts


def put_rows(out_ref, first, stride, tiles):
    modes = tiles[0].shape[0] // 2
    parts = [part for tile in tiles for part in (tile[:modes], tile[modes:])]
    if len(parts) == SUBLANES:
        whole = interleaved([part.reshape(modes // SUBLANES, SUBLANES, LANES) for part in parts])
        for mode in range(modes):
            here = pl.ds(pl.multiple_of(first + mode * stride, SUBLANES), SUBLANES)
            out_ref[here, :] = whole[mode % SUBLANES][mode // SUBLANES]
    else:
        for i, part in enumerate(parts):
            out_ref[pl.ds(first + i, modes, stride=stride), :] = part


def derive_kernel(count, arrived, *refs):
    in_refs = refs[:arrived]
    prev_ref, next_ref, radial_ref, axial_ref, radius_ref, columns_ref = refs[arrived : arrived + 6]
    induction_ref, momentum_ref, extended_ref = refs[arrived + 6 :]
    me = lax.axis_index("mode")
    components, held, rows, _ = in_refs[0].shape
    mode_count = rows // 2
    node_tiles = arrived * held
    halo_tiles = prev_ref.shape[1]

    def extend(at, tile):
        extended_ref[0, at] = tile
        extended_ref[1, at] = jnp.concatenate([tile[:, BLK:], tile[:, :BLK]], axis=1)

    for at, tile in tiles_of(in_refs, count):
        extend(at, tile)
    for t in range(halo_tiles):
        extend(node_tiles + t, prev_ref[:, t].reshape(components * rows, LANES))
        extend(node_tiles + halo_tiles + t, next_ref[:, t].reshape(components * rows, LANES))
    modes = (lax.broadcasted_iota(jnp.int32, (mode_count, LANES), 0) + me * mode_count).astype(jnp.float32)
    low = lax.broadcasted_iota(jnp.int32, (components * rows, LANES), 1) < BLK
    lane = lax.broadcasted_iota(jnp.int32, (1, 2 * LANES), 1)
    in_first = jnp.where(lax.rem(lane, LANES) < BLK, 1.0, 0.0)
    in_half = [in_first.astype(jnp.bfloat16), (1.0 - in_first).astype(jnp.bfloat16)]

    def rotated(values):
        return jnp.concatenate([-modes * values[mode_count:], modes * values[:mode_count]], axis=0)

    def tile_of(b):
        here = pl.ds(pl.multiple_of(b * LANES, LANES), LANES)
        left, right = [], []
        for k in range(NNZB):
            weights = jnp.concatenate([radial_ref[k, :, here], axial_ref[k, :, here]], axis=1)
            first, second = columns_ref[k, 2 * b], columns_ref[k, 2 * b + 1]
            first_tile = extended_ref[lax.rem(first, 2), lax.div(first, 2)]
            second_tile = extended_ref[1 - lax.rem(second, 2), lax.div(second, 2)]
            left.append(jnp.where(low, first_tile, second_tile))
            right += [weights * in_half[0], weights * in_half[1]]
        total = jnp.dot(
            jnp.concatenate(left, axis=1),
            jnp.concatenate(right, axis=0),
            preferred_element_type=jnp.float32,
        )
        along_r = [total[c * rows : (c + 1) * rows, :LANES] for c in range(components)]
        along_z = [total[c * rows : (c + 1) * rows, LANES:] for c in range(components)]
        values = [extended_ref[0, b, c * rows : (c + 1) * rows].astype(jnp.float32) for c in range(components)]
        inv_radius = 1.0 / radius_ref[:, here]
        momentum_ref[0, b] = along_r[3]
        momentum_ref[1, b] = rotated(values[3]) * inv_radius
        momentum_ref[2, b] = along_z[3]
        return [
            rotated(values[2]) * inv_radius - along_z[1],
            along_z[0] - along_r[2],
            along_r[1] + values[1] * inv_radius - rotated(values[0]) * inv_radius,
        ]

    stride = 2 * node_tiles
    together = SUBLANES // 2 if node_tiles % (SUBLANES // 2) == 0 else 1

    def tiles_at(q, carry):
        induction = [tile_of(q * together + i) for i in range(together)]
        for i in range(3):
            put_rows(induction_ref, i * mode_count * stride + 2 * q * together, stride, [tile[i] for tile in induction])
        return carry

    lax.fori_loop(0, node_tiles // together, tiles_at, 0)


def derive(received, from_prev, from_next, radial_blocks, axial_blocks, radius, columns, count):
    components, held, rows, _ = received[0].shape
    node_tiles = len(received) * held
    halo_tiles = from_prev.shape[1]
    out_rows = 3 * rows * node_tiles
    return pl.pallas_call(
        functools.partial(derive_kernel, count, len(received)),
        in_specs=[vmem()] * (len(received) + 5) + [pl.BlockSpec(memory_space=pltpu.SMEM)],
        out_specs=[vmem()] * 2,
        out_shape=[
            jax.ShapeDtypeStruct((out_rows, LANES), jnp.float32),
            jax.ShapeDtypeStruct((3, node_tiles, rows, LANES), jnp.float32),
        ],
        scratch_shapes=[pltpu.VMEM((2, node_tiles + 2 * halo_tiles, components * rows, LANES), jnp.bfloat16)],
        compiler_params=params(),
        cost_estimate=cost(),
    )(*received, from_prev, from_next, radial_blocks, axial_blocks, radius, columns)


def momentum_kernel(count, arrived, *refs):
    in_refs, (gradient_ref, out_ref, total_ref, sems) = refs[:arrived], refs[arrived:]
    me = lax.axis_index("mode")
    components, _, rows, _ = in_refs[0].shape
    tiles = gradient_ref.shape[1] // count
    holders = [(part, t) for part in range(arrived // count) for t in range(in_refs[part * count].shape[1])]
    mode_count = rows // 2
    stride = 2 * count * tiles
    out_rows = mode_count * stride
    copies = []
    for c in range(components):
        for step, offset in enumerate(offsets(count, SECOND_RETURN)):
            share = source_of(me, offset, count)
            for start in range(0, tiles, SUBLANES // 2):
                values = []
                for t in range(start, min(tiles, start + SUBLANES // 2)):
                    part, at = holders[t]
                    piece = in_refs[part * count + step][c, at].astype(jnp.float32)
                    values.append(piece - gradient_ref[c, share * tiles + t])
                put_rows(total_ref, c * out_rows + 2 * (share * tiles + start), stride, values)
        done = pl.ds(c * out_rows, out_rows)
        copies.append(pltpu.make_async_copy(total_ref.at[done], out_ref.at[done], sems.at[c]))
        copies[c].start()
    for copy in copies:
        copy.wait()


def momentum_of(received, gradient, count):
    components, _, rows, _ = received[0].shape
    shape = (components * rows * gradient.shape[1], LANES)
    return pl.pallas_call(
        functools.partial(momentum_kernel, count, len(received)),
        in_specs=[vmem()] * (len(received) + 1),
        out_specs=pl.BlockSpec(memory_space=pl.ANY),
        out_shape=jax.ShapeDtypeStruct(shape, jnp.float32),
        scratch_shapes=[pltpu.VMEM(shape, jnp.float32), pltpu.SemaphoreType.DMA((components,))],
        compiler_params=params(),
        cost_estimate=cost(),
    )(*received, gradient)


def whole_output(value, mode_count, width):
    value = value.reshape(3, mode_count, width // LANES, 2, LANES)
    return value.transpose(0, 1, 3, 2, 4).reshape(3, mode_count, 2, width)


def body(mode_fields, radius, radial_blocks, axial_blocks, block_columns, interface_nodes):
    _, mode_count, _, width = mode_fields.shape
    count = lax.axis_size("mode")
    rows = 2 * mode_count
    inverse, forward = tables(M, THETA, count)
    inverse, forward = jnp.asarray(inverse), jnp.asarray(forward)

    def joined(pieces):
        return [piece.reshape(piece.shape[:-3] + (rows, LANES)) for piece in pieces]

    tiles = width // count // LANES
    groups, spans = groups_of(tiles), spans_of(tiles)
    held = tiles // groups
    flow = load(mode_fields, 6)
    arrived = []
    for group in range(groups):
        order = offsets(count, FIRST_SEND)
        parcels = [pack(flow, 0, 6, offset, group * held, held) for offset in order[1:]]
        arrived.append(exchange(parcels, order[1:]))
    parcels = [(0, 6, 0, group * held, held) for group in range(groups)]
    *own, inverse, forward = pack_rest(flow, parcels, [inverse, forward])
    arrived[0][1:2], carried = lax.optimization_barrier((arrived[0][1:2], [inverse, forward]))
    order = offsets(count, SECOND_SEND)
    parcels = [(6, 12, offset) + span for span in spans for offset in order]
    *shares, later_inverse, later_forward = pack_rest(mode_fields, parcels, carried)
    local, physical = [], []
    for group in range(groups):
        if group == 0:
            tables_here = (later_inverse, later_forward)
        else:
            tables_here = (inverse, forward)
        *terms, velocity_magnetic = first_physics(joined([own[group]] + arrived[group]), *tables_here)
        local += exchange(terms, offsets(count, FIRST_RETURN))
        physical.append(velocity_magnetic)
    for group in range(groups):
        back, sent = slice(count if group == 0 else 0, None), slice(1, 2) if group == 0 else slice(2, count)
        local[back], shares[sent] = lax.optimization_barrier((local[back], shares[sent]))
    toward_prev, toward_next = interface(local, interface_nodes, count)
    halos = (from_behind(toward_next, "mer", 1), from_behind(toward_prev, "mer", -1))
    local, shares[count:] = lax.optimization_barrier((local, shares[count:]))
    induction, gradient = derive(
        local, *halos, radial_blocks, axial_blocks, radius.reshape(1, width), block_columns.T, count
    )
    lorentz = []
    for part, (begin, _) in enumerate(spans):
        sources = exchange(shares[part * count : (part + 1) * count], order)
        if part == len(spans) - 1:
            sources, gradient = lax.optimization_barrier((sources, gradient))
        terms = list(second_physics(joined(sources), physical, begin, later_inverse, later_forward))
        lorentz += exchange(terms, offsets(count, SECOND_RETURN))
    momentum = momentum_of(lorentz, gradient, count)
    return (whole_output(induction, mode_count, width), whole_output(momentum, mode_count, width))


def solution(mesh):
    placed = (
        P(None, "mode", None, "mer"),
        P("mer"),
        P(None, None, "mer"),
        P(None, None, "mer"),
        P("mer", None),
        P("mer", None),
    )
    return jax.shard_map(
        body,
        mesh=mesh,
        in_specs=placed,
        out_specs=(P(None, "mode", None, "mer"), P(None, "mode", None, "mer")),
        check_vma=False,
    )
```

```python
import functools
import math

import jax
import jax.numpy as jnp
import ml_dtypes
import numpy as np
from jax import lax
from jax.experimental import pallas as pl
from jax.experimental.pallas import tpu as pltpu
from jax.sharding import PartitionSpec as P

M = 128
THETA = 256
BLK = 64
NNZB = 5
LANES = 128
VMEM_LIMIT = 24 * 1024 * 1024


def params(limit=VMEM_LIMIT):
    return pltpu.CompilerParams(vmem_limit_bytes=limit)


def vmem():
    return pl.BlockSpec(memory_space=pltpu.VMEM)


def cost():
    return pl.CostEstimate(flops=1024, bytes_accessed=1024, transcendentals=0)


FIRST_SEND, FIRST_RETURN, SECOND_SEND, SECOND_RETURN = 1, 1, 1, 1


def offsets(count, place):
    order = list(range(count - 1))
    order.insert(count - 1 if place is None else min(place, count - 1), count - 1)
    return order


def dest_of(me, offset, count):
    if count & (count - 1) == 0:
        return jnp.bitwise_xor(me, offset)
    return lax.rem(me + offset, count)


def source_of(me, offset, count):
    if count & (count - 1) == 0:
        return jnp.bitwise_xor(me, offset)
    return lax.rem(me + count - offset, count)


def exchange(pieces, order):
    count = lax.axis_size("mode")
    power = count & (count - 1) == 0
    received = []
    for piece, offset in zip(pieces, order):
        if offset == 0:
            received.append(piece)
            continue
        pairs = [(i, i ^ offset if power else (i + offset) % count) for i in range(count)]
        received.append(lax.ppermute(piece, "mode", pairs))
    return received


def from_behind(value, axis, steps):
    count = lax.axis_size(axis)
    initial, last = (max(0, -steps), min(count, count - steps))
    return lax.ppermute(value, axis, [(source, source + steps) for source in range(initial, last)])


def tables(mode_total, angle_total, share_count):
    mode_ids = np.arange(mode_total)
    angle_ids = np.arange(angle_total)
    phase = angle_ids[:, None] * mode_ids[None, :] % angle_total
    angle = phase.astype(np.float32) * np.float32(2.0 * math.pi / angle_total)
    weight = np.where(mode_ids == 0, 1.0, 2.0).astype(np.float32)
    cosines = np.cos(angle)
    sines = np.sin(angle)
    inverse = np.stack([weight * cosines, -weight * sines], axis=-1).astype(ml_dtypes.bfloat16)
    forward = np.stack([cosines.T, -sines.T], axis=1) / np.float32(angle_total)
    forward = forward.reshape(share_count, mode_total // share_count, 2, angle_total)
    forward = forward.transpose(0, 2, 1, 3).reshape(2 * mode_total, angle_total).astype(ml_dtypes.bfloat16)
    return (inverse.reshape(angle_total, 2 * mode_total), forward)


def groups_of(tiles):
    return 2 if tiles % 2 == 0 else 1


def spans_of(tiles):
    return [(0, tiles // 2), (tiles // 2, tiles - tiles // 2)] if tiles > 1 else [(0, tiles)]


def pieces_of(fields_ref, first, share, begin, out_ref):
    count = lax.axis_size("mode")
    tiles = fields_ref.shape[3] // count // LANES
    components, held = out_ref.shape[:2]
    pairs = []
    for t in range(held):
        start = pl.multiple_of((share * tiles + begin + t) * LANES, LANES)
        pairs.append((fields_ref.at[pl.ds(first, components), :, :, pl.ds(start, LANES)], out_ref.at[:, t]))
    return pairs


def run_copies(pairs, sems, beside=()):
    copies = [pltpu.make_async_copy(source, target, sems.at[i]) for i, (source, target) in enumerate(pairs)]
    for copy in copies:
        copy.start()
    for source, target in beside:
        target[...] = source[...]
    for copy in copies:
        copy.wait()


def load(fields, components):
    shape = (components,) + fields.shape[1:]

    def kernel(fields_ref, out_ref, sems):
        run_copies([(fields_ref.at[c], out_ref.at[c]) for c in range(components)], sems)

    return pl.pallas_call(
        kernel,
        in_specs=[pl.BlockSpec(memory_space=pltpu.HBM)],
        out_specs=vmem(),
        out_shape=jax.ShapeDtypeStruct(shape, fields.dtype),
        scratch_shapes=[pltpu.SemaphoreType.DMA((components,))],
        compiler_params=params(),
        cost_estimate=cost(),
    )(pltpu.with_memory_space_constraint(fields, pltpu.HBM))


def packed_shape(fields, first, last, held):
    return (last - first, held, fields.shape[1], 2, LANES)


def pack(fields, first, last, offset, begin, held):
    count = lax.axis_size("mode")
    shape = packed_shape(fields, first, last, held)

    def kernel(fields_ref, out_ref, sems):
        share = dest_of(lax.axis_index("mode"), offset, count)
        run_copies(pieces_of(fields_ref, first, share, begin, out_ref), sems)

    return pl.pallas_call(
        kernel,
        in_specs=[pl.BlockSpec(memory_space=pl.ANY)],
        out_specs=vmem(),
        out_shape=jax.ShapeDtypeStruct(shape, jnp.bfloat16),
        scratch_shapes=[pltpu.SemaphoreType.DMA((shape[1],))],
        compiler_params=params(),
        cost_estimate=cost(),
    )(fields)


def pack_rest(fields, parcels, carried):
    count = lax.axis_size("mode")
    shapes = [packed_shape(fields, first, last, held) for first, last, _, _, held in parcels]

    def kernel(fields_ref, *refs):
        inputs, refs = refs[: len(carried)], refs[len(carried) :]
        parcel_refs, outputs = refs[: len(parcels)], refs[len(parcels) : -1]
        me = lax.axis_index("mode")
        pairs = []
        for (first, _, offset, begin, _), parcel_ref in zip(parcels, parcel_refs):
            pairs += pieces_of(fields_ref, first, dest_of(me, offset, count), begin, parcel_ref)
        run_copies(pairs, refs[-1], zip(inputs, outputs))

    return pl.pallas_call(
        kernel,
        in_specs=[pl.BlockSpec(memory_space=pl.ANY)] + [vmem()] * len(carried),
        out_specs=[vmem()] * (len(parcels) + len(carried)),
        out_shape=[jax.ShapeDtypeStruct(shape, jnp.bfloat16) for shape in shapes]
        + [jax.ShapeDtypeStruct(value.shape, value.dtype) for value in carried],
        scratch_shapes=[pltpu.SemaphoreType.DMA((sum(shape[1] for shape in shapes),))],
        compiler_params=params(),
        cost_estimate=cost(),
    )(fields, *carried)


def cross(a, b):
    return [a[1] * b[2] - a[2] * b[1], a[2] * b[0] - a[0] * b[2], a[0] * b[1] - a[1] * b[0]]


def to_physical(order, in_refs, inverse, x_ref, store):
    me = lax.axis_index("mode")
    components, tiles, rows, _ = in_refs[0].shape
    for in_ref, offset in zip(in_refs, order):
        at = pl.multiple_of(source_of(me, offset, len(order)) * rows, rows)
        for c in range(components):
            for t in range(tiles):
                x_ref[c, pl.ds(at, rows), t * LANES : (t + 1) * LANES] = in_ref[c, t]
    for c in range(components):
        store(c, jnp.dot(inverse, x_ref[c], preferred_element_type=jnp.float32))


def to_modes(order, forward_ref, table_ref, product_ref, out_refs):
    count = len(order)
    me = lax.axis_index("mode")
    components, tiles, rows, _ = out_refs[0].shape
    for step, offset in enumerate(order):
        at = pl.multiple_of(dest_of(me, offset, count) * rows, rows)
        table_ref[step * rows : (step + 1) * rows] = forward_ref[pl.ds(at, rows)]
    for c in range(components):
        terms = jnp.dot(table_ref[...], product_ref[c], preferred_element_type=jnp.float32)
        terms = terms.astype(jnp.bfloat16)
        for step in range(count):
            for t in range(tiles):
                out_refs[step][c, t] = terms[step * rows : (step + 1) * rows, t * LANES : (t + 1) * LANES]


CHUNK = 32


def first_kernel(count, *refs):
    in_refs, (inverse_ref, forward_ref) = refs[:count], refs[count : count + 2]
    out_refs, (physical_ref, x_ref, product_ref, table_ref) = refs[count + 2 : 2 * count + 2], refs[2 * count + 2 :]

    def store(c, value):
        physical_ref[c] = value

    to_physical(offsets(count, FIRST_SEND), in_refs, inverse_ref[...], x_ref, store)
    for i in range(THETA // CHUNK):
        at = slice(i * CHUNK, (i + 1) * CHUNK)
        velocity = [physical_ref[c, at] for c in range(3)]
        magnetic = [physical_ref[c, at] for c in range(3, 6)]
        energy = 0.5 * (velocity[0] * velocity[0] + velocity[1] * velocity[1] + velocity[2] * velocity[2])
        for c, value in enumerate(cross(velocity, magnetic) + [energy]):
            product_ref[c, at] = value.astype(jnp.bfloat16)
    to_modes(offsets(count, FIRST_RETURN), forward_ref, table_ref, product_ref, out_refs)


def first_physics(received, inverse, forward):
    count = len(received)
    components, tiles, rows, _ = received[0].shape
    width = tiles * LANES
    return pl.pallas_call(
        functools.partial(first_kernel, count),
        in_specs=[vmem()] * (count + 2),
        out_specs=[vmem()] * (count + 1),
        out_shape=[jax.ShapeDtypeStruct((4, tiles, rows, LANES), jnp.bfloat16)] * count
        + [jax.ShapeDtypeStruct((components, THETA, width), jnp.float32)],
        scratch_shapes=[
            pltpu.VMEM((components, 2 * M, width), jnp.bfloat16),
            pltpu.VMEM((4, THETA, width), jnp.bfloat16),
            pltpu.VMEM((2 * M, THETA), jnp.bfloat16),
        ],
        compiler_params=params(),
        cost_estimate=cost(),
    )(*received, inverse, forward)


def second_kernel(count, groups, begin, *refs):
    in_refs, refs = refs[:count], refs[count:]
    first_refs, (inverse_ref, forward_ref) = refs[:groups], refs[groups : groups + 2]
    out_refs, (physical_ref, x_ref, product_ref, table_ref) = refs[groups + 2 : groups + 2 + count], refs[groups + 2 + count :]
    in_group = first_refs[0].shape[2] // LANES

    def store(c, value):
        physical_ref[c] = value

    to_physical(offsets(count, SECOND_SEND), in_refs, inverse_ref[...], x_ref, store)
    for t in range(in_refs[0].shape[1]):
        lanes = slice(t * LANES, (t + 1) * LANES)
        first_ref, place = first_refs[(begin + t) // in_group], (begin + t) % in_group
        first_lanes = slice(place * LANES, (place + 1) * LANES)
        for i in range(THETA // CHUNK):
            at = slice(i * CHUNK, (i + 1) * CHUNK)
            velocity = [first_ref[c, at, first_lanes] for c in range(3)]
            magnetic = [first_ref[c, at, first_lanes] for c in range(3, 6)]
            current = [physical_ref[c, at, lanes] for c in range(3)]
            vorticity = [physical_ref[c, at, lanes] for c in range(3, 6)]
            lorentz = [a + b for a, b in zip(cross(current, magnetic), cross(velocity, vorticity))]
            for c, value in enumerate(lorentz):
                product_ref[c, at, lanes] = value.astype(jnp.bfloat16)
    to_modes(offsets(count, SECOND_RETURN), forward_ref, table_ref, product_ref, out_refs)


def second_physics(received, physical, begin, inverse, forward):
    count, groups = len(received), len(physical)
    components, tiles, rows, _ = received[0].shape
    width = tiles * LANES
    return pl.pallas_call(
        functools.partial(second_kernel, count, groups, begin),
        in_specs=[vmem()] * (count + groups + 2),
        out_specs=[vmem()] * count,
        out_shape=[jax.ShapeDtypeStruct((3, tiles, rows, LANES), jnp.bfloat16)] * count,
        scratch_shapes=[
            pltpu.VMEM((components, THETA, width), jnp.float32),
            pltpu.VMEM((components, 2 * M, width), jnp.bfloat16),
            pltpu.VMEM((3, THETA, width), jnp.bfloat16),
            pltpu.VMEM((2 * M, THETA), jnp.bfloat16),
        ],
        compiler_params=params(),
        cost_estimate=cost(),
    )(*received, *physical, inverse, forward)


def tiles_of(in_refs, count):
    me = lax.axis_index("mode")
    components, held, rows, _ = in_refs[0].shape
    groups = len(in_refs) // count
    for group in range(groups):
        for step, offset in enumerate(offsets(count, FIRST_RETURN)):
            share = source_of(me, offset, count)
            for t in range(held):
                at = share * (groups * held) + group * held + t
                yield at, in_refs[group * count + step][:, t].reshape(components * rows, LANES)


def interface_kernel(count, arrived, *refs):
    in_refs, (nodes_ref, prev_ref, next_ref) = refs[:arrived], refs[arrived:]
    components, _, rows, _ = in_refs[0].shape
    halo = nodes_ref.shape[1]
    totals = [jnp.zeros((components * rows, halo), jnp.float32) for _ in range(2)]
    inner = lax.broadcasted_iota(jnp.int32, (LANES, halo), 0)
    for at, values in tiles_of(in_refs, count):
        ids = inner + at * LANES
        for way in range(2):
            chosen = jnp.where(ids == nodes_ref[way : way + 1, :], 1.0, 0.0).astype(jnp.bfloat16)
            totals[way] += jnp.dot(values, chosen, preferred_element_type=jnp.float32)
    for out_ref, total in zip((prev_ref, next_ref), totals):
        picked = total.astype(jnp.bfloat16)
        for c in range(components):
            for t in range(halo // LANES):
                out_ref[c, t] = picked[c * rows : (c + 1) * rows, t * LANES : (t + 1) * LANES]


def interface(received, interface_nodes, count):
    components, _, rows, _ = received[0].shape
    halo = interface_nodes.shape[1]
    shape = jax.ShapeDtypeStruct((components, halo // LANES, rows, LANES), jnp.bfloat16)
    return pl.pallas_call(
        functools.partial(interface_kernel, count, len(received)),
        in_specs=[vmem()] * (len(received) + 1),
        out_specs=[vmem()] * 2,
        out_shape=[shape] * 2,
        compiler_params=params(),
        cost_estimate=cost(),
    )(*received, interface_nodes)


SUBLANES = 8


def interleaved(parts):
    parts = list(parts)
    row = lax.broadcasted_iota(jnp.int32, parts[0].shape, 1)
    for distance in (1, 2, 4):
        upper = jnp.bitwise_and(row, distance) != 0
        for k in range(SUBLANES):
            if k & distance == 0:
                first, second = parts[k], parts[k + distance]
                parts[k] = jnp.where(upper, pltpu.roll(second, distance, 1), first)
                parts[k + distance] = jnp.where(upper, second, pltpu.roll(first, SUBLANES - distance, 1))
    return parts


def put_rows(out_ref, first, stride, tiles):
    modes = tiles[0].shape[0] // 2
    parts = [part for tile in tiles for part in (tile[:modes], tile[modes:])]
    if len(parts) == SUBLANES:
        whole = interleaved([part.reshape(modes // SUBLANES, SUBLANES, LANES) for part in parts])
        for mode in range(modes):
            here = pl.ds(pl.multiple_of(first + mode * stride, SUBLANES), SUBLANES)
            out_ref[here, :] = whole[mode % SUBLANES][mode // SUBLANES]
    else:
        for i, part in enumerate(parts):
            out_ref[pl.ds(first + i, modes, stride=stride), :] = part


def derive_kernel(count, arrived, *refs):
    in_refs = refs[:arrived]
    prev_ref, next_ref, radial_ref, axial_ref, radius_ref, columns_ref = refs[arrived : arrived + 6]
    induction_ref, momentum_ref, extended_ref = refs[arrived + 6 :]
    me = lax.axis_index("mode")
    components, held, rows, _ = in_refs[0].shape
    mode_count = rows // 2
    node_tiles = arrived * held
    halo_tiles = prev_ref.shape[1]

    def extend(at, tile):
        extended_ref[0, at] = tile
        extended_ref[1, at] = jnp.concatenate([tile[:, BLK:], tile[:, :BLK]], axis=1)

    for at, tile in tiles_of(in_refs, count):
        extend(at, tile)
    for t in range(halo_tiles):
        extend(node_tiles + t, prev_ref[:, t].reshape(components * rows, LANES))
        extend(node_tiles + halo_tiles + t, next_ref[:, t].reshape(components * rows, LANES))
    modes = (lax.broadcasted_iota(jnp.int32, (mode_count, LANES), 0) + me * mode_count).astype(jnp.float32)
    low = lax.broadcasted_iota(jnp.int32, (components * rows, LANES), 1) < BLK
    lane = lax.broadcasted_iota(jnp.int32, (1, 2 * LANES), 1)
    in_first = jnp.where(lax.rem(lane, LANES) < BLK, 1.0, 0.0)
    in_half = [in_first.astype(jnp.bfloat16), (1.0 - in_first).astype(jnp.bfloat16)]

    def rotated(values):
        return jnp.concatenate([-modes * values[mode_count:], modes * values[:mode_count]], axis=0)

    def tile_of(b):
        here = pl.ds(pl.multiple_of(b * LANES, LANES), LANES)
        left, right = [], []
        for k in range(NNZB):
            weights = jnp.concatenate([radial_ref[k, :, here], axial_ref[k, :, here]], axis=1)
            first, second = columns_ref[k, 2 * b], columns_ref[k, 2 * b + 1]
            first_tile = extended_ref[lax.rem(first, 2), lax.div(first, 2)]
            second_tile = extended_ref[1 - lax.rem(second, 2), lax.div(second, 2)]
            left.append(jnp.where(low, first_tile, second_tile))
            right += [weights * in_half[0], weights * in_half[1]]
        total = jnp.dot(
            jnp.concatenate(left, axis=1),
            jnp.concatenate(right, axis=0),
            preferred_element_type=jnp.float32,
        )
        along_r = [total[c * rows : (c + 1) * rows, :LANES] for c in range(components)]
        along_z = [total[c * rows : (c + 1) * rows, LANES:] for c in range(components)]
        values = [extended_ref[0, b, c * rows : (c + 1) * rows].astype(jnp.float32) for c in range(components)]
        inv_radius = 1.0 / radius_ref[:, here]
        momentum_ref[0, b] = along_r[3]
        momentum_ref[1, b] = rotated(values[3]) * inv_radius
        momentum_ref[2, b] = along_z[3]
        return [
            rotated(values[2]) * inv_radius - along_z[1],
            along_z[0] - along_r[2],
            along_r[1] + values[1] * inv_radius - rotated(values[0]) * inv_radius,
        ]

    stride = 2 * node_tiles
    together = SUBLANES // 2 if node_tiles % (SUBLANES // 2) == 0 else 1

    def tiles_at(q, carry):
        induction = [tile_of(q * together + i) for i in range(together)]
        for i in range(3):
            put_rows(induction_ref, i * mode_count * stride + 2 * q * together, stride, [tile[i] for tile in induction])
        return carry

    lax.fori_loop(0, node_tiles // together, tiles_at, 0)


def derive(received, from_prev, from_next, radial_blocks, axial_blocks, radius, columns, count):
    components, held, rows, _ = received[0].shape
    node_tiles = len(received) * held
    halo_tiles = from_prev.shape[1]
    out_rows = 3 * rows * node_tiles
    return pl.pallas_call(
        functools.partial(derive_kernel, count, len(received)),
        in_specs=[vmem()] * (len(received) + 5) + [pl.BlockSpec(memory_space=pltpu.SMEM)],
        out_specs=[vmem()] * 2,
        out_shape=[
            jax.ShapeDtypeStruct((out_rows, LANES), jnp.float32),
            jax.ShapeDtypeStruct((3, node_tiles, rows, LANES), jnp.float32),
        ],
        scratch_shapes=[pltpu.VMEM((2, node_tiles + 2 * halo_tiles, components * rows, LANES), jnp.bfloat16)],
        compiler_params=params(),
        cost_estimate=cost(),
    )(*received, from_prev, from_next, radial_blocks, axial_blocks, radius, columns)


def momentum_kernel(count, arrived, *refs):
    in_refs, (gradient_ref, out_ref, total_ref, sems) = refs[:arrived], refs[arrived:]
    me = lax.axis_index("mode")
    components, _, rows, _ = in_refs[0].shape
    tiles = gradient_ref.shape[1] // count
    holders = [(part, t) for part in range(arrived // count) for t in range(in_refs[part * count].shape[1])]
    mode_count = rows // 2
    stride = 2 * count * tiles
    out_rows = mode_count * stride
    copies = []
    for c in range(components):
        for step, offset in enumerate(offsets(count, SECOND_RETURN)):
            share = source_of(me, offset, count)
            for start in range(0, tiles, SUBLANES // 2):
                values = []
                for t in range(start, min(tiles, start + SUBLANES // 2)):
                    part, at = holders[t]
                    piece = in_refs[part * count + step][c, at].astype(jnp.float32)
                    values.append(piece - gradient_ref[c, share * tiles + t])
                put_rows(total_ref, c * out_rows + 2 * (share * tiles + start), stride, values)
        done = pl.ds(c * out_rows, out_rows)
        copies.append(pltpu.make_async_copy(total_ref.at[done], out_ref.at[done], sems.at[c]))
        copies[c].start()
    for copy in copies:
        copy.wait()


def momentum_of(received, gradient, count):
    components, _, rows, _ = received[0].shape
    shape = (components * rows * gradient.shape[1], LANES)
    return pl.pallas_call(
        functools.partial(momentum_kernel, count, len(received)),
        in_specs=[vmem()] * (len(received) + 1),
        out_specs=pl.BlockSpec(memory_space=pl.ANY),
        out_shape=jax.ShapeDtypeStruct(shape, jnp.float32),
        scratch_shapes=[pltpu.VMEM(shape, jnp.float32), pltpu.SemaphoreType.DMA((components,))],
        compiler_params=params(),
        cost_estimate=cost(),
    )(*received, gradient)


def whole_output(value, mode_count, width):
    value = value.reshape(3, mode_count, width // LANES, 2, LANES)
    return value.transpose(0, 1, 3, 2, 4).reshape(3, mode_count, 2, width)


def body(mode_fields, radius, radial_blocks, axial_blocks, block_columns, interface_nodes):
    _, mode_count, _, width = mode_fields.shape
    count = lax.axis_size("mode")
    rows = 2 * mode_count
    inverse, forward = tables(M, THETA, count)
    inverse, forward = jnp.asarray(inverse), jnp.asarray(forward)

    def joined(pieces):
        return [piece.reshape(piece.shape[:-3] + (rows, LANES)) for piece in pieces]

    tiles = width // count // LANES
    groups, spans = groups_of(tiles), spans_of(tiles)
    held = tiles // groups
    flow = load(mode_fields, 6)
    arrived = []
    for group in range(groups):
        order = offsets(count, FIRST_SEND)
        parcels = [pack(flow, 0, 6, offset, group * held, held) for offset in order[1:]]
        arrived.append(exchange(parcels, order[1:]))
    parcels = [(0, 6, 0, group * held, held) for group in range(groups)]
    *own, inverse, forward = pack_rest(flow, parcels, [inverse, forward])
    arrived[0][1:2], carried = lax.optimization_barrier((arrived[0][1:2], [inverse, forward]))
    order = offsets(count, SECOND_SEND)
    parcels = [(6, 12, offset) + span for span in spans for offset in order]
    *shares, later_inverse, later_forward = pack_rest(mode_fields, parcels, carried)
    local, physical = [], []
    for group in range(groups):
        if group == 0:
            tables_here = (later_inverse, later_forward)
        else:
            tables_here = (inverse, forward)
        *terms, velocity_magnetic = first_physics(joined([own[group]] + arrived[group]), *tables_here)
        local += exchange(terms, offsets(count, FIRST_RETURN))
        physical.append(velocity_magnetic)
    for group in range(groups):
        back, sent = slice(count if group == 0 else 0, None), slice(1, 2) if group == 0 else slice(2, count)
        local[back], shares[sent] = lax.optimization_barrier((local[back], shares[sent]))
    toward_prev, toward_next = interface(local, interface_nodes, count)
    halos = (from_behind(toward_next, "mer", 1), from_behind(toward_prev, "mer", -1))
    local, shares[count:] = lax.optimization_barrier((local, shares[count:]))
    lorentz = []
    for part, (begin, _) in enumerate(spans):
        sources = exchange(shares[part * count : (part + 1) * count], order)
        if part == len(spans) - 1:
            halos, sources[1] = lax.optimization_barrier((halos, sources[1]))
            induction, gradient = derive(
                local, *halos, radial_blocks, axial_blocks, radius.reshape(1, width), block_columns.T, count
            )
            sources, gradient = lax.optimization_barrier((sources, gradient))
        terms = list(second_physics(joined(sources), physical, begin, later_inverse, later_forward))
        lorentz += exchange(terms, offsets(count, SECOND_RETURN))
    momentum = momentum_of(lorentz, gradient, count)
    return (whole_output(induction, mode_count, width), whole_output(momentum, mode_count, width))


def solution(mesh):
    placed = (
        P(None, "mode", None, "mer"),
        P("mer"),
        P(None, None, "mer"),
        P(None, None, "mer"),
        P("mer", None),
        P("mer", None),
    )
    return jax.shard_map(
        body,
        mesh=mesh,
        in_specs=placed,
        out_specs=(P(None, "mode", None, "mer"), P(None, "mode", None, "mer")),
        check_vma=False,
    )
```

```python
import functools
import math

import jax
import jax.numpy as jnp
import ml_dtypes
import numpy as np
from jax import lax
from jax.experimental import pallas as pl
from jax.experimental.pallas import tpu as pltpu
from jax.sharding import PartitionSpec as P

M = 128
THETA = 256
BLK = 64
NNZB = 5
LANES = 128
VMEM_LIMIT = 24 * 1024 * 1024


def params(limit=VMEM_LIMIT):
    return pltpu.CompilerParams(vmem_limit_bytes=limit)


def vmem():
    return pl.BlockSpec(memory_space=pltpu.VMEM)


def cost():
    return pl.CostEstimate(flops=1024, bytes_accessed=1024, transcendentals=0)


FIRST_SEND, FIRST_RETURN, SECOND_SEND, SECOND_RETURN = 1, 1, 1, 1


def offsets(count, place):
    order = list(range(count - 1))
    order.insert(count - 1 if place is None else min(place, count - 1), count - 1)
    return order


def dest_of(me, offset, count):
    if count & (count - 1) == 0:
        return jnp.bitwise_xor(me, offset)
    return lax.rem(me + offset, count)


def source_of(me, offset, count):
    if count & (count - 1) == 0:
        return jnp.bitwise_xor(me, offset)
    return lax.rem(me + count - offset, count)


def exchange(pieces, order):
    count = lax.axis_size("mode")
    power = count & (count - 1) == 0
    received = []
    for piece, offset in zip(pieces, order):
        if offset == 0:
            received.append(piece)
            continue
        pairs = [(i, i ^ offset if power else (i + offset) % count) for i in range(count)]
        received.append(lax.ppermute(piece, "mode", pairs))
    return received


def from_behind(value, axis, steps):
    count = lax.axis_size(axis)
    initial, last = (max(0, -steps), min(count, count - steps))
    return lax.ppermute(value, axis, [(source, source + steps) for source in range(initial, last)])


def tables(mode_total, angle_total, share_count):
    mode_ids = np.arange(mode_total)
    angle_ids = np.arange(angle_total)
    phase = angle_ids[:, None] * mode_ids[None, :] % angle_total
    angle = phase.astype(np.float32) * np.float32(2.0 * math.pi / angle_total)
    weight = np.where(mode_ids == 0, 1.0, 2.0).astype(np.float32)
    cosines = np.cos(angle)
    sines = np.sin(angle)
    inverse = np.stack([weight * cosines, -weight * sines], axis=-1).astype(ml_dtypes.bfloat16)
    forward = np.stack([cosines.T, -sines.T], axis=1) / np.float32(angle_total)
    forward = forward.reshape(share_count, mode_total // share_count, 2, angle_total)
    forward = forward.transpose(0, 2, 1, 3).reshape(2 * mode_total, angle_total).astype(ml_dtypes.bfloat16)
    return (inverse.reshape(angle_total, 2 * mode_total), forward)


def groups_of(tiles):
    return 2 if tiles % 2 == 0 else 1


def spans_of(tiles):
    return [(0, tiles // 2), (tiles // 2, tiles - tiles // 2)] if tiles > 1 else [(0, tiles)]


def pieces_of(fields_ref, first, share, begin, out_ref):
    count = lax.axis_size("mode")
    tiles = fields_ref.shape[3] // count // LANES
    components, held = out_ref.shape[:2]
    pairs = []
    for t in range(held):
        start = pl.multiple_of((share * tiles + begin + t) * LANES, LANES)
        pairs.append((fields_ref.at[pl.ds(first, components), :, :, pl.ds(start, LANES)], out_ref.at[:, t]))
    return pairs


def run_copies(pairs, sems, beside=()):
    copies = [pltpu.make_async_copy(source, target, sems.at[i]) for i, (source, target) in enumerate(pairs)]
    for copy in copies:
        copy.start()
    for source, target in beside:
        target[...] = source[...]
    for copy in copies:
        copy.wait()


def load(fields, components):
    shape = (components,) + fields.shape[1:]

    def kernel(fields_ref, out_ref, sems):
        run_copies([(fields_ref.at[c], out_ref.at[c]) for c in range(components)], sems)

    return pl.pallas_call(
        kernel,
        in_specs=[pl.BlockSpec(memory_space=pltpu.HBM)],
        out_specs=vmem(),
        out_shape=jax.ShapeDtypeStruct(shape, fields.dtype),
        scratch_shapes=[pltpu.SemaphoreType.DMA((components,))],
        compiler_params=params(),
        cost_estimate=cost(),
    )(pltpu.with_memory_space_constraint(fields, pltpu.HBM))


def packed_shape(fields, first, last, held):
    return (last - first, held, fields.shape[1], 2, LANES)


def pack(fields, first, last, offset, begin, held):
    count = lax.axis_size("mode")
    shape = packed_shape(fields, first, last, held)

    def kernel(fields_ref, out_ref, sems):
        share = dest_of(lax.axis_index("mode"), offset, count)
        run_copies(pieces_of(fields_ref, first, share, begin, out_ref), sems)

    return pl.pallas_call(
        kernel,
        in_specs=[pl.BlockSpec(memory_space=pl.ANY)],
        out_specs=vmem(),
        out_shape=jax.ShapeDtypeStruct(shape, jnp.bfloat16),
        scratch_shapes=[pltpu.SemaphoreType.DMA((shape[1],))],
        compiler_params=params(),
        cost_estimate=cost(),
    )(fields)


def pack_rest(fields, parcels, carried):
    count = lax.axis_size("mode")
    shapes = [packed_shape(fields, first, last, held) for first, last, _, _, held in parcels]

    def kernel(fields_ref, *refs):
        inputs, refs = refs[: len(carried)], refs[len(carried) :]
        parcel_refs, outputs = refs[: len(parcels)], refs[len(parcels) : -1]
        me = lax.axis_index("mode")
        pairs = []
        for (first, _, offset, begin, _), parcel_ref in zip(parcels, parcel_refs):
            pairs += pieces_of(fields_ref, first, dest_of(me, offset, count), begin, parcel_ref)
        run_copies(pairs, refs[-1], zip(inputs, outputs))

    return pl.pallas_call(
        kernel,
        in_specs=[pl.BlockSpec(memory_space=pl.ANY)] + [vmem()] * len(carried),
        out_specs=[vmem()] * (len(parcels) + len(carried)),
        out_shape=[jax.ShapeDtypeStruct(shape, jnp.bfloat16) for shape in shapes]
        + [jax.ShapeDtypeStruct(value.shape, value.dtype) for value in carried],
        scratch_shapes=[pltpu.SemaphoreType.DMA((sum(shape[1] for shape in shapes),))],
        compiler_params=params(),
        cost_estimate=cost(),
    )(fields, *carried)


def cross(a, b):
    return [a[1] * b[2] - a[2] * b[1], a[2] * b[0] - a[0] * b[2], a[0] * b[1] - a[1] * b[0]]


def to_physical(order, in_refs, inverse, x_ref, store):
    me = lax.axis_index("mode")
    components, tiles, rows, _ = in_refs[0].shape
    for in_ref, offset in zip(in_refs, order):
        at = pl.multiple_of(source_of(me, offset, len(order)) * rows, rows)
        for c in range(components):
            for t in range(tiles):
                x_ref[c, pl.ds(at, rows), t * LANES : (t + 1) * LANES] = in_ref[c, t]
    for c in range(components):
        store(c, jnp.dot(inverse, x_ref[c], preferred_element_type=jnp.float32))


def to_modes(order, forward_ref, table_ref, product_ref, out_refs):
    count = len(order)
    me = lax.axis_index("mode")
    components, tiles, rows, _ = out_refs[0].shape
    for step, offset in enumerate(order):
        at = pl.multiple_of(dest_of(me, offset, count) * rows, rows)
        table_ref[step * rows : (step + 1) * rows] = forward_ref[pl.ds(at, rows)]
    for c in range(components):
        terms = jnp.dot(table_ref[...], product_ref[c], preferred_element_type=jnp.float32)
        terms = terms.astype(jnp.bfloat16)
        for step in range(count):
            for t in range(tiles):
                out_refs[step][c, t] = terms[step * rows : (step + 1) * rows, t * LANES : (t + 1) * LANES]


CHUNK = 32


def first_kernel(count, *refs):
    in_refs, (inverse_ref, forward_ref) = refs[:count], refs[count : count + 2]
    out_refs, (physical_ref, x_ref, product_ref, table_ref) = refs[count + 2 : 2 * count + 2], refs[2 * count + 2 :]

    def store(c, value):
        physical_ref[c] = value

    to_physical(offsets(count, FIRST_SEND), in_refs, inverse_ref[...], x_ref, store)
    for i in range(THETA // CHUNK):
        at = slice(i * CHUNK, (i + 1) * CHUNK)
        velocity = [physical_ref[c, at] for c in range(3)]
        magnetic = [physical_ref[c, at] for c in range(3, 6)]
        energy = 0.5 * (velocity[0] * velocity[0] + velocity[1] * velocity[1] + velocity[2] * velocity[2])
        for c, value in enumerate(cross(velocity, magnetic) + [energy]):
            product_ref[c, at] = value.astype(jnp.bfloat16)
    to_modes(offsets(count, FIRST_RETURN), forward_ref, table_ref, product_ref, out_refs)


def first_physics(received, inverse, forward):
    count = len(received)
    components, tiles, rows, _ = received[0].shape
    width = tiles * LANES
    return pl.pallas_call(
        functools.partial(first_kernel, count),
        in_specs=[vmem()] * (count + 2),
        out_specs=[vmem()] * (count + 1),
        out_shape=[jax.ShapeDtypeStruct((4, tiles, rows, LANES), jnp.bfloat16)] * count
        + [jax.ShapeDtypeStruct((components, THETA, width), jnp.float32)],
        scratch_shapes=[
            pltpu.VMEM((components, 2 * M, width), jnp.bfloat16),
            pltpu.VMEM((4, THETA, width), jnp.bfloat16),
            pltpu.VMEM((2 * M, THETA), jnp.bfloat16),
        ],
        compiler_params=params(),
        cost_estimate=cost(),
    )(*received, inverse, forward)


def second_kernel(count, groups, begin, *refs):
    in_refs, refs = refs[:count], refs[count:]
    first_refs, (inverse_ref, forward_ref) = refs[:groups], refs[groups : groups + 2]
    out_refs, (physical_ref, x_ref, product_ref, table_ref) = refs[groups + 2 : groups + 2 + count], refs[groups + 2 + count :]
    in_group = first_refs[0].shape[2] // LANES

    def store(c, value):
        physical_ref[c] = value

    to_physical(offsets(count, SECOND_SEND), in_refs, inverse_ref[...], x_ref, store)
    for t in range(in_refs[0].shape[1]):
        lanes = slice(t * LANES, (t + 1) * LANES)
        first_ref, place = first_refs[(begin + t) // in_group], (begin + t) % in_group
        first_lanes = slice(place * LANES, (place + 1) * LANES)
        for i in range(THETA // CHUNK):
            at = slice(i * CHUNK, (i + 1) * CHUNK)
            velocity = [first_ref[c, at, first_lanes] for c in range(3)]
            magnetic = [first_ref[c, at, first_lanes] for c in range(3, 6)]
            current = [physical_ref[c, at, lanes] for c in range(3)]
            vorticity = [physical_ref[c, at, lanes] for c in range(3, 6)]
            lorentz = [a + b for a, b in zip(cross(current, magnetic), cross(velocity, vorticity))]
            for c, value in enumerate(lorentz):
                product_ref[c, at, lanes] = value.astype(jnp.bfloat16)
    to_modes(offsets(count, SECOND_RETURN), forward_ref, table_ref, product_ref, out_refs)


def second_physics(received, physical, begin, inverse, forward):
    count, groups = len(received), len(physical)
    components, tiles, rows, _ = received[0].shape
    width = tiles * LANES
    return pl.pallas_call(
        functools.partial(second_kernel, count, groups, begin),
        in_specs=[vmem()] * (count + groups + 2),
        out_specs=[vmem()] * count,
        out_shape=[jax.ShapeDtypeStruct((3, tiles, rows, LANES), jnp.bfloat16)] * count,
        scratch_shapes=[
            pltpu.VMEM((components, THETA, width), jnp.float32),
            pltpu.VMEM((components, 2 * M, width), jnp.bfloat16),
            pltpu.VMEM((3, THETA, width), jnp.bfloat16),
            pltpu.VMEM((2 * M, THETA), jnp.bfloat16),
        ],
        compiler_params=params(),
        cost_estimate=cost(),
    )(*received, *physical, inverse, forward)


def tiles_of(in_refs, count):
    me = lax.axis_index("mode")
    components, held, rows, _ = in_refs[0].shape
    groups = len(in_refs) // count
    for group in range(groups):
        for step, offset in enumerate(offsets(count, FIRST_RETURN)):
            share = source_of(me, offset, count)
            for t in range(held):
                at = share * (groups * held) + group * held + t
                yield at, in_refs[group * count + step][:, t].reshape(components * rows, LANES)


def interface_kernel(count, arrived, *refs):
    in_refs, (nodes_ref, prev_ref, next_ref) = refs[:arrived], refs[arrived:]
    components, _, rows, _ = in_refs[0].shape
    halo = nodes_ref.shape[1]
    totals = [jnp.zeros((components * rows, halo), jnp.float32) for _ in range(2)]
    inner = lax.broadcasted_iota(jnp.int32, (LANES, halo), 0)
    for at, values in tiles_of(in_refs, count):
        ids = inner + at * LANES
        for way in range(2):
            chosen = jnp.where(ids == nodes_ref[way : way + 1, :], 1.0, 0.0).astype(jnp.bfloat16)
            totals[way] += jnp.dot(values, chosen, preferred_element_type=jnp.float32)
    for out_ref, total in zip((prev_ref, next_ref), totals):
        picked = total.astype(jnp.bfloat16)
        for c in range(components):
            for t in range(halo // LANES):
                out_ref[c, t] = picked[c * rows : (c + 1) * rows, t * LANES : (t + 1) * LANES]


def interface(received, interface_nodes, count):
    components, _, rows, _ = received[0].shape
    halo = interface_nodes.shape[1]
    shape = jax.ShapeDtypeStruct((components, halo // LANES, rows, LANES), jnp.bfloat16)
    return pl.pallas_call(
        functools.partial(interface_kernel, count, len(received)),
        in_specs=[vmem()] * (len(received) + 1),
        out_specs=[vmem()] * 2,
        out_shape=[shape] * 2,
        compiler_params=params(),
        cost_estimate=cost(),
    )(*received, interface_nodes)


SUBLANES = 8


def interleaved(parts):
    parts = list(parts)
    row = lax.broadcasted_iota(jnp.int32, parts[0].shape, 1)
    for distance in (1, 2, 4):
        upper = jnp.bitwise_and(row, distance) != 0
        for k in range(SUBLANES):
            if k & distance == 0:
                first, second = parts[k], parts[k + distance]
                parts[k] = jnp.where(upper, pltpu.roll(second, distance, 1), first)
                parts[k + distance] = jnp.where(upper, second, pltpu.roll(first, SUBLANES - distance, 1))
    return parts


def put_rows(out_ref, first, stride, tiles):
    modes = tiles[0].shape[0] // 2
    parts = [part for tile in tiles for part in (tile[:modes], tile[modes:])]
    if len(parts) == SUBLANES:
        whole = interleaved([part.reshape(modes // SUBLANES, SUBLANES, LANES) for part in parts])
        for mode in range(modes):
            here = pl.ds(pl.multiple_of(first + mode * stride, SUBLANES), SUBLANES)
            out_ref[here, :] = whole[mode % SUBLANES][mode // SUBLANES]
    else:
        for i, part in enumerate(parts):
            out_ref[pl.ds(first + i, modes, stride=stride), :] = part


def derive_kernel(count, arrived, *refs):
    in_refs = refs[:arrived]
    prev_ref, next_ref, radial_ref, axial_ref, radius_ref, columns_ref = refs[arrived : arrived + 6]
    induction_ref, momentum_ref, extended_ref = refs[arrived + 6 :]
    me = lax.axis_index("mode")
    components, held, rows, _ = in_refs[0].shape
    mode_count = rows // 2
    node_tiles = arrived * held
    halo_tiles = prev_ref.shape[1]

    def extend(at, tile):
        extended_ref[0, at] = tile
        extended_ref[1, at] = jnp.concatenate([tile[:, BLK:], tile[:, :BLK]], axis=1)

    for at, tile in tiles_of(in_refs, count):
        extend(at, tile)
    for t in range(halo_tiles):
        extend(node_tiles + t, prev_ref[:, t].reshape(components * rows, LANES))
        extend(node_tiles + halo_tiles + t, next_ref[:, t].reshape(components * rows, LANES))
    modes = (lax.broadcasted_iota(jnp.int32, (mode_count, LANES), 0) + me * mode_count).astype(jnp.float32)
    low = lax.broadcasted_iota(jnp.int32, (components * rows, LANES), 1) < BLK
    lane = lax.broadcasted_iota(jnp.int32, (1, 2 * LANES), 1)
    in_first = jnp.where(lax.rem(lane, LANES) < BLK, 1.0, 0.0)
    in_half = [in_first.astype(jnp.bfloat16), (1.0 - in_first).astype(jnp.bfloat16)]

    def rotated(values):
        return jnp.concatenate([-modes * values[mode_count:], modes * values[:mode_count]], axis=0)

    def tile_of(b):
        here = pl.ds(pl.multiple_of(b * LANES, LANES), LANES)
        left, right = [], []
        for k in range(NNZB):
            weights = jnp.concatenate([radial_ref[k, :, here], axial_ref[k, :, here]], axis=1)
            first, second = columns_ref[k, 2 * b], columns_ref[k, 2 * b + 1]
            first_tile = extended_ref[lax.rem(first, 2), lax.div(first, 2)]
            second_tile = extended_ref[1 - lax.rem(second, 2), lax.div(second, 2)]
            left.append(jnp.where(low, first_tile, second_tile))
            right += [weights * in_half[0], weights * in_half[1]]
        total = jnp.dot(
            jnp.concatenate(left, axis=1),
            jnp.concatenate(right, axis=0),
            preferred_element_type=jnp.float32,
        )
        along_r = [total[c * rows : (c + 1) * rows, :LANES] for c in range(components)]
        along_z = [total[c * rows : (c + 1) * rows, LANES:] for c in range(components)]
        values = [extended_ref[0, b, c * rows : (c + 1) * rows].astype(jnp.float32) for c in range(components)]
        inv_radius = 1.0 / radius_ref[:, here]
        momentum_ref[0, b] = along_r[3]
        momentum_ref[1, b] = rotated(values[3]) * inv_radius
        momentum_ref[2, b] = along_z[3]
        return [
            rotated(values[2]) * inv_radius - along_z[1],
            along_z[0] - along_r[2],
            along_r[1] + values[1] * inv_radius - rotated(values[0]) * inv_radius,
        ]

    stride = 2 * node_tiles
    together = SUBLANES // 2 if node_tiles % (SUBLANES // 2) == 0 else 1

    def tiles_at(q, carry):
        induction = [tile_of(q * together + i) for i in range(together)]
        for i in range(3):
            put_rows(induction_ref, i * mode_count * stride + 2 * q * together, stride, [tile[i] for tile in induction])
        return carry

    lax.fori_loop(0, node_tiles // together, tiles_at, 0, unroll=True)


def derive(received, from_prev, from_next, radial_blocks, axial_blocks, radius, columns, count):
    components, held, rows, _ = received[0].shape
    node_tiles = len(received) * held
    halo_tiles = from_prev.shape[1]
    out_rows = 3 * rows * node_tiles
    return pl.pallas_call(
        functools.partial(derive_kernel, count, len(received)),
        in_specs=[vmem()] * (len(received) + 5) + [pl.BlockSpec(memory_space=pltpu.SMEM)],
        out_specs=[vmem()] * 2,
        out_shape=[
            jax.ShapeDtypeStruct((out_rows, LANES), jnp.float32),
            jax.ShapeDtypeStruct((3, node_tiles, rows, LANES), jnp.float32),
        ],
        scratch_shapes=[pltpu.VMEM((2, node_tiles + 2 * halo_tiles, components * rows, LANES), jnp.bfloat16)],
        compiler_params=params(),
        cost_estimate=cost(),
    )(*received, from_prev, from_next, radial_blocks, axial_blocks, radius, columns)


def momentum_kernel(count, arrived, *refs):
    in_refs, (gradient_ref, out_ref, total_ref, sems) = refs[:arrived], refs[arrived:]
    me = lax.axis_index("mode")
    components, _, rows, _ = in_refs[0].shape
    tiles = gradient_ref.shape[1] // count
    holders = [(part, t) for part in range(arrived // count) for t in range(in_refs[part * count].shape[1])]
    mode_count = rows // 2
    stride = 2 * count * tiles
    out_rows = mode_count * stride
    copies = []
    for c in range(components):
        for step, offset in enumerate(offsets(count, SECOND_RETURN)):
            share = source_of(me, offset, count)
            for start in range(0, tiles, SUBLANES // 2):
                values = []
                for t in range(start, min(tiles, start + SUBLANES // 2)):
                    part, at = holders[t]
                    piece = in_refs[part * count + step][c, at].astype(jnp.float32)
                    values.append(piece - gradient_ref[c, share * tiles + t])
                put_rows(total_ref, c * out_rows + 2 * (share * tiles + start), stride, values)
        done = pl.ds(c * out_rows, out_rows)
        copies.append(pltpu.make_async_copy(total_ref.at[done], out_ref.at[done], sems.at[c]))
        copies[c].start()
    for copy in copies:
        copy.wait()


def momentum_of(received, gradient, count):
    components, _, rows, _ = received[0].shape
    shape = (components * rows * gradient.shape[1], LANES)
    return pl.pallas_call(
        functools.partial(momentum_kernel, count, len(received)),
        in_specs=[vmem()] * (len(received) + 1),
        out_specs=pl.BlockSpec(memory_space=pl.ANY),
        out_shape=jax.ShapeDtypeStruct(shape, jnp.float32),
        scratch_shapes=[pltpu.VMEM(shape, jnp.float32), pltpu.SemaphoreType.DMA((components,))],
        compiler_params=params(),
        cost_estimate=cost(),
    )(*received, gradient)


def whole_output(value, mode_count, width):
    value = value.reshape(3, mode_count, width // LANES, 2, LANES)
    return value.transpose(0, 1, 3, 2, 4).reshape(3, mode_count, 2, width)


def body(mode_fields, radius, radial_blocks, axial_blocks, block_columns, interface_nodes):
    _, mode_count, _, width = mode_fields.shape
    count = lax.axis_size("mode")
    rows = 2 * mode_count
    inverse, forward = tables(M, THETA, count)
    inverse, forward = jnp.asarray(inverse), jnp.asarray(forward)

    def joined(pieces):
        return [piece.reshape(piece.shape[:-3] + (rows, LANES)) for piece in pieces]

    tiles = width // count // LANES
    groups, spans = groups_of(tiles), spans_of(tiles)
    held = tiles // groups
    flow = load(mode_fields, 6)
    arrived = []
    for group in range(groups):
        order = offsets(count, FIRST_SEND)
        parcels = [pack(flow, 0, 6, offset, group * held, held) for offset in order[1:]]
        arrived.append(exchange(parcels, order[1:]))
    parcels = [(0, 6, 0, group * held, held) for group in range(groups)]
    *own, inverse, forward = pack_rest(flow, parcels, [inverse, forward])
    arrived[0][1:2], carried = lax.optimization_barrier((arrived[0][1:2], [inverse, forward]))
    order = offsets(count, SECOND_SEND)
    parcels = [(6, 12, offset) + span for span in spans for offset in order]
    *shares, later_inverse, later_forward = pack_rest(mode_fields, parcels, carried)
    local, physical = [], []
    for group in range(groups):
        if group == 0:
            tables_here = (later_inverse, later_forward)
        else:
            tables_here = (inverse, forward)
        *terms, velocity_magnetic = first_physics(joined([own[group]] + arrived[group]), *tables_here)
        local += exchange(terms, offsets(count, FIRST_RETURN))
        physical.append(velocity_magnetic)
    for group in range(groups):
        back, sent = slice(count if group == 0 else 0, None), slice(1, 2) if group == 0 else slice(2, count)
        local[back], shares[sent] = lax.optimization_barrier((local[back], shares[sent]))
    toward_prev, toward_next = interface(local, interface_nodes, count)
    halos = (from_behind(toward_next, "mer", 1), from_behind(toward_prev, "mer", -1))
    local, shares[count:] = lax.optimization_barrier((local, shares[count:]))
    lorentz = []
    for part, (begin, _) in enumerate(spans):
        sources = exchange(shares[part * count : (part + 1) * count], order)
        if part == len(spans) - 1:
            sources, halos = lax.optimization_barrier((sources, halos))
        terms = list(second_physics(joined(sources), physical, begin, later_inverse, later_forward))
        if part == len(spans) - 1:
            terms, radius = lax.optimization_barrier((terms, radius))
        lorentz += exchange(terms, offsets(count, SECOND_RETURN))
    induction, gradient = derive(
        local, *halos, radial_blocks, axial_blocks, radius.reshape(1, width), block_columns.T, count
    )
    momentum = momentum_of(lorentz, gradient, count)
    return (whole_output(induction, mode_count, width), whole_output(momentum, mode_count, width))


def solution(mesh):
    placed = (
        P(None, "mode", None, "mer"),
        P("mer"),
        P(None, None, "mer"),
        P(None, None, "mer"),
        P("mer", None),
        P("mer", None),
    )
    return jax.shard_map(
        body,
        mesh=mesh,
        in_specs=placed,
        out_specs=(P(None, "mode", None, "mer"), P(None, "mode", None, "mer")),
        check_vma=False,
    )
```
